32 devices in a mesh: gx: 8 (over z, core), gy: 4 (over y, x).
Axes of the slice: x: 2, y: 2, z: 4, core: 2. Of those that a mesh axis runs over, the one named last changes fastest.
Arguments:
- right_side: float32 [32, 128, 512], P(None, 'gx', 'gy'), may hold values from -8 to 8
- kappa_sq: float32 [32, 128, 512], P(None, 'gx', 'gy'), may hold values from 0.0001 to 0.003
- cond_x: float32 [32, 128, 512], P(None, 'gx', 'gy'), may hold values from 0.3 to 3
- cond_y: float32 [32, 128, 512], P(None, 'gx', 'gy'), may hold values from 0.3 to 3
- cond_z: float32 [32, 128, 512], P(None, 'gx', 'gy'), may hold values from 0.05 to 2
Outputs:
- solution_field: float32 [32, 128, 512], P(None, 'gx', 'gy')
- residual: float32 [32, 128, 512], P(None, 'gx', 'gy')
The draws below stay inside these ranges and needn't reach their ends.
All inputs are finite; a program needn't handle non-finite values.
Results may differ from the reference program's by a relative error of at most 0.00014.
Values sent between devices are 32-bit elements; how exact they have to be, the bound alone decides.
No kernel may reach another device: no remote copies, remote signals or barrier semaphores. Data moves between devices by JAX's collectives and lax.ppermute only.
A program may use at most 128 MiB of HBM per device.

```python
import math
import jax
import jax.numpy as jnp
from jax import lax

NZ = 32
LEVELS = 4
COARSE_SWEEPS = 16
NX = 128
NY = 512


def block_scale(key, dims, pieces, least, high):
    def one(position, shards_of):
        heights = jax.random.uniform(jax.random.fold_in(jax.random.fold_in(key, 6), position), (shards_of,), jnp.float32, least / len(pieces), high / len(pieces))
        return jnp.repeat(jnp.exp(heights), dims[position] // shards_of).reshape((-1,) + (1,) * (len(dims) - position - 1))

    loudness = one(*pieces[0])
    for cut in pieces[1:]:
        loudness = loudness * one(*cut)
    return loudness


def bell_draw(own_key, dims, scale, reach, cuts=(), kind=jnp.bfloat16):
    values = scale * jax.random.normal(own_key, dims, jnp.float32)
    if cuts:
        values = values * block_scale(own_key, dims, cuts, -0.22, 0.18)
    return jnp.clip(values, -reach, reach).astype(kind)


def setup_inputs(seed: int = 0) -> dict:
    streams_of = jax.random.split(jax.random.key(seed), 6)
    right_side = bell_draw(streams_of[0], (NZ, NX, NY), 1.0, 8.0, ((1, 8), (2, 4)), jnp.float32)
    kappa_sq = jnp.clip(jnp.exp(math.log(0.003) - 3.4011974 * jax.random.uniform(streams_of[1], (NZ, NX, NY), jnp.float32) ** block_scale(streams_of[1], (NZ, NX, NY), ((1, 8), (2, 4)), -0.2, 0.2)), 0.0001, 0.003)
    cond_x = jnp.clip(jnp.exp(math.log(3.0) - 2.3025851 * jax.random.uniform(streams_of[2], (NZ, NX, NY), jnp.float32) ** block_scale(streams_of[2], (NZ, NX, NY), ((1, 8), (2, 4)), -0.2, 0.2)), 0.3, 3.0)
    cond_y = jnp.clip(jnp.exp(math.log(3.0) - 2.3025851 * jax.random.uniform(streams_of[3], (NZ, NX, NY), jnp.float32) ** block_scale(streams_of[3], (NZ, NX, NY), ((1, 8), (2, 4)), -0.2, 0.2)), 0.3, 3.0)
    cond_z = jnp.clip(jnp.exp(math.log(2.0) - 3.6888794 * jax.random.uniform(streams_of[4], (NZ, NX, NY), jnp.float32) ** block_scale(streams_of[4], (NZ, NX, NY), ((1, 8), (2, 4)), -0.2, 0.2)), 0.05, 2.0)
    return {"right_side": right_side, "kappa_sq": kappa_sq, "cond_x": cond_x, "cond_y": cond_y, "cond_z": cond_z}


OMEGA = 0.8


def pad_plane(u):
    return jnp.pad(u, ((0, 0), (1, 1), (1, 1)))


def fine_coeffs(kappa_sq, cond_x, cond_y, cond_z):
    px = jnp.pad(cond_x, ((0, 0), (1, 1), (0, 0)))
    py = jnp.pad(cond_y, ((0, 0), (0, 0), (1, 1)))
    pz = jnp.pad(cond_z, ((1, 1), (0, 0), (0, 0)))
    x_up = 0.5 * (cond_x + px[:, 2:, :])
    x_low = 0.5 * (cond_x + px[:, :-2, :])
    y_up = 0.5 * (cond_y + py[:, :, 2:])
    y_low = 0.5 * (cond_y + py[:, :, :-2])
    z_up = 0.5 * (cond_z + pz[2:])
    z_low = 0.5 * (cond_z + pz[:-2])
    return (kappa_sq, x_up, x_low, y_up, y_low, z_up, z_low)


def apply_op(field, padded, coeffs):
    kappa, x_up, x_low, y_up, y_low, z_up, z_low = coeffs
    zpad = jnp.pad(field, ((1, 1), (0, 0), (0, 0)))
    out = kappa * field + x_up * (field - padded[:, 2:, 1:-1]) + x_low * (field - padded[:, :-2, 1:-1])
    out = out + y_up * (field - padded[:, 1:-1, 2:]) + y_low * (field - padded[:, 1:-1, :-2])
    return out + z_up * (field - zpad[2:]) + z_low * (field - zpad[:-2])


def line_factors(coeffs):
    kappa, x_up, x_low, y_up, y_low, z_up, z_low = coeffs
    diag = kappa + x_up + x_low + y_up + y_low + z_up + z_low
    upper_src = z_up.at[-1].set(jnp.zeros_like(z_up[-1]))

    def factor_step(upper_prev, planes):
        diag_k, low_k, up_k = planes
        inv = 1.0 / (diag_k + low_k * upper_prev)
        upper = -up_k * inv
        return upper, (inv, upper)

    start = jnp.zeros_like(diag[0])
    unused, stacked = lax.scan(factor_step, start, (diag, z_low, upper_src), unroll=True)
    return stacked


def line_solve(rhs, factors, z_low):
    inverses, uppers = factors

    def forward_step(prev, planes):
        rhs_k, low_k, inv_k = planes
        value = (rhs_k + low_k * prev) * inv_k
        return value, value

    start = jnp.zeros_like(rhs[0])
    unused, forward = lax.scan(forward_step, start, (rhs, z_low, inverses), unroll=True)

    def back_step(after, planes):
        fwd_k, up_k = planes
        value = fwd_k - up_k * after
        return value, value

    unused, result = lax.scan(back_step, start, (forward, uppers), reverse=True, unroll=True)
    return result


def mean_four(field):
    depth, rows, cols = field.shape
    return field.reshape(depth, rows // 2, 2, cols // 2, 2).mean(axis=(2, 4))


def coarsen(coeffs):
    kappa, x_up, x_low, y_up, y_low, z_up, z_low = coeffs
    depth, rows, cols = kappa.shape
    shape = (depth, rows // 2, 2, cols // 2, 2)
    xu_c = x_up.reshape(shape)[:, :, 1].mean(axis=-1) * 0.25
    xl_c = x_low.reshape(shape)[:, :, 0].mean(axis=-1) * 0.25
    yu_c = y_up.reshape(shape)[:, :, :, :, 1].mean(axis=2) * 0.25
    yl_c = y_low.reshape(shape)[:, :, :, :, 0].mean(axis=2) * 0.25
    return (mean_four(kappa), xu_c, xl_c, yu_c, yl_c, mean_four(z_up), mean_four(z_low))


def prolong(padded):
    depth = padded.shape[0]
    rows = padded.shape[1] - 2
    cols = padded.shape[2] - 2
    centre = padded[:, 1:-1, :]
    even = 0.75 * centre + 0.25 * padded[:, :-2, :]
    odd = 0.75 * centre + 0.25 * padded[:, 2:, :]
    spread = jnp.stack([even, odd], axis=2).reshape(depth, 2 * rows, cols + 2)
    centre = spread[:, :, 1:-1]
    even = 0.75 * centre + 0.25 * spread[:, :, :-2]
    odd = 0.75 * centre + 0.25 * spread[:, :, 2:]
    return jnp.stack([even, odd], axis=3).reshape(depth, 2 * rows, 2 * cols)


def coarse_solve(rhs, coeffs):
    factors = line_factors(coeffs)
    field = OMEGA * line_solve(rhs, factors, coeffs[6])
    for sweep in range(COARSE_SWEEPS - 1):
        defect = rhs - apply_op(field, pad_plane(field), coeffs)
        field = field + OMEGA * line_solve(defect, factors, coeffs[6])
    return field


def cycle(rhs, coeffs, level):
    if level == LEVELS:
        return coarse_solve(rhs, coeffs)
    factors = line_factors(coeffs)
    field = OMEGA * line_solve(rhs, factors, coeffs[6])
    defect = rhs - apply_op(field, pad_plane(field), coeffs)
    correction = cycle(mean_four(defect), coarsen(coeffs), level + 1)
    field = field + prolong(pad_plane(correction))
    defect = rhs - apply_op(field, pad_plane(field), coeffs)
    return field + OMEGA * line_solve(defect, factors, coeffs[6])


def reference(right_side, kappa_sq, cond_x, cond_y, cond_z):
    coeffs = fine_coeffs(kappa_sq, cond_x, cond_y, cond_z)
    solution_field = cycle(right_side, coeffs, 0)
    residual = right_side - apply_op(solution_field, pad_plane(solution_field), coeffs)
    return solution_field, residual
```

```python
import functools

import jax
import jax.numpy as jnp
from jax import lax
from jax.experimental import pallas as pl
from jax.experimental.pallas import tpu as pltpu
from jax.sharding import PartitionSpec as P

LEVELS = 4
COARSE_SWEEPS = 16


OMEGA = 0.8


def with_halo(cells, sides, width):
    for axis, dim in sides:
        count = lax.axis_size(axis)
        ends = count - 1
        head = lax.slice_in_dim(cells, 0, width, axis=dim)
        tail = lax.slice_in_dim(cells, cells.shape[dim] - width, cells.shape[dim], axis=dim)
        cells = jnp.concatenate(
            [
                lax.ppermute(tail, axis, [(i, (i + 1) % count) for i in range(ends)]),
                cells,
                lax.ppermute(head, axis, [((i + 1) % count, i) for i in range(ends)]),
            ],
            axis=dim,
        )
    return cells


def apply_op(field, padded, coeffs):
    kappa, x_up, x_low, y_up, y_low, z_up, z_low = coeffs
    zpad = jnp.pad(field, ((1, 1), (0, 0), (0, 0)))
    out = (
        kappa * field
        + x_up * (field - padded[:, 2:, 1:-1])
        + x_low * (field - padded[:, :-2, 1:-1])
    )
    out = out + y_up * (field - padded[:, 1:-1, 2:]) + y_low * (field - padded[:, 1:-1, :-2])
    return out + z_up * (field - zpad[2:]) + z_low * (field - zpad[:-2])


def face_pad(field):
    return with_halo(field, (("gx", 1), ("gy", 2)), 1)


def line_factors(coeffs):
    kappa, x_up, x_low, y_up, y_low, z_up, z_low = coeffs
    diag = kappa + x_up + x_low + y_up + y_low + z_up + z_low
    upper_src = z_up.at[-1].set(jnp.zeros_like(z_up[-1]))

    def factor_step(upper_prev, planes):
        diag_k, low_k, up_k = planes
        inv = 1.0 / (diag_k + low_k * upper_prev)
        upper = -up_k * inv
        return (upper, (inv, upper))

    start = jnp.zeros_like(diag[0])
    unused, stacked = lax.scan(factor_step, start, (diag, z_low, upper_src), unroll=True)
    return stacked


def line_solve(rhs, factors, z_low):
    inverses, uppers = factors

    def forward_step(prev, planes):
        rhs_k, low_k, inv_k = planes
        value = (rhs_k + low_k * prev) * inv_k
        return (value, value)

    start = jnp.zeros_like(rhs[0])
    unused, forward = lax.scan(forward_step, start, (rhs, z_low, inverses), unroll=True)

    def back_step(after, planes):
        fwd_k, up_k = planes
        value = fwd_k - up_k * after
        return (value, value)

    unused, result = lax.scan(back_step, start, (forward, uppers), reverse=True, unroll=True)
    return result


def mean_four(field):
    depth, rows, cols = field.shape
    return field.reshape(depth, rows // 2, 2, cols // 2, 2).mean(axis=(2, 4))


def coarsen(coeffs):
    kappa, x_up, x_low, y_up, y_low, z_up, z_low = coeffs
    depth, rows, cols = kappa.shape
    shape = (depth, rows // 2, 2, cols // 2, 2)
    xu_c = x_up.reshape(shape)[:, :, 1].mean(axis=-1) * 0.25
    xl_c = x_low.reshape(shape)[:, :, 0].mean(axis=-1) * 0.25
    yu_c = y_up.reshape(shape)[:, :, :, :, 1].mean(axis=2) * 0.25
    yl_c = y_low.reshape(shape)[:, :, :, :, 0].mean(axis=2) * 0.25
    return (mean_four(kappa), xu_c, xl_c, yu_c, yl_c, mean_four(z_up), mean_four(z_low))


def prolong(padded):
    depth = padded.shape[0]
    rows = padded.shape[1] - 2
    cols = padded.shape[2] - 2
    centre = padded[:, 1:-1, :]
    even = 0.75 * centre + 0.25 * padded[:, :-2, :]
    odd = 0.75 * centre + 0.25 * padded[:, 2:, :]
    spread = jnp.stack([even, odd], axis=2).reshape(depth, 2 * rows, cols + 2)
    centre = spread[:, :, 1:-1]
    even = 0.75 * centre + 0.25 * spread[:, :, :-2]
    odd = 0.75 * centre + 0.25 * spread[:, :, 2:]
    return jnp.stack([even, odd], axis=3).reshape(depth, 2 * rows, 2 * cols)


def coarse_solve(rhs, coeffs):
    factors = line_factors(coeffs)
    field = OMEGA * line_solve(rhs, factors, coeffs[6])

    def spread_sweep(sweep, current):
        padded = with_halo(current, (("gx", 1), ("gy", 2)), 1)
        defect = rhs - apply_op(current, padded, coeffs)
        return current + OMEGA * line_solve(defect, factors, coeffs[6])

    field = lax.fori_loop(0, COARSE_SWEEPS - 1, spread_sweep, field)
    return field


def cycle(rhs, coeffs, level):
    if level == LEVELS:
        return coarse_solve(rhs, coeffs)
    factors = line_factors(coeffs)
    field = OMEGA * line_solve(rhs, factors, coeffs[6])
    padded = face_pad(field)
    defect = rhs - apply_op(field, padded, coeffs)
    correction = cycle(mean_four(defect), coarsen(coeffs), level + 1)
    rimmed = with_halo(correction, (("gx", 1), ("gy", 2)), 1)
    field = field + prolong(rimmed)
    padded = face_pad(field)
    defect = rhs - apply_op(field, padded, coeffs)
    return field + OMEGA * line_solve(defect, factors, coeffs[6])


def spread_body(right_side, kappa_sq, cond_x, cond_y, cond_z):
    padded_x = with_halo(cond_x, (("gx", 1),), 1)
    padded_y = with_halo(cond_y, (("gy", 2),), 1)
    padded_z = jnp.pad(cond_z, ((1, 1), (0, 0), (0, 0)))
    x_up = 0.5 * (cond_x + padded_x[:, 2:, :])
    x_low = 0.5 * (cond_x + padded_x[:, :-2, :])
    y_up = 0.5 * (cond_y + padded_y[:, :, 2:])
    y_low = 0.5 * (cond_y + padded_y[:, :, :-2])
    z_up = 0.5 * (cond_z + padded_z[2:])
    z_low = 0.5 * (cond_z + padded_z[:-2])
    coeffs = (kappa_sq, x_up, x_low, y_up, y_low, z_up, z_low)
    solution_field = cycle(right_side, coeffs, 0)
    residual = right_side - apply_op(solution_field, face_pad(solution_field), coeffs)
    return (solution_field, residual)


F32 = jnp.float32
BF16 = jnp.bfloat16
NZ = 32
TX, TY = 16, 128
HALO = 8
VMEM = pl.BlockSpec(memory_space=pltpu.VMEM)
ANY = pl.BlockSpec(memory_space=pl.ANY)


def iota(shape, dim):
    return lax.broadcasted_iota(jnp.int32, shape, dim)


def shift(x, by, axis):
    return pltpu.roll(x, by % x.shape[axis], axis)


def mix(x, weights):
    high = x.astype(BF16)
    rest = x - high.astype(F32)
    mid = rest.astype(BF16)
    low = (rest - mid.astype(F32)).astype(BF16)
    dot = functools.partial(jnp.dot, preferred_element_type=F32)
    return dot(low, weights) + dot(mid, weights) + dot(high, weights)


def plane(k, rows):
    return pl.ds(pl.multiple_of(k * rows, rows), rows)


def matrix(mask):
    return mask.astype(F32).astype(BF16)


def pair_matrix(fine, coarse, offsets=(0, 1)):
    y, j = iota((fine, coarse), 0), iota((fine, coarse), 1)
    keep = y // 2 == j
    if len(offsets) == 1:
        keep = keep & (y % 2 == offsets[0])
    return matrix(keep)


def spread_matrix(coarse, fine_index, parent, partner, valid):
    j = iota((coarse, fine_index.shape[1]), 0)
    weights = jnp.where(j == parent, 0.75, jnp.where(j == partner, 0.25, 0.0))
    return jnp.where(valid, weights, 0.0).astype(BF16)


def pack_kernel(f, kappa, cx, cy, cz, x_head, x_tail, y_head, y_tail):
    group = iota((8, 128), 1) // 8
    refs = (f, kappa, cx, cy, cz)
    for a, ref in enumerate(refs):
        cells = ref[...].reshape(NZ, TX, TY)
        x_head[pl.ds(a * NZ * HALO, NZ * HALO), :] = cells[:, :HALO].reshape(NZ * HALO, TY)
        x_tail[pl.ds(a * NZ * HALO, NZ * HALO), :] = cells[:, TX - HALO :].reshape(NZ * HALO, TY)
    for half in range(2):
        for a, ref in enumerate(refs):
            for zo in range(2):
                head = jnp.zeros((8, 128), F32)
                tail = jnp.zeros((8, 128), F32)
                for zi in range(16):
                    cells = ref[pl.ds((zo * 16 + zi) * TX + 8 * half, 8), :]
                    cells = shift(cells, 8 * zi, 1)
                    head = jnp.where(group == zi, cells, head)
                    tail = jnp.where(group == (zi - 1) % 16, cells, tail)
                at = ((half * 5 + a) * 2 + zo) * 8
                y_head[pl.ds(at, 8), :] = head
                y_tail[pl.ds(at, 8), :] = tail


def coarse_rows(ref, row, rows):
    return ref[pl.ds(row, NZ, stride=rows), :]


def coeff_kernel(kappa, cx, cy, cz, out):
    iy = lax.axis_index("gy")
    y, lane = iota((128, 128), 0), iota((128, 128), 1)
    first = jnp.zeros((4 * NZ, 128), F32)
    second = jnp.zeros((NZ, 256), F32)
    for xi in range(4):
        place = (lane // 32 == (xi + iy) % 4) & (lane % 32 == y // 4)
        rows = [4 * xi + a for a in range(4)]
        total = lambda ref: sum(coarse_rows(ref, r, TX) for r in rows)
        stack = [coarse_rows(cx, rows[0], TX), coarse_rows(cx, rows[3], TX), total(kappa), total(cz)]
        first = first + mix(jnp.concatenate(stack, axis=0), matrix(place))
        ends = [matrix(place & (y % 4 == 0)), matrix(place & (y % 4 == 3))]
        second = second + mix(total(cy), jnp.concatenate(ends, axis=1))
    out[pl.ds(0, 2 * NZ), :] = first[: 2 * NZ] * (1 / 128)
    out[pl.ds(2 * NZ, NZ), :] = second[:, :128] * (1 / 128)
    out[pl.ds(3 * NZ, NZ), :] = second[:, 128:] * (1 / 128)
    out[pl.ds(4 * NZ, 2 * NZ), :] = first[2 * NZ :] * (1 / 16)


def assemble(gathered, kinds, kind, dest, gx, gy):
    group = iota((NZ, 128), 1) // 32
    for ix in range(gx):
        blocks = [gathered[pl.ds(((ix * gy + iy) * kinds + kind) * NZ, NZ), :] for iy in range(gy)]
        for xi in range(4):
            cells = blocks[0]
            for iy in range(1, gy):
                cells = jnp.where(group == (iy + xi) % 4, blocks[iy], cells)
            dest[pl.ds(4 * ix + xi, NZ, stride=4 * gx), :] = shift(cells, -32 * xi, 1)


def factor_global(rows, cols, xl, xu, yl, yu, kappa, cz, out):
    x, y = iota((rows, 128), 0), iota((rows, 128), 1)
    masks = [(x > 0).astype(F32), (x < rows - 1).astype(F32), (y > 0).astype(F32), (y < cols - 1).astype(F32)]
    size = NZ * rows

    def step(k, carry, last=False):
        c_prev, cz_k, z_low = carry
        at = plane(k, rows)
        cz_next = jnp.zeros_like(cz_k) if last else cz[plane(k + 1, rows), :]
        z_up = 0.5 * (cz_k + cz_next)
        diag = jnp.where(y < cols, kappa[at, :], 1.0) + z_up + z_low
        for n, ref in enumerate((xl, xu, yl, yu)):
            face = ref[at, :]
            diag = diag + face
            out[pl.ds(pl.multiple_of(n * size + k * rows, rows), rows), :] = face * masks[n]
        inv = 1.0 / (diag + z_low * c_prev)
        c = jnp.zeros_like(inv) if last else -z_up * inv
        for n, value in ((4, inv), (5, z_low * inv), (6, c)):
            out[pl.ds(pl.multiple_of(n * size + k * rows, rows), rows), :] = value
        return c, cz_next, z_up

    cz_0 = cz[pl.ds(0, rows), :]
    carry = lax.fori_loop(0, NZ - 1, step, (jnp.zeros_like(cz_0), cz_0, 0.5 * cz_0))
    step(NZ - 1, carry, last=True)


def global_kernel(gx, gy, gathered, out2, out3, out4, *scratch):
    fine, mid, low = scratch[:8], scratch[8:14], scratch[14:20]
    rows, cols = 4 * gx, 32 * gy
    for kind in range(6):
        assemble(gathered, 6, kind, fine[kind], gx, gy)
    a_ref, b_ref, c_ref, d_ref, kappa, cz, xl, yl = fine
    x, y = iota((1, rows, 128), 1), iota((1, rows, 128), 2)
    cube = lambda ref: ref[...].reshape(NZ, rows, 128)
    a, b = cube(a_ref), cube(b_ref)
    xl[...] = (a + jnp.where(x > 0, shift(b, 1, 1), 0.0)).reshape(NZ * rows, 128)
    b_ref[...] = (b + jnp.where(x < rows - 1, shift(a, -1, 1), 0.0)).reshape(NZ * rows, 128)
    c, d = cube(c_ref), cube(d_ref)
    yl[...] = (c + jnp.where(y > 0, shift(d, 1, 2), 0.0)).reshape(NZ * rows, 128)
    d_ref[...] = (d + jnp.where(y < cols - 1, shift(c, -1, 2), 0.0)).reshape(NZ * rows, 128)
    level = (xl, b_ref, yl, d_ref, kappa, cz)
    factor_global(rows, cols, *level, out2)
    pair, even, odd = pair_matrix(128, 128), pair_matrix(128, 128, (0,)), pair_matrix(128, 128, (1,))
    for coarse, out in ((mid, out3), (low, out4)):
        rows, cols = rows // 2, cols // 2
        size = NZ * rows
        first = lambda ref: ref[pl.ds(0, size, stride=2), :]
        second = lambda ref: ref[pl.ds(1, size, stride=2), :]
        xl, xu, yl, yu, kappa, cz = level
        coarse[0][...] = 0.125 * mix(first(xl), pair)
        coarse[1][...] = 0.125 * mix(second(xu), pair)
        coarse[2][...] = 0.125 * mix(first(yl) + second(yl), even)
        coarse[3][...] = 0.125 * mix(first(yu) + second(yu), odd)
        coarse[4][...] = 0.25 * mix(first(kappa) + second(kappa), pair)
        coarse[5][...] = 0.25 * mix(first(cz) + second(cz), pair)
        level = coarse
        factor_global(rows, cols, *level, out)


def neighbours(cells, xl, xu, yl, yu):
    out = xl * shift(cells, 1, 0) + xu * shift(cells, -1, 0)
    return out + yl * shift(cells, 1, 1) + yu * shift(cells, -1, 1)


def back_down(rows, f, u, r, coeffs, c):
    def step(n, after):
        k = NZ - 1 - n
        at = plane(k, rows)
        value = u[at, :] - c(k) * after
        field = OMEGA * value
        u[at, :] = field
        r[at, :] = (1.0 - OMEGA) * f[at, :] + neighbours(field, *[get(k) for get in coeffs])
        return value

    lax.fori_loop(0, NZ, step, jnp.zeros((rows, u.shape[1]), F32))


def forward_down(rows, f, u, inv, g):
    def step(k, prev):
        at = plane(k, rows)
        value = f[at, :] * inv(k) + g(k) * prev
        u[at, :] = value
        return value

    lax.fori_loop(0, NZ, step, jnp.zeros((rows, u.shape[1]), F32))


def sweep_up(rows, f, u, w, e, coeffs, inv, g, c, mask):
    def forward(k, prev):
        at = plane(k, rows)
        field = u[at, :] + e[at, :]
        if mask is not None:
            field = field * mask
        u[at, :] = field
        value = (f(k) + neighbours(field, *[get(k) for get in coeffs])) * inv(k) + g(k) * prev
        w[at, :] = value
        return value

    def backward(n, after):
        k = NZ - 1 - n
        at = plane(k, rows)
        value = w[at, :] - c(k) * after
        u[at, :] = (1.0 - OMEGA) * u[at, :] + OMEGA * value
        return value

    start = jnp.zeros((rows, u.shape[1]), F32)
    lax.fori_loop(0, NZ, forward, start)
    lax.fori_loop(0, NZ, backward, start)


def getter(ref, n, rows):
    return lambda k: ref[pl.ds(pl.multiple_of(n * NZ * rows + k * rows, rows), rows), :]


def window_mask(rows, cols, halo, ix, iy, nx, ny):
    tile_x, tile_y = rows // 2, cols // 2
    x, y = iota((rows, cols), 0), iota((rows, cols), 1)
    x = jnp.where(x < tile_x + halo, x, x - rows)
    y = jnp.where(y < tile_y + tile_y // 2, y, y - cols)
    valid = (y >= -halo) & (y < tile_y + halo)
    x, y = x + ix * tile_x, y + iy * tile_y
    return (valid & (x >= 0) & (x < nx) & (y >= 0) & (y < ny)).astype(F32)


SAVED = 9


def window_down(rows, cols, mask, f, kappa, faces, cz, out, r, diag_out=None):
    size = NZ * rows

    def put(n, k, value):
        out[pl.ds(pl.multiple_of(n * size + k * rows, rows), rows), :] = value

    def step(k, carry, last=False):
        c_prev, w_prev, cz_k, z_low = carry
        at = plane(k, rows)
        x_face, y_face = faces(k)
        xl, xu = x_face * mask, shift(x_face, -1, 0) * mask
        yl, yu = y_face * mask, shift(y_face, -1, 1) * mask
        cz_next = jnp.zeros_like(cz_k) if last else cz[plane(k + 1, rows), :]
        z_up = 0.5 * (cz_k + cz_next)
        diag = jnp.where(mask > 0, kappa[at, :], 1.0) + xl + xu + yl + yu + z_up + z_low
        if diag_out is not None:
            diag_out[plane(k, TX), :] = diag[:TX, :TY]
        inv = 1.0 / (diag + z_low * c_prev)
        c = jnp.zeros_like(inv) if last else -z_up * inv
        g = z_low * inv
        f_k = f[at, :]
        w = f_k * inv + g * w_prev
        for n, value in enumerate((xl, xu, yl, yu, inv, g, c, w, f_k)):
            put(n, k, value)
        return c, w, cz_next, z_up

    cz_0 = cz[pl.ds(0, rows), :]
    zero = jnp.zeros((rows, cols), F32)
    carry = lax.fori_loop(0, NZ - 1, step, (zero, zero, cz_0, 0.5 * cz_0))
    step(NZ - 1, carry, last=True)
    u, kept = out.at[pl.ds(7 * size, size), :], out.at[pl.ds(8 * size, size), :]
    get = [getter(out, n, rows) for n in range(7)]
    back_down(rows, kept, u, r, get[:4], get[6])


def down_kernel(nx, ny, *refs):
    f, kappa, cx, cy, cz, xr, xl, yr, yl, corner_r, corner_l = refs[:11]
    send, saved0, saved1, diag = refs[11:15]
    w_f, w_kappa, w_cx, w_cy, w_cz, x_face, y_face, r0 = refs[15:23]
    f1, kappa1, cz1, x_face1, y_face1, r1 = refs[23:]
    ix, iy = lax.axis_index("gx"), lax.axis_index("gy")
    rows, cols = 2 * TX, 2 * TY
    group = iota((8, 128), 1) // 8

    def build(z, carry):
        zo, zi = z // 16, z % 16
        after, before = group == zi, group == (zi + 15) % 16
        turn = (128 - 8 * zi) % 128
        for a, (tile, dest) in enumerate(zip((f, kappa, cx, cy, cz), (w_f, w_kappa, w_cx, w_cy, w_cz))):
            base = pl.multiple_of(z * rows, rows)
            dest[pl.ds(base, TX), :TY] = tile[plane(z, TX), :]
            slab = pl.ds(pl.multiple_of(a * NZ * HALO + z * HALO, HALO), HALO)
            dest[pl.ds(base + TX, HALO), :TY] = xr[slab, :]
            dest[pl.ds(base + TX + HALO, HALO), :TY] = xl[slab, :]
            for t in range(4):
                at = pl.ds(pl.multiple_of((((t % 2) * 5 * (t < 2) + a) * 2 + zo) * 8, 8), 8)
                far = pl.ds(pl.multiple_of((10 + a * 2 + zo) * 8, 8), 8)
                right, left = ((yr[at, :], yl[at, :]) if t < 2 else
                               (corner_r[far, :], corner_r[at, :]) if t == 2 else
                               (corner_l[far, :], corner_l[at, :]))
                cells = jnp.where(after, right, jnp.where(before, left, 0.0))
                dest[pl.ds(base + 8 * t, 8), TY:] = pltpu.roll(cells, turn, 1)
        return carry

    lax.fori_loop(0, NZ, build, 0)

    def faces0(k):
        at = plane(k, rows)
        cx_k, cy_k = w_cx[at, :], w_cy[at, :]
        x_k, y_k = 0.5 * (cx_k + shift(cx_k, 1, 0)), 0.5 * (cy_k + shift(cy_k, 1, 1))
        x_face[at, :] = x_k
        y_face[at, :] = y_k
        return x_k, y_k

    mask0 = window_mask(rows, cols, HALO, ix, iy, nx, ny)
    window_down(rows, cols, mask0, w_f, w_kappa, faces0, w_cz, saved0, r0, diag)
    rows, cols = rows // 2, cols // 2
    pair, even = pair_matrix(256, 128), pair_matrix(256, 128, (0,))
    part = 128
    for at in range(0, NZ * rows, part):
        here = pl.ds(at, part)
        first = lambda ref: ref[pl.ds(2 * at, 2 * part), :].reshape(part, 2, 256)[:, 0, :]
        both = lambda ref: ref[pl.ds(2 * at, 2 * part), :].reshape(part, 2, 256).sum(axis=1)
        f1[here, :] = 0.25 * mix(both(r0), pair)
        kappa1[here, :] = 0.25 * mix(both(w_kappa), pair)
        cz1[here, :] = 0.25 * mix(both(w_cz), pair)
        x_face1[here, :] = 0.125 * mix(first(x_face), pair)
        y_face1[here, :] = 0.125 * mix(both(y_face), even)
    mask1 = window_mask(rows, cols, HALO // 2, ix, iy, nx // 2, ny // 2)
    faces1 = lambda k: (x_face1[plane(k, rows), :], y_face1[plane(k, rows), :])
    window_down(rows, cols, mask1, f1, kappa1, faces1, cz1, saved1, r1)
    y, lane = iota((128, 128), 0), iota((128, 128), 1)
    total = jnp.zeros((NZ, 128), F32)
    for xi in range(4):
        place = (lane // 32 == (xi + iy) % 4) & (lane % 32 == y // 2) & (y < 64)
        cells = coarse_rows(r1, 2 * xi, rows) + coarse_rows(r1, 2 * xi + 1, rows)
        total = total + mix(cells, matrix(place))
    send[...] = 0.25 * total


def spread_rows(cells, x_before, x_after, dest, planes, rows):
    size = planes * rows
    even = 0.75 * cells + 0.25 * x_before
    odd = 0.75 * cells + 0.25 * x_after
    dest[pl.ds(0, size, stride=2), :] = even.reshape(size, 128)
    dest[pl.ds(1, size, stride=2), :] = odd.reshape(size, 128)


def up_kernel(gx, gy, *refs):
    gathered, k2, k3, k4, saved0, saved1, diag, cz, solution_out, residual_out = refs[:10]
    f2, u2, r2, f3, u3, r3, f4, u4, wide, e, w0, e0, s0, s1, sems = refs[10:]
    ix, iy = lax.axis_index("gx"), lax.axis_index("gy")
    copy1 = pltpu.make_async_copy(saved1, s1, sems.at[0])
    copy0 = pltpu.make_async_copy(saved0, s0, sems.at[1])
    copy1.start()
    copy0.start()
    assemble(gathered, 1, 0, f2, gx, gy)
    pair = pair_matrix(128, 128)
    rows2, cols2 = 4 * gx, 32 * gy

    rows = rows2
    for f, u, r, k, coarse in ((f2, u2, r2, k2, f3), (f3, u3, r3, k3, f4)):
        get = [getter(k, n, rows) for n in range(7)]
        forward_down(rows, f, u, get[4], get[5])
        back_down(rows, f, u, r, get[:4], get[6])
        rows = rows // 2
        size = NZ * rows
        cells = r[pl.ds(0, size, stride=2), :] + r[pl.ds(1, size, stride=2), :]
        coarse[...] = 0.25 * mix(cells, pair)

    get = [getter(k4, n, rows) for n in range(7)]

    def coarse_solve(rhs, damped):
        prev = jnp.zeros((rows, 128), F32)
        forward = []
        for k in range(NZ):
            prev = rhs[k] * get[4](k) + get[5](k) * prev
            forward.append(prev)
        out = [None] * NZ
        after = jnp.zeros((rows, 128), F32)
        for k in reversed(range(NZ)):
            after = forward[k] - get[6](k) * after
            out[k] = damped[k] + OMEGA * after
        return out

    f_at = lambda k: f4[pl.ds(k * rows, rows), :]
    field = coarse_solve([f_at(k) for k in range(NZ)], [0.0] * NZ)
    for k in range(NZ):
        u4[pl.ds(k * rows, rows), :] = field[k]

    def relax(sweep, carry):
        old = [u4[pl.ds(k * rows, rows), :] for k in range(NZ)]
        rhs = [f_at(k) + neighbours(old[k], *[g(k) for g in get[:4]]) for k in range(NZ)]
        new = coarse_solve(rhs, [(1.0 - OMEGA) * v for v in old])
        for k in range(NZ):
            u4[pl.ds(k * rows, rows), :] = new[k]
        return carry

    lax.fori_loop(0, COARSE_SWEEPS - 1, relax, 0)

    coarse, cols = u4, cols2 // 4
    for f, u, w, k in ((f3, u3, r3, k3), (f2, u2, r2, k2)):
        cells = coarse[...].reshape(NZ, rows, 128)
        x = iota((1, rows, 128), 1)
        before = jnp.where(x > 0, shift(cells, 1, 1), 0.0)
        after = jnp.where(x < rows - 1, shift(cells, -1, 1), 0.0)
        spread_rows(cells, before, after, wide, NZ, rows)
        y = iota((128, 128), 1)
        partner = y // 2 + 2 * (y % 2) - 1
        weights = spread_matrix(128, y, y // 2, jnp.where(partner < cols, partner, -1), y < 2 * cols)
        rows, cols = 2 * rows, 2 * cols
        size = NZ * rows
        e[pl.ds(0, size), :] = mix(wide[pl.ds(0, size), :], weights)
        get = [getter(k, n, rows) for n in range(7)]
        f_of = functools.partial(lambda ref, count, n: ref[plane(n, count), :], f, rows)
        sweep_up(rows, f_of, u, w, e, get[:4], get[4], get[5], get[6], None)
        coarse = u

    cells = pltpu.roll(u2[...].reshape(NZ, rows2, 128), (rows2 - 4 * ix) % rows2, 1)
    q = iota((1, 8, 128), 1)
    place = 4 * ix + jnp.where(q < 6, q, q - 8)
    cells = jnp.where(q < 6, cells[:, :8], cells[:, rows2 - 8 :])
    cells = jnp.where((place >= 0) & (place < rows2), cells, 0.0)
    spread_rows(cells, shift(cells, 1, 1), shift(cells, -1, 1), wide, NZ, 8)
    y = iota((128, 128), 1)
    y = jnp.where(y < 96, y, y - 128) + 64 * iy
    partner = (y + 128) // 2 - 64 + 2 * (y % 2) - 1
    weights = spread_matrix(128, y, (y + 128) // 2 - 64, partner, (y >= 0) & (y < 2 * cols2))
    size = NZ * TX
    e[pl.ds(0, size), :] = mix(wide[pl.ds(0, size), :], weights)
    copy1.wait()
    get = [getter(s1, n, TX) for n in range(SAVED)]
    mask1 = window_mask(TX, TY, HALO // 2, ix, iy, 2 * rows2, 2 * cols2)
    u1 = s1.at[pl.ds(7 * size, size), :]
    sweep_up(TX, get[8], u1, r2, e, get[:4], get[4], get[5], get[6], mask1)

    cells = u1[...].reshape(NZ, TX, 128)
    spread_rows(cells, shift(cells, 1, 1), shift(cells, -1, 1), wide, NZ, TX)
    y = iota((128, 256), 1)
    partner = (y // 2 + 2 * (y % 2) - 1 + 128) % 128
    weights = spread_matrix(128, y, y // 2, partner, y >= 0)
    for at in range(0, NZ * 2 * TX, 256):
        e0[pl.ds(at, 256), :] = mix(wide[pl.ds(at, 256), :], weights)
    copy0.wait()
    rows = 2 * TX
    size = NZ * rows
    get = [getter(s0, n, rows) for n in range(SAVED)]
    mask0 = window_mask(rows, 2 * TY, HALO, ix, iy, 4 * rows2, 4 * cols2)
    u0 = s0.at[pl.ds(7 * size, size), :]
    sweep_up(rows, get[8], u0, w0, e0, get[:4], get[4], get[5], get[6], mask0)

    def residual(k, carry, last=False):
        below, cz_k, z_low = carry
        field = u0[plane(k, rows), :]
        tile = field[:TX, :TY]
        side = neighbours(field, *[g(k) for g in get[:4]])[:TX, :TY]
        cz_next = jnp.zeros_like(cz_k) if last else cz[plane(k + 1, TX), :]
        above = jnp.zeros_like(cz_k) if last else u0[plane(k + 1, rows), :][:TX, :TY]
        z_up = 0.5 * (cz_k + cz_next)
        out = get[8](k)[:TX, :TY] + side - diag[plane(k, TX), :] * tile + z_up * above + z_low * below
        solution_out[plane(k, TX), :] = tile
        residual_out[plane(k, TX), :] = out
        return tile, cz_next, z_up

    cz_0 = cz[pl.ds(0, TX), :]
    carry = lax.fori_loop(0, NZ - 1, residual, (jnp.zeros_like(cz_0), cz_0, 0.5 * cz_0))
    residual(NZ - 1, carry, last=True)


def call(kernel, name, outs, ins, scratch=(), specs=None, flops=1000000):
    shapes = [jax.ShapeDtypeStruct(s, F32) for s in outs]
    return pl.pallas_call(
        kernel,
        name=name,
        out_shape=shapes,
        in_specs=specs or [VMEM] * len(ins),
        out_specs=[VMEM] * len(outs),
        scratch_shapes=list(scratch),
        compiler_params=pltpu.CompilerParams(vmem_limit_bytes=56 * 1024 * 1024),
        cost_estimate=pl.CostEstimate(flops=flops, bytes_accessed=4 * sum(x.size for x in ins), transcendentals=0),
    )(*ins)


def body(right_side, kappa_sq, cond_x, cond_y, cond_z):
    gx, gy = lax.axis_size("gx"), lax.axis_size("gy")
    tiles = [v.reshape(NZ * TX, TY) for v in (right_side, kappa_sq, cond_x, cond_y, cond_z)]
    slab, strip = (5 * NZ * HALO, 128), (160, 128)
    x_head, x_tail, y_head, y_tail = call(pack_kernel, "pack", [slab, slab, strip, strip], tiles)
    share = call(coeff_kernel, "coeff_share", [(6 * NZ, 128)], tiles[1:])[0]
    up = lambda n: [(i, i + 1) for i in range(n - 1)]
    down = lambda n: [(i + 1, i) for i in range(n - 1)]
    yr = lax.ppermute(y_head, "gy", down(gy))
    yl = lax.ppermute(y_tail, "gy", up(gy))
    xr = lax.ppermute(x_head, "gx", down(gx))
    xl = lax.ppermute(x_tail, "gx", up(gx))
    shares = lax.all_gather(share, ("gx", "gy")).reshape(gx * gy * 6 * NZ, 128)
    corner_r = lax.ppermute(jnp.concatenate([yl[:80], yr[:80]]), "gx", down(gx))
    corner_l = lax.ppermute(jnp.concatenate([yl[80:], yr[80:]]), "gx", up(gx))
    vm = lambda *shape: pltpu.VMEM(shape, F32)
    big, mid, low = NZ * 4 * gx, NZ * 2 * gx, NZ * gx
    k2, k3, k4 = call(
        functools.partial(global_kernel, gx, gy),
        "global_coeffs",
        [(7 * big, 128), (7 * mid, 128), (7 * low, 128)],
        [shares],
        [vm(big, 128)] * 8 + [vm(mid, 128)] * 6 + [vm(low, 128)] * 6,
    )
    size0, size1 = NZ * 2 * TX, NZ * TX
    send, saved0, saved1, diag = call(
        functools.partial(down_kernel, gx * TX, gy * TY),
        "down",
        [(NZ, 128), (SAVED * size0, 2 * TY), (SAVED * size1, TY), (NZ * TX, TY)],
        [*tiles, xr, xl, yr, yl, corner_r, corner_l],
        [vm(size0, 256)] * 8 + [vm(size1, 128)] * 6,
    )
    gathered = lax.all_gather(send, ("gx", "gy")).reshape(gx * gy * NZ, 128)
    field, residual = call(
        functools.partial(up_kernel, gx, gy),
        "up",
        [(NZ * TX, TY)] * 2,
        [gathered, k2, k3, k4, saved0, saved1, diag, tiles[4]],
        [vm(big, 128)] * 3 + [vm(mid, 128)] * 3 + [vm(low, 128)] * 2
        + [vm(size0, 128), vm(size0, 128), vm(size0, 256), vm(size0, 256)]
        + [vm(SAVED * size0, 256), vm(SAVED * size1, 128), pltpu.SemaphoreType.DMA((2,))],
        [VMEM] * 4 + [ANY] * 2 + [VMEM] * 2,
    )
    return field.reshape(right_side.shape), residual.reshape(right_side.shape)


def solution(mesh):
    spec = P(None, "gx", "gy")
    fits = (mesh.shape["gx"], mesh.shape["gy"]) == (8, 4)
    plan = body if fits else spread_body
    return jax.shard_map(plan, mesh=mesh, in_specs=(spec,) * 5, out_specs=(spec, spec), check_vma=False)
```

```python
import functools

import jax
import jax.numpy as jnp
from jax import lax
from jax.experimental import pallas as pl
from jax.experimental.pallas import tpu as pltpu
from jax.sharding import PartitionSpec as P

LEVELS = 4
COARSE_SWEEPS = 16


OMEGA = 0.8


def with_halo(cells, sides, width):
    for axis, dim in sides:
        count = lax.axis_size(axis)
        ends = count - 1
        head = lax.slice_in_dim(cells, 0, width, axis=dim)
        tail = lax.slice_in_dim(cells, cells.shape[dim] - width, cells.shape[dim], axis=dim)
        cells = jnp.concatenate(
            [
                lax.ppermute(tail, axis, [(i, (i + 1) % count) for i in range(ends)]),
                cells,
                lax.ppermute(head, axis, [((i + 1) % count, i) for i in range(ends)]),
            ],
            axis=dim,
        )
    return cells


def apply_op(field, padded, coeffs):
    kappa, x_up, x_low, y_up, y_low, z_up, z_low = coeffs
    zpad = jnp.pad(field, ((1, 1), (0, 0), (0, 0)))
    out = (
        kappa * field
        + x_up * (field - padded[:, 2:, 1:-1])
        + x_low * (field - padded[:, :-2, 1:-1])
    )
    out = out + y_up * (field - padded[:, 1:-1, 2:]) + y_low * (field - padded[:, 1:-1, :-2])
    return out + z_up * (field - zpad[2:]) + z_low * (field - zpad[:-2])


def face_pad(field):
    return with_halo(field, (("gx", 1), ("gy", 2)), 1)


def line_factors(coeffs):
    kappa, x_up, x_low, y_up, y_low, z_up, z_low = coeffs
    diag = kappa + x_up + x_low + y_up + y_low + z_up + z_low
    upper_src = z_up.at[-1].set(jnp.zeros_like(z_up[-1]))

    def factor_step(upper_prev, planes):
        diag_k, low_k, up_k = planes
        inv = 1.0 / (diag_k + low_k * upper_prev)
        upper = -up_k * inv
        return (upper, (inv, upper))

    start = jnp.zeros_like(diag[0])
    unused, stacked = lax.scan(factor_step, start, (diag, z_low, upper_src), unroll=True)
    return stacked


def line_solve(rhs, factors, z_low):
    inverses, uppers = factors

    def forward_step(prev, planes):
        rhs_k, low_k, inv_k = planes
        value = (rhs_k + low_k * prev) * inv_k
        return (value, value)

    start = jnp.zeros_like(rhs[0])
    unused, forward = lax.scan(forward_step, start, (rhs, z_low, inverses), unroll=True)

    def back_step(after, planes):
        fwd_k, up_k = planes
        value = fwd_k - up_k * after
        return (value, value)

    unused, result = lax.scan(back_step, start, (forward, uppers), reverse=True, unroll=True)
    return result


def mean_four(field):
    depth, rows, cols = field.shape
    return field.reshape(depth, rows // 2, 2, cols // 2, 2).mean(axis=(2, 4))


def coarsen(coeffs):
    kappa, x_up, x_low, y_up, y_low, z_up, z_low = coeffs
    depth, rows, cols = kappa.shape
    shape = (depth, rows // 2, 2, cols // 2, 2)
    xu_c = x_up.reshape(shape)[:, :, 1].mean(axis=-1) * 0.25
    xl_c = x_low.reshape(shape)[:, :, 0].mean(axis=-1) * 0.25
    yu_c = y_up.reshape(shape)[:, :, :, :, 1].mean(axis=2) * 0.25
    yl_c = y_low.reshape(shape)[:, :, :, :, 0].mean(axis=2) * 0.25
    return (mean_four(kappa), xu_c, xl_c, yu_c, yl_c, mean_four(z_up), mean_four(z_low))


def prolong(padded):
    depth = padded.shape[0]
    rows = padded.shape[1] - 2
    cols = padded.shape[2] - 2
    centre = padded[:, 1:-1, :]
    even = 0.75 * centre + 0.25 * padded[:, :-2, :]
    odd = 0.75 * centre + 0.25 * padded[:, 2:, :]
    spread = jnp.stack([even, odd], axis=2).reshape(depth, 2 * rows, cols + 2)
    centre = spread[:, :, 1:-1]
    even = 0.75 * centre + 0.25 * spread[:, :, :-2]
    odd = 0.75 * centre + 0.25 * spread[:, :, 2:]
    return jnp.stack([even, odd], axis=3).reshape(depth, 2 * rows, 2 * cols)


def coarse_solve(rhs, coeffs):
    factors = line_factors(coeffs)
    field = OMEGA * line_solve(rhs, factors, coeffs[6])

    def spread_sweep(sweep, current):
        padded = with_halo(current, (("gx", 1), ("gy", 2)), 1)
        defect = rhs - apply_op(current, padded, coeffs)
        return current + OMEGA * line_solve(defect, factors, coeffs[6])

    field = lax.fori_loop(0, COARSE_SWEEPS - 1, spread_sweep, field)
    return field


def cycle(rhs, coeffs, level):
    if level == LEVELS:
        return coarse_solve(rhs, coeffs)
    factors = line_factors(coeffs)
    field = OMEGA * line_solve(rhs, factors, coeffs[6])
    padded = face_pad(field)
    defect = rhs - apply_op(field, padded, coeffs)
    correction = cycle(mean_four(defect), coarsen(coeffs), level + 1)
    rimmed = with_halo(correction, (("gx", 1), ("gy", 2)), 1)
    field = field + prolong(rimmed)
    padded = face_pad(field)
    defect = rhs - apply_op(field, padded, coeffs)
    return field + OMEGA * line_solve(defect, factors, coeffs[6])


def spread_body(right_side, kappa_sq, cond_x, cond_y, cond_z):
    padded_x = with_halo(cond_x, (("gx", 1),), 1)
    padded_y = with_halo(cond_y, (("gy", 2),), 1)
    padded_z = jnp.pad(cond_z, ((1, 1), (0, 0), (0, 0)))
    x_up = 0.5 * (cond_x + padded_x[:, 2:, :])
    x_low = 0.5 * (cond_x + padded_x[:, :-2, :])
    y_up = 0.5 * (cond_y + padded_y[:, :, 2:])
    y_low = 0.5 * (cond_y + padded_y[:, :, :-2])
    z_up = 0.5 * (cond_z + padded_z[2:])
    z_low = 0.5 * (cond_z + padded_z[:-2])
    coeffs = (kappa_sq, x_up, x_low, y_up, y_low, z_up, z_low)
    solution_field = cycle(right_side, coeffs, 0)
    residual = right_side - apply_op(solution_field, face_pad(solution_field), coeffs)
    return (solution_field, residual)


F32 = jnp.float32
BF16 = jnp.bfloat16
NZ = 32
HALF = NZ // 2
TX, TY = 16, 128
HALO = 8
SLAB = 5 * NZ * HALO
STRIP = 160
VMEM = pl.BlockSpec(memory_space=pltpu.VMEM)
ANY = pl.BlockSpec(memory_space=pl.ANY)


def iota(shape, dim):
    return lax.broadcasted_iota(jnp.int32, shape, dim)


def shift(x, by, axis):
    by = by % x.shape[axis]
    return pltpu.roll(x, by, axis) if by else x


def mix(x, weights):
    high = x.astype(BF16)
    rest = x - high.astype(F32)
    mid = rest.astype(BF16)
    low = (rest - mid.astype(F32)).astype(BF16)
    dot = functools.partial(jnp.dot, preferred_element_type=F32)
    return dot(low, weights) + dot(mid, weights) + dot(high, weights)


def matrix(mask, weight=1.0):
    return jnp.where(mask, weight, 0.0).astype(BF16)


def span(start, size):
    if not isinstance(start, int):
        start = pl.multiple_of(start, 8)
    return pl.ds(start, size)


class Field:
    def __init__(self, ref, rows, tiles=1, planes=NZ):
        self.ref, self.rows, self.tiles, self.planes = ref, rows, tiles, planes

    def base(self, tile, k):
        return tile * self.planes * self.rows + k * self.rows

    def part(self, tile, k):
        return self.ref[span(self.base(tile, k), self.rows), :]

    def __getitem__(self, k):
        parts = [self.part(t, k) for t in range(self.tiles)]
        return parts[0] if self.tiles == 1 else jnp.concatenate(parts, axis=1)

    def __setitem__(self, k, value):
        for t in range(self.tiles):
            self.put(t, k, value[:, 128 * t : 128 * (t + 1)])

    def put(self, tile, k, value):
        self.ref[span(self.base(tile, k), self.rows), :] = value

    def every_second(self, at, count, odd):
        parts = []
        for t in range(self.tiles):
            first = t * self.planes * self.rows + 2 * at + odd
            parts.append(self.ref[pl.ds(first, count, stride=2), :])
        return parts[0] if self.tiles == 1 else jnp.concatenate(parts, axis=1)

    def row(self, row):
        return self.ref[pl.ds(row, self.planes, stride=self.rows), :]


def loop(count, step, carry, unroll=None):
    if unroll is None or unroll >= count:
        for i in range(count):
            carry = step(i, carry)
        return carry
    return lax.fori_loop(0, count, step, carry, unroll=unroll)


def neighbours(field, x_face, y_face):
    out = x_face * shift(field, 1, 0) + shift(x_face * field, -1, 0)
    return out + (y_face * shift(field, 1, 1) + shift(y_face * field, -1, 1))


class Line:
    def __init__(self, inv, z_face):
        self.inv, self.z_face = inv, z_face

    def inward(self, k, upper):
        return self.z_face[k + 1 if upper else k] * self.inv[k]

    def outward(self, k, upper):
        return self.z_face[k if upper else k + 1] * self.inv[k]


class StoredLine:
    def __init__(self, inv, g, c):
        self.inv, self.g, self.c = inv, g, c

    def inward(self, k, upper):
        return self.g[k]

    def outward(self, k, upper):
        return self.c[k]


def sweep_in(rhs, line, keep, start, unroll):
    def step(i, carry):
        low, high = carry
        k, m = i, NZ - 1 - i
        low = rhs(k) * line.inv[k] + line.inward(k, False) * low
        high = rhs(m) * line.inv[m] + line.inward(m, True) * high
        keep[k] = low
        keep[m] = high
        return low, high

    return loop(HALF, step, (start, start), unroll)


def sweep_out(ends, kept, line, emit, unroll):
    low, high = ends
    a, b = line.outward(HALF - 1, False), line.outward(HALF, True)
    low = (low + a * high) * (1.0 / (1.0 - a * b))
    high = high + b * low

    def step(i, carry):
        low, high = carry
        k, m = HALF - 1 - i, HALF + i
        emit(k, low)
        emit(m, high)
        low = kept[k - 1] + line.outward(k - 1, False) * low
        high = kept[m + 1] + line.outward(m + 1, True) * high
        return low, high

    low, high = loop(HALF - 1, step, (low, high), unroll)
    emit(0, low)
    emit(NZ - 1, high)


def factor(diag, z_face, tiles, inv_out, unroll, rhs=None, keep=None, g_out=None, c_out=None):
    ends = []
    for t in range(tiles):
        zero = jnp.zeros((diag.rows, 128), F32)

        def one(k, upper, inv_prev, prev):
            below, above = z_face.part(t, k), z_face.part(t, k + 1)
            inner, outer = (above, below) if upper else (below, above)
            inv = 1.0 / (diag.part(t, k) + below + above - inner * inner * inv_prev)
            inv_out.put(t, k, inv)
            if g_out is not None:
                g_out.put(t, k, inner * inv)
                c_out.put(t, k, outer * inv)
            if rhs is None:
                return inv, prev
            value = (rhs.part(t, k) + inner * prev) * inv
            keep.put(t, k, value)
            return inv, value

        def step(i, carry):
            low, high = carry
            return one(i, False, *low), one(NZ - 1 - i, True, *high)

        low, high = loop(HALF, step, ((zero, zero), (zero, zero)), unroll)
        ends.append((low[1], high[1]))
    join = lambda n: ends[0][n] if tiles == 1 else jnp.concatenate([e[n] for e in ends], axis=1)
    return join(0), join(1)


def z_faces(cz, out, tiles=1):
    for t in range(tiles):
        before = None
        for k in range(NZ + 1):
            here = cz.part(t, k) if k < NZ else None
            both = here if before is None else before if here is None else here + before
            out.put(t, k, 0.5 * both)
            before = here


def base_diag(kappa, x_face, y_face):
    return kappa + (x_face + shift(x_face, -1, 0)) + (y_face + shift(y_face, -1, 1))


def window_mask(rows, lanes, tile_x, tile_y, halo, ix, iy, nx, ny):
    x, y = iota((rows, lanes), 0), iota((rows, lanes), 1)
    x = jnp.where(x < (rows + tile_x) // 2, x, x - rows)
    y = jnp.where(y < (lanes + tile_y) // 2, y, y - lanes)
    valid = (y >= -halo) & (y < tile_y + halo) & (x >= -halo) & (x < tile_x + halo)
    x, y = x + ix * tile_x, y + iy * tile_y
    return (valid & (x >= 0) & (x < nx) & (y >= 0) & (y < ny)).astype(F32)


def smooth_down(f, x_face, y_face, line, ends, kept, u, r, unroll):
    def emit(k, value):
        field = OMEGA * value
        u[k] = field
        r[k] = (1.0 - OMEGA) * f[k] + neighbours(field, x_face[k], y_face[k])

    sweep_out(ends, kept, line, emit, unroll)


def smooth_up(f, x_face, y_face, line, u, e, kept, mask, unroll):
    masked = (lambda v: v) if mask is None else (lambda v: v * mask)

    def rhs(k):
        field = masked(u[k] + e[k])
        u[k] = field
        return masked(f[k] + neighbours(field, x_face[k], y_face[k]))

    def emit(k, value):
        u[k] = (1.0 - OMEGA) * u[k] + OMEGA * value

    zero = jnp.zeros((u.rows, 128 * u.tiles), F32)
    ends = sweep_in(rhs, line, kept, zero, unroll)
    sweep_out(ends, kept, line, emit, unroll)


def spread_rows(cells, before, after, dest, size):
    dest[pl.ds(0, size, stride=2), :] = (0.75 * cells + 0.25 * before).reshape(size, 128)
    dest[pl.ds(1, size, stride=2), :] = (0.75 * cells + 0.25 * after).reshape(size, 128)


def spread_matrix(fine, base, coarse_count, circular=False):
    j = iota((128, fine.shape[1]), 0) + base
    parent = (fine + 2048) // 2 - 1024
    partner = parent + 2 * ((fine + 2048) % 2) - 1
    if circular:
        j, parent, partner = j % 128, parent % 128, partner % 128
    weights = jnp.where(j == parent, 0.75, jnp.where(j == partner, 0.25, 0.0))
    if not circular:
        inside = (j >= 0) & (j < coarse_count) & (fine >= 0) & (fine < 2 * coarse_count)
        weights = jnp.where(inside, weights, 0.0)
    return weights.astype(BF16)


def lane_group(rows, width):
    return iota((rows, 128), 1) // width


def fold_planes(cells, turn):
    group = lane_group(8, 32)
    out = cells[:8]
    for n in range(1, 4):
        out = jnp.where(group == n, cells[8 * n : 8 * n + 8], out)
    return pltpu.roll(out, turn, 1)


def pack_kernel(f, kappa, cx, cy, cz, x_head, x_tail, y_head, y_tail, share3):
    iy = lax.axis_index("gy")
    y, lane = iota((128, 128), 0), iota((128, 128), 1)
    fourth = y // 4 == lane % 32
    rows = lambda ref: [Field(ref, TX).row(r) for r in range(TX)]
    cx_rows, cy_rows, kappa_rows, cz_rows = rows(cx), rows(cy), rows(kappa), rows(cz)
    totals = lambda v: [(v[4 * i] + v[4 * i + 1]) + (v[4 * i + 2] + v[4 * i + 3]) for i in range(4)]
    stack = [cx_rows[4 * i] for i in range(4)] + [cx_rows[4 * i + 3] for i in range(4)]
    stack = mix(jnp.concatenate(stack + totals(kappa_rows) + totals(cz_rows), axis=0), matrix(fourth))
    ends = [matrix(fourth & (y % 4 == 0)), matrix(fourth & (y % 4 == 3))]
    sides = mix(jnp.concatenate(totals(cy_rows), axis=0), jnp.concatenate(ends, axis=1))
    group = lane_group(NZ, 32)

    def merge(cells, scale):
        out = cells[:NZ]
        for xi in range(1, 4):
            out = jnp.where(group == xi, cells[NZ * xi : NZ * (xi + 1)], out)
        return out * scale

    kinds = [merge(stack[:128], 1 / 128), merge(stack[128:256], 1 / 128)]
    kinds += [merge(sides[:, :128], 1 / 128), merge(sides[:, 128:], 1 / 128)]
    kinds += [merge(stack[256:384], 1 / 16), merge(stack[384:], 1 / 16)]
    head = [jnp.zeros((8, 128), F32)] * 3
    tail = [jnp.zeros((8, 128), F32)] * 3
    slot = iota((8, 128), 1) % 32 // 4
    for t, cells in enumerate(kinds):
        at = pl.ds(SLAB + t * NZ, NZ)
        x_head[at, :] = cells
        x_tail[at, :] = cells
        for zv in range(4):
            n = 4 * t + zv
            piece = cells[8 * zv : 8 * zv + 8]
            head[n // 8] = jnp.where(slot == n % 8, shift(piece, 4 * (n % 8), 1), head[n // 8])
            tail[n // 8] = jnp.where(slot == n % 8, shift(piece, 4 * (n % 8) + 4, 1), tail[n // 8])
    for n in range(3):
        y_head[pl.ds(STRIP + 8 * n, 8), :] = head[n]
        y_tail[pl.ds(STRIP + 8 * n, 8), :] = tail[n]

    x_in, y_in = y // 32, y % 32
    x_out, y_out = lane % 32 // 16, lane % 16
    pair_y, pair_x = y_in // 2 == y_out, x_in // 2 == x_out
    folds = [
        matrix(pair_y & (x_in == 2 * x_out), 0.125),
        matrix(pair_y & (x_in == 2 * x_out + 1), 0.125),
        matrix(pair_x & (y_in == 2 * y_out), 0.125),
        matrix(pair_x & (y_in == 2 * y_out + 1), 0.125),
        matrix(pair_x & pair_y, 0.25),
    ]
    for t, cells in enumerate(kinds):
        share3[pl.ds(8 * t, 8), :] = fold_planes(mix(cells, folds[min(t, 4)]), 16 * iy)

    group = lane_group(8, 8)
    for a, ref in enumerate((f, kappa, cx, cy, cz)):
        cells = ref[...].reshape(NZ, TX, TY)
        at = pl.ds(a * NZ * HALO, NZ * HALO)
        x_head[at, :] = cells[:, :HALO].reshape(NZ * HALO, TY)
        x_tail[at, :] = cells[:, TX - HALO :].reshape(NZ * HALO, TY)
        for half in range(2):
            for zo in range(2):
                head = jnp.zeros((8, 128), F32)
                tail = jnp.zeros((8, 128), F32)
                for zi in range(16):
                    cells = ref[pl.ds((zo * 16 + zi) * TX + 8 * half, 8), :]
                    cells = shift(cells, 8 * zi, 1)
                    head = jnp.where(group == zi, cells, head)
                    tail = jnp.where(group == (zi - 1) % 16, cells, tail)
                at = pl.ds(((half * 5 + a) * 2 + zo) * 8, 8)
                y_head[at, :] = head
                y_tail[at, :] = tail


def window2(tile, after, before, dest, first):
    lane = iota((NZ, 128), 1)
    for xi in range(4):
        turned = (lane - 32 * xi + 128) % 128
        cells = jnp.where(turned < 32, tile, jnp.where(turned < 36, after, jnp.where(turned >= 124, before, 0.0)))
        dest[pl.ds(first + xi, NZ, stride=TX), :] = shift(cells, -32 * xi, 1)


def window_kernel(x_head, xr, xl, yr, yl, cr, cl, x_face, y_face, inv, z_face, a, b, c, d, kappa, cz, diag):
    ix, iy = lax.axis_index("gx"), lax.axis_index("gy")
    nx, ny = lax.axis_size("gx") * 4, lax.axis_size("gy") * 32
    refs = (a, b, c, d, kappa, cz)

    def unpack(ref, first, t, turn):
        pieces = []
        for zv in range(4):
            n = 4 * t + zv
            pieces.append(shift(ref[pl.ds(first + 8 * (n // 8), 8), :], turn - 4 * (n % 8), 1))
        return jnp.concatenate(pieces, axis=0)

    half = STRIP // 2
    for t, dest in enumerate(refs):
        at = pl.ds(SLAB + t * NZ, NZ)
        for first, tile, right, left, r_at, l_at in (
            (0, x_head, yr, yl, STRIP, STRIP),
            (4, xr, cr, cr, half + 24 + half, half),
            (12, xl, cl, cl, half + 24 + half, half),
        ):
            window2(tile[at, :], unpack(right, r_at, t, 32), unpack(left, l_at, t, 92), dest, first)
        for x in range(8, 12):
            dest[pl.ds(x, NZ, stride=TX), :] = jnp.zeros((NZ, 128), F32)
    mask = window_mask(TX, 128, 4, 32, 4, ix, iy, nx, ny)
    fields = [Field(ref, TX) for ref in (*refs, x_face, y_face, diag, inv)]
    a, b, c, d, kappa, cz, x_face, y_face, diag, inv = fields
    for k in range(NZ):
        x_k = a[k] + shift(b[k], 1, 0)
        y_k = c[k] + shift(d[k], 1, 1)
        x_face[k] = x_k
        y_face[k] = y_k
        diag[k] = base_diag(jnp.where(mask > 0, kappa[k], 1.0), x_k, y_k)
    z_face = Field(z_face, TX, 1, NZ + 1)
    z_faces(cz, z_face)
    factor(diag, z_face, 1, inv, None)


def assemble3(gathered, stride, first, dest, gx, gy, rows):
    group = lane_group(8, 16)
    for ix in range(gx):
        blocks = [gathered[pl.ds((ix * gy + iy) * stride + first, 8), :] for iy in range(gy)]
        for zo in range(4):
            for xi in range(2):
                q = 2 * zo + xi
                cells = blocks[0]
                for iy in range(1, gy):
                    cells = jnp.where(group == (iy + q) % 8, blocks[iy], cells)
                dest[pl.ds(8 * zo * rows + 2 * ix + xi, 8, stride=rows), :] = shift(cells, -16 * q, 1)


def global_kernel(gx, gy, gathered, *refs):
    outs3, outs4 = refs[:5], refs[5:10]
    raw3, raw4 = refs[10:18], refs[18:26]
    rows, cols = 2 * gx, 16 * gy
    for t in range(6):
        assemble3(gathered, 48, 8 * t, raw3[t], gx, gy, rows)
    a, b, c, d = (Field(ref, rows) for ref in raw3[:4])
    x, y = iota((rows, 128), 0), iota((rows, 128), 1)
    for k in range(NZ):
        a_k, b_k, c_k, d_k = a[k], b[k], c[k], d[k]
        a[k] = a_k + jnp.where(x > 0, shift(b_k, 1, 0), 0.0)
        b[k] = b_k + jnp.where(x < rows - 1, shift(a_k, -1, 0), 0.0)
        c[k] = jnp.where(y < cols, c_k + jnp.where(y > 0, shift(d_k, 1, 1), 0.0), 0.0)
        d[k] = jnp.where(y < cols, d_k + jnp.where(y < cols - 1, shift(c_k, -1, 1), 0.0), 0.0)
    yy, jj = iota((128, 128), 0), iota((128, 128), 1)
    keep = yy // 2 == jj
    pair, even, odd = matrix(keep), matrix(keep & (yy % 2 == 0)), matrix(keep & (yy % 2 == 1))
    size = NZ * rows // 2
    lows = [Field(ref, rows) for ref in raw3]
    first = lambda n: lows[n].every_second(0, size, 0)
    second = lambda n: lows[n].every_second(0, size, 1)
    raw4[0][...] = 0.125 * mix(first(0), pair)
    raw4[1][...] = 0.125 * mix(second(1), pair)
    raw4[2][...] = 0.125 * mix(first(2) + second(2), even)
    raw4[3][...] = 0.125 * mix(first(3) + second(3), odd)
    raw4[4][...] = 0.25 * mix(first(4) + second(4), pair)
    raw4[5][...] = 0.25 * mix(first(5) + second(5), pair)
    for raw, outs in ((raw3, outs3), (raw4, outs4)):
        x, y = iota((rows, 128), 0), iota((rows, 128), 1)
        xl, xu, yl, yu, kappa, cz = (Field(ref, rows) for ref in raw[:6])
        z_face, diag = Field(raw[6], rows, 1, NZ + 1), Field(raw[7], rows)
        x_face, y_face, inv, g, c = (Field(ref, rows) for ref in outs)
        inside_x, inside_y = (x > 0).astype(F32), ((y > 0) & (y < cols)).astype(F32)
        for k in range(NZ):
            xl_k, yl_k = xl[k], yl[k]
            diag[k] = jnp.where(y < cols, kappa[k], 1.0) + (xl_k + xu[k]) + (yl_k + yu[k])
            x_face[k] = xl_k * inside_x
            y_face[k] = yl_k * inside_y
        z_faces(cz, z_face)
        factor(diag, z_face, 1, inv, None, g_out=g, c_out=c)
        rows, cols = rows // 2, cols // 2


def down_kernel(nx, ny, *refs):
    f, kappa, cx, cy, cz, xr, xl, yr, yl, corner_r, corner_l = refs[:11]
    send, outs0, outs1 = refs[11], refs[12:18], refs[18:24]
    scratch = list(refs[24:-1])
    sems = refs[-1]
    take = lambda n: [scratch.pop(0) for _ in range(n)]
    ix, iy = lax.axis_index("gx"), lax.axis_index("gy")
    rows, tiles = 2 * TX, 2
    whole = take(11)
    names = [Field(ref, rows, tiles) for ref in whole[:10]]
    x_face, y_face, inv, u, f0, kappa0, cz0, diag, kept, r = names
    z_face = Field(whole[10], rows, tiles, NZ + 1)
    group = lane_group(8, 8)

    def window(a, tile, z, after, before, turn):
        zo = z // 16
        slab = span(a * NZ * HALO + z * HALO, HALO)
        main = jnp.concatenate([tile[span(z * TX, TX), :], xr[slab, :], xl[slab, :]], axis=0)
        at = lambda first: span(first + (a * 2 + zo) * 8, 8)
        half = STRIP // 2
        sides = []
        for right, left in (
            (yr[at(0), :], yl[at(0), :]),
            (yr[at(half), :], yl[at(half), :]),
            (corner_r[at(half + 24), :], corner_r[at(0), :]),
            (corner_l[at(half + 24), :], corner_l[at(0), :]),
        ):
            cells = jnp.where(after, right, jnp.where(before, left, 0.0))
            sides.append(pltpu.roll(cells, turn, 1))
        return jnp.concatenate([main, jnp.concatenate(sides, axis=0)], axis=1)

    mask0 = window_mask(rows, 256, TX, TY, HALO, ix, iy, nx, ny)

    def prepare(z, cz_prev):
        zi = z % 16
        after, before = group == zi, group == (zi + 15) % 16
        turn = (128 - 8 * zi) % 128
        f_k, kappa_k, cx_k, cy_k, cz_k = (
            window(a, tile, z, after, before, turn) for a, tile in enumerate((f, kappa, cx, cy, cz))
        )
        f0[z] = f_k
        kappa0[z] = kappa_k
        cz0[z] = cz_k
        z_face[z] = 0.5 * (cz_k + cz_prev)
        x_k, y_k = 0.5 * (cx_k + shift(cx_k, 1, 0)), 0.5 * (cy_k + shift(cy_k, 1, 1))
        x_face[z] = x_k
        y_face[z] = y_k
        diag[z] = base_diag(jnp.where(mask0 > 0, kappa_k, 1.0), x_k, y_k)
        return cz_k

    last = loop(NZ, prepare, jnp.zeros((rows, 256), F32), 2)
    z_face[NZ] = 0.5 * last
    ends = factor(diag, z_face, tiles, inv, 4, f0, kept)
    sources = [x_face, y_face, inv, z_face, u, f0]
    copies = [pltpu.make_async_copy(s.ref, o, sems.at[n]) for n, (s, o) in enumerate(zip(sources, outs0))]
    for n in (0, 1, 2, 3, 5):
        copies[n].start()
    smooth_down(f0, x_face, y_face, Line(inv, z_face), ends, kept, u, r, 2)
    copies[4].start()

    fine = (r, kappa0, cz0, x_face, y_face)
    lanes, tile_x, tile_y, halo, outs = 256, TX, TY, HALO, outs1
    for level in (1, 2):
        rows, tile_x, tile_y, halo = rows // 2, tile_x // 2, tile_y // 2, halo // 2
        nx, ny = nx // 2, ny // 2
        whole = take(11)
        names = [Field(ref, rows) for ref in whole[:10]]
        x_face, y_face, inv, u, f1, kappa1, cz1, diag, kept, r = names
        z_face = Field(whole[10], rows, 1, NZ + 1)
        mask = window_mask(rows, 128, tile_x, tile_y, halo, ix, iy, nx, ny)
        y, j = iota((lanes, 128), 0), iota((lanes, 128), 1)
        if lanes == 128:
            j = jnp.where(j < 48, j, jnp.where(j >= 80, j - 64, -1))
        pair, even = matrix(y // 2 == j), matrix(y == 2 * j)
        part = min(128, NZ * rows)
        for at in range(0, NZ * rows, part):
            here = pl.ds(at, part)
            both = lambda n: fine[n].every_second(at, part, 0) + fine[n].every_second(at, part, 1)
            f1.ref[here, :] = 0.25 * mix(both(0), pair)
            kappa1.ref[here, :] = 0.25 * mix(both(1), pair)
            cz1.ref[here, :] = 0.25 * mix(both(2), pair)
            x_face.ref[here, :] = 0.125 * mix(fine[3].every_second(at, part, 0), pair)
            y_face.ref[here, :] = 0.125 * mix(both(4), even)
        for k in range(NZ):
            f1[k] = f1[k] * mask
            diag[k] = base_diag(jnp.where(mask > 0, kappa1[k], 1.0), x_face[k], y_face[k])
        z_faces(cz1, z_face)
        ends = factor(diag, z_face, 1, inv, None, f1, kept)
        smooth_down(f1, x_face, y_face, Line(inv, z_face), ends, kept, u, r, None)
        if level == 1:
            sources = [x_face, y_face, inv, z_face, u, f1]
            more = [pltpu.make_async_copy(s.ref, o, sems.at[6 + n]) for n, (s, o) in enumerate(zip(sources, outs1))]
            for copy in more:
                copy.start()
            copies += more
        fine, lanes = (r, kappa1, cz1, x_face, y_face), 128

    group = lane_group(NZ, 32)
    out = f1.row(0)
    for xi in range(1, 4):
        out = jnp.where(group == xi, shift(f1.row(xi), 32 * xi, 1), out)
    send[pl.ds(0, NZ), :] = out
    y, lane = iota((128, 128), 0), iota((128, 128), 1)
    total = jnp.zeros((NZ, 128), F32)
    for xi in range(2):
        place = (lane % 32 // 16 == xi) & (y // 2 == lane % 16) & (y < 32)
        total = total + mix(r.row(2 * xi) + r.row(2 * xi + 1), matrix(place, 0.25))
    send[pl.ds(NZ, 8), :] = fold_planes(total, 16 * iy)
    for copy in copies:
        copy.wait()


def up_kernel(gx, gy, *refs):
    gathered, kappa = refs[:2]
    k3, k4, k2 = refs[2:7], refs[7:12], refs[12:16]
    saved0, saved1 = refs[16:22], refs[22:28]
    solution_out, residual_out = refs[28:30]
    scratch = list(refs[30:-1])
    sems = refs[-1]
    take = lambda n: [scratch.pop(0) for _ in range(n)]
    ix, iy = lax.axis_index("gx"), lax.axis_index("gy")
    held0, held1 = take(6), take(6)
    copies = []
    for n, (source, dest) in enumerate(zip((*saved1, *saved0), (*held1, *held0))):
        copies.append(pltpu.make_async_copy(source, dest, sems.at[n]))
        copies[-1].start()
    f3, u3, r3, f2, u2, kept2, f4, u4, wide, e_ref, e0_ref, kept0 = take(12)

    rows, cols = 2 * gx, 16 * gy
    assemble3(gathered, NZ + 8, NZ, f3, gx, gy, rows)
    y, lane = iota((128, 128), 0), iota((128, 128), 1)
    f3, u3, r3 = (Field(ref, rows) for ref in (f3, u3, r3))
    y = iota((rows, 128), 1)
    x_face3, y_face3, inv3, g3, c3 = (Field(ref, rows) for ref in k3)
    line3 = StoredLine(inv3, g3, c3)
    clean = (y < cols).astype(F32)
    for k in range(NZ):
        f3[k] = f3[k] * clean
    zero = jnp.zeros((rows, 128), F32)
    ends = sweep_in(lambda k: f3[k], line3, r3, zero, None)
    smooth_down(f3, x_face3, y_face3, line3, ends, r3, u3, Field(e_ref, rows), None)
    fine = Field(e_ref, rows)
    rows, cols = rows // 2, cols // 2
    size = NZ * rows
    yy, jj = iota((128, 128), 0), iota((128, 128), 1)
    f4[...] = 0.25 * mix(fine.every_second(0, size, 0) + fine.every_second(0, size, 1), matrix(yy // 2 == jj))
    f4, u4 = Field(f4, rows), Field(u4, rows)
    x_face4, y_face4, inv4, g4, c4 = (Field(ref, rows) for ref in k4)
    line4 = StoredLine(inv4, g4, c4)
    zero = jnp.zeros((rows, 128), F32)

    def solve4(rhs, old):
        kept, out = {}, {}
        ends = sweep_in(rhs, line4, kept, zero, None)

        def emit(k, value):
            out[k] = OMEGA * value if old is None else (1.0 - OMEGA) * old[k] + OMEGA * value

        sweep_out(ends, kept, line4, emit, None)
        for k in range(NZ):
            u4[k] = out[k]

    solve4(lambda k: f4[k], None)

    def relax(sweep, carry):
        old = [u4[k] for k in range(NZ)]
        solve4(lambda k: f4[k] + neighbours(old[k], x_face4[k], y_face4[k]), old)
        return carry

    lax.fori_loop(0, COARSE_SWEEPS - 1, relax, 0)

    cells = u4.ref[...].reshape(NZ, rows, 128)
    x = iota((1, rows, 128), 1)
    before = jnp.where(x > 0, shift(cells, 1, 1), 0.0)
    after = jnp.where(x < rows - 1, shift(cells, -1, 1), 0.0)
    spread_rows(cells, before, after, wide, size)
    e_ref[...] = mix(wide[pl.ds(0, 2 * size), :], spread_matrix(iota((128, 128), 1), 0, cols))
    rows, cols = 2 * rows, 2 * cols
    smooth_up(f3, x_face3, y_face3, line3, u3, Field(e_ref, rows), r3, None, None)

    def block(dx, dy):
        jx, jy = ix + dx, iy + dy
        inside = ((jx >= 0) & (jx < gx) & (jy >= 0) & (jy < gy)).astype(F32)
        device = jnp.clip(jx, 0, gx - 1) * gy + jnp.clip(jy, 0, gy - 1)
        return gathered[span(device * (NZ + 8), NZ), :] * inside

    for first, dx in ((0, 0), (4, 1), (12, -1)):
        window2(block(dx, 0), shift(block(dx, 1), 32, 1), shift(block(dx, -1), 96, 1), f2, first)
    for x in range(8, 12):
        f2[pl.ds(x, NZ, stride=TX), :] = jnp.zeros((NZ, 128), F32)
    f2, u2, kept2 = (Field(ref, TX) for ref in (f2, u2, kept2))
    x_face2, y_face2, inv2 = (Field(ref, TX) for ref in k2[:3])
    line2 = Line(inv2, Field(k2[3], TX, 1, NZ + 1))
    zero = jnp.zeros((TX, 128), F32)
    ends = sweep_in(lambda k: f2[k], line2, kept2, zero, None)

    def emit2(k, value):
        u2[k] = OMEGA * value

    sweep_out(ends, kept2, line2, emit2, None)

    cells = pltpu.roll(u3.ref[...].reshape(NZ, rows, 128), (rows - 2 * ix) % rows, 1)
    x = iota((1, rows, 128), 1)
    place = 2 * ix + jnp.where(x < rows // 2, x, x - rows)
    cells = jnp.where((place >= 0) & (place < rows), cells, 0.0)
    ring = lambda v, first: jnp.where(iota((1, 8, 128), 1) < first, v[:, :8], v[:, rows - 8 :])
    spread_rows(ring(cells, 4), ring(shift(cells, 1, 1), 4), ring(shift(cells, -1, 1), 4), wide, NZ * 8)
    lane = iota((128, 128), 1)
    fine_y = jnp.where(lane < 80, lane, lane - 128) + 32 * iy
    e_ref[...] = mix(wide[pl.ds(0, NZ * TX), :], spread_matrix(fine_y, 0, cols))
    mask2 = window_mask(TX, 128, 4, 32, 4, ix, iy, 4 * gx, 32 * gy)
    smooth_up(f2, x_face2, y_face2, line2, u2, Field(e_ref, TX), kept2, mask2, None)

    cells = u2.ref[...].reshape(NZ, TX, 128)
    ring = lambda v: jnp.where(iota((1, 8, 128), 1) < 6, v[:, :8], v[:, 8:])
    spread_rows(ring(cells), ring(shift(cells, 1, 1)), ring(shift(cells, -1, 1)), wide, NZ * 8)
    fine_y = jnp.where(lane < 96, lane, lane - 128)
    e_ref[...] = mix(wide[pl.ds(0, NZ * TX), :], spread_matrix(fine_y, 0, 0, circular=True))
    for copy in copies[:6]:
        copy.wait()
    x_face1, y_face1, inv1, z_face1, u1, f1 = held1
    x_face1, y_face1, inv1, u1, f1 = (Field(ref, TX) for ref in (x_face1, y_face1, inv1, u1, f1))
    line1 = Line(inv1, Field(z_face1, TX, 1, NZ + 1))
    mask1 = window_mask(TX, 128, 8, 64, 4, ix, iy, 8 * gx, 64 * gy)
    smooth_up(f1, x_face1, y_face1, line1, u1, Field(e_ref, TX), kept2, mask1, None)

    cells = u1.ref[...].reshape(NZ, TX, 128)
    spread_rows(cells, shift(cells, 1, 1), shift(cells, -1, 1), wide, NZ * TX)
    rows = 2 * TX
    weights = spread_matrix(iota((128, 256), 1), 0, 0, circular=True)
    e0 = Field(e0_ref, rows, 2)
    for k in range(0, NZ, 8):
        cells = mix(wide[pl.ds(k * rows, 8 * rows), :], weights)
        for t in range(2):
            e0_ref[pl.ds(e0.base(t, k), 8 * rows), :] = cells[:, 128 * t : 128 * (t + 1)]
    for copy in copies[6:]:
        copy.wait()
    x_face0, y_face0, inv0, z_face0, u0, f0 = held0
    x_face0, y_face0, inv0, u0, f0 = (Field(ref, rows, 2) for ref in (x_face0, y_face0, inv0, u0, f0))
    z_face0 = Field(z_face0, rows, 2, NZ + 1)
    mask0 = window_mask(rows, 256, TX, TY, HALO, ix, iy, TX * gx, TY * gy)
    smooth_up(f0, x_face0, y_face0, Line(inv0, z_face0), u0, e0, Field(kept0, rows, 2), mask0, 2)

    kappa = Field(kappa, TX)
    tile = lambda v: v[:TX, :TY]

    def residual(k, carry):
        below, flux_z = carry
        field = u0[k]
        flux_x = x_face0[k] * (field - shift(field, 1, 0))
        flux_y = y_face0[k] * (field - shift(field, 1, 1))
        side = (flux_x - shift(flux_x, -1, 0)) + (flux_y - shift(flux_y, -1, 1))
        here = tile(field)
        above = u0.part(0, k + 1)[:TX] if k is not NZ - 1 else jnp.zeros((TX, TY), F32)
        flux_up = z_face0.part(0, k + 1)[:TX] * (above - here)
        solution_out[span(k * TX, TX), :] = here
        out = f0.part(0, k)[:TX] - kappa[k] * here - tile(side) - flux_z + flux_up
        residual_out[span(k * TX, TX), :] = out
        return here, flux_up

    start = z_face0.part(0, 0)[:TX] * tile(u0[0])
    carry = loop(NZ - 1, residual, (start, start), 2)
    residual(NZ - 1, carry)


def call(kernel, name, outs, ins, scratch=(), in_specs=None, out_specs=None, flops=1000000):
    shapes = [jax.ShapeDtypeStruct(s, F32) for s in outs]
    return pl.pallas_call(
        kernel,
        name=name,
        out_shape=shapes,
        in_specs=in_specs or [VMEM] * len(ins),
        out_specs=out_specs or [VMEM] * len(outs),
        scratch_shapes=list(scratch),
        compiler_params=pltpu.CompilerParams(vmem_limit_bytes=56 * 1024 * 1024),
        cost_estimate=pl.CostEstimate(flops=flops, bytes_accessed=4 * sum(x.size for x in ins), transcendentals=0),
    )(*ins)


def body(right_side, kappa_sq, cond_x, cond_y, cond_z):
    gx, gy = lax.axis_size("gx"), lax.axis_size("gy")
    tiles = [v.reshape(NZ * TX, TY) for v in (right_side, kappa_sq, cond_x, cond_y, cond_z)]
    slab, strip = (SLAB + 6 * NZ, 128), (STRIP + 24, 128)
    x_head, x_tail, y_head, y_tail, share3 = call(pack_kernel, "pack", [slab, slab, strip, strip, (48, 128)], tiles)
    up = lambda n: [(i, i + 1) for i in range(n - 1)]
    down = lambda n: [(i + 1, i) for i in range(n - 1)]
    yr = lax.ppermute(y_head, "gy", down(gy))
    yl = lax.ppermute(y_tail, "gy", up(gy))
    xr = lax.ppermute(x_head, "gx", down(gx))
    xl = lax.ppermute(x_tail, "gx", up(gx))
    shares = lax.all_gather(lax.all_gather(share3, "gy"), "gx").reshape(gx * gy * 48, 128)
    half = STRIP // 2
    corner_r = lax.ppermute(jnp.concatenate([yl[:half], yl[STRIP:], yr[:half], yr[STRIP:]]), "gx", down(gx))
    corner_l = lax.ppermute(jnp.concatenate([yl[half:STRIP], yl[STRIP:], yr[half:STRIP], yr[STRIP:]]), "gx", up(gx))
    vm = lambda *shape: pltpu.VMEM(shape, F32)
    level = lambda rows, n: [vm(NZ * rows, 128)] * n
    faces = lambda rows, tiles: vm(tiles * (NZ + 1) * rows, 128)
    rows3, rows4 = 2 * gx, gx
    whole = call(
        functools.partial(global_kernel, gx, gy),
        "global_coeffs",
        [(NZ * rows3, 128)] * 5 + [(NZ * rows4, 128)] * 5,
        [shares],
        level(rows3, 6) + [faces(rows3, 1)] + level(rows3, 1) + level(rows4, 6) + [faces(rows4, 1)] + level(rows4, 1),
    )
    size, tall = (NZ * TX, 128), ((NZ + 1) * TX, 128)
    k2 = call(
        window_kernel, "window_coeffs", [size, size, size, tall], [x_head, xr, xl, yr, yl, corner_r, corner_l], level(TX, 7)
    )
    big, big_z = (2 * NZ * 2 * TX, 128), (2 * (NZ + 1) * 2 * TX, 128)
    send, *saved = call(
        functools.partial(down_kernel, gx * TX, gy * TY),
        "down",
        [(NZ + 8, 128), big, big, big, big_z, big, big, size, size, size, tall, size, size],
        [*tiles, xr, xl, yr, yl, corner_r, corner_l],
        [vm(*big)] * 10 + [vm(*big_z)] + level(TX, 10) + [faces(TX, 1)] + level(8, 10) + [faces(8, 1)]
        + [pltpu.SemaphoreType.DMA((12,))],
        out_specs=[VMEM] + [ANY] * 12,
    )
    copies = jnp.broadcast_to(send[None], (gx * gy, NZ + 8, 128))
    gathered = lax.all_to_all(copies, ("gx", "gy"), 0, 0).reshape(gx * gy * (NZ + 8), 128)
    field, residual = call(
        functools.partial(up_kernel, gx, gy),
        "up",
        [(NZ * TX, TY)] * 2,
        [gathered, tiles[1], *whole, *k2, *saved],
        [vm(*big), vm(*big), vm(*big), vm(*big_z), vm(*big), vm(*big), vm(*size), vm(*size), vm(*size), vm(*tall), vm(*size), vm(*size)]
        + level(rows3, 3) + level(TX, 3) + level(rows4, 2)
        + [vm(NZ * 2 * TX, 128), vm(*size), vm(*big), vm(*big), pltpu.SemaphoreType.DMA((12,))],
        in_specs=[VMEM] * 16 + [ANY] * 12,
    )
    return field.reshape(right_side.shape), residual.reshape(right_side.shape)


def solution(mesh):
    spec = P(None, "gx", "gy")
    fits = (mesh.shape["gx"], mesh.shape["gy"]) == (8, 4)
    plan = body if fits else spread_body
    return jax.shard_map(plan, mesh=mesh, in_specs=(spec,) * 5, out_specs=(spec, spec), check_vma=False)
```

```python
import functools

import jax
import jax.numpy as jnp
from jax import lax
from jax.experimental import pallas as pl
from jax.experimental.pallas import tpu as pltpu
from jax.sharding import PartitionSpec as P

LEVELS = 4
COARSE_SWEEPS = 16


OMEGA = 0.8


def with_halo(cells, sides, width):
    for axis, dim in sides:
        count = lax.axis_size(axis)
        ends = count - 1
        head = lax.slice_in_dim(cells, 0, width, axis=dim)
        tail = lax.slice_in_dim(cells, cells.shape[dim] - width, cells.shape[dim], axis=dim)
        cells = jnp.concatenate(
            [
                lax.ppermute(tail, axis, [(i, (i + 1) % count) for i in range(ends)]),
                cells,
                lax.ppermute(head, axis, [((i + 1) % count, i) for i in range(ends)]),
            ],
            axis=dim,
        )
    return cells


def apply_op(field, padded, coeffs):
    kappa, x_up, x_low, y_up, y_low, z_up, z_low = coeffs
    zpad = jnp.pad(field, ((1, 1), (0, 0), (0, 0)))
    out = (
        kappa * field
        + x_up * (field - padded[:, 2:, 1:-1])
        + x_low * (field - padded[:, :-2, 1:-1])
    )
    out = out + y_up * (field - padded[:, 1:-1, 2:]) + y_low * (field - padded[:, 1:-1, :-2])
    return out + z_up * (field - zpad[2:]) + z_low * (field - zpad[:-2])


def face_pad(field):
    return with_halo(field, (("gx", 1), ("gy", 2)), 1)


def line_factors(coeffs):
    kappa, x_up, x_low, y_up, y_low, z_up, z_low = coeffs
    diag = kappa + x_up + x_low + y_up + y_low + z_up + z_low
    upper_src = z_up.at[-1].set(jnp.zeros_like(z_up[-1]))

    def factor_step(upper_prev, planes):
        diag_k, low_k, up_k = planes
        inv = 1.0 / (diag_k + low_k * upper_prev)
        upper = -up_k * inv
        return (upper, (inv, upper))

    start = jnp.zeros_like(diag[0])
    unused, stacked = lax.scan(factor_step, start, (diag, z_low, upper_src), unroll=True)
    return stacked


def line_solve(rhs, factors, z_low):
    inverses, uppers = factors

    def forward_step(prev, planes):
        rhs_k, low_k, inv_k = planes
        value = (rhs_k + low_k * prev) * inv_k
        return (value, value)

    start = jnp.zeros_like(rhs[0])
    unused, forward = lax.scan(forward_step, start, (rhs, z_low, inverses), unroll=True)

    def back_step(after, planes):
        fwd_k, up_k = planes
        value = fwd_k - up_k * after
        return (value, value)

    unused, result = lax.scan(back_step, start, (forward, uppers), reverse=True, unroll=True)
    return result


def mean_four(field):
    depth, rows, cols = field.shape
    return field.reshape(depth, rows // 2, 2, cols // 2, 2).mean(axis=(2, 4))


def coarsen(coeffs):
    kappa, x_up, x_low, y_up, y_low, z_up, z_low = coeffs
    depth, rows, cols = kappa.shape
    shape = (depth, rows // 2, 2, cols // 2, 2)
    xu_c = x_up.reshape(shape)[:, :, 1].mean(axis=-1) * 0.25
    xl_c = x_low.reshape(shape)[:, :, 0].mean(axis=-1) * 0.25
    yu_c = y_up.reshape(shape)[:, :, :, :, 1].mean(axis=2) * 0.25
    yl_c = y_low.reshape(shape)[:, :, :, :, 0].mean(axis=2) * 0.25
    return (mean_four(kappa), xu_c, xl_c, yu_c, yl_c, mean_four(z_up), mean_four(z_low))


def prolong(padded):
    depth = padded.shape[0]
    rows = padded.shape[1] - 2
    cols = padded.shape[2] - 2
    centre = padded[:, 1:-1, :]
    even = 0.75 * centre + 0.25 * padded[:, :-2, :]
    odd = 0.75 * centre + 0.25 * padded[:, 2:, :]
    spread = jnp.stack([even, odd], axis=2).reshape(depth, 2 * rows, cols + 2)
    centre = spread[:, :, 1:-1]
    even = 0.75 * centre + 0.25 * spread[:, :, :-2]
    odd = 0.75 * centre + 0.25 * spread[:, :, 2:]
    return jnp.stack([even, odd], axis=3).reshape(depth, 2 * rows, 2 * cols)


def coarse_solve(rhs, coeffs):
    factors = line_factors(coeffs)
    field = OMEGA * line_solve(rhs, factors, coeffs[6])

    def spread_sweep(sweep, current):
        padded = with_halo(current, (("gx", 1), ("gy", 2)), 1)
        defect = rhs - apply_op(current, padded, coeffs)
        return current + OMEGA * line_solve(defect, factors, coeffs[6])

    field = lax.fori_loop(0, COARSE_SWEEPS - 1, spread_sweep, field)
    return field


def cycle(rhs, coeffs, level):
    if level == LEVELS:
        return coarse_solve(rhs, coeffs)
    factors = line_factors(coeffs)
    field = OMEGA * line_solve(rhs, factors, coeffs[6])
    padded = face_pad(field)
    defect = rhs - apply_op(field, padded, coeffs)
    correction = cycle(mean_four(defect), coarsen(coeffs), level + 1)
    rimmed = with_halo(correction, (("gx", 1), ("gy", 2)), 1)
    field = field + prolong(rimmed)
    padded = face_pad(field)
    defect = rhs - apply_op(field, padded, coeffs)
    return field + OMEGA * line_solve(defect, factors, coeffs[6])


def spread_body(right_side, kappa_sq, cond_x, cond_y, cond_z):
    padded_x = with_halo(cond_x, (("gx", 1),), 1)
    padded_y = with_halo(cond_y, (("gy", 2),), 1)
    padded_z = jnp.pad(cond_z, ((1, 1), (0, 0), (0, 0)))
    x_up = 0.5 * (cond_x + padded_x[:, 2:, :])
    x_low = 0.5 * (cond_x + padded_x[:, :-2, :])
    y_up = 0.5 * (cond_y + padded_y[:, :, 2:])
    y_low = 0.5 * (cond_y + padded_y[:, :, :-2])
    z_up = 0.5 * (cond_z + padded_z[2:])
    z_low = 0.5 * (cond_z + padded_z[:-2])
    coeffs = (kappa_sq, x_up, x_low, y_up, y_low, z_up, z_low)
    solution_field = cycle(right_side, coeffs, 0)
    residual = right_side - apply_op(solution_field, face_pad(solution_field), coeffs)
    return (solution_field, residual)


F32 = jnp.float32
BF16 = jnp.bfloat16
NZ = 32
HALF = NZ // 2
TX, TY = 16, 128
HALO = 8
SLAB = 5 * NZ * HALO
STRIP = 160
Y_BLOCK = STRIP + 24 + 48
VMEM = pl.BlockSpec(memory_space=pltpu.VMEM)
ANY = pl.BlockSpec(memory_space=pl.ANY)


def iota(shape, dim):
    return lax.broadcasted_iota(jnp.int32, shape, dim)


def shift(x, by, axis):
    by = by % x.shape[axis]
    return pltpu.roll(x, by, axis) if by else x


def mix(x, weights, parts=2):
    out = None
    for n in range(parts):
        part = x.astype(BF16)
        term = jnp.dot(part, weights, preferred_element_type=F32)
        out = term if out is None else out + term
        if n < parts - 1:
            x = x - part.astype(F32)
    return out


def matrix(mask, weight=1.0):
    return jnp.where(mask, weight, 0.0).astype(BF16)


def span(start, size):
    if not isinstance(start, int):
        start = pl.multiple_of(start, 8)
    return pl.ds(start, size)


class Field:
    def __init__(self, ref, rows, tiles=1, planes=NZ):
        self.ref, self.rows, self.tiles, self.planes = ref, rows, tiles, planes

    def base(self, tile, k):
        return tile * self.planes * self.rows + k * self.rows

    def part(self, tile, k):
        return self.ref[span(self.base(tile, k), self.rows), :]

    def __getitem__(self, k):
        parts = [self.part(t, k) for t in range(self.tiles)]
        return parts[0] if self.tiles == 1 else jnp.concatenate(parts, axis=1)

    def __setitem__(self, k, value):
        for t in range(self.tiles):
            self.put(t, k, value[:, 128 * t : 128 * (t + 1)])

    def put(self, tile, k, value):
        self.ref[span(self.base(tile, k), self.rows), :] = value

    def every_second(self, at, count, odd):
        parts = []
        for t in range(self.tiles):
            first = t * self.planes * self.rows + 2 * at + odd
            parts.append(self.ref[pl.ds(first, count, stride=2), :])
        return parts[0] if self.tiles == 1 else jnp.concatenate(parts, axis=1)

    def row(self, row):
        return self.ref[pl.ds(row, self.planes, stride=self.rows), :]


def loop(count, step, carry, unroll=None):
    if unroll is None or unroll >= count:
        for i in range(count):
            carry = step(i, carry)
        return carry
    return lax.fori_loop(0, count, step, carry, unroll=unroll)


def neighbours(field, x_face, y_face):
    out = x_face * shift(field, 1, 0) + shift(x_face * field, -1, 0)
    return out + (y_face * shift(field, 1, 1) + shift(y_face * field, -1, 1))


class Line:
    def __init__(self, inv, z_face):
        self.inv, self.z_face = inv, z_face

    def inward(self, k, upper):
        return self.z_face[k + 1 if upper else k] * self.inv[k]

    def outward(self, k, upper):
        return self.z_face[k if upper else k + 1] * self.inv[k]


class StoredLine:
    def __init__(self, inv, g, c):
        self.inv, self.g, self.c = inv, g, c

    def inward(self, k, upper):
        return self.g[k]

    def outward(self, k, upper):
        return self.c[k]


def sweep_in(rhs, line, keep, start, unroll):
    def step(i, carry):
        low, high = carry
        k, m = i, NZ - 1 - i
        low = rhs(k) * line.inv[k] + line.inward(k, False) * low
        high = rhs(m) * line.inv[m] + line.inward(m, True) * high
        keep[k] = low
        keep[m] = high
        return low, high

    return loop(HALF, step, (start, start), unroll)


def sweep_out(ends, kept, line, emit, unroll):
    low, high = ends
    a, b = line.outward(HALF - 1, False), line.outward(HALF, True)
    low = (low + a * high) * (1.0 / (1.0 - a * b))
    high = high + b * low

    def step(i, carry):
        low, high = carry
        k, m = HALF - 1 - i, HALF + i
        emit(k, low)
        emit(m, high)
        low = kept[k - 1] + line.outward(k - 1, False) * low
        high = kept[m + 1] + line.outward(m + 1, True) * high
        return low, high

    low, high = loop(HALF - 1, step, (low, high), unroll)
    emit(0, low)
    emit(NZ - 1, high)


def factor(diag, z_face, tiles, inv_out, unroll, rhs=None, keep=None, g_out=None, c_out=None):
    ends = []
    for t in range(tiles):
        zero = jnp.zeros((diag.rows, 128), F32)

        def one(k, upper, inv_prev, prev):
            below, above = z_face.part(t, k), z_face.part(t, k + 1)
            inner, outer = (above, below) if upper else (below, above)
            inv = 1.0 / (diag.part(t, k) + below + above - inner * inner * inv_prev)
            inv_out.put(t, k, inv)
            if g_out is not None:
                g_out.put(t, k, inner * inv)
                c_out.put(t, k, outer * inv)
            if rhs is None:
                return inv, prev
            value = (rhs.part(t, k) + inner * prev) * inv
            keep.put(t, k, value)
            return inv, value

        def step(i, carry):
            low, high = carry
            return one(i, False, *low), one(NZ - 1 - i, True, *high)

        low, high = loop(HALF, step, ((zero, zero), (zero, zero)), unroll)
        ends.append((low[1], high[1]))
    join = lambda n: ends[0][n] if tiles == 1 else jnp.concatenate([e[n] for e in ends], axis=1)
    return join(0), join(1)


def z_faces(cz, out, tiles=1):
    for t in range(tiles):
        before = None
        for k in range(NZ + 1):
            here = cz.part(t, k) if k < NZ else None
            both = here if before is None else before if here is None else here + before
            out.put(t, k, 0.5 * both)
            before = here


def base_diag(kappa, x_face, y_face):
    return kappa + (x_face + shift(x_face, -1, 0)) + (y_face + shift(y_face, -1, 1))


def window_mask(rows, lanes, tile_x, tile_y, halo, ix, iy, nx, ny):
    x, y = iota((rows, lanes), 0), iota((rows, lanes), 1)
    x = jnp.where(x < (rows + tile_x) // 2, x, x - rows)
    y = jnp.where(y < (lanes + tile_y) // 2, y, y - lanes)
    valid = (y >= -halo) & (y < tile_y + halo) & (x >= -halo) & (x < tile_x + halo)
    x, y = x + ix * tile_x, y + iy * tile_y
    return (valid & (x >= 0) & (x < nx) & (y >= 0) & (y < ny)).astype(F32)


def smooth_down(f, x_face, y_face, line, ends, kept, u, r, unroll):
    def emit(k, value):
        field = OMEGA * value
        u[k] = field
        r[k] = (1.0 - OMEGA) * f[k] + neighbours(field, x_face[k], y_face[k])

    sweep_out(ends, kept, line, emit, unroll)


def smooth_up(f, x_face, y_face, line, u, e, kept, mask, unroll):
    masked = (lambda v: v) if mask is None else (lambda v: v * mask)

    def rhs(k):
        field = masked(u[k] + e[k])
        u[k] = field
        return masked(f[k] + neighbours(field, x_face[k], y_face[k]))

    def emit(k, value):
        u[k] = (1.0 - OMEGA) * u[k] + OMEGA * value

    zero = jnp.zeros((u.rows, 128 * u.tiles), F32)
    ends = sweep_in(rhs, line, kept, zero, unroll)
    sweep_out(ends, kept, line, emit, unroll)


def spread_rows(cells, before, after, dest, size):
    dest[pl.ds(0, size, stride=2), :] = (0.75 * cells + 0.25 * before).reshape(size, 128)
    dest[pl.ds(1, size, stride=2), :] = (0.75 * cells + 0.25 * after).reshape(size, 128)


def spread_matrix(fine, base, coarse_count, circular=False):
    j = iota((128, fine.shape[1]), 0) + base
    parent = (fine + 2048) // 2 - 1024
    partner = parent + 2 * ((fine + 2048) % 2) - 1
    if circular:
        j, parent, partner = j % 128, parent % 128, partner % 128
    weights = jnp.where(j == parent, 0.75, jnp.where(j == partner, 0.25, 0.0))
    if not circular:
        inside = (j >= 0) & (j < coarse_count) & (fine >= 0) & (fine < 2 * coarse_count)
        weights = jnp.where(inside, weights, 0.0)
    return weights.astype(BF16)


def lane_group(rows, width):
    return iota((rows, 128), 1) // width


def fold_planes(cells, turn):
    group = lane_group(8, 32)
    out = cells[:8]
    for n in range(1, 4):
        out = jnp.where(group == n, cells[8 * n : 8 * n + 8], out)
    return pltpu.roll(out, turn, 1)


def pack_x_kernel(f, kappa, cx, cy, cz, share2, x_head, x_tail):
    for a, ref in enumerate((f, kappa, cx, cy, cz)):
        cells = ref[...].reshape(NZ, TX, TY)
        at = pl.ds(a * NZ * HALO, NZ * HALO)
        x_head[at, :] = cells[:, :HALO].reshape(NZ * HALO, TY)
        x_tail[at, :] = cells[:, TX - HALO :].reshape(NZ * HALO, TY)
    x_head[pl.ds(SLAB, 6 * NZ), :] = share2[...]
    x_tail[pl.ds(SLAB, 6 * NZ), :] = share2[...]


def pack_y_kernel(gy, f, kappa, cx, cy, cz, y_blocks, share2, y_head, y_tail):
    iy = lax.axis_index("gy")
    y, lane = iota((128, 128), 0), iota((128, 128), 1)
    fourth = y // 4 == lane % 32
    rows = lambda ref: [Field(ref, TX).row(r) for r in range(TX)]
    cx_rows, cy_rows, kappa_rows, cz_rows = rows(cx), rows(cy), rows(kappa), rows(cz)
    totals = lambda v: [(v[4 * i] + v[4 * i + 1]) + (v[4 * i + 2] + v[4 * i + 3]) for i in range(4)]
    stack = [cx_rows[4 * i] for i in range(4)] + [cx_rows[4 * i + 3] for i in range(4)]
    stack = mix(jnp.concatenate(stack + totals(kappa_rows) + totals(cz_rows), axis=0), matrix(fourth))
    ends = [matrix(fourth & (y % 4 == 0)), matrix(fourth & (y % 4 == 3))]
    sides = mix(jnp.concatenate(totals(cy_rows), axis=0), jnp.concatenate(ends, axis=1))
    group = lane_group(NZ, 32)

    def merge(cells, scale):
        out = cells[:NZ]
        for xi in range(1, 4):
            out = jnp.where(group == xi, cells[NZ * xi : NZ * (xi + 1)], out)
        return out * scale

    kinds = [merge(stack[:128], 1 / 128), merge(stack[128:256], 1 / 128)]
    kinds += [merge(sides[:, :128], 1 / 128), merge(sides[:, 128:], 1 / 128)]
    kinds += [merge(stack[256:384], 1 / 16), merge(stack[384:], 1 / 16)]
    head = [jnp.zeros((8, 128), F32)] * 3
    tail = [jnp.zeros((8, 128), F32)] * 3
    slot = iota((8, 128), 1) % 32 // 4
    for t, cells in enumerate(kinds):
        share2[pl.ds(t * NZ, NZ), :] = cells
        for zv in range(4):
            n = 4 * t + zv
            piece = cells[8 * zv : 8 * zv + 8]
            head[n // 8] = jnp.where(slot == n % 8, shift(piece, 4 * (n % 8), 1), head[n // 8])
            tail[n // 8] = jnp.where(slot == n % 8, shift(piece, 4 * (n % 8) + 4, 1), tail[n // 8])
    for n in range(3):
        y_head[pl.ds(STRIP + 8 * n, 8), :] = head[n]
        y_tail[pl.ds(STRIP + 8 * n, 8), :] = tail[n]

    x_in, y_in = y // 32, y % 32
    x_out, y_out = lane % 32 // 16, lane % 16
    pair_y, pair_x = y_in // 2 == y_out, x_in // 2 == x_out
    folds = [
        matrix(pair_y & (x_in == 2 * x_out), 0.125),
        matrix(pair_y & (x_in == 2 * x_out + 1), 0.125),
        matrix(pair_x & (y_in == 2 * y_out), 0.125),
        matrix(pair_x & (y_in == 2 * y_out + 1), 0.125),
        matrix(pair_x & pair_y, 0.25),
    ]
    for t, cells in enumerate(kinds):
        cells = fold_planes(mix(cells, folds[min(t, 4)]), 16 * iy)
        for j in range(gy):
            y_blocks[pl.ds(j * Y_BLOCK + STRIP + 24 + 8 * t, 8), :] = cells

    group = lane_group(8, 8)
    for a, ref in enumerate((f, kappa, cx, cy, cz)):
        for half in range(2):
            for zo in range(2):
                head = jnp.zeros((8, 128), F32)
                tail = jnp.zeros((8, 128), F32)
                for zi in range(16):
                    cells = ref[pl.ds((zo * 16 + zi) * TX + 8 * half, 8), :]
                    cells = shift(cells, 8 * zi, 1)
                    head = jnp.where(group == zi, cells, head)
                    tail = jnp.where(group == (zi - 1) % 16, cells, tail)
                at = pl.ds(((half * 5 + a) * 2 + zo) * 8, 8)
                y_head[at, :] = head
                y_tail[at, :] = tail
    for j in range(gy):
        y_blocks[pl.ds(j * Y_BLOCK, STRIP + 24), :] = jnp.where(iy < j, y_tail[...], y_head[...])


def forward_kernel(gx, gy, y_all, corner_head, corner_tail, copies, shares, sem):
    iy = lax.axis_index("gy")
    for j in range(gy):
        shares[pl.ds(j * 48, 48), :] = y_all[pl.ds(j * Y_BLOCK + STRIP + 24, 48), :]
    sends = [pltpu.make_async_copy(shares, copies.at[pl.ds(j * gy * 48, gy * 48), :], sem.at[j]) for j in range(gx)]
    for send in sends:
        send.start()
    half = STRIP // 2
    for n, source in enumerate((jnp.maximum(iy - 1, 0), jnp.minimum(iy + 1, gy - 1))):
        for first, dest in ((0, corner_head), (half, corner_tail)):
            dest[pl.ds(n * 104, half), :] = y_all[span(source * Y_BLOCK + first, half), :]
            dest[pl.ds(n * 104 + half, 24), :] = y_all[span(source * Y_BLOCK + STRIP, 24), :]
    for send in sends:
        send.wait()


def window2(tile, after, before, dest, first, iy, gy):
    lane = iota((NZ, 128), 1)
    first_after, first_before = jnp.where(iy < gy - 1, 36, 0), jnp.where(iy > 0, 124, 128)
    for xi in range(4):
        turned = (lane - 32 * xi + 128) % 128
        cells = jnp.where(turned < 32, tile, jnp.where(turned < first_after, after, jnp.where(turned >= first_before, before, 0.0)))
        dest[pl.ds(first + xi, NZ, stride=TX), :] = shift(cells, -32 * xi, 1)


def window_kernel(share2, xr, xl, y_all, cr, cl, x_face, y_face, inv, z_face, a, b, c, d, kappa, cz, diag):
    ix, iy = lax.axis_index("gx"), lax.axis_index("gy")
    gy = lax.axis_size("gy")
    nx, ny = lax.axis_size("gx") * 4, gy * 32
    refs = (a, b, c, d, kappa, cz)
    y_after, y_before = jnp.minimum(iy + 1, gy - 1) * Y_BLOCK, jnp.maximum(iy - 1, 0) * Y_BLOCK

    def unpack(ref, first, t, turn):
        pieces = []
        for zv in range(4):
            n = 4 * t + zv
            pieces.append(shift(ref[span(first + 8 * (n // 8), 8), :], turn - 4 * (n % 8), 1))
        return jnp.concatenate(pieces, axis=0)

    half = STRIP // 2
    for t, dest in enumerate(refs):
        for first, tile, base, right, left, r_at, l_at in (
            (0, share2, 0, y_all, y_all, y_after + STRIP, y_before + STRIP),
            (4, xr, SLAB, cr, cr, half + 24 + half, half),
            (12, xl, SLAB, cl, cl, half + 24 + half, half),
        ):
            cells = tile[pl.ds(base + t * NZ, NZ), :]
            window2(cells, unpack(right, r_at, t, 32), unpack(left, l_at, t, 92), dest, first, iy, gy)
        for x in range(8, 12):
            dest[pl.ds(x, NZ, stride=TX), :] = jnp.zeros((NZ, 128), F32)
    mask = window_mask(TX, 128, 4, 32, 4, ix, iy, nx, ny)
    fields = [Field(ref, TX) for ref in (*refs, x_face, y_face, diag, inv)]
    a, b, c, d, kappa, cz, x_face, y_face, diag, inv = fields
    for k in range(NZ):
        x_k = a[k] + shift(b[k], 1, 0)
        y_k = c[k] + shift(d[k], 1, 1)
        x_face[k] = x_k
        y_face[k] = y_k
        diag[k] = base_diag(jnp.where(mask > 0, kappa[k], 1.0), x_k, y_k)
    z_face = Field(z_face, TX, 1, NZ + 1)
    z_faces(cz, z_face)
    factor(diag, z_face, 1, inv, None)


def assemble3(gathered, dest, gx, gy, rows, at=slice(None)):
    group = lane_group(8, 16)
    for ix in range(gx):
        blocks = [gathered[ix * gy + iy, at, :] for iy in range(gy)]
        for zo in range(4):
            for xi in range(2):
                q = 2 * zo + xi
                cells = blocks[0]
                for iy in range(1, gy):
                    cells = jnp.where(group == (iy + q) % 8, blocks[iy], cells)
                dest[pl.ds(8 * zo * rows + 2 * ix + xi, 8, stride=rows), :] = shift(cells, -16 * q, 1)


def global_kernel(gx, gy, gathered, *refs):
    outs3, outs4 = refs[:5], refs[5:10]
    raw3, raw4 = refs[10:18], refs[18:26]
    rows, cols = 2 * gx, 16 * gy
    for t in range(6):
        assemble3(gathered, raw3[t], gx, gy, rows, pl.ds(8 * t, 8))
    a, b, c, d = (Field(ref, rows) for ref in raw3[:4])
    x, y = iota((rows, 128), 0), iota((rows, 128), 1)
    for k in range(NZ):
        a_k, b_k, c_k, d_k = a[k], b[k], c[k], d[k]
        a[k] = a_k + jnp.where(x > 0, shift(b_k, 1, 0), 0.0)
        b[k] = b_k + jnp.where(x < rows - 1, shift(a_k, -1, 0), 0.0)
        c[k] = jnp.where(y < cols, c_k + jnp.where(y > 0, shift(d_k, 1, 1), 0.0), 0.0)
        d[k] = jnp.where(y < cols, d_k + jnp.where(y < cols - 1, shift(c_k, -1, 1), 0.0), 0.0)
    yy, jj = iota((128, 128), 0), iota((128, 128), 1)
    keep = yy // 2 == jj
    pair, even, odd = matrix(keep), matrix(keep & (yy % 2 == 0)), matrix(keep & (yy % 2 == 1))
    size = NZ * rows // 2
    lows = [Field(ref, rows) for ref in raw3]
    first = lambda n: lows[n].every_second(0, size, 0)
    second = lambda n: lows[n].every_second(0, size, 1)
    raw4[0][...] = 0.125 * mix(first(0), pair)
    raw4[1][...] = 0.125 * mix(second(1), pair)
    raw4[2][...] = 0.125 * mix(first(2) + second(2), even)
    raw4[3][...] = 0.125 * mix(first(3) + second(3), odd)
    raw4[4][...] = 0.25 * mix(first(4) + second(4), pair)
    raw4[5][...] = 0.25 * mix(first(5) + second(5), pair)
    for raw, outs in ((raw3, outs3), (raw4, outs4)):
        x, y = iota((rows, 128), 0), iota((rows, 128), 1)
        xl, xu, yl, yu, kappa, cz = (Field(ref, rows) for ref in raw[:6])
        z_face, diag = Field(raw[6], rows, 1, NZ + 1), Field(raw[7], rows)
        x_face, y_face, inv, g, c = (Field(ref, rows) for ref in outs)
        inside_x, inside_y = (x > 0).astype(F32), ((y > 0) & (y < cols)).astype(F32)
        for k in range(NZ):
            xl_k, yl_k = xl[k], yl[k]
            diag[k] = jnp.where(y < cols, kappa[k], 1.0) + (xl_k + xu[k]) + (yl_k + yu[k])
            x_face[k] = xl_k * inside_x
            y_face[k] = yl_k * inside_y
        z_faces(cz, z_face)
        factor(diag, z_face, 1, inv, None, g_out=g, c_out=c)
        rows, cols = rows // 2, cols // 2


def down_kernel(nx, ny, *refs):
    f, kappa, cx, cy, cz, xr, xl, y_all, corner_r, corner_l = refs[:10]
    sends, outs0, outs1 = refs[10], refs[11:17], refs[17:23]
    scratch = list(refs[23:-1])
    sems = refs[-1]
    take = lambda n: [scratch.pop(0) for _ in range(n)]
    ix, iy = lax.axis_index("gx"), lax.axis_index("gy")
    gx, gy = lax.axis_size("gx"), lax.axis_size("gy")
    y_after, y_before = jnp.minimum(iy + 1, gy - 1) * Y_BLOCK, jnp.maximum(iy - 1, 0) * Y_BLOCK
    rows, tiles = 2 * TX, 2
    whole = take(11)
    names = [Field(ref, rows, tiles) for ref in whole[:10]]
    x_face, y_face, inv, u, f0, kappa0, cz0, diag, kept, r = names
    z_face = Field(whole[10], rows, tiles, NZ + 1)
    group = lane_group(8, 8)

    def window(a, tile, z, after, before, turn):
        zo = z // 16
        slab = span(a * NZ * HALO + z * HALO, HALO)
        main = jnp.concatenate([tile[span(z * TX, TX), :], xr[slab, :], xl[slab, :]], axis=0)
        at = lambda first: span(first + (a * 2 + zo) * 8, 8)
        half = STRIP // 2
        sides = []
        for right, left in (
            (y_all[at(y_after), :], y_all[at(y_before), :]),
            (y_all[at(y_after + half), :], y_all[at(y_before + half), :]),
            (corner_r[at(half + 24), :], corner_r[at(0), :]),
            (corner_l[at(half + 24), :], corner_l[at(0), :]),
        ):
            cells = jnp.where(after, right, jnp.where(before, left, 0.0))
            sides.append(pltpu.roll(cells, turn, 1))
        return jnp.concatenate([main, jnp.concatenate(sides, axis=0)], axis=1)

    mask0 = window_mask(rows, 256, TX, TY, HALO, ix, iy, nx, ny)

    def prepare(z, cz_prev):
        zi = z % 16
        after, before = (group == zi) & (iy < gy - 1), (group == (zi + 15) % 16) & (iy > 0)
        turn = (128 - 8 * zi) % 128
        f_k, kappa_k, cx_k, cy_k, cz_k = (
            window(a, tile, z, after, before, turn) for a, tile in enumerate((f, kappa, cx, cy, cz))
        )
        f0[z] = f_k
        kappa0[z] = kappa_k
        cz0[z] = cz_k
        z_face[z] = 0.5 * (cz_k + cz_prev)
        x_k, y_k = 0.5 * (cx_k + shift(cx_k, 1, 0)), 0.5 * (cy_k + shift(cy_k, 1, 1))
        x_face[z] = x_k
        y_face[z] = y_k
        diag[z] = base_diag(jnp.where(mask0 > 0, kappa_k, 1.0), x_k, y_k)
        return cz_k

    last = loop(NZ, prepare, jnp.zeros((rows, 256), F32), 2)
    z_face[NZ] = 0.5 * last
    ends = factor(diag, z_face, tiles, inv, 4, f0, kept)
    sources = [x_face, y_face, inv, z_face, u, f0]
    copies = [pltpu.make_async_copy(s.ref, o, sems.at[n]) for n, (s, o) in enumerate(zip(sources, outs0))]
    for n in (0, 1, 2, 3, 5):
        copies[n].start()
    smooth_down(f0, x_face, y_face, Line(inv, z_face), ends, kept, u, r, 2)
    copies[4].start()

    fine = (r, kappa0, cz0, x_face, y_face)
    lanes, tile_x, tile_y, halo, outs = 256, TX, TY, HALO, outs1
    for level in (1, 2):
        rows, tile_x, tile_y, halo = rows // 2, tile_x // 2, tile_y // 2, halo // 2
        nx, ny = nx // 2, ny // 2
        whole = take(11)
        names = [Field(ref, rows) for ref in whole[:10]]
        x_face, y_face, inv, u, f1, kappa1, cz1, diag, kept, r = names
        z_face = Field(whole[10], rows, 1, NZ + 1)
        mask = window_mask(rows, 128, tile_x, tile_y, halo, ix, iy, nx, ny)
        y, j = iota((lanes, 128), 0), iota((lanes, 128), 1)
        if lanes == 128:
            j = jnp.where(j < 48, j, jnp.where(j >= 80, j - 64, -1))
        pair, even = matrix(y // 2 == j), matrix(y == 2 * j)
        part = min(128, NZ * rows)
        for at in range(0, NZ * rows, part):
            here = pl.ds(at, part)
            both = lambda n: fine[n].every_second(at, part, 0) + fine[n].every_second(at, part, 1)
            f1.ref[here, :] = 0.25 * mix(both(0), pair)
            kappa1.ref[here, :] = 0.25 * mix(both(1), pair)
            cz1.ref[here, :] = 0.25 * mix(both(2), pair)
            x_face.ref[here, :] = 0.125 * mix(fine[3].every_second(at, part, 0), pair)
            y_face.ref[here, :] = 0.125 * mix(both(4), even)
        for k in range(NZ):
            f1[k] = f1[k] * mask
            diag[k] = base_diag(jnp.where(mask > 0, kappa1[k], 1.0), x_face[k], y_face[k])
        z_faces(cz1, z_face)
        ends = factor(diag, z_face, 1, inv, None, f1, kept)
        smooth_down(f1, x_face, y_face, Line(inv, z_face), ends, kept, u, r, None)
        if level == 1:
            sources = [x_face, y_face, inv, z_face, u, f1]
            more = [pltpu.make_async_copy(s.ref, o, sems.at[6 + n]) for n, (s, o) in enumerate(zip(sources, outs1))]
            for copy in more:
                copy.start()
            copies += more
        fine, lanes = (r, kappa1, cz1, x_face, y_face), 128

    send = take(1)[0]
    group = lane_group(NZ, 32)
    out = f1.row(0)
    for xi in range(1, 4):
        out = jnp.where(group == xi, shift(f1.row(xi), 32 * xi, 1), out)
    send[pl.ds(0, NZ), :] = out
    y, lane = iota((128, 128), 0), iota((128, 128), 1)
    total = jnp.zeros((NZ, 128), F32)
    for xi in range(2):
        place = (lane % 32 // 16 == xi) & (y // 2 == lane % 16) & (y < 32)
        total = total + mix(r.row(2 * xi) + r.row(2 * xi + 1), matrix(place, 0.25))
    send[pl.ds(NZ, 8), :] = fold_planes(total, 16 * iy)
    for n in range(gx * gy):
        copies.append(pltpu.make_async_copy(send, sends.at[pl.ds(n * (NZ + 8), NZ + 8), :], sems.at[12 + n]))
        copies[-1].start()
    for copy in copies:
        copy.wait()


def up_kernel(gx, gy, *refs):
    gathered, kappa = refs[:2]
    k3, k4 = refs[2:7], refs[7:12]
    saved2, saved0, saved1 = refs[12:16], refs[16:22], refs[22:28]
    solution_out, residual_out = refs[28:30]
    scratch = list(refs[30:-1])
    sems = refs[-1]
    take = lambda n: [scratch.pop(0) for _ in range(n)]
    ix, iy = lax.axis_index("gx"), lax.axis_index("gy")
    held0, held1, k2, whole3, blocks = take(6), take(6), take(4), take(1)[0], take(1)[0]
    fetch = pltpu.make_async_copy(gathered.at[:, pl.ds(NZ, 8), :], whole3, sems.at[16])
    fetch.start()
    fetches = []
    sides = [(dx, dy) for dx in (0, 1, -1) for dy in (0, 1, -1)]
    for n, (dx, dy) in enumerate(sides):
        device = jnp.clip(ix + dx, 0, gx - 1) * gy + jnp.clip(iy + dy, 0, gy - 1)
        source = gathered.at[device, pl.ds(0, NZ), :]
        fetches.append(pltpu.make_async_copy(source, blocks.at[n], sems.at[17 + n]))
        fetches[-1].start()
    copies = []
    for n, (source, dest) in enumerate(zip((*saved2, *saved1, *saved0), (*k2, *held1, *held0))):
        copies.append(pltpu.make_async_copy(source, dest, sems.at[n]))
        copies[-1].start()
    f3, u3, r3, f2, u2, kept2, f4, u4, wide, e_ref, e0_ref, kept0 = take(12)

    rows, cols = 2 * gx, 16 * gy
    fetch.wait()
    assemble3(whole3, f3, gx, gy, rows)
    y, lane = iota((128, 128), 0), iota((128, 128), 1)
    f3, u3, r3 = (Field(ref, rows) for ref in (f3, u3, r3))
    y = iota((rows, 128), 1)
    x_face3, y_face3, inv3, g3, c3 = (Field(ref, rows) for ref in k3)
    line3 = StoredLine(inv3, g3, c3)
    clean = (y < cols).astype(F32)
    for k in range(NZ):
        f3[k] = f3[k] * clean
    zero = jnp.zeros((rows, 128), F32)
    ends = sweep_in(lambda k: f3[k], line3, r3, zero, None)
    smooth_down(f3, x_face3, y_face3, line3, ends, r3, u3, Field(e_ref, rows), None)
    fine = Field(e_ref, rows)
    rows, cols = rows // 2, cols // 2
    size = NZ * rows
    yy, jj = iota((128, 128), 0), iota((128, 128), 1)
    f4[...] = 0.25 * mix(fine.every_second(0, size, 0) + fine.every_second(0, size, 1), matrix(yy // 2 == jj))
    f4, u4 = Field(f4, rows), Field(u4, rows)
    x_face4, y_face4, inv4, g4, c4 = (Field(ref, rows) for ref in k4)
    line4 = StoredLine(inv4, g4, c4)
    zero = jnp.zeros((rows, 128), F32)

    def solve4(rhs, old):
        kept, out = {}, {}
        ends = sweep_in(rhs, line4, kept, zero, None)

        def emit(k, value):
            out[k] = OMEGA * value if old is None else (1.0 - OMEGA) * old[k] + OMEGA * value

        sweep_out(ends, kept, line4, emit, None)
        for k in range(NZ):
            u4[k] = out[k]

    solve4(lambda k: f4[k], None)

    def relax(sweep, carry):
        old = [u4[k] for k in range(NZ)]
        solve4(lambda k: f4[k] + neighbours(old[k], x_face4[k], y_face4[k]), old)
        return carry

    lax.fori_loop(0, COARSE_SWEEPS - 1, relax, 0)

    cells = u4.ref[...].reshape(NZ, rows, 128)
    x = iota((1, rows, 128), 1)
    before = jnp.where(x > 0, shift(cells, 1, 1), 0.0)
    after = jnp.where(x < rows - 1, shift(cells, -1, 1), 0.0)
    spread_rows(cells, before, after, wide, size)
    e_ref[...] = mix(wide[pl.ds(0, 2 * size), :], spread_matrix(iota((128, 128), 1), 0, cols), 3)
    rows, cols = 2 * rows, 2 * cols
    smooth_up(f3, x_face3, y_face3, line3, u3, Field(e_ref, rows), r3, None, None)

    def block(dx, dy):
        inside = ((ix + dx >= 0) & (ix + dx < gx)).astype(F32)
        return blocks[sides.index((dx, dy))] * inside

    for copy in fetches + copies[:4]:
        copy.wait()
    for first, dx in ((0, 0), (4, 1), (12, -1)):
        window2(block(dx, 0), shift(block(dx, 1), 32, 1), shift(block(dx, -1), 96, 1), f2, first, iy, gy)
    for x in range(8, 12):
        f2[pl.ds(x, NZ, stride=TX), :] = jnp.zeros((NZ, 128), F32)
    f2, u2, kept2 = (Field(ref, TX) for ref in (f2, u2, kept2))
    x_face2, y_face2, inv2 = (Field(ref, TX) for ref in k2[:3])
    line2 = Line(inv2, Field(k2[3], TX, 1, NZ + 1))
    zero = jnp.zeros((TX, 128), F32)
    ends = sweep_in(lambda k: f2[k], line2, kept2, zero, None)

    def emit2(k, value):
        u2[k] = OMEGA * value

    sweep_out(ends, kept2, line2, emit2, None)

    cells = pltpu.roll(u3.ref[...].reshape(NZ, rows, 128), (rows - 2 * ix) % rows, 1)
    x = iota((1, rows, 128), 1)
    place = 2 * ix + jnp.where(x < rows // 2, x, x - rows)
    cells = jnp.where((place >= 0) & (place < rows), cells, 0.0)
    ring = lambda v, first: jnp.where(iota((1, 8, 128), 1) < first, v[:, :8], v[:, rows - 8 :])
    spread_rows(ring(cells, 4), ring(shift(cells, 1, 1), 4), ring(shift(cells, -1, 1), 4), wide, NZ * 8)
    lane = iota((128, 128), 1)
    fine_y = jnp.where(lane < 80, lane, lane - 128) + 32 * iy
    e_ref[...] = mix(wide[pl.ds(0, NZ * TX), :], spread_matrix(fine_y, 0, cols), 3)
    mask2 = window_mask(TX, 128, 4, 32, 4, ix, iy, 4 * gx, 32 * gy)
    smooth_up(f2, x_face2, y_face2, line2, u2, Field(e_ref, TX), kept2, mask2, None)

    cells = u2.ref[...].reshape(NZ, TX, 128)
    ring = lambda v: jnp.where(iota((1, 8, 128), 1) < 6, v[:, :8], v[:, 8:])
    spread_rows(ring(cells), ring(shift(cells, 1, 1)), ring(shift(cells, -1, 1)), wide, NZ * 8)
    fine_y = jnp.where(lane < 96, lane, lane - 128)
    e_ref[...] = mix(wide[pl.ds(0, NZ * TX), :], spread_matrix(fine_y, 0, 0, circular=True), 3)
    for copy in copies[4:10]:
        copy.wait()
    x_face1, y_face1, inv1, z_face1, u1, f1 = held1
    x_face1, y_face1, inv1, u1, f1 = (Field(ref, TX) for ref in (x_face1, y_face1, inv1, u1, f1))
    line1 = Line(inv1, Field(z_face1, TX, 1, NZ + 1))
    mask1 = window_mask(TX, 128, 8, 64, 4, ix, iy, 8 * gx, 64 * gy)
    smooth_up(f1, x_face1, y_face1, line1, u1, Field(e_ref, TX), kept2, mask1, None)

    cells = u1.ref[...].reshape(NZ, TX, 128)
    spread_rows(cells, shift(cells, 1, 1), shift(cells, -1, 1), wide, NZ * TX)
    rows = 2 * TX
    weights = spread_matrix(iota((128, 256), 1), 0, 0, circular=True)
    e0 = Field(e0_ref, rows, 2)
    for k in range(0, NZ, 8):
        cells = mix(wide[pl.ds(k * rows, 8 * rows), :], weights, 3)
        for t in range(2):
            e0_ref[pl.ds(e0.base(t, k), 8 * rows), :] = cells[:, 128 * t : 128 * (t + 1)]
    for copy in copies[10:]:
        copy.wait()
    x_face0, y_face0, inv0, z_face0, u0, f0 = held0
    x_face0, y_face0, inv0, u0, f0 = (Field(ref, rows, 2) for ref in (x_face0, y_face0, inv0, u0, f0))
    z_face0 = Field(z_face0, rows, 2, NZ + 1)
    mask0 = window_mask(rows, 256, TX, TY, HALO, ix, iy, TX * gx, TY * gy)
    smooth_up(f0, x_face0, y_face0, Line(inv0, z_face0), u0, e0, Field(kept0, rows, 2), mask0, 2)

    kappa = Field(kappa, TX)
    tile = lambda v: v[:TX, :TY]

    def residual(k, carry):
        below, flux_z = carry
        field = u0[k]
        flux_x = x_face0[k] * (field - shift(field, 1, 0))
        flux_y = y_face0[k] * (field - shift(field, 1, 1))
        side = (flux_x - shift(flux_x, -1, 0)) + (flux_y - shift(flux_y, -1, 1))
        here = tile(field)
        above = u0.part(0, k + 1)[:TX] if k is not NZ - 1 else jnp.zeros((TX, TY), F32)
        flux_up = z_face0.part(0, k + 1)[:TX] * (above - here)
        solution_out[span(k * TX, TX), :] = here
        out = f0.part(0, k)[:TX] - kappa[k] * here - tile(side) - flux_z + flux_up
        residual_out[span(k * TX, TX), :] = out
        return here, flux_up

    start = z_face0.part(0, 0)[:TX] * tile(u0[0])
    carry = loop(NZ - 1, residual, (start, start), 2)
    residual(NZ - 1, carry)


def call(kernel, name, outs, ins, scratch=(), in_specs=None, out_specs=None, flops=1000000):
    shapes = [jax.ShapeDtypeStruct(s, F32) for s in outs]
    return pl.pallas_call(
        kernel,
        name=name,
        out_shape=shapes,
        in_specs=in_specs or [VMEM] * len(ins),
        out_specs=out_specs or [VMEM] * len(outs),
        scratch_shapes=list(scratch),
        compiler_params=pltpu.CompilerParams(vmem_limit_bytes=56 * 1024 * 1024),
        cost_estimate=pl.CostEstimate(flops=flops, bytes_accessed=4 * sum(x.size for x in ins), transcendentals=0),
    )(*ins)


def body(right_side, kappa_sq, cond_x, cond_y, cond_z):
    gx, gy = lax.axis_size("gx"), lax.axis_size("gy")
    tiles = [v.reshape(NZ * TX, TY) for v in (right_side, kappa_sq, cond_x, cond_y, cond_z)]
    slab, strip = (SLAB + 6 * NZ, 128), (STRIP + 24, 128)
    vm = lambda *shape: pltpu.VMEM(shape, F32)
    pack_y = functools.partial(pack_y_kernel, gy)
    y_blocks, share2 = call(pack_y, "pack_y", [(gy * Y_BLOCK, 128), (6 * NZ, 128)], tiles, [vm(*strip)] * 2)
    y_all = lax.all_to_all(y_blocks.reshape(gy, Y_BLOCK, 128), "gy", 0, 0).reshape(gy * Y_BLOCK, 128)
    x_head, x_tail = call(pack_x_kernel, "pack_x", [slab, slab], [*tiles, share2])
    up = lambda n: [(i, i + 1) for i in range(n - 1)]
    down = lambda n: [(i + 1, i) for i in range(n - 1)]
    xr = lax.ppermute(x_head, "gx", down(gx))
    xl = lax.ppermute(x_tail, "gx", up(gx))
    corner_head, corner_tail, copies = call(
        functools.partial(forward_kernel, gx, gy),
        "forward",
        [(208, 128), (208, 128), (gx * gy * 48, 128)],
        [y_all],
        [vm(gy * 48, 128), pltpu.SemaphoreType.DMA((gx,))],
        out_specs=[VMEM, VMEM, ANY],
    )
    corner_r = lax.ppermute(corner_head, "gx", down(gx))
    corner_l = lax.ppermute(corner_tail, "gx", up(gx))
    shares = lax.all_to_all(copies.reshape(gx, gy * 48, 128), "gx", 0, 0).reshape(gx * gy, 48, 128)
    level = lambda rows, n: [vm(NZ * rows, 128)] * n
    faces = lambda rows, tiles: vm(tiles * (NZ + 1) * rows, 128)
    rows3, rows4 = 2 * gx, gx
    whole = call(
        functools.partial(global_kernel, gx, gy),
        "global_coeffs",
        [(NZ * rows3, 128)] * 5 + [(NZ * rows4, 128)] * 5,
        [shares],
        level(rows3, 6) + [faces(rows3, 1)] + level(rows3, 1) + level(rows4, 6) + [faces(rows4, 1)] + level(rows4, 1),
    )
    size, tall = (NZ * TX, 128), ((NZ + 1) * TX, 128)
    k2 = call(
        window_kernel, "window_coeffs", [size, size, size, tall], [share2, xr, xl, y_all, corner_r, corner_l], level(TX, 7)
    )
    big, big_z = (2 * NZ * 2 * TX, 128), (2 * (NZ + 1) * 2 * TX, 128)
    sends, *saved = call(
        functools.partial(down_kernel, gx * TX, gy * TY),
        "down",
        [(gx * gy * (NZ + 8), 128), big, big, big, big_z, big, big, size, size, size, tall, size, size],
        [*tiles, xr, xl, y_all, corner_r, corner_l],
        [vm(*big)] * 10 + [vm(*big_z)] + level(TX, 10) + [faces(TX, 1)] + level(8, 10) + [faces(8, 1)]
        + [vm(NZ + 8, 128), pltpu.SemaphoreType.DMA((12 + gx * gy,))],
        out_specs=[ANY] * 13,
    )
    gathered = lax.all_to_all(sends.reshape(gx * gy, NZ + 8, 128), ("gx", "gy"), 0, 0)
    field, residual = call(
        functools.partial(up_kernel, gx, gy),
        "up",
        [(NZ * TX, TY)] * 2,
        [gathered, tiles[1], *whole, *k2, *saved],
        [vm(*big), vm(*big), vm(*big), vm(*big_z), vm(*big), vm(*big), vm(*size), vm(*size), vm(*size), vm(*tall), vm(*size), vm(*size)]
        + [vm(*size), vm(*size), vm(*size), vm(*tall), vm(gx * gy, 8, 128), vm(9, NZ, 128)]
        + level(rows3, 3) + level(TX, 3) + level(rows4, 2)
        + [vm(NZ * 2 * TX, 128), vm(*size), vm(*big), vm(*big), pltpu.SemaphoreType.DMA((26,))],
        in_specs=[ANY] + [VMEM] * 11 + [ANY] * 16,
    )
    return field.reshape(right_side.shape), residual.reshape(right_side.shape)


def solution(mesh):
    spec = P(None, "gx", "gy")
    fits = (mesh.shape["gx"], mesh.shape["gy"]) == (8, 4)
    plan = body if fits else spread_body
    return jax.shard_map(plan, mesh=mesh, in_specs=(spec,) * 5, out_specs=(spec, spec), check_vma=False)
```

```python
import functools

import jax
import jax.numpy as jnp
from jax import lax
from jax.experimental import pallas as pl
from jax.experimental.pallas import tpu as pltpu
from jax.sharding import PartitionSpec as P

LEVELS = 4
COARSE_SWEEPS = 16


OMEGA = 0.8


def with_halo(cells, sides, width):
    for axis, dim in sides:
        count = lax.axis_size(axis)
        ends = count - 1
        head = lax.slice_in_dim(cells, 0, width, axis=dim)
        tail = lax.slice_in_dim(cells, cells.shape[dim] - width, cells.shape[dim], axis=dim)
        cells = jnp.concatenate(
            [
                lax.ppermute(tail, axis, [(i, (i + 1) % count) for i in range(ends)]),
                cells,
                lax.ppermute(head, axis, [((i + 1) % count, i) for i in range(ends)]),
            ],
            axis=dim,
        )
    return cells


def apply_op(field, padded, coeffs):
    kappa, x_up, x_low, y_up, y_low, z_up, z_low = coeffs
    zpad = jnp.pad(field, ((1, 1), (0, 0), (0, 0)))
    out = (
        kappa * field
        + x_up * (field - padded[:, 2:, 1:-1])
        + x_low * (field - padded[:, :-2, 1:-1])
    )
    out = out + y_up * (field - padded[:, 1:-1, 2:]) + y_low * (field - padded[:, 1:-1, :-2])
    return out + z_up * (field - zpad[2:]) + z_low * (field - zpad[:-2])


def face_pad(field):
    return with_halo(field, (("gx", 1), ("gy", 2)), 1)


def line_factors(coeffs):
    kappa, x_up, x_low, y_up, y_low, z_up, z_low = coeffs
    diag = kappa + x_up + x_low + y_up + y_low + z_up + z_low
    upper_src = z_up.at[-1].set(jnp.zeros_like(z_up[-1]))

    def factor_step(upper_prev, planes):
        diag_k, low_k, up_k = planes
        inv = 1.0 / (diag_k + low_k * upper_prev)
        upper = -up_k * inv
        return (upper, (inv, upper))

    start = jnp.zeros_like(diag[0])
    unused, stacked = lax.scan(factor_step, start, (diag, z_low, upper_src), unroll=True)
    return stacked


def line_solve(rhs, factors, z_low):
    inverses, uppers = factors

    def forward_step(prev, planes):
        rhs_k, low_k, inv_k = planes
        value = (rhs_k + low_k * prev) * inv_k
        return (value, value)

    start = jnp.zeros_like(rhs[0])
    unused, forward = lax.scan(forward_step, start, (rhs, z_low, inverses), unroll=True)

    def back_step(after, planes):
        fwd_k, up_k = planes
        value = fwd_k - up_k * after
        return (value, value)

    unused, result = lax.scan(back_step, start, (forward, uppers), reverse=True, unroll=True)
    return result


def mean_four(field):
    depth, rows, cols = field.shape
    return field.reshape(depth, rows // 2, 2, cols // 2, 2).mean(axis=(2, 4))


def coarsen(coeffs):
    kappa, x_up, x_low, y_up, y_low, z_up, z_low = coeffs
    depth, rows, cols = kappa.shape
    shape = (depth, rows // 2, 2, cols // 2, 2)
    xu_c = x_up.reshape(shape)[:, :, 1].mean(axis=-1) * 0.25
    xl_c = x_low.reshape(shape)[:, :, 0].mean(axis=-1) * 0.25
    yu_c = y_up.reshape(shape)[:, :, :, :, 1].mean(axis=2) * 0.25
    yl_c = y_low.reshape(shape)[:, :, :, :, 0].mean(axis=2) * 0.25
    return (mean_four(kappa), xu_c, xl_c, yu_c, yl_c, mean_four(z_up), mean_four(z_low))


def prolong(padded):
    depth = padded.shape[0]
    rows = padded.shape[1] - 2
    cols = padded.shape[2] - 2
    centre = padded[:, 1:-1, :]
    even = 0.75 * centre + 0.25 * padded[:, :-2, :]
    odd = 0.75 * centre + 0.25 * padded[:, 2:, :]
    spread = jnp.stack([even, odd], axis=2).reshape(depth, 2 * rows, cols + 2)
    centre = spread[:, :, 1:-1]
    even = 0.75 * centre + 0.25 * spread[:, :, :-2]
    odd = 0.75 * centre + 0.25 * spread[:, :, 2:]
    return jnp.stack([even, odd], axis=3).reshape(depth, 2 * rows, 2 * cols)


def coarse_solve(rhs, coeffs):
    factors = line_factors(coeffs)
    field = OMEGA * line_solve(rhs, factors, coeffs[6])

    def spread_sweep(sweep, current):
        padded = with_halo(current, (("gx", 1), ("gy", 2)), 1)
        defect = rhs - apply_op(current, padded, coeffs)
        return current + OMEGA * line_solve(defect, factors, coeffs[6])

    field = lax.fori_loop(0, COARSE_SWEEPS - 1, spread_sweep, field)
    return field


def cycle(rhs, coeffs, level):
    if level == LEVELS:
        return coarse_solve(rhs, coeffs)
    factors = line_factors(coeffs)
    field = OMEGA * line_solve(rhs, factors, coeffs[6])
    padded = face_pad(field)
    defect = rhs - apply_op(field, padded, coeffs)
    correction = cycle(mean_four(defect), coarsen(coeffs), level + 1)
    rimmed = with_halo(correction, (("gx", 1), ("gy", 2)), 1)
    field = field + prolong(rimmed)
    padded = face_pad(field)
    defect = rhs - apply_op(field, padded, coeffs)
    return field + OMEGA * line_solve(defect, factors, coeffs[6])


def spread_body(right_side, kappa_sq, cond_x, cond_y, cond_z):
    padded_x = with_halo(cond_x, (("gx", 1),), 1)
    padded_y = with_halo(cond_y, (("gy", 2),), 1)
    padded_z = jnp.pad(cond_z, ((1, 1), (0, 0), (0, 0)))
    x_up = 0.5 * (cond_x + padded_x[:, 2:, :])
    x_low = 0.5 * (cond_x + padded_x[:, :-2, :])
    y_up = 0.5 * (cond_y + padded_y[:, :, 2:])
    y_low = 0.5 * (cond_y + padded_y[:, :, :-2])
    z_up = 0.5 * (cond_z + padded_z[2:])
    z_low = 0.5 * (cond_z + padded_z[:-2])
    coeffs = (kappa_sq, x_up, x_low, y_up, y_low, z_up, z_low)
    solution_field = cycle(right_side, coeffs, 0)
    residual = right_side - apply_op(solution_field, face_pad(solution_field), coeffs)
    return (solution_field, residual)


F32 = jnp.float32
BF16 = jnp.bfloat16
NZ = 32
HALF = NZ // 2
TX, TY = 16, 128
HALO = 8
SLAB = 5 * NZ * HALO
STRIP = 160
CORNER = SLAB + 6 * NZ
VMEM = pl.BlockSpec(memory_space=pltpu.VMEM)
ANY = pl.BlockSpec(memory_space=pl.ANY)


def iota(shape, dim):
    return lax.broadcasted_iota(jnp.int32, shape, dim)


def shift(x, by, axis):
    by = by % x.shape[axis]
    return pltpu.roll(x, by, axis) if by else x


def mix(x, weights, parts=2):
    out = None
    for n in range(parts):
        part = x.astype(BF16)
        term = jnp.dot(part, weights, preferred_element_type=F32)
        out = term if out is None else out + term
        if n < parts - 1:
            x = x - part.astype(F32)
    return out


def matrix(mask, weight=1.0):
    return jnp.where(mask, weight, 0.0).astype(BF16)


def span(start, size):
    if not isinstance(start, int):
        start = pl.multiple_of(start, 8)
    return pl.ds(start, size)


class Field:
    def __init__(self, ref, rows, tiles=1, planes=NZ):
        self.ref, self.rows, self.tiles, self.planes = ref, rows, tiles, planes

    def base(self, tile, k):
        return tile * self.planes * self.rows + k * self.rows

    def part(self, tile, k):
        return self.ref[span(self.base(tile, k), self.rows), :]

    def __getitem__(self, k):
        parts = [self.part(t, k) for t in range(self.tiles)]
        return parts[0] if self.tiles == 1 else jnp.concatenate(parts, axis=1)

    def __setitem__(self, k, value):
        for t in range(self.tiles):
            self.put(t, k, value[:, 128 * t : 128 * (t + 1)])

    def put(self, tile, k, value):
        self.ref[span(self.base(tile, k), self.rows), :] = value

    def every_second(self, at, count, odd):
        parts = []
        for t in range(self.tiles):
            first = t * self.planes * self.rows + 2 * at + odd
            parts.append(self.ref[pl.ds(first, count, stride=2), :])
        return parts[0] if self.tiles == 1 else jnp.concatenate(parts, axis=1)

    def row(self, row):
        return self.ref[pl.ds(row, self.planes, stride=self.rows), :]


def loop(count, step, carry, unroll=None):
    if unroll is None or unroll >= count:
        for i in range(count):
            carry = step(i, carry)
        return carry
    return lax.fori_loop(0, count, step, carry, unroll=unroll)


def neighbours(field, x_face, y_face):
    out = x_face * shift(field, 1, 0) + shift(x_face * field, -1, 0)
    return out + (y_face * shift(field, 1, 1) + shift(y_face * field, -1, 1))


class Line:
    def __init__(self, inv, z_face):
        self.inv, self.z_face = inv, z_face

    def inward(self, k, upper):
        return self.z_face[k + 1 if upper else k] * self.inv[k]

    def outward(self, k, upper):
        return self.z_face[k if upper else k + 1] * self.inv[k]


class StoredLine:
    def __init__(self, inv, g, c):
        self.inv, self.g, self.c = inv, g, c

    def inward(self, k, upper):
        return self.g[k]

    def outward(self, k, upper):
        return self.c[k]


def sweep_in(rhs, line, keep, start, unroll):
    def step(i, carry):
        low, high = carry
        k, m = i, NZ - 1 - i
        low = rhs(k) * line.inv[k] + line.inward(k, False) * low
        high = rhs(m) * line.inv[m] + line.inward(m, True) * high
        keep[k] = low
        keep[m] = high
        return low, high

    return loop(HALF, step, (start, start), unroll)


def sweep_out(ends, kept, line, emit, unroll):
    low, high = ends
    a, b = line.outward(HALF - 1, False), line.outward(HALF, True)
    low = (low + a * high) * (1.0 / (1.0 - a * b))
    high = high + b * low

    def step(i, carry):
        low, high = carry
        k, m = HALF - 1 - i, HALF + i
        emit(k, low)
        emit(m, high)
        low = kept[k - 1] + line.outward(k - 1, False) * low
        high = kept[m + 1] + line.outward(m + 1, True) * high
        return low, high

    low, high = loop(HALF - 1, step, (low, high), unroll)
    emit(0, low)
    emit(NZ - 1, high)


def factor(diag, z_face, tiles, inv_out, unroll, rhs=None, keep=None, g_out=None, c_out=None):
    ends = []
    for t in range(tiles):
        zero = jnp.zeros((diag.rows, 128), F32)

        def one(k, upper, inv_prev, prev):
            below, above = z_face.part(t, k), z_face.part(t, k + 1)
            inner, outer = (above, below) if upper else (below, above)
            inv = 1.0 / (diag.part(t, k) + below + above - inner * inner * inv_prev)
            inv_out.put(t, k, inv)
            if g_out is not None:
                g_out.put(t, k, inner * inv)
                c_out.put(t, k, outer * inv)
            if rhs is None:
                return inv, prev
            value = (rhs.part(t, k) + inner * prev) * inv
            keep.put(t, k, value)
            return inv, value

        def step(i, carry):
            low, high = carry
            return one(i, False, *low), one(NZ - 1 - i, True, *high)

        low, high = loop(HALF, step, ((zero, zero), (zero, zero)), unroll)
        ends.append((low[1], high[1]))
    join = lambda n: ends[0][n] if tiles == 1 else jnp.concatenate([e[n] for e in ends], axis=1)
    return join(0), join(1)


def z_faces(cz, out, tiles=1):
    for t in range(tiles):
        before = None
        for k in range(NZ + 1):
            here = cz.part(t, k) if k < NZ else None
            both = here if before is None else before if here is None else here + before
            out.put(t, k, 0.5 * both)
            before = here


def base_diag(kappa, x_face, y_face):
    return kappa + (x_face + shift(x_face, -1, 0)) + (y_face + shift(y_face, -1, 1))


def window_mask(rows, lanes, tile_x, tile_y, halo, ix, iy, nx, ny):
    x, y = iota((rows, lanes), 0), iota((rows, lanes), 1)
    x = jnp.where(x < (rows + tile_x) // 2, x, x - rows)
    y = jnp.where(y < (lanes + tile_y) // 2, y, y - lanes)
    valid = (y >= -halo) & (y < tile_y + halo) & (x >= -halo) & (x < tile_x + halo)
    x, y = x + ix * tile_x, y + iy * tile_y
    return (valid & (x >= 0) & (x < nx) & (y >= 0) & (y < ny)).astype(F32)


def smooth_down(f, x_face, y_face, line, ends, kept, u, r, unroll):
    def emit(k, value):
        field = OMEGA * value
        u[k] = field
        r[k] = (1.0 - OMEGA) * f[k] + neighbours(field, x_face[k], y_face[k])

    sweep_out(ends, kept, line, emit, unroll)


def smooth_up(f, x_face, y_face, line, u, e, kept, mask, unroll):
    masked = (lambda v: v) if mask is None else (lambda v: v * mask)

    def rhs(k):
        field = masked(u[k] + e[k])
        u[k] = field
        return masked(f[k] + neighbours(field, x_face[k], y_face[k]))

    def emit(k, value):
        u[k] = (1.0 - OMEGA) * u[k] + OMEGA * value

    zero = jnp.zeros((u.rows, 128 * u.tiles), F32)
    ends = sweep_in(rhs, line, kept, zero, unroll)
    sweep_out(ends, kept, line, emit, unroll)


def spread_rows(cells, before, after, dest, size):
    dest[pl.ds(0, size, stride=2), :] = (0.75 * cells + 0.25 * before).reshape(size, 128)
    dest[pl.ds(1, size, stride=2), :] = (0.75 * cells + 0.25 * after).reshape(size, 128)


def spread_matrix(fine, base, coarse_count, circular=False):
    j = iota((128, fine.shape[1]), 0) + base
    parent = (fine + 2048) // 2 - 1024
    partner = parent + 2 * ((fine + 2048) % 2) - 1
    if circular:
        j, parent, partner = j % 128, parent % 128, partner % 128
    weights = jnp.where(j == parent, 0.75, jnp.where(j == partner, 0.25, 0.0))
    if not circular:
        inside = (j >= 0) & (j < coarse_count) & (fine >= 0) & (fine < 2 * coarse_count)
        weights = jnp.where(inside, weights, 0.0)
    return weights.astype(BF16)


def lane_group(rows, width):
    return iota((rows, 128), 1) // width


def fold_planes(cells, turn):
    group = lane_group(8, 32)
    out = cells[:8]
    for n in range(1, 4):
        out = jnp.where(group == n, cells[8 * n : 8 * n + 8], out)
    return pltpu.roll(out, turn, 1)


def pack_x_kernel(devices, f, kappa, cx, cy, cz, share2, x_head, x_tail, copies):
    iy = lax.axis_index("gy")
    for a, ref in enumerate((f, kappa, cx, cy, cz)):
        cells = ref[...].reshape(NZ, TX, TY)
        at = pl.ds(a * NZ * HALO, NZ * HALO)
        x_head[at, :] = cells[:, :HALO].reshape(NZ * HALO, TY)
        x_tail[at, :] = cells[:, TX - HALO :].reshape(NZ * HALO, TY)
    x_head[pl.ds(SLAB, 6 * NZ), :] = share2[...]
    x_tail[pl.ds(SLAB, 6 * NZ), :] = share2[...]
    y, lane = iota((128, 128), 0), iota((128, 128), 1)
    x_in, y_in = y // 32, y % 32
    x_out, y_out = lane % 32 // 16, lane % 16
    pair_y, pair_x = y_in // 2 == y_out, x_in // 2 == x_out
    folds = [
        matrix(pair_y & (x_in == 2 * x_out), 0.125),
        matrix(pair_y & (x_in == 2 * x_out + 1), 0.125),
        matrix(pair_x & (y_in == 2 * y_out), 0.125),
        matrix(pair_x & (y_in == 2 * y_out + 1), 0.125),
        matrix(pair_x & pair_y, 0.25),
    ]
    for t in range(6):
        cells = fold_planes(mix(share2[pl.ds(t * NZ, NZ), :], folds[min(t, 4)]), 16 * iy)
        for n in range(devices):
            copies[pl.ds(n * 48 + 8 * t, 8), :] = cells


def pack_corner_kernel(head_in, tail_in, yr, yl, x_head, x_tail, sem):
    half = STRIP // 2
    copies = []
    for n, source in enumerate((yl, yr)):
        for first, dest in ((0, x_head), (half, x_tail)):
            for at, to, rows in ((first, 0, half), (STRIP, half, 24)):
                into = dest.at[pl.ds(CORNER + n * 104 + to, rows), :]
                copies.append(pltpu.make_async_copy(source.at[pl.ds(at, rows), :], into, sem.at[len(copies)]))
                copies[-1].start()
    for copy in copies:
        copy.wait()


def pack_y_kernel(f, kappa, cx, cy, cz, y_head, y_tail, share2):
    y, lane = iota((128, 128), 0), iota((128, 128), 1)
    fourth = y // 4 == lane % 32
    rows = lambda ref: [Field(ref, TX).row(r) for r in range(TX)]
    cx_rows, cy_rows, kappa_rows, cz_rows = rows(cx), rows(cy), rows(kappa), rows(cz)
    totals = lambda v: [(v[4 * i] + v[4 * i + 1]) + (v[4 * i + 2] + v[4 * i + 3]) for i in range(4)]
    stack = [cx_rows[4 * i] for i in range(4)] + [cx_rows[4 * i + 3] for i in range(4)]
    stack = mix(jnp.concatenate(stack + totals(kappa_rows) + totals(cz_rows), axis=0), matrix(fourth))
    ends = [matrix(fourth & (y % 4 == 0)), matrix(fourth & (y % 4 == 3))]
    sides = mix(jnp.concatenate(totals(cy_rows), axis=0), jnp.concatenate(ends, axis=1))
    group = lane_group(NZ, 32)

    def merge(cells, scale):
        out = cells[:NZ]
        for xi in range(1, 4):
            out = jnp.where(group == xi, cells[NZ * xi : NZ * (xi + 1)], out)
        return out * scale

    kinds = [merge(stack[:128], 1 / 128), merge(stack[128:256], 1 / 128)]
    kinds += [merge(sides[:, :128], 1 / 128), merge(sides[:, 128:], 1 / 128)]
    kinds += [merge(stack[256:384], 1 / 16), merge(stack[384:], 1 / 16)]
    head = [jnp.zeros((8, 128), F32)] * 3
    tail = [jnp.zeros((8, 128), F32)] * 3
    slot = iota((8, 128), 1) % 32 // 4
    for t, cells in enumerate(kinds):
        share2[pl.ds(t * NZ, NZ), :] = cells
        for zv in range(4):
            n = 4 * t + zv
            piece = cells[8 * zv : 8 * zv + 8]
            head[n // 8] = jnp.where(slot == n % 8, shift(piece, 4 * (n % 8), 1), head[n // 8])
            tail[n // 8] = jnp.where(slot == n % 8, shift(piece, 4 * (n % 8) + 4, 1), tail[n // 8])
    for n in range(3):
        y_head[pl.ds(STRIP + 8 * n, 8), :] = head[n]
        y_tail[pl.ds(STRIP + 8 * n, 8), :] = tail[n]

    group = lane_group(8, 8)
    for a, ref in enumerate((f, kappa, cx, cy, cz)):
        for half in range(2):
            for zo in range(2):
                head = jnp.zeros((8, 128), F32)
                tail = jnp.zeros((8, 128), F32)
                for zi in range(16):
                    cells = ref[pl.ds((zo * 16 + zi) * TX + 8 * half, 8), :]
                    cells = shift(cells, 8 * zi, 1)
                    head = jnp.where(group == zi, cells, head)
                    tail = jnp.where(group == (zi - 1) % 16, cells, tail)
                at = pl.ds(((half * 5 + a) * 2 + zo) * 8, 8)
                y_head[at, :] = head
                y_tail[at, :] = tail


def window2(tile, after, before, dest, first, iy, gy):
    lane = iota((NZ, 128), 1)
    first_after, first_before = jnp.where(iy < gy - 1, 36, 0), jnp.where(iy > 0, 124, 128)
    for xi in range(4):
        turned = (lane - 32 * xi + 128) % 128
        cells = jnp.where(turned < 32, tile, jnp.where(turned < first_after, after, jnp.where(turned >= first_before, before, 0.0)))
        dest[pl.ds(first + xi, NZ, stride=TX), :] = shift(cells, -32 * xi, 1)


def window_kernel(share2, xr, xl, yr, yl, x_face, y_face, inv, z_face, a, b, c, d, kappa, cz, diag):
    ix, iy = lax.axis_index("gx"), lax.axis_index("gy")
    gy = lax.axis_size("gy")
    nx, ny = lax.axis_size("gx") * 4, gy * 32
    refs = (a, b, c, d, kappa, cz)

    def unpack(ref, first, t, turn):
        pieces = []
        for zv in range(4):
            n = 4 * t + zv
            pieces.append(shift(ref[span(first + 8 * (n // 8), 8), :], turn - 4 * (n % 8), 1))
        return jnp.concatenate(pieces, axis=0)

    near, far = CORNER + STRIP // 2, CORNER + 104 + STRIP // 2
    for t, dest in enumerate(refs):
        for first, tile, base, right, left, r_at, l_at in (
            (0, share2, 0, yr, yl, STRIP, STRIP),
            (4, xr, SLAB, xr, xr, far, near),
            (12, xl, SLAB, xl, xl, far, near),
        ):
            cells = tile[pl.ds(base + t * NZ, NZ), :]
            window2(cells, unpack(right, r_at, t, 32), unpack(left, l_at, t, 92), dest, first, iy, gy)
        for x in range(8, 12):
            dest[pl.ds(x, NZ, stride=TX), :] = jnp.zeros((NZ, 128), F32)
    mask = window_mask(TX, 128, 4, 32, 4, ix, iy, nx, ny)
    fields = [Field(ref, TX) for ref in (*refs, x_face, y_face, diag, inv)]
    a, b, c, d, kappa, cz, x_face, y_face, diag, inv = fields
    for k in range(NZ):
        x_k = a[k] + shift(b[k], 1, 0)
        y_k = c[k] + shift(d[k], 1, 1)
        x_face[k] = x_k
        y_face[k] = y_k
        diag[k] = base_diag(jnp.where(mask > 0, kappa[k], 1.0), x_k, y_k)
    z_face = Field(z_face, TX, 1, NZ + 1)
    z_faces(cz, z_face)
    factor(diag, z_face, 1, inv, None)


def assemble3(gathered, dest, gx, gy, rows, at=slice(None)):
    group = lane_group(8, 16)
    for ix in range(gx):
        blocks = [gathered[ix * gy + iy, at, :] for iy in range(gy)]
        for zo in range(4):
            for xi in range(2):
                q = 2 * zo + xi
                cells = blocks[0]
                for iy in range(1, gy):
                    cells = jnp.where(group == (iy + q) % 8, blocks[iy], cells)
                dest[pl.ds(8 * zo * rows + 2 * ix + xi, 8, stride=rows), :] = shift(cells, -16 * q, 1)


def global_kernel(gx, gy, gathered, *refs):
    outs3, outs4 = refs[:5], refs[5:10]
    raw3, raw4 = refs[10:18], refs[18:26]
    rows, cols = 2 * gx, 16 * gy
    for t in range(6):
        assemble3(gathered, raw3[t], gx, gy, rows, pl.ds(8 * t, 8))
    a, b, c, d = (Field(ref, rows) for ref in raw3[:4])
    x, y = iota((rows, 128), 0), iota((rows, 128), 1)
    for k in range(NZ):
        a_k, b_k, c_k, d_k = a[k], b[k], c[k], d[k]
        a[k] = a_k + jnp.where(x > 0, shift(b_k, 1, 0), 0.0)
        b[k] = b_k + jnp.where(x < rows - 1, shift(a_k, -1, 0), 0.0)
        c[k] = jnp.where(y < cols, c_k + jnp.where(y > 0, shift(d_k, 1, 1), 0.0), 0.0)
        d[k] = jnp.where(y < cols, d_k + jnp.where(y < cols - 1, shift(c_k, -1, 1), 0.0), 0.0)
    yy, jj = iota((128, 128), 0), iota((128, 128), 1)
    keep = yy // 2 == jj
    pair, even, odd = matrix(keep), matrix(keep & (yy % 2 == 0)), matrix(keep & (yy % 2 == 1))
    size = NZ * rows // 2
    lows = [Field(ref, rows) for ref in raw3]
    first = lambda n: lows[n].every_second(0, size, 0)
    second = lambda n: lows[n].every_second(0, size, 1)
    raw4[0][...] = 0.125 * mix(first(0), pair)
    raw4[1][...] = 0.125 * mix(second(1), pair)
    raw4[2][...] = 0.125 * mix(first(2) + second(2), even)
    raw4[3][...] = 0.125 * mix(first(3) + second(3), odd)
    raw4[4][...] = 0.25 * mix(first(4) + second(4), pair)
    raw4[5][...] = 0.25 * mix(first(5) + second(5), pair)
    for raw, outs in ((raw3, outs3), (raw4, outs4)):
        x, y = iota((rows, 128), 0), iota((rows, 128), 1)
        xl, xu, yl, yu, kappa, cz = (Field(ref, rows) for ref in raw[:6])
        z_face, diag = Field(raw[6], rows, 1, NZ + 1), Field(raw[7], rows)
        x_face, y_face, inv, g, c = (Field(ref, rows) for ref in outs)
        inside_x, inside_y = (x > 0).astype(F32), ((y > 0) & (y < cols)).astype(F32)
        for k in range(NZ):
            xl_k, yl_k = xl[k], yl[k]
            diag[k] = jnp.where(y < cols, kappa[k], 1.0) + (xl_k + xu[k]) + (yl_k + yu[k])
            x_face[k] = xl_k * inside_x
            y_face[k] = yl_k * inside_y
        z_faces(cz, z_face)
        factor(diag, z_face, 1, inv, None, g_out=g, c_out=c)
        rows, cols = rows // 2, cols // 2


def down_kernel(nx, ny, *refs):
    f, kappa, cx, cy, cz, yr, yl, xr_in, xl_in = refs[:9]
    sends3, sends2, outs0, outs1 = refs[9], refs[10], refs[11:17], refs[17:23]
    scratch = list(refs[23:-1])
    sems = refs[-1]
    take = lambda n: [scratch.pop(0) for _ in range(n)]
    ix, iy = lax.axis_index("gx"), lax.axis_index("gy")
    gx, gy = lax.axis_size("gx"), lax.axis_size("gy")
    xr, xl = take(2)
    fetches = [pltpu.make_async_copy(xr_in, xr, sems.at[12]), pltpu.make_async_copy(xl_in, xl, sems.at[13])]
    for fetch in fetches:
        fetch.start()
    rows, tiles = 2 * TX, 2
    whole = take(11)
    names = [Field(ref, rows, tiles) for ref in whole[:10]]
    x_face, y_face, inv, u, f0, kappa0, cz0, diag, kept, r = names
    z_face = Field(whole[10], rows, tiles, NZ + 1)
    group = lane_group(8, 8)

    def window(a, tile, z, after, before, turn):
        zo = z // 16
        slab = span(a * NZ * HALO + z * HALO, HALO)
        main = jnp.concatenate([tile[span(z * TX, TX), :], xr[slab, :], xl[slab, :]], axis=0)
        at = lambda first: span(first + (a * 2 + zo) * 8, 8)
        half = STRIP // 2
        sides = []
        for right, left in (
            (yr[at(0), :], yl[at(0), :]),
            (yr[at(half), :], yl[at(half), :]),
            (xr[at(CORNER + 104), :], xr[at(CORNER), :]),
            (xl[at(CORNER + 104), :], xl[at(CORNER), :]),
        ):
            cells = jnp.where(after, right, jnp.where(before, left, 0.0))
            sides.append(pltpu.roll(cells, turn, 1))
        return jnp.concatenate([main, jnp.concatenate(sides, axis=0)], axis=1)

    mask0 = window_mask(rows, 256, TX, TY, HALO, ix, iy, nx, ny)

    def prepare(z, cz_prev):
        zi = z % 16
        after, before = group == zi, group == (zi + 15) % 16
        turn = (128 - 8 * zi) % 128
        f_k, kappa_k, cx_k, cy_k, cz_k = (
            window(a, tile, z, after, before, turn) for a, tile in enumerate((f, kappa, cx, cy, cz))
        )
        f0[z] = f_k
        kappa0[z] = kappa_k
        cz0[z] = cz_k
        z_face[z] = 0.5 * (cz_k + cz_prev)
        x_k, y_k = 0.5 * (cx_k + shift(cx_k, 1, 0)), 0.5 * (cy_k + shift(cy_k, 1, 1))
        x_face[z] = x_k
        y_face[z] = y_k
        diag[z] = base_diag(jnp.where(mask0 > 0, kappa_k, 1.0), x_k, y_k)
        return cz_k

    for fetch in fetches:
        fetch.wait()
    last = loop(NZ, prepare, jnp.zeros((rows, 256), F32), 2)
    z_face[NZ] = 0.5 * last
    ends = factor(diag, z_face, tiles, inv, 4, f0, kept)
    sources = [x_face, y_face, inv, z_face, u, f0]
    copies = [pltpu.make_async_copy(s.ref, o, sems.at[n]) for n, (s, o) in enumerate(zip(sources, outs0))]
    for n in (0, 1, 2, 3, 5):
        copies[n].start()
    smooth_down(f0, x_face, y_face, Line(inv, z_face), ends, kept, u, r, 2)
    copies[4].start()

    fine = (r, kappa0, cz0, x_face, y_face)
    lanes, tile_x, tile_y, halo, outs = 256, TX, TY, HALO, outs1
    for level in (1, 2):
        rows, tile_x, tile_y, halo = rows // 2, tile_x // 2, tile_y // 2, halo // 2
        nx, ny = nx // 2, ny // 2
        whole = take(11)
        names = [Field(ref, rows) for ref in whole[:10]]
        x_face, y_face, inv, u, f1, kappa1, cz1, diag, kept, r = names
        z_face = Field(whole[10], rows, 1, NZ + 1)
        mask = window_mask(rows, 128, tile_x, tile_y, halo, ix, iy, nx, ny)
        y, j = iota((lanes, 128), 0), iota((lanes, 128), 1)
        if lanes == 128:
            j = jnp.where(j < 48, j, jnp.where(j >= 80, j - 64, -1))
        pair, even = matrix(y // 2 == j), matrix(y == 2 * j)
        part = min(128, NZ * rows)
        for at in range(0, NZ * rows, part):
            here = pl.ds(at, part)
            both = lambda n: fine[n].every_second(at, part, 0) + fine[n].every_second(at, part, 1)
            f1.ref[here, :] = 0.25 * mix(both(0), pair)
            kappa1.ref[here, :] = 0.25 * mix(both(1), pair)
            cz1.ref[here, :] = 0.25 * mix(both(2), pair)
            x_face.ref[here, :] = 0.125 * mix(fine[3].every_second(at, part, 0), pair)
            y_face.ref[here, :] = 0.125 * mix(both(4), even)
        for k in range(NZ):
            f1[k] = f1[k] * mask
            diag[k] = base_diag(jnp.where(mask > 0, kappa1[k], 1.0), x_face[k], y_face[k])
        z_faces(cz1, z_face)
        ends = factor(diag, z_face, 1, inv, None, f1, kept)
        smooth_down(f1, x_face, y_face, Line(inv, z_face), ends, kept, u, r, None)
        if level == 1:
            sources = [x_face, y_face, inv, z_face, u, f1]
            more = [pltpu.make_async_copy(s.ref, o, sems.at[6 + n]) for n, (s, o) in enumerate(zip(sources, outs1))]
            for copy in more:
                copy.start()
            copies += more
        fine, lanes = (r, kappa1, cz1, x_face, y_face), 128

    group = lane_group(NZ, 32)
    out = f1.row(0)
    for xi in range(1, 4):
        out = jnp.where(group == xi, shift(f1.row(xi), 32 * xi, 1), out)
    for n in range(gx * gy):
        sends2[pl.ds(n * NZ, NZ), :] = out
    y, lane = iota((128, 128), 0), iota((128, 128), 1)
    total = jnp.zeros((NZ, 128), F32)
    for xi in range(2):
        place = (lane % 32 // 16 == xi) & (y // 2 == lane % 16) & (y < 32)
        total = total + mix(r.row(2 * xi) + r.row(2 * xi + 1), matrix(place, 0.25))
    total = fold_planes(total, 16 * iy)
    for n in range(gx * gy):
        sends3[pl.ds(n * 8, 8), :] = total
    for copy in copies:
        copy.wait()


def coarse_kernel(gx, gy, *refs):
    gathered, k3, k4 = refs[0], refs[1:6], refs[6:11]
    u3, f3, r3, f4, u4, wide, e_ref = refs[11:]

    rows, cols = 2 * gx, 16 * gy
    assemble3(gathered, f3, gx, gy, rows)
    f3, u3, r3 = (Field(ref, rows) for ref in (f3, u3, r3))
    y = iota((rows, 128), 1)
    x_face3, y_face3, inv3, g3, c3 = (Field(ref, rows) for ref in k3)
    line3 = StoredLine(inv3, g3, c3)
    clean = (y < cols).astype(F32)
    for k in range(NZ):
        f3[k] = f3[k] * clean
    zero = jnp.zeros((rows, 128), F32)
    ends = sweep_in(lambda k: f3[k], line3, r3, zero, None)
    smooth_down(f3, x_face3, y_face3, line3, ends, r3, u3, Field(e_ref, rows), None)
    fine = Field(e_ref, rows)
    rows, cols = rows // 2, cols // 2
    size = NZ * rows
    yy, jj = iota((128, 128), 0), iota((128, 128), 1)
    f4[...] = 0.25 * mix(fine.every_second(0, size, 0) + fine.every_second(0, size, 1), matrix(yy // 2 == jj))
    f4, u4 = Field(f4, rows), Field(u4, rows)
    x_face4, y_face4, inv4, g4, c4 = (Field(ref, rows) for ref in k4)
    line4 = StoredLine(inv4, g4, c4)
    zero = jnp.zeros((rows, 128), F32)

    def solve4(rhs, old):
        kept, out = {}, {}
        ends = sweep_in(rhs, line4, kept, zero, None)

        def emit(k, value):
            out[k] = OMEGA * value if old is None else (1.0 - OMEGA) * old[k] + OMEGA * value

        sweep_out(ends, kept, line4, emit, None)
        for k in range(NZ):
            u4[k] = out[k]

    solve4(lambda k: f4[k], None)

    def relax(sweep, carry):
        old = [u4[k] for k in range(NZ)]
        solve4(lambda k: f4[k] + neighbours(old[k], x_face4[k], y_face4[k]), old)
        return carry

    lax.fori_loop(0, COARSE_SWEEPS - 1, relax, 0)

    cells = u4.ref[...].reshape(NZ, rows, 128)
    x = iota((1, rows, 128), 1)
    before = jnp.where(x > 0, shift(cells, 1, 1), 0.0)
    after = jnp.where(x < rows - 1, shift(cells, -1, 1), 0.0)
    spread_rows(cells, before, after, wide, size)
    e_ref[...] = mix(wide[pl.ds(0, 2 * size), :], spread_matrix(iota((128, 128), 1), 0, cols), 3)
    rows, cols = 2 * rows, 2 * cols
    smooth_up(f3, x_face3, y_face3, line3, u3, Field(e_ref, rows), r3, None, None)

def up_kernel(gx, gy, *refs):
    gathered, u3, kappa = refs[:3]
    saved2, saved0, saved1 = refs[3:7], refs[7:13], refs[13:19]
    solution_out, residual_out = refs[19:21]
    scratch = list(refs[21:-1])
    sems = refs[-1]
    take = lambda n: [scratch.pop(0) for _ in range(n)]
    ix, iy = lax.axis_index("gx"), lax.axis_index("gy")
    held0, held1, k2, blocks = take(6), take(6), take(4), take(1)[0]
    fetches = []
    sides = [(dx, dy) for dx in (0, 1, -1) for dy in (0, 1, -1)]
    for n, (dx, dy) in enumerate(sides):
        device = jnp.clip(ix + dx, 0, gx - 1) * gy + jnp.clip(iy + dy, 0, gy - 1)
        source = gathered.at[device]
        fetches.append(pltpu.make_async_copy(source, blocks.at[n], sems.at[16 + n]))
        fetches[-1].start()
    copies = []
    for n, (source, dest) in enumerate(zip((*saved2, *saved1, *saved0), (*k2, *held1, *held0))):
        copies.append(pltpu.make_async_copy(source, dest, sems.at[n]))
        copies[-1].start()
    f2, u2, kept2, wide, e_ref, e0_ref, kept0 = take(7)

    rows, cols = 2 * gx, 16 * gy
    def block(dx, dy):
        inside = ((ix + dx >= 0) & (ix + dx < gx)).astype(F32)
        return blocks[sides.index((dx, dy))] * inside

    for copy in fetches + copies[:4]:
        copy.wait()
    for first, dx in ((0, 0), (4, 1), (12, -1)):
        window2(block(dx, 0), shift(block(dx, 1), 32, 1), shift(block(dx, -1), 96, 1), f2, first, iy, gy)
    for x in range(8, 12):
        f2[pl.ds(x, NZ, stride=TX), :] = jnp.zeros((NZ, 128), F32)
    f2, u2, kept2 = (Field(ref, TX) for ref in (f2, u2, kept2))
    x_face2, y_face2, inv2 = (Field(ref, TX) for ref in k2[:3])
    line2 = Line(inv2, Field(k2[3], TX, 1, NZ + 1))
    zero = jnp.zeros((TX, 128), F32)
    ends = sweep_in(lambda k: f2[k], line2, kept2, zero, None)

    def emit2(k, value):
        u2[k] = OMEGA * value

    sweep_out(ends, kept2, line2, emit2, None)

    cells = pltpu.roll(u3[...].reshape(NZ, rows, 128), (rows - 2 * ix) % rows, 1)
    x = iota((1, rows, 128), 1)
    place = 2 * ix + jnp.where(x < rows // 2, x, x - rows)
    cells = jnp.where((place >= 0) & (place < rows), cells, 0.0)
    ring = lambda v, first: jnp.where(iota((1, 8, 128), 1) < first, v[:, :8], v[:, rows - 8 :])
    spread_rows(ring(cells, 4), ring(shift(cells, 1, 1), 4), ring(shift(cells, -1, 1), 4), wide, NZ * 8)
    lane = iota((128, 128), 1)
    fine_y = jnp.where(lane < 80, lane, lane - 128) + 32 * iy
    e_ref[...] = mix(wide[pl.ds(0, NZ * TX), :], spread_matrix(fine_y, 0, cols), 3)
    mask2 = window_mask(TX, 128, 4, 32, 4, ix, iy, 4 * gx, 32 * gy)
    smooth_up(f2, x_face2, y_face2, line2, u2, Field(e_ref, TX), kept2, mask2, None)

    cells = u2.ref[...].reshape(NZ, TX, 128)
    ring = lambda v: jnp.where(iota((1, 8, 128), 1) < 6, v[:, :8], v[:, 8:])
    spread_rows(ring(cells), ring(shift(cells, 1, 1)), ring(shift(cells, -1, 1)), wide, NZ * 8)
    fine_y = jnp.where(lane < 96, lane, lane - 128)
    e_ref[...] = mix(wide[pl.ds(0, NZ * TX), :], spread_matrix(fine_y, 0, 0, circular=True), 3)
    for copy in copies[4:10]:
        copy.wait()
    x_face1, y_face1, inv1, z_face1, u1, f1 = held1
    x_face1, y_face1, inv1, u1, f1 = (Field(ref, TX) for ref in (x_face1, y_face1, inv1, u1, f1))
    line1 = Line(inv1, Field(z_face1, TX, 1, NZ + 1))
    mask1 = window_mask(TX, 128, 8, 64, 4, ix, iy, 8 * gx, 64 * gy)
    smooth_up(f1, x_face1, y_face1, line1, u1, Field(e_ref, TX), kept2, mask1, None)

    cells = u1.ref[...].reshape(NZ, TX, 128)
    spread_rows(cells, shift(cells, 1, 1), shift(cells, -1, 1), wide, NZ * TX)
    rows = 2 * TX
    weights = spread_matrix(iota((128, 256), 1), 0, 0, circular=True)
    e0 = Field(e0_ref, rows, 2)
    for k in range(0, NZ, 8):
        cells = mix(wide[pl.ds(k * rows, 8 * rows), :], weights, 3)
        for t in range(2):
            e0_ref[pl.ds(e0.base(t, k), 8 * rows), :] = cells[:, 128 * t : 128 * (t + 1)]
    for copy in copies[10:]:
        copy.wait()
    x_face0, y_face0, inv0, z_face0, u0, f0 = held0
    x_face0, y_face0, inv0, u0, f0 = (Field(ref, rows, 2) for ref in (x_face0, y_face0, inv0, u0, f0))
    z_face0 = Field(z_face0, rows, 2, NZ + 1)
    mask0 = window_mask(rows, 256, TX, TY, HALO, ix, iy, TX * gx, TY * gy)
    smooth_up(f0, x_face0, y_face0, Line(inv0, z_face0), u0, e0, Field(kept0, rows, 2), mask0, 2)

    kappa = Field(kappa, TX)
    tile = lambda v: v[:TX, :TY]

    def residual(k, carry):
        below, flux_z = carry
        field = u0[k]
        flux_x = x_face0[k] * (field - shift(field, 1, 0))
        flux_y = y_face0[k] * (field - shift(field, 1, 1))
        side = (flux_x - shift(flux_x, -1, 0)) + (flux_y - shift(flux_y, -1, 1))
        here = tile(field)
        above = u0.part(0, k + 1)[:TX] if k is not NZ - 1 else jnp.zeros((TX, TY), F32)
        flux_up = z_face0.part(0, k + 1)[:TX] * (above - here)
        solution_out[span(k * TX, TX), :] = here
        out = f0.part(0, k)[:TX] - kappa[k] * here - tile(side) - flux_z + flux_up
        residual_out[span(k * TX, TX), :] = out
        return here, flux_up

    start = z_face0.part(0, 0)[:TX] * tile(u0[0])
    carry = loop(NZ - 1, residual, (start, start), 2)
    residual(NZ - 1, carry)


COSTS = {
    "pack_y": 2 * 10**9, "pack_x": 3 * 10**9, "pack_corner": 10**9, "down": 10**10,
    "window_coeffs": 4 * 10**9, "global_coeffs": 4 * 10**9, "coarse": 6 * 10**9, "up": 8 * 10**9,
}


def call(kernel, name, outs, ins, scratch=(), in_specs=None, out_specs=None, aliases=None):
    shapes = [jax.ShapeDtypeStruct(s, F32) for s in outs]
    return pl.pallas_call(
        kernel,
        name=name,
        out_shape=shapes,
        in_specs=in_specs or [VMEM] * len(ins),
        out_specs=out_specs or [VMEM] * len(outs),
        scratch_shapes=list(scratch),
        input_output_aliases=aliases or {},
        compiler_params=pltpu.CompilerParams(vmem_limit_bytes=56 * 1024 * 1024),
        cost_estimate=pl.CostEstimate(flops=COSTS[name], bytes_accessed=4 * sum(x.size for x in ins), transcendentals=0),
    )(*ins)


def body(right_side, kappa_sq, cond_x, cond_y, cond_z):
    gx, gy = lax.axis_size("gx"), lax.axis_size("gy")
    tiles = [v.reshape(NZ * TX, TY) for v in (right_side, kappa_sq, cond_x, cond_y, cond_z)]
    slab, strip = (CORNER + 208, 128), (STRIP + 24, 128)
    vm = lambda *shape: pltpu.VMEM(shape, F32)
    dma = lambda n: pltpu.SemaphoreType.DMA((n,))
    devices = gx * gy
    up = lambda n: [(i, i + 1) for i in range(n - 1)]
    down = lambda n: [(i + 1, i) for i in range(n - 1)]
    y_head, y_tail, share2 = call(pack_y_kernel, "pack_y", [strip, strip, (6 * NZ, 128)], tiles)
    yr = lax.ppermute(y_head, "gy", down(gy))
    yl = lax.ppermute(y_tail, "gy", up(gy))
    pack_x = functools.partial(pack_x_kernel, devices)
    x_head, x_tail, copies = call(pack_x, "pack_x", [slab, slab, (devices * 48, 128)], [*tiles, share2])
    x_head, x_tail = call(
        pack_corner_kernel, "pack_corner", [slab, slab], [x_head, x_tail, yr, yl], [dma(8)], [ANY] * 4, [ANY] * 2, {0: 0, 1: 1}
    )
    xr = lax.ppermute(x_head, "gx", down(gx))
    xl = lax.ppermute(x_tail, "gx", up(gx))
    copies, xr, xl = lax.optimization_barrier((copies, xr, xl))
    shares = lax.all_to_all(copies.reshape(devices, 48, 128), ("gx", "gy"), 0, 0)
    level = lambda rows, n: [vm(NZ * rows, 128)] * n
    faces = lambda rows, tiles: vm(tiles * (NZ + 1) * rows, 128)
    rows3, rows4 = 2 * gx, gx
    whole = call(
        functools.partial(global_kernel, gx, gy),
        "global_coeffs",
        [(NZ * rows3, 128)] * 5 + [(NZ * rows4, 128)] * 5,
        [shares],
        level(rows3, 6) + [faces(rows3, 1)] + level(rows3, 1) + level(rows4, 6) + [faces(rows4, 1)] + level(rows4, 1),
    )
    size, tall = (NZ * TX, 128), ((NZ + 1) * TX, 128)
    k2 = call(
        window_kernel, "window_coeffs", [size, size, size, tall], [share2, xr, xl, yr, yl], level(TX, 7)
    )
    big, big_z = (2 * NZ * 2 * TX, 128), (2 * (NZ + 1) * 2 * TX, 128)
    sends3, sends2, *saved = call(
        functools.partial(down_kernel, gx * TX, gy * TY),
        "down",
        [(devices * 8, 128), (devices * NZ, 128), big, big, big, big_z, big, big, size, size, size, tall, size, size],
        [*tiles, yr, yl, xr, xl],
        [vm(*slab)] * 2 + [vm(*big)] * 10 + [vm(*big_z)] + level(TX, 10) + [faces(TX, 1)] + level(8, 10) + [faces(8, 1)]
        + [dma(14)],
        in_specs=[VMEM] * 7 + [ANY] * 2,
        out_specs=[VMEM] * 2 + [ANY] * 12,
    )
    gathered3 = lax.all_to_all(sends3.reshape(devices, 8, 128), ("gx", "gy"), 0, 0)
    gathered2 = lax.all_to_all(sends2.reshape(devices, NZ, 128), ("gx", "gy"), 0, 0)
    u3 = call(
        functools.partial(coarse_kernel, gx, gy),
        "coarse",
        [(NZ * rows3, 128)],
        [gathered3, *whole],
        level(rows3, 2) + level(rows4, 2) + level(rows3, 2),
    )[0]
    field, residual = call(
        functools.partial(up_kernel, gx, gy),
        "up",
        [(NZ * TX, TY)] * 2,
        [gathered2, u3, tiles[1], *k2, *saved],
        [vm(*big), vm(*big), vm(*big), vm(*big_z), vm(*big), vm(*big), vm(*size), vm(*size), vm(*size), vm(*tall), vm(*size), vm(*size)]
        + [vm(*size), vm(*size), vm(*size), vm(*tall), vm(9, NZ, 128)]
        + level(TX, 3) + [vm(NZ * 2 * TX, 128), vm(*size), vm(*big), vm(*big), dma(25)],
        in_specs=[ANY] + [VMEM] * 2 + [ANY] * 16,
    )
    return field.reshape(right_side.shape), residual.reshape(right_side.shape)


def solution(mesh):
    spec = P(None, "gx", "gy")
    fits = (mesh.shape["gx"], mesh.shape["gy"]) == (8, 4)
    plan = body if fits else spread_body
    return jax.shard_map(plan, mesh=mesh, in_specs=(spec,) * 5, out_specs=(spec, spec), check_vma=False)
```

```python
import functools

import jax
import jax.numpy as jnp
from jax import lax
from jax.experimental import pallas as pl
from jax.experimental.pallas import tpu as pltpu
from jax.sharding import PartitionSpec as P

LEVELS = 4
COARSE_SWEEPS = 16


OMEGA = 0.8


def with_halo(cells, sides, width):
    for axis, dim in sides:
        count = lax.axis_size(axis)
        ends = count - 1
        head = lax.slice_in_dim(cells, 0, width, axis=dim)
        tail = lax.slice_in_dim(cells, cells.shape[dim] - width, cells.shape[dim], axis=dim)
        cells = jnp.concatenate(
            [
                lax.ppermute(tail, axis, [(i, (i + 1) % count) for i in range(ends)]),
                cells,
                lax.ppermute(head, axis, [((i + 1) % count, i) for i in range(ends)]),
            ],
            axis=dim,
        )
    return cells


def apply_op(field, padded, coeffs):
    kappa, x_up, x_low, y_up, y_low, z_up, z_low = coeffs
    zpad = jnp.pad(field, ((1, 1), (0, 0), (0, 0)))
    out = (
        kappa * field
        + x_up * (field - padded[:, 2:, 1:-1])
        + x_low * (field - padded[:, :-2, 1:-1])
    )
    out = out + y_up * (field - padded[:, 1:-1, 2:]) + y_low * (field - padded[:, 1:-1, :-2])
    return out + z_up * (field - zpad[2:]) + z_low * (field - zpad[:-2])


def face_pad(field):
    return with_halo(field, (("gx", 1), ("gy", 2)), 1)


def line_factors(coeffs):
    kappa, x_up, x_low, y_up, y_low, z_up, z_low = coeffs
    diag = kappa + x_up + x_low + y_up + y_low + z_up + z_low
    upper_src = z_up.at[-1].set(jnp.zeros_like(z_up[-1]))

    def factor_step(upper_prev, planes):
        diag_k, low_k, up_k = planes
        inv = 1.0 / (diag_k + low_k * upper_prev)
        upper = -up_k * inv
        return (upper, (inv, upper))

    start = jnp.zeros_like(diag[0])
    unused, stacked = lax.scan(factor_step, start, (diag, z_low, upper_src), unroll=True)
    return stacked


def line_solve(rhs, factors, z_low):
    inverses, uppers = factors

    def forward_step(prev, planes):
        rhs_k, low_k, inv_k = planes
        value = (rhs_k + low_k * prev) * inv_k
        return (value, value)

    start = jnp.zeros_like(rhs[0])
    unused, forward = lax.scan(forward_step, start, (rhs, z_low, inverses), unroll=True)

    def back_step(after, planes):
        fwd_k, up_k = planes
        value = fwd_k - up_k * after
        return (value, value)

    unused, result = lax.scan(back_step, start, (forward, uppers), reverse=True, unroll=True)
    return result


def mean_four(field):
    depth, rows, cols = field.shape
    return field.reshape(depth, rows // 2, 2, cols // 2, 2).mean(axis=(2, 4))


def coarsen(coeffs):
    kappa, x_up, x_low, y_up, y_low, z_up, z_low = coeffs
    depth, rows, cols = kappa.shape
    shape = (depth, rows // 2, 2, cols // 2, 2)
    xu_c = x_up.reshape(shape)[:, :, 1].mean(axis=-1) * 0.25
    xl_c = x_low.reshape(shape)[:, :, 0].mean(axis=-1) * 0.25
    yu_c = y_up.reshape(shape)[:, :, :, :, 1].mean(axis=2) * 0.25
    yl_c = y_low.reshape(shape)[:, :, :, :, 0].mean(axis=2) * 0.25
    return (mean_four(kappa), xu_c, xl_c, yu_c, yl_c, mean_four(z_up), mean_four(z_low))


def prolong(padded):
    depth = padded.shape[0]
    rows = padded.shape[1] - 2
    cols = padded.shape[2] - 2
    centre = padded[:, 1:-1, :]
    even = 0.75 * centre + 0.25 * padded[:, :-2, :]
    odd = 0.75 * centre + 0.25 * padded[:, 2:, :]
    spread = jnp.stack([even, odd], axis=2).reshape(depth, 2 * rows, cols + 2)
    centre = spread[:, :, 1:-1]
    even = 0.75 * centre + 0.25 * spread[:, :, :-2]
    odd = 0.75 * centre + 0.25 * spread[:, :, 2:]
    return jnp.stack([even, odd], axis=3).reshape(depth, 2 * rows, 2 * cols)


def coarse_solve(rhs, coeffs):
    factors = line_factors(coeffs)
    field = OMEGA * line_solve(rhs, factors, coeffs[6])

    def spread_sweep(sweep, current):
        padded = with_halo(current, (("gx", 1), ("gy", 2)), 1)
        defect = rhs - apply_op(current, padded, coeffs)
        return current + OMEGA * line_solve(defect, factors, coeffs[6])

    field = lax.fori_loop(0, COARSE_SWEEPS - 1, spread_sweep, field)
    return field


def cycle(rhs, coeffs, level):
    if level == LEVELS:
        return coarse_solve(rhs, coeffs)
    factors = line_factors(coeffs)
    field = OMEGA * line_solve(rhs, factors, coeffs[6])
    padded = face_pad(field)
    defect = rhs - apply_op(field, padded, coeffs)
    correction = cycle(mean_four(defect), coarsen(coeffs), level + 1)
    rimmed = with_halo(correction, (("gx", 1), ("gy", 2)), 1)
    field = field + prolong(rimmed)
    padded = face_pad(field)
    defect = rhs - apply_op(field, padded, coeffs)
    return field + OMEGA * line_solve(defect, factors, coeffs[6])


def spread_body(right_side, kappa_sq, cond_x, cond_y, cond_z):
    padded_x = with_halo(cond_x, (("gx", 1),), 1)
    padded_y = with_halo(cond_y, (("gy", 2),), 1)
    padded_z = jnp.pad(cond_z, ((1, 1), (0, 0), (0, 0)))
    x_up = 0.5 * (cond_x + padded_x[:, 2:, :])
    x_low = 0.5 * (cond_x + padded_x[:, :-2, :])
    y_up = 0.5 * (cond_y + padded_y[:, :, 2:])
    y_low = 0.5 * (cond_y + padded_y[:, :, :-2])
    z_up = 0.5 * (cond_z + padded_z[2:])
    z_low = 0.5 * (cond_z + padded_z[:-2])
    coeffs = (kappa_sq, x_up, x_low, y_up, y_low, z_up, z_low)
    solution_field = cycle(right_side, coeffs, 0)
    residual = right_side - apply_op(solution_field, face_pad(solution_field), coeffs)
    return (solution_field, residual)


F32 = jnp.float32
BF16 = jnp.bfloat16
NZ = 32
HALF = NZ // 2
TX, TY = 16, 128
HALO = 8
SLAB = 5 * NZ * HALO
STRIP = 160
CORNER = 104
SHARE = 40
BLOCK = NZ + 8
VMEM = pl.BlockSpec(memory_space=pltpu.VMEM)
HBM = pl.BlockSpec(memory_space=pltpu.HBM)


def iota(shape, dim):
    return lax.broadcasted_iota(jnp.int32, shape, dim)


def shift(x, by, axis):
    by = by % x.shape[axis]
    return pltpu.roll(x, by, axis) if by else x


def mix(x, weights, parts=2):
    out = None
    for n in range(parts):
        part = x.astype(BF16)
        term = jnp.dot(part, weights, preferred_element_type=F32)
        out = term if out is None else out + term
        if n < parts - 1:
            x = x - part.astype(F32)
    return out


def matrix(mask, weight=1.0):
    return jnp.where(mask, weight, 0.0).astype(BF16)


def span(start, size):
    if not isinstance(start, int):
        start = pl.multiple_of(start, 8)
    return pl.ds(start, size)


class Field:
    def __init__(self, ref, rows, tiles=1, planes=NZ):
        self.ref, self.rows, self.tiles, self.planes = ref, rows, tiles, planes

    def base(self, tile, k):
        return tile * self.planes * self.rows + k * self.rows

    def part(self, tile, k):
        return self.ref[span(self.base(tile, k), self.rows), :]

    def __getitem__(self, k):
        parts = [self.part(t, k) for t in range(self.tiles)]
        return parts[0] if self.tiles == 1 else jnp.concatenate(parts, axis=1)

    def __setitem__(self, k, value):
        for t in range(self.tiles):
            self.put(t, k, value[:, 128 * t : 128 * (t + 1)])

    def put(self, tile, k, value):
        self.ref[span(self.base(tile, k), self.rows), :] = value

    def every_second(self, at, count, odd):
        parts = []
        for t in range(self.tiles):
            first = t * self.planes * self.rows + 2 * at + odd
            parts.append(self.ref[pl.ds(first, count, stride=2), :])
        return parts[0] if self.tiles == 1 else jnp.concatenate(parts, axis=1)

    def row(self, row):
        return self.ref[pl.ds(row, self.planes, stride=self.rows), :]


def loop(count, step, carry, unroll=None):
    if unroll is None or unroll >= count:
        for i in range(count):
            carry = step(i, carry)
        return carry
    return lax.fori_loop(0, count, step, carry, unroll=unroll)


def neighbours(field, x_face, y_face):
    out = x_face * shift(field, 1, 0) + shift(x_face * field, -1, 0)
    return out + (y_face * shift(field, 1, 1) + shift(y_face * field, -1, 1))


class Line:
    def __init__(self, inv, z_face):
        self.inv, self.z_face = inv, z_face

    def inward(self, k, upper):
        return self.z_face[k + 1 if upper else k] * self.inv[k]

    def outward(self, k, upper):
        return self.z_face[k if upper else k + 1] * self.inv[k]


class StoredLine:
    def __init__(self, inv, g, c):
        self.inv, self.g, self.c = inv, g, c

    def inward(self, k, upper):
        return self.g[k]

    def outward(self, k, upper):
        return self.c[k]


def sweep_in(rhs, line, keep, start, unroll):
    def step(i, carry):
        low, high = carry
        k, m = i, NZ - 1 - i
        low = rhs(k) * line.inv[k] + line.inward(k, False) * low
        high = rhs(m) * line.inv[m] + line.inward(m, True) * high
        keep[k] = low
        keep[m] = high
        return low, high

    return loop(HALF, step, (start, start), unroll)


def sweep_out(ends, kept, line, emit, unroll):
    low, high = ends
    a, b = line.outward(HALF - 1, False), line.outward(HALF, True)
    low = (low + a * high) * (1.0 / (1.0 - a * b))
    high = high + b * low

    def step(i, carry):
        low, high = carry
        k, m = HALF - 1 - i, HALF + i
        emit(k, low)
        emit(m, high)
        low = kept[k - 1] + line.outward(k - 1, False) * low
        high = kept[m + 1] + line.outward(m + 1, True) * high
        return low, high

    low, high = loop(HALF - 1, step, (low, high), unroll)
    emit(0, low)
    emit(NZ - 1, high)


def factor(diag, z_face, tiles, inv_out, unroll, rhs=None, keep=None, g_out=None, c_out=None):
    ends = []
    for t in range(tiles):
        zero = diag.part(t, 0) * 0.0

        def one(k, upper, before, last, prev):
            below, above = z_face.part(t, k), z_face.part(t, k + 1)
            inner, outer = (above, below) if upper else (below, above)
            minor = (diag.part(t, k) + below + above) * last - (inner * inner) * before
            inv = last * (1.0 / minor)
            inv_out.put(t, k, inv)
            if g_out is not None:
                g_out.put(t, k, inner * inv)
                c_out.put(t, k, outer * inv)
            if rhs is not None:
                prev = rhs.part(t, k) * inv + (inner * inv) * prev
                keep.put(t, k, prev)
            return last, minor, prev

        def step(i, carry):
            low, high = carry
            return one(i, False, *low), one(NZ - 1 - i, True, *high)

        start = (zero, zero + 1.0, zero)
        low, high = loop(HALF, step, (start, start), unroll)
        ends.append((low[2], high[2]))
    join = lambda n: ends[0][n] if tiles == 1 else jnp.concatenate([e[n] for e in ends], axis=1)
    return join(0), join(1)


def z_faces(cz, out, tiles=1):
    for t in range(tiles):
        before = None
        for k in range(NZ + 1):
            here = cz.part(t, k) if k < NZ else None
            both = here if before is None else before if here is None else here + before
            out.put(t, k, 0.5 * both)
            before = here


def base_diag(kappa, x_face, y_face):
    return kappa + (x_face + shift(x_face, -1, 0)) + (y_face + shift(y_face, -1, 1))


def window_mask(rows, lanes, tile_x, tile_y, halo, ix, iy, nx, ny):
    x, y = iota((rows, lanes), 0), iota((rows, lanes), 1)
    x = jnp.where(x < (rows + tile_x) // 2, x, x - rows)
    y = jnp.where(y < (lanes + tile_y) // 2, y, y - lanes)
    valid = (y >= -halo) & (y < tile_y + halo) & (x >= -halo) & (x < tile_x + halo)
    x, y = x + ix * tile_x, y + iy * tile_y
    return (valid & (x >= 0) & (x < nx) & (y >= 0) & (y < ny)).astype(F32)


def smooth_down(f, x_face, y_face, line, ends, kept, u, r, unroll):
    def emit(k, value):
        field = OMEGA * value
        u[k] = field
        r[k] = (1.0 - OMEGA) * f[k] + neighbours(field, x_face[k], y_face[k])

    sweep_out(ends, kept, line, emit, unroll)


def smooth_up(f, x_face, y_face, line, u, e, kept, mask, unroll):
    masked = (lambda v: v) if mask is None else (lambda v: v * mask)

    def rhs(k):
        field = masked(u[k] + e[k])
        u[k] = field
        return masked(f[k] + neighbours(field, x_face[k], y_face[k]))

    def emit(k, value):
        u[k] = (1.0 - OMEGA) * u[k] + OMEGA * value

    zero = jnp.zeros((u.rows, 128 * u.tiles), F32)
    ends = sweep_in(rhs, line, kept, zero, unroll)
    sweep_out(ends, kept, line, emit, unroll)


def spread_rows(cells, before, after, dest, size):
    dest[pl.ds(0, size, stride=2), :] = (0.75 * cells + 0.25 * before).reshape(size, 128)
    dest[pl.ds(1, size, stride=2), :] = (0.75 * cells + 0.25 * after).reshape(size, 128)


def spread_matrix(fine, base, coarse_count, circular=False):
    j = iota((128, fine.shape[1]), 0) + base
    parent = (fine + 2048) // 2 - 1024
    partner = parent + 2 * ((fine + 2048) % 2) - 1
    if circular:
        j, parent, partner = j % 128, parent % 128, partner % 128
    weights = jnp.where(j == parent, 0.75, jnp.where(j == partner, 0.25, 0.0))
    if not circular:
        inside = (j >= 0) & (j < coarse_count) & (fine >= 0) & (fine < 2 * coarse_count)
        weights = jnp.where(inside, weights, 0.0)
    return weights.astype(BF16)


def lane_group(rows, width):
    return iota((rows, 128), 1) // width


def fold_planes(cells, turn):
    group = lane_group(8, 32)
    out = cells[:8]
    for n in range(1, 4):
        out = jnp.where(group == n, cells[8 * n : 8 * n + 8], out)
    return pltpu.roll(out, turn, 1)


def pack_x_kernel(f, kappa, cx, cy, cz, share2, x_head, x_tail):
    for a, ref in enumerate((f, kappa, cx, cy, cz)):
        cells = ref[...].reshape(NZ, TX, TY)
        at = pl.ds(a * NZ * HALO, NZ * HALO)
        x_head[at, :] = cells[:, :HALO].reshape(NZ * HALO, TY)
        x_tail[at, :] = cells[:, TX - HALO :].reshape(NZ * HALO, TY)
    x_head[pl.ds(SLAB, 6 * NZ), :] = share2[...]
    x_tail[pl.ds(SLAB, 6 * NZ), :] = share2[...]


def share_kernel(devices, share2, copies):
    iy = lax.axis_index("gy")
    y, lane = iota((128, 128), 0), iota((128, 128), 1)
    x_in, y_in = y // 32, y % 32
    x_out, y_out = lane % 32 // 16, lane % 16
    pair_y, pair_x = y_in // 2 == y_out, x_in // 2 == x_out
    a, b, c, d, kappa, cz = (share2[pl.ds(t * NZ, NZ), :] for t in range(6))
    eighth = lambda mask: matrix(mask, 0.125)
    blocks = [
        mix(a, eighth(pair_y & (x_in == 2 * x_out))) + mix(b, eighth(pair_y & (x_in == 1) & (x_out == 1))),
        mix(b, eighth(pair_y & (x_in == 3) & (x_out == 0)))
        + mix(d, eighth((x_out == 1) & (y_in == 31) & (x_in // 2 == y_out))),
        mix(c, eighth(pair_x & (y_in == 2 * y_out))) + mix(d, eighth(pair_x & (y_in == 2 * y_out - 1))),
        mix(kappa, matrix(pair_x & pair_y, 0.25)),
        mix(cz, matrix(pair_x & pair_y, 0.25)),
    ]
    for t, cells in enumerate(blocks):
        cells = fold_planes(cells, 16 * iy)
        for n in range(devices):
            copies[pl.ds(n * SHARE + 8 * t, 8), :] = cells


def pack_y_kernel(f, kappa, cx, cy, cz, y_head, y_tail, share2):
    y, lane = iota((128, 128), 0), iota((128, 128), 1)
    fourth = y // 4 == lane % 32
    rows = lambda ref: [Field(ref, TX).row(r) for r in range(TX)]
    cx_rows, cy_rows, kappa_rows, cz_rows = rows(cx), rows(cy), rows(kappa), rows(cz)
    totals = lambda v: [(v[4 * i] + v[4 * i + 1]) + (v[4 * i + 2] + v[4 * i + 3]) for i in range(4)]
    stack = [cx_rows[4 * i] for i in range(4)] + [cx_rows[4 * i + 3] for i in range(4)]
    stack = mix(jnp.concatenate(stack + totals(kappa_rows) + totals(cz_rows), axis=0), matrix(fourth))
    ends = [matrix(fourth & (y % 4 == 0)), matrix(fourth & (y % 4 == 3))]
    sides = mix(jnp.concatenate(totals(cy_rows), axis=0), jnp.concatenate(ends, axis=1))
    group = lane_group(NZ, 32)

    def merge(cells, scale):
        out = cells[:NZ]
        for xi in range(1, 4):
            out = jnp.where(group == xi, cells[NZ * xi : NZ * (xi + 1)], out)
        return out * scale

    kinds = [merge(stack[:128], 1 / 128), merge(stack[128:256], 1 / 128)]
    kinds += [merge(sides[:, :128], 1 / 128), merge(sides[:, 128:], 1 / 128)]
    kinds += [merge(stack[256:384], 1 / 16), merge(stack[384:], 1 / 16)]
    head = [jnp.zeros((8, 128), F32)] * 3
    tail = [jnp.zeros((8, 128), F32)] * 3
    slot = iota((8, 128), 1) % 32 // 4
    for t, cells in enumerate(kinds):
        share2[pl.ds(t * NZ, NZ), :] = cells
        for zv in range(4):
            n = 4 * t + zv
            piece = cells[8 * zv : 8 * zv + 8]
            head[n // 8] = jnp.where(slot == n % 8, shift(piece, 4 * (n % 8), 1), head[n // 8])
            tail[n // 8] = jnp.where(slot == n % 8, shift(piece, 4 * (n % 8) + 4, 1), tail[n // 8])
    for n in range(3):
        y_head[pl.ds(STRIP + 8 * n, 8), :] = head[n]
        y_tail[pl.ds(STRIP + 8 * n, 8), :] = tail[n]

    group = lane_group(8, 8)
    for a, ref in enumerate((f, kappa, cx, cy, cz)):
        for half in range(2):
            for zo in range(2):
                head = jnp.zeros((8, 128), F32)
                tail = jnp.zeros((8, 128), F32)
                for zi in range(16):
                    cells = ref[pl.ds((zo * 16 + zi) * TX + 8 * half, 8), :]
                    cells = shift(cells, 8 * zi, 1)
                    head = jnp.where(group == zi, cells, head)
                    tail = jnp.where(group == (zi - 1) % 16, cells, tail)
                at = pl.ds(((half * 5 + a) * 2 + zo) * 8, 8)
                y_head[at, :] = head
                y_tail[at, :] = tail


def window2(tile, after, before, dest, first, iy, gy):
    lane = iota((NZ, 128), 1)
    first_after, first_before = jnp.where(iy < gy - 1, 36, 0), jnp.where(iy > 0, 124, 128)
    for xi in range(4):
        turned = (lane - 32 * xi + 128) % 128
        cells = jnp.where(turned < 32, tile, jnp.where(turned < first_after, after, jnp.where(turned >= first_before, before, 0.0)))
        dest[pl.ds(first + xi, NZ, stride=TX), :] = shift(cells, -32 * xi, 1)


def window_kernel(share2, xr, xl, yr, yl, cr, cl, x_face, y_face, inv, z_face, a, b, c, d, kappa, cz, diag):
    ix, iy = lax.axis_index("gx"), lax.axis_index("gy")
    gy = lax.axis_size("gy")
    nx, ny = lax.axis_size("gx") * 4, gy * 32
    refs = (a, b, c, d, kappa, cz)

    def unpack(ref, first, t, turn):
        pieces = []
        for zv in range(4):
            n = 4 * t + zv
            pieces.append(shift(ref[span(first + 8 * (n // 8), 8), :], turn - 4 * (n % 8), 1))
        return jnp.concatenate(pieces, axis=0)

    near, far = STRIP // 2, CORNER + STRIP // 2
    for t, dest in enumerate(refs):
        for first, tile, base, right, left, r_at, l_at in (
            (0, share2, 0, yr, yl, STRIP, STRIP),
            (4, xr, SLAB, cr, cr, far, near),
            (12, xl, SLAB, cl, cl, far, near),
        ):
            cells = tile[pl.ds(base + t * NZ, NZ), :]
            window2(cells, unpack(right, r_at, t, 32), unpack(left, l_at, t, 92), dest, first, iy, gy)
        for x in range(8, 12):
            dest[pl.ds(x, NZ, stride=TX), :] = jnp.zeros((NZ, 128), F32)
    mask = window_mask(TX, 128, 4, 32, 4, ix, iy, nx, ny)
    fields = [Field(ref, TX) for ref in (*refs, x_face, y_face, diag, inv)]
    a, b, c, d, kappa, cz, x_face, y_face, diag, inv = fields
    for k in range(NZ):
        x_k = a[k] + shift(b[k], 1, 0)
        y_k = c[k] + shift(d[k], 1, 1)
        x_face[k] = x_k
        y_face[k] = y_k
        diag[k] = base_diag(jnp.where(mask > 0, kappa[k], 1.0), x_k, y_k)
    z_face = Field(z_face, TX, 1, NZ + 1)
    z_faces(cz, z_face)
    factor(diag, z_face, 1, inv, None)


def assemble3(gathered, dest, gx, gy, rows, at=slice(None)):
    group = lane_group(8, 16)
    for ix in range(gx):
        blocks = [gathered[ix * gy + iy, at, :] for iy in range(gy)]
        for zo in range(4):
            for xi in range(2):
                q = 2 * zo + xi
                cells = blocks[0]
                for iy in range(1, gy):
                    cells = jnp.where(group == (iy + q) % 8, blocks[iy], cells)
                dest[pl.ds(8 * zo * rows + 2 * ix + xi, 8, stride=rows), :] = shift(cells, -16 * q, 1)


def global_kernel(gx, gy, gathered, *refs):
    outs3, outs4 = refs[:5], refs[5:10]
    raw3, raw4 = refs[10:18], refs[18:26]
    rows, cols = 2 * gx, 16 * gy
    for t, n in enumerate((0, 1, 2, 4, 5)):
        assemble3(gathered, raw3[n], gx, gy, rows, pl.ds(8 * t, 8))
    xl, xu, yl, yu = (Field(ref, rows) for ref in raw3[:4])
    x, y = iota((rows, 128), 0), iota((rows, 128), 1)
    odd_row, inside = x % 2 == 1, y < cols
    for k in range(NZ):
        half = jnp.where(inside, xu[k], 0.0)
        below = jnp.where(odd_row | (x < 2), 0.0, shift(half, 2, 0))
        x_k = jnp.where(inside, xl[k] + below, 0.0)
        xl[k] = x_k
        xu[k] = jnp.where(x == rows - 1, shift(half, 1, 0), shift(x_k, -1, 0))
        next_row = shift(half, -1, 0)
        below = jnp.where(odd_row, shift(half, 15, 1), shift(next_row, 16, 1))
        y_k = jnp.where(inside, yl[k] + jnp.where((y % 16 == 0) & (y > 0), below, 0.0), 0.0)
        yl[k] = y_k
        above = jnp.where(odd_row, shift(half, 14, 1), shift(next_row, 15, 1))
        yu[k] = jnp.where(y == cols - 1, above, jnp.where(inside, shift(y_k, -1, 1), 0.0))
    yy, jj = iota((128, 128), 0), iota((128, 128), 1)
    keep = yy // 2 == jj
    pair, even, odd = matrix(keep), matrix(keep & (yy % 2 == 0)), matrix(keep & (yy % 2 == 1))
    size = NZ * rows // 2
    lows = [Field(ref, rows) for ref in raw3]
    first = lambda n: lows[n].every_second(0, size, 0)
    second = lambda n: lows[n].every_second(0, size, 1)
    raw4[0][...] = 0.125 * mix(first(0), pair)
    raw4[1][...] = 0.125 * mix(second(1), pair)
    raw4[2][...] = 0.125 * mix(first(2) + second(2), even)
    raw4[3][...] = 0.125 * mix(first(3) + second(3), odd)
    raw4[4][...] = 0.25 * mix(first(4) + second(4), pair)
    raw4[5][...] = 0.25 * mix(first(5) + second(5), pair)
    for raw, outs in ((raw3, outs3), (raw4, outs4)):
        x, y = iota((rows, 128), 0), iota((rows, 128), 1)
        xl, xu, yl, yu, kappa, cz = (Field(ref, rows) for ref in raw[:6])
        z_face, diag = Field(raw[6], rows, 1, NZ + 1), Field(raw[7], rows)
        x_face, y_face, inv, g, c = (Field(ref, rows) for ref in outs)
        inside_x, inside_y = (x > 0).astype(F32), ((y > 0) & (y < cols)).astype(F32)
        for k in range(NZ):
            xl_k, yl_k = xl[k], yl[k]
            diag[k] = jnp.where(y < cols, kappa[k], 1.0) + (xl_k + xu[k]) + (yl_k + yu[k])
            x_face[k] = xl_k * inside_x
            y_face[k] = yl_k * inside_y
        z_faces(cz, z_face)
        factor(diag, z_face, 1, inv, None, g_out=g, c_out=c)
        rows, cols = rows // 2, cols // 2


def down_kernel(nx, ny, *refs):
    f, kappa, cx, cy, cz, yr, yl, corner_r, corner_l, xr_in, xl_in = refs[:11]
    sends, outs0, outs1 = refs[11], refs[12:18], refs[18:24]
    scratch = list(refs[24:-1])
    sems = refs[-1]
    take = lambda n: [scratch.pop(0) for _ in range(n)]
    ix, iy = lax.axis_index("gx"), lax.axis_index("gy")
    gx, gy = lax.axis_size("gx"), lax.axis_size("gy")
    xr, xl = take(2)
    fetches = [pltpu.make_async_copy(xr_in, xr, sems.at[12]), pltpu.make_async_copy(xl_in, xl, sems.at[13])]
    for fetch in fetches:
        fetch.start()
    rows, tiles = 2 * TX, 2
    whole = take(11)
    names = [Field(ref, rows, tiles) for ref in whole[:10]]
    x_face, y_face, inv, u, f0, kappa0, cz0, diag, kept, r = names
    z_face = Field(whole[10], rows, tiles, NZ + 1)
    group = lane_group(8, 8)

    def window(a, tile, z, after, before, turn):
        zo = z // 16
        slab = span(a * NZ * HALO + z * HALO, HALO)
        main = jnp.concatenate([tile[span(z * TX, TX), :], xr[slab, :], xl[slab, :]], axis=0)
        at = lambda first: span(first + (a * 2 + zo) * 8, 8)
        half = STRIP // 2
        sides = []
        for right, left in (
            (yr[at(0), :], yl[at(0), :]),
            (yr[at(half), :], yl[at(half), :]),
            (corner_r[at(CORNER), :], corner_r[at(0), :]),
            (corner_l[at(CORNER), :], corner_l[at(0), :]),
        ):
            cells = jnp.where(after, right, jnp.where(before, left, 0.0))
            sides.append(pltpu.roll(cells, turn, 1))
        return jnp.concatenate([main, jnp.concatenate(sides, axis=0)], axis=1)

    mask0 = window_mask(rows, 256, TX, TY, HALO, ix, iy, nx, ny)

    def prepare(z, cz_prev):
        zi = z % 16
        after, before = group == zi, group == (zi + 15) % 16
        turn = (128 - 8 * zi) % 128
        f_k, kappa_k, cx_k, cy_k, cz_k = (
            window(a, tile, z, after, before, turn) for a, tile in enumerate((f, kappa, cx, cy, cz))
        )
        f0[z] = f_k
        kappa0[z] = kappa_k
        cz0[z] = cz_k
        z_face[z] = 0.5 * (cz_k + cz_prev)
        x_k, y_k = 0.5 * (cx_k + shift(cx_k, 1, 0)), 0.5 * (cy_k + shift(cy_k, 1, 1))
        x_face[z] = x_k
        y_face[z] = y_k
        diag[z] = base_diag(jnp.where(mask0 > 0, kappa_k, 1.0), x_k, y_k)
        return cz_k

    for fetch in fetches:
        fetch.wait()
    last = loop(NZ, prepare, jnp.zeros((rows, 256), F32), 2)
    z_face[NZ] = 0.5 * last
    ends = factor(diag, z_face, tiles, inv, 4, f0, kept)
    sources = [x_face, y_face, inv, z_face, u, f0]
    copies = [pltpu.make_async_copy(s.ref, o, sems.at[n]) for n, (s, o) in enumerate(zip(sources, outs0))]
    for n in (0, 1, 2, 3, 5):
        copies[n].start()
    smooth_down(f0, x_face, y_face, Line(inv, z_face), ends, kept, u, r, 2)
    copies[4].start()

    fine = (r, kappa0, cz0, x_face, y_face)
    lanes, tile_x, tile_y, halo, outs = 256, TX, TY, HALO, outs1
    for level in (1, 2):
        rows, tile_x, tile_y, halo = rows // 2, tile_x // 2, tile_y // 2, halo // 2
        nx, ny = nx // 2, ny // 2
        whole = take(11)
        names = [Field(ref, rows) for ref in whole[:10]]
        x_face, y_face, inv, u, f1, kappa1, cz1, diag, kept, r = names
        z_face = Field(whole[10], rows, 1, NZ + 1)
        mask = window_mask(rows, 128, tile_x, tile_y, halo, ix, iy, nx, ny)
        y, j = iota((lanes, 128), 0), iota((lanes, 128), 1)
        if lanes == 128:
            j = jnp.where(j < 48, j, jnp.where(j >= 80, j - 64, -1))
        pair, even = matrix(y // 2 == j), matrix(y == 2 * j)
        part = min(128, NZ * rows)
        for at in range(0, NZ * rows, part):
            here = pl.ds(at, part)
            both = lambda n: fine[n].every_second(at, part, 0) + fine[n].every_second(at, part, 1)
            f1.ref[here, :] = 0.25 * mix(both(0), pair)
            kappa1.ref[here, :] = 0.25 * mix(both(1), pair)
            cz1.ref[here, :] = 0.25 * mix(both(2), pair)
            x_face.ref[here, :] = 0.125 * mix(fine[3].every_second(at, part, 0), pair)
            y_face.ref[here, :] = 0.125 * mix(both(4), even)
        for k in range(NZ):
            f1[k] = f1[k] * mask
            diag[k] = base_diag(jnp.where(mask > 0, kappa1[k], 1.0), x_face[k], y_face[k])
        z_faces(cz1, z_face)
        ends = factor(diag, z_face, 1, inv, None, f1, kept)
        smooth_down(f1, x_face, y_face, Line(inv, z_face), ends, kept, u, r, None)
        if level == 1:
            sources = [x_face, y_face, inv, z_face, u, f1]
            more = [pltpu.make_async_copy(s.ref, o, sems.at[6 + n]) for n, (s, o) in enumerate(zip(sources, outs1))]
            for copy in more:
                copy.start()
            copies += more
        fine, lanes = (r, kappa1, cz1, x_face, y_face), 128

    group = lane_group(NZ, 32)
    out = f1.row(0)
    for xi in range(1, 4):
        out = jnp.where(group == xi, shift(f1.row(xi), 32 * xi, 1), out)
    for n in range(gx * gy):
        sends[pl.ds(n * BLOCK, NZ), :] = out
    y, lane = iota((128, 128), 0), iota((128, 128), 1)
    total = jnp.zeros((NZ, 128), F32)
    for xi in range(2):
        place = (lane % 32 // 16 == xi) & (y // 2 == lane % 16) & (y < 32)
        total = total + mix(r.row(2 * xi) + r.row(2 * xi + 1), matrix(place, 0.25))
    total = fold_planes(total, 16 * iy)
    for n in range(gx * gy):
        sends[pl.ds(n * BLOCK + NZ, 8), :] = total
    for copy in copies:
        copy.wait()


def up_kernel(gx, gy, *refs):
    gathered, kappa, k3, k4 = refs[0], refs[1], refs[2:7], refs[7:12]
    saved2, saved0, saved1 = refs[12:16], refs[16:22], refs[22:28]
    solution_out, residual_out = refs[28:30]
    scratch = list(refs[30:-1])
    sems = refs[-1]
    take = lambda n: [scratch.pop(0) for _ in range(n)]
    ix, iy = lax.axis_index("gx"), lax.axis_index("gy")
    held0, held1, k2, whole3, blocks = take(6), take(6), take(4), take(1)[0], take(1)[0]
    fetch = pltpu.make_async_copy(gathered.at[:, pl.ds(NZ, 8), :], whole3, sems.at[25])
    fetch.start()
    fetches = []
    sides = [(dx, dy) for dx in (0, 1, -1) for dy in (0, 1, -1)]
    for n, (dx, dy) in enumerate(sides):
        device = jnp.clip(ix + dx, 0, gx - 1) * gy + jnp.clip(iy + dy, 0, gy - 1)
        source = gathered.at[device, pl.ds(0, NZ), :]
        fetches.append(pltpu.make_async_copy(source, blocks.at[n], sems.at[16 + n]))
        fetches[-1].start()
    copies = []
    for n, (source, dest) in enumerate(zip((*saved2, *saved1, *saved0), (*k2, *held1, *held0))):
        copies.append(pltpu.make_async_copy(source, dest, sems.at[n]))
        copies[-1].start()
    f2, u2, kept2, wide, e_ref, e0_ref, kept0, u3, f3, r3, f4, u4 = take(12)

    rows, cols = 2 * gx, 16 * gy
    fetch.wait()
    assemble3(whole3, f3, gx, gy, rows)
    f3, u3, r3 = (Field(ref, rows) for ref in (f3, u3, r3))
    y = iota((rows, 128), 1)
    x_face3, y_face3, inv3, g3, c3 = (Field(ref, rows) for ref in k3)
    line3 = StoredLine(inv3, g3, c3)
    clean = (y < cols).astype(F32)
    for k in range(NZ):
        f3[k] = f3[k] * clean
    zero = jnp.zeros((rows, 128), F32)
    ends = sweep_in(lambda k: f3[k], line3, r3, zero, None)
    smooth_down(f3, x_face3, y_face3, line3, ends, r3, u3, Field(e_ref, rows), None)
    fine = Field(e_ref, rows)
    rows, cols = rows // 2, cols // 2
    size = NZ * rows
    yy, jj = iota((128, 128), 0), iota((128, 128), 1)
    f4[...] = 0.25 * mix(fine.every_second(0, size, 0) + fine.every_second(0, size, 1), matrix(yy // 2 == jj))
    f4, u4 = Field(f4, rows), Field(u4, rows)
    x_face4, y_face4, inv4, g4, c4 = (Field(ref, rows) for ref in k4)
    line4 = StoredLine(inv4, g4, c4)
    zero = jnp.zeros((rows, 128), F32)

    def solve4(rhs, old):
        kept, out = {}, {}
        ends = sweep_in(rhs, line4, kept, zero, None)

        def emit(k, value):
            out[k] = OMEGA * value if old is None else (1.0 - OMEGA) * old[k] + OMEGA * value

        sweep_out(ends, kept, line4, emit, None)
        for k in range(NZ):
            u4[k] = out[k]

    solve4(lambda k: f4[k], None)

    def relax(sweep, carry):
        old = [u4[k] for k in range(NZ)]
        solve4(lambda k: f4[k] + neighbours(old[k], x_face4[k], y_face4[k]), old)
        return carry

    lax.fori_loop(0, COARSE_SWEEPS - 1, relax, 0)

    cells = u4.ref[...].reshape(NZ, rows, 128)
    x = iota((1, rows, 128), 1)
    before = jnp.where(x > 0, shift(cells, 1, 1), 0.0)
    after = jnp.where(x < rows - 1, shift(cells, -1, 1), 0.0)
    spread_rows(cells, before, after, wide, size)
    e_ref[...] = mix(wide[pl.ds(0, 2 * size), :], spread_matrix(iota((128, 128), 1), 0, cols), 3)
    rows, cols = 2 * rows, 2 * cols
    smooth_up(f3, x_face3, y_face3, line3, u3, Field(e_ref, rows), r3, None, None)

    def block(dx, dy):
        inside = ((ix + dx >= 0) & (ix + dx < gx)).astype(F32)
        return blocks[sides.index((dx, dy))] * inside

    for copy in fetches + copies[:4]:
        copy.wait()
    for first, dx in ((0, 0), (4, 1), (12, -1)):
        window2(block(dx, 0), shift(block(dx, 1), 32, 1), shift(block(dx, -1), 96, 1), f2, first, iy, gy)
    for x in range(8, 12):
        f2[pl.ds(x, NZ, stride=TX), :] = jnp.zeros((NZ, 128), F32)
    f2, u2, kept2 = (Field(ref, TX) for ref in (f2, u2, kept2))
    x_face2, y_face2, inv2 = (Field(ref, TX) for ref in k2[:3])
    line2 = Line(inv2, Field(k2[3], TX, 1, NZ + 1))
    zero = jnp.zeros((TX, 128), F32)
    ends = sweep_in(lambda k: f2[k], line2, kept2, zero, None)

    def emit2(k, value):
        u2[k] = OMEGA * value

    sweep_out(ends, kept2, line2, emit2, None)

    cells = pltpu.roll(u3.ref[...].reshape(NZ, rows, 128), (rows - 2 * ix) % rows, 1)
    x = iota((1, rows, 128), 1)
    place = 2 * ix + jnp.where(x < rows // 2, x, x - rows)
    cells = jnp.where((place >= 0) & (place < rows), cells, 0.0)
    ring = lambda v, first: jnp.where(iota((1, 8, 128), 1) < first, v[:, :8], v[:, rows - 8 :])
    spread_rows(ring(cells, 4), ring(shift(cells, 1, 1), 4), ring(shift(cells, -1, 1), 4), wide, NZ * 8)
    lane = iota((128, 128), 1)
    fine_y = jnp.where(lane < 80, lane, lane - 128) + 32 * iy
    e_ref[...] = mix(wide[pl.ds(0, NZ * TX), :], spread_matrix(fine_y, 0, cols), 3)
    mask2 = window_mask(TX, 128, 4, 32, 4, ix, iy, 4 * gx, 32 * gy)
    smooth_up(f2, x_face2, y_face2, line2, u2, Field(e_ref, TX), kept2, mask2, None)

    cells = u2.ref[...].reshape(NZ, TX, 128)
    ring = lambda v: jnp.where(iota((1, 8, 128), 1) < 6, v[:, :8], v[:, 8:])
    spread_rows(ring(cells), ring(shift(cells, 1, 1)), ring(shift(cells, -1, 1)), wide, NZ * 8)
    fine_y = jnp.where(lane < 96, lane, lane - 128)
    e_ref[...] = mix(wide[pl.ds(0, NZ * TX), :], spread_matrix(fine_y, 0, 0, circular=True), 3)
    for copy in copies[4:10]:
        copy.wait()
    x_face1, y_face1, inv1, z_face1, u1, f1 = held1
    x_face1, y_face1, inv1, u1, f1 = (Field(ref, TX) for ref in (x_face1, y_face1, inv1, u1, f1))
    line1 = Line(inv1, Field(z_face1, TX, 1, NZ + 1))
    mask1 = window_mask(TX, 128, 8, 64, 4, ix, iy, 8 * gx, 64 * gy)
    smooth_up(f1, x_face1, y_face1, line1, u1, Field(e_ref, TX), kept2, mask1, None)

    cells = u1.ref[...].reshape(NZ, TX, 128)
    spread_rows(cells, shift(cells, 1, 1), shift(cells, -1, 1), wide, NZ * TX)
    rows = 2 * TX
    weights = spread_matrix(iota((128, 256), 1), 0, 0, circular=True)
    e0 = Field(e0_ref, rows, 2)
    for k in range(0, NZ, 8):
        cells = mix(wide[pl.ds(k * rows, 8 * rows), :], weights, 3)
        for t in range(2):
            e0_ref[pl.ds(e0.base(t, k), 8 * rows), :] = cells[:, 128 * t : 128 * (t + 1)]
    for copy in copies[10:]:
        copy.wait()
    x_face0, y_face0, inv0, z_face0, u0, f0 = held0
    x_face0, y_face0, inv0, u0, f0 = (Field(ref, rows, 2) for ref in (x_face0, y_face0, inv0, u0, f0))
    z_face0 = Field(z_face0, rows, 2, NZ + 1)
    mask0 = window_mask(rows, 256, TX, TY, HALO, ix, iy, TX * gx, TY * gy)
    smooth_up(f0, x_face0, y_face0, Line(inv0, z_face0), u0, e0, Field(kept0, rows, 2), mask0, 2)

    kappa = Field(kappa, TX)

    def residual(k, carry):
        below, flux_z = carry
        column = u0.part(0, k)
        here = column[:TX]
        flux_x = (x_face0.part(0, k) * (column - shift(column, 1, 0)))[: TX + 8]
        row = u0[k][:TX]
        flux_y = y_face0[k][:TX] * (row - shift(row, 1, 1))
        side = (flux_x - shift(flux_x, -1, 0))[:TX] + (flux_y - shift(flux_y, -1, 1))[:, :TY]
        above = u0.part(0, k + 1)[:TX] if k is not NZ - 1 else jnp.zeros((TX, TY), F32)
        flux_up = z_face0.part(0, k + 1)[:TX] * (above - here)
        solution_out[span(k * TX, TX), :] = here
        out = f0.part(0, k)[:TX] - kappa[k] * here - side - flux_z + flux_up
        residual_out[span(k * TX, TX), :] = out
        return here, flux_up

    start = z_face0.part(0, 0)[:TX] * u0.part(0, 0)[:TX]
    carry = loop(NZ - 1, residual, (start, start), 4)
    residual(NZ - 1, carry)


COSTS = {
    "pack_y": 2 * 10**9, "pack_x": 2 * 10**9, "share": 10**9, "down": 10**10,
    "window_coeffs": 4 * 10**9, "global_coeffs": 4 * 10**9, "up": 12 * 10**9,
}


def call(kernel, name, outs, ins, scratch=(), in_specs=None, out_specs=None, aliases=None):
    shapes = [jax.ShapeDtypeStruct(s, F32) for s in outs]
    return pl.pallas_call(
        kernel,
        name=name,
        out_shape=shapes,
        in_specs=in_specs or [VMEM] * len(ins),
        out_specs=out_specs or [VMEM] * len(outs),
        scratch_shapes=list(scratch),
        input_output_aliases=aliases or {},
        compiler_params=pltpu.CompilerParams(vmem_limit_bytes=56 * 1024 * 1024),
        cost_estimate=pl.CostEstimate(flops=COSTS[name], bytes_accessed=4 * sum(x.size for x in ins), transcendentals=0),
    )(*ins)


def body(right_side, kappa_sq, cond_x, cond_y, cond_z):
    gx, gy = lax.axis_size("gx"), lax.axis_size("gy")
    tiles = [v.reshape(NZ * TX, TY) for v in (right_side, kappa_sq, cond_x, cond_y, cond_z)]
    slab, strip = (SLAB + 6 * NZ, 128), (STRIP + 24, 128)
    vm = lambda *shape: pltpu.VMEM(shape, F32)
    dma = lambda n: pltpu.SemaphoreType.DMA((n,))
    devices = gx * gy
    up = lambda n: [(i, i + 1) for i in range(n - 1)]
    down = lambda n: [(i + 1, i) for i in range(n - 1)]
    y_head, y_tail, share2 = call(pack_y_kernel, "pack_y", [strip, strip, (6 * NZ, 128)], tiles)
    yr = lax.ppermute(y_head, "gy", down(gy))
    yl = lax.ppermute(y_tail, "gy", up(gy))
    x_head, x_tail = call(pack_x_kernel, "pack_x", [slab, slab], [*tiles, share2])
    xr = lax.ppermute(x_head, "gx", down(gx))
    xl = lax.ppermute(x_tail, "gx", up(gx))
    copies = call(functools.partial(share_kernel, devices), "share", [(devices * SHARE, 128)], [share2])[0]
    copies, yr, yl = lax.optimization_barrier((copies, yr, yl))
    half = STRIP // 2
    corner_r = lax.ppermute(jnp.concatenate([yl[:half], yl[STRIP:], yr[:half], yr[STRIP:]]), "gx", down(gx))
    corner_l = lax.ppermute(jnp.concatenate([yl[half:], yr[half:]]), "gx", up(gx))
    shares = lax.all_to_all(copies.reshape(devices, SHARE, 128), ("gx", "gy"), 0, 0)
    level = lambda rows, n: [vm(NZ * rows, 128)] * n
    faces = lambda rows, tiles: vm(tiles * (NZ + 1) * rows, 128)
    rows3, rows4 = 2 * gx, gx
    size, tall = (NZ * TX, 128), ((NZ + 1) * TX, 128)
    k2 = call(
        window_kernel, "window_coeffs", [size, size, size, tall], [share2, xr, xl, yr, yl, corner_r, corner_l], level(TX, 7)
    )
    big, big_z = (2 * NZ * 2 * TX, 128), (2 * (NZ + 1) * 2 * TX, 128)
    sends, *saved = call(
        functools.partial(down_kernel, gx * TX, gy * TY),
        "down",
        [(devices * BLOCK, 128), big, big, big, big_z, big, big, size, size, size, tall, size, size],
        [*tiles, yr, yl, corner_r, corner_l, xr, xl],
        [vm(*slab)] * 2 + [vm(*big)] * 10 + [vm(*big_z)] + level(TX, 10) + [faces(TX, 1)] + level(8, 10) + [faces(8, 1)]
        + [dma(14)],
        in_specs=[VMEM] * 9 + [HBM] * 2,
        out_specs=[VMEM] + [HBM] * 12,
    )
    sends, shares = lax.optimization_barrier((sends, shares))
    gathered = lax.all_to_all(sends.reshape(devices, BLOCK, 128), ("gx", "gy"), 0, 0)
    whole = call(
        functools.partial(global_kernel, gx, gy),
        "global_coeffs",
        [(NZ * rows3, 128)] * 5 + [(NZ * rows4, 128)] * 5,
        [shares],
        level(rows3, 6) + [faces(rows3, 1)] + level(rows3, 1) + level(rows4, 6) + [faces(rows4, 1)] + level(rows4, 1),
    )
    field, residual = call(
        functools.partial(up_kernel, gx, gy),
        "up",
        [(NZ * TX, TY)] * 2,
        [gathered, tiles[1], *whole, *k2, *saved],
        [vm(*big), vm(*big), vm(*big), vm(*big_z), vm(*big), vm(*big), vm(*size), vm(*size), vm(*size), vm(*tall), vm(*size), vm(*size)]
        + [vm(*size), vm(*size), vm(*size), vm(*tall), vm(devices, 8, 128), vm(9, NZ, 128)]
        + level(TX, 3) + [vm(NZ * 2 * TX, 128), vm(*size), vm(*big), vm(*big)]
        + level(rows3, 3) + level(rows4, 2) + [dma(26)],
        in_specs=[HBM] + [VMEM] * 11 + [HBM] * 16,
    )
    return field.reshape(right_side.shape), residual.reshape(right_side.shape)


def solution(mesh):
    spec = P(None, "gx", "gy")
    fits = (mesh.shape["gx"], mesh.shape["gy"]) == (8, 4)
    plan = body if fits else spread_body
    return jax.shard_map(plan, mesh=mesh, in_specs=(spec,) * 5, out_specs=(spec, spec), check_vma=False)
```

```python
import functools

import jax
import jax.numpy as jnp
from jax import lax
from jax.experimental import pallas as pl
from jax.experimental.pallas import tpu as pltpu
from jax.sharding import PartitionSpec as P

LEVELS = 4
COARSE_SWEEPS = 16


OMEGA = 0.8


def with_halo(cells, sides, width):
    for axis, dim in sides:
        count = lax.axis_size(axis)
        ends = count - 1
        head = lax.slice_in_dim(cells, 0, width, axis=dim)
        tail = lax.slice_in_dim(cells, cells.shape[dim] - width, cells.shape[dim], axis=dim)
        cells = jnp.concatenate(
            [
                lax.ppermute(tail, axis, [(i, (i + 1) % count) for i in range(ends)]),
                cells,
                lax.ppermute(head, axis, [((i + 1) % count, i) for i in range(ends)]),
            ],
            axis=dim,
        )
    return cells


def apply_op(field, padded, coeffs):
    kappa, x_up, x_low, y_up, y_low, z_up, z_low = coeffs
    zpad = jnp.pad(field, ((1, 1), (0, 0), (0, 0)))
    out = (
        kappa * field
        + x_up * (field - padded[:, 2:, 1:-1])
        + x_low * (field - padded[:, :-2, 1:-1])
    )
    out = out + y_up * (field - padded[:, 1:-1, 2:]) + y_low * (field - padded[:, 1:-1, :-2])
    return out + z_up * (field - zpad[2:]) + z_low * (field - zpad[:-2])


def face_pad(field):
    return with_halo(field, (("gx", 1), ("gy", 2)), 1)


def line_factors(coeffs):
    kappa, x_up, x_low, y_up, y_low, z_up, z_low = coeffs
    diag = kappa + x_up + x_low + y_up + y_low + z_up + z_low
    upper_src = z_up.at[-1].set(jnp.zeros_like(z_up[-1]))

    def factor_step(upper_prev, planes):
        diag_k, low_k, up_k = planes
        inv = 1.0 / (diag_k + low_k * upper_prev)
        upper = -up_k * inv
        return (upper, (inv, upper))

    start = jnp.zeros_like(diag[0])
    unused, stacked = lax.scan(factor_step, start, (diag, z_low, upper_src), unroll=True)
    return stacked


def line_solve(rhs, factors, z_low):
    inverses, uppers = factors

    def forward_step(prev, planes):
        rhs_k, low_k, inv_k = planes
        value = (rhs_k + low_k * prev) * inv_k
        return (value, value)

    start = jnp.zeros_like(rhs[0])
    unused, forward = lax.scan(forward_step, start, (rhs, z_low, inverses), unroll=True)

    def back_step(after, planes):
        fwd_k, up_k = planes
        value = fwd_k - up_k * after
        return (value, value)

    unused, result = lax.scan(back_step, start, (forward, uppers), reverse=True, unroll=True)
    return result


def mean_four(field):
    depth, rows, cols = field.shape
    return field.reshape(depth, rows // 2, 2, cols // 2, 2).mean(axis=(2, 4))


def coarsen(coeffs):
    kappa, x_up, x_low, y_up, y_low, z_up, z_low = coeffs
    depth, rows, cols = kappa.shape
    shape = (depth, rows // 2, 2, cols // 2, 2)
    xu_c = x_up.reshape(shape)[:, :, 1].mean(axis=-1) * 0.25
    xl_c = x_low.reshape(shape)[:, :, 0].mean(axis=-1) * 0.25
    yu_c = y_up.reshape(shape)[:, :, :, :, 1].mean(axis=2) * 0.25
    yl_c = y_low.reshape(shape)[:, :, :, :, 0].mean(axis=2) * 0.25
    return (mean_four(kappa), xu_c, xl_c, yu_c, yl_c, mean_four(z_up), mean_four(z_low))


def prolong(padded):
    depth = padded.shape[0]
    rows = padded.shape[1] - 2
    cols = padded.shape[2] - 2
    centre = padded[:, 1:-1, :]
    even = 0.75 * centre + 0.25 * padded[:, :-2, :]
    odd = 0.75 * centre + 0.25 * padded[:, 2:, :]
    spread = jnp.stack([even, odd], axis=2).reshape(depth, 2 * rows, cols + 2)
    centre = spread[:, :, 1:-1]
    even = 0.75 * centre + 0.25 * spread[:, :, :-2]
    odd = 0.75 * centre + 0.25 * spread[:, :, 2:]
    return jnp.stack([even, odd], axis=3).reshape(depth, 2 * rows, 2 * cols)


def coarse_solve(rhs, coeffs):
    factors = line_factors(coeffs)
    field = OMEGA * line_solve(rhs, factors, coeffs[6])

    def spread_sweep(sweep, current):
        padded = with_halo(current, (("gx", 1), ("gy", 2)), 1)
        defect = rhs - apply_op(current, padded, coeffs)
        return current + OMEGA * line_solve(defect, factors, coeffs[6])

    field = lax.fori_loop(0, COARSE_SWEEPS - 1, spread_sweep, field)
    return field


def cycle(rhs, coeffs, level):
    if level == LEVELS:
        return coarse_solve(rhs, coeffs)
    factors = line_factors(coeffs)
    field = OMEGA * line_solve(rhs, factors, coeffs[6])
    padded = face_pad(field)
    defect = rhs - apply_op(field, padded, coeffs)
    correction = cycle(mean_four(defect), coarsen(coeffs), level + 1)
    rimmed = with_halo(correction, (("gx", 1), ("gy", 2)), 1)
    field = field + prolong(rimmed)
    padded = face_pad(field)
    defect = rhs - apply_op(field, padded, coeffs)
    return field + OMEGA * line_solve(defect, factors, coeffs[6])


def spread_body(right_side, kappa_sq, cond_x, cond_y, cond_z):
    padded_x = with_halo(cond_x, (("gx", 1),), 1)
    padded_y = with_halo(cond_y, (("gy", 2),), 1)
    padded_z = jnp.pad(cond_z, ((1, 1), (0, 0), (0, 0)))
    x_up = 0.5 * (cond_x + padded_x[:, 2:, :])
    x_low = 0.5 * (cond_x + padded_x[:, :-2, :])
    y_up = 0.5 * (cond_y + padded_y[:, :, 2:])
    y_low = 0.5 * (cond_y + padded_y[:, :, :-2])
    z_up = 0.5 * (cond_z + padded_z[2:])
    z_low = 0.5 * (cond_z + padded_z[:-2])
    coeffs = (kappa_sq, x_up, x_low, y_up, y_low, z_up, z_low)
    solution_field = cycle(right_side, coeffs, 0)
    residual = right_side - apply_op(solution_field, face_pad(solution_field), coeffs)
    return (solution_field, residual)


F32 = jnp.float32
BF16 = jnp.bfloat16
NZ = 32
HALF = NZ // 2
TX, TY = 16, 128
HALO = 8
SLAB = 5 * NZ * HALO
STRIP = 160
CORNER = 104
SHARE = 40
BLOCK = NZ + 8
VMEM = pl.BlockSpec(memory_space=pltpu.VMEM)
ANY = pl.BlockSpec(memory_space=pl.ANY)


def iota(shape, dim):
    return lax.broadcasted_iota(jnp.int32, shape, dim)


def shift(x, by, axis):
    by = by % x.shape[axis]
    return pltpu.roll(x, by, axis) if by else x


def mix(x, weights, parts=2):
    pieces = []
    for n in range(parts):
        piece = x.astype(BF16)
        pieces.append(piece)
        if n < parts - 1:
            x = x - piece.astype(F32)
    out = jnp.dot(jnp.concatenate(pieces, axis=0), weights, preferred_element_type=F32)
    rows = x.shape[0]
    return sum(out[n * rows : (n + 1) * rows] for n in reversed(range(parts)))


def matrix(mask, weight=1.0):
    return jnp.where(mask, weight, 0.0).astype(BF16)


def span(start, size):
    if not isinstance(start, int):
        start = pl.multiple_of(start, 8)
    return pl.ds(start, size)


class Field:
    def __init__(self, ref, rows, tiles=1, planes=NZ):
        self.ref, self.rows, self.tiles, self.planes = ref, rows, tiles, planes

    def base(self, tile, k):
        return tile * self.planes * self.rows + k * self.rows

    def part(self, tile, k):
        return self.ref[span(self.base(tile, k), self.rows), :]

    def __getitem__(self, k):
        parts = [self.part(t, k) for t in range(self.tiles)]
        return parts[0] if self.tiles == 1 else jnp.concatenate(parts, axis=1)

    def __setitem__(self, k, value):
        for t in range(self.tiles):
            self.put(t, k, value[:, 128 * t : 128 * (t + 1)])

    def put(self, tile, k, value):
        self.ref[span(self.base(tile, k), self.rows), :] = value

    def every_second(self, at, count, odd):
        parts = []
        for t in range(self.tiles):
            first = t * self.planes * self.rows + 2 * at + odd
            parts.append(self.ref[pl.ds(first, count, stride=2), :])
        return parts[0] if self.tiles == 1 else jnp.concatenate(parts, axis=1)

    def row(self, row):
        return self.ref[pl.ds(row, self.planes, stride=self.rows), :]


def loop(count, step, carry, unroll=None):
    if unroll is None or unroll >= count:
        for i in range(count):
            carry = step(i, carry)
        return carry
    return lax.fori_loop(0, count, step, carry, unroll=unroll)


def neighbours(field, x_face, y_face):
    out = x_face * shift(field, 1, 0) + shift(x_face * field, -1, 0)
    return out + (y_face * shift(field, 1, 1) + shift(y_face * field, -1, 1))


class Line:
    def __init__(self, inv, z_face):
        self.inv, self.z_face = inv, z_face

    def inward(self, k, upper):
        return self.z_face[k + 1 if upper else k] * self.inv[k]

    def outward(self, k, upper):
        return self.z_face[k if upper else k + 1] * self.inv[k]


class StoredLine:
    def __init__(self, inv, g, c):
        self.inv, self.g, self.c = inv, g, c

    def inward(self, k, upper):
        return self.g[k]

    def outward(self, k, upper):
        return self.c[k]


def sweep_in(rhs, line, keep, start, unroll):
    def step(i, carry):
        low, high = carry
        k, m = i, NZ - 1 - i
        low = rhs(k) * line.inv[k] + line.inward(k, False) * low
        high = rhs(m) * line.inv[m] + line.inward(m, True) * high
        keep[k] = low
        keep[m] = high
        return low, high

    return loop(HALF, step, (start, start), unroll)


def sweep_out(ends, kept, line, emit, unroll):
    low, high = ends
    a, b = line.outward(HALF - 1, False), line.outward(HALF, True)
    low = (low + a * high) * (1.0 / (1.0 - a * b))
    high = high + b * low

    def step(i, carry):
        low, high = carry
        k, m = HALF - 1 - i, HALF + i
        emit(k, low)
        emit(m, high)
        low = kept[k - 1] + line.outward(k - 1, False) * low
        high = kept[m + 1] + line.outward(m + 1, True) * high
        return low, high

    low, high = loop(HALF - 1, step, (low, high), unroll)
    emit(0, low)
    emit(NZ - 1, high)


def factor(diag, z_face, tiles, inv_out, unroll, rhs=None, keep=None, g_out=None, c_out=None):
    ends = []
    for t in range(tiles):
        zero = diag.part(t, 0) * 0.0

        def one(k, upper, before, last, prev):
            below, above = z_face.part(t, k), z_face.part(t, k + 1)
            inner, outer = (above, below) if upper else (below, above)
            minor = (diag.part(t, k) + below + above) * last - (inner * inner) * before
            inv = last * (1.0 / minor)
            inv_out.put(t, k, inv)
            if g_out is not None:
                g_out.put(t, k, inner * inv)
                c_out.put(t, k, outer * inv)
            if rhs is not None:
                prev = rhs.part(t, k) * inv + (inner * inv) * prev
                keep.put(t, k, prev)
            return last, minor, prev

        def step(i, carry):
            low, high = carry
            return one(i, False, *low), one(NZ - 1 - i, True, *high)

        start = (zero, zero + 1.0, zero)
        low, high = loop(HALF, step, (start, start), unroll)
        ends.append((low[2], high[2]))
    join = lambda n: ends[0][n] if tiles == 1 else jnp.concatenate([e[n] for e in ends], axis=1)
    return join(0), join(1)


def z_faces(cz, out, tiles=1):
    for t in range(tiles):
        before = None
        for k in range(NZ + 1):
            here = cz.part(t, k) if k < NZ else None
            both = here if before is None else before if here is None else here + before
            out.put(t, k, 0.5 * both)
            before = here


def base_diag(kappa, x_face, y_face):
    return kappa + (x_face + shift(x_face, -1, 0)) + (y_face + shift(y_face, -1, 1))


def window_mask(rows, lanes, tile_x, tile_y, halo, ix, iy, nx, ny):
    x, y = iota((rows, lanes), 0), iota((rows, lanes), 1)
    x = jnp.where(x < (rows + tile_x) // 2, x, x - rows)
    y = jnp.where(y < (lanes + tile_y) // 2, y, y - lanes)
    valid = (y >= -halo) & (y < tile_y + halo) & (x >= -halo) & (x < tile_x + halo)
    x, y = x + ix * tile_x, y + iy * tile_y
    return (valid & (x >= 0) & (x < nx) & (y >= 0) & (y < ny)).astype(F32)


def smooth_down(f, x_face, y_face, line, ends, kept, u, r, unroll):
    def emit(k, value):
        field = OMEGA * value
        u[k] = field
        r[k] = (1.0 - OMEGA) * f[k] + neighbours(field, x_face[k], y_face[k])

    sweep_out(ends, kept, line, emit, unroll)


def smooth_up(f, x_face, y_face, line, u, e, kept, mask, unroll):
    masked = (lambda v: v) if mask is None else (lambda v: v * mask)

    def rhs(k):
        field = masked(u[k] + e[k])
        u[k] = field
        return masked(f[k] + neighbours(field, x_face[k], y_face[k]))

    def emit(k, value):
        u[k] = (1.0 - OMEGA) * u[k] + OMEGA * value

    zero = jnp.zeros((u.rows, 128 * u.tiles), F32)
    ends = sweep_in(rhs, line, kept, zero, unroll)
    sweep_out(ends, kept, line, emit, unroll)


def spread_rows(cells, before, after, dest, size):
    dest[pl.ds(0, size, stride=2), :] = (0.75 * cells + 0.25 * before).reshape(size, 128)
    dest[pl.ds(1, size, stride=2), :] = (0.75 * cells + 0.25 * after).reshape(size, 128)


def spread_matrix(fine, base, coarse_count, circular=False):
    j = iota((128, fine.shape[1]), 0) + base
    parent = (fine + 2048) // 2 - 1024
    partner = parent + 2 * ((fine + 2048) % 2) - 1
    if circular:
        j, parent, partner = j % 128, parent % 128, partner % 128
    weights = jnp.where(j == parent, 0.75, jnp.where(j == partner, 0.25, 0.0))
    if not circular:
        inside = (j >= 0) & (j < coarse_count) & (fine >= 0) & (fine < 2 * coarse_count)
        weights = jnp.where(inside, weights, 0.0)
    return weights.astype(BF16)


def lane_group(rows, width):
    return iota((rows, 128), 1) // width


def fold_planes(cells, turn):
    group = lane_group(8, 32)
    out = cells[:8]
    for n in range(1, 4):
        out = jnp.where(group == n, cells[8 * n : 8 * n + 8], out)
    return pltpu.roll(out, turn, 1)


def pack_x_kernel(f, kappa, cx, cy, cz, share2, x_head, x_tail):
    for a, ref in enumerate((f, kappa, cx, cy, cz)):
        cells = ref[...].reshape(NZ, TX, TY)
        at = pl.ds(a * NZ * HALO, NZ * HALO)
        x_head[at, :] = cells[:, :HALO].reshape(NZ * HALO, TY)
        x_tail[at, :] = cells[:, TX - HALO :].reshape(NZ * HALO, TY)
    x_head[pl.ds(SLAB, 6 * NZ), :] = share2[...]
    x_tail[pl.ds(SLAB, 6 * NZ), :] = share2[...]


def share_kernel(devices, share2, copies):
    iy = lax.axis_index("gy")
    y, lane = iota((128, 128), 0), iota((128, 128), 1)
    x_in, y_in = y // 32, y % 32
    x_out, y_out = lane % 32 // 16, lane % 16
    pair_y, pair_x = y_in // 2 == y_out, x_in // 2 == x_out
    a, b, c, d, kappa, cz = (share2[pl.ds(t * NZ, NZ), :] for t in range(6))
    eighth = lambda mask: matrix(mask, 0.125)
    blocks = [
        mix(a, eighth(pair_y & (x_in == 2 * x_out))) + mix(b, eighth(pair_y & (x_in == 1) & (x_out == 1))),
        mix(b, eighth(pair_y & (x_in == 3) & (x_out == 0)))
        + mix(d, eighth((x_out == 1) & (y_in == 31) & (x_in // 2 == y_out))),
        mix(c, eighth(pair_x & (y_in == 2 * y_out))) + mix(d, eighth(pair_x & (y_in == 2 * y_out - 1))),
        mix(kappa, matrix(pair_x & pair_y, 0.25)),
        mix(cz, matrix(pair_x & pair_y, 0.25)),
    ]
    for t, cells in enumerate(blocks):
        cells = fold_planes(cells, 16 * iy)
        for n in range(devices):
            copies[pl.ds(n * SHARE + 8 * t, 8), :] = cells


def pack_y_kernel(f, kappa, cx, cy, cz, y_head, y_tail, share2):
    y, lane = iota((128, 128), 0), iota((128, 128), 1)
    fourth = y // 4 == lane % 32
    rows = lambda ref: [Field(ref, TX).row(r) for r in range(TX)]
    cx_rows, cy_rows, kappa_rows, cz_rows = rows(cx), rows(cy), rows(kappa), rows(cz)
    totals = lambda v: [(v[4 * i] + v[4 * i + 1]) + (v[4 * i + 2] + v[4 * i + 3]) for i in range(4)]
    stack = [cx_rows[4 * i] for i in range(4)] + [cx_rows[4 * i + 3] for i in range(4)]
    stack = mix(jnp.concatenate(stack + totals(kappa_rows) + totals(cz_rows), axis=0), matrix(fourth))
    ends = [matrix(fourth & (y % 4 == 0)), matrix(fourth & (y % 4 == 3))]
    sides = mix(jnp.concatenate(totals(cy_rows), axis=0), jnp.concatenate(ends, axis=1))
    group = lane_group(NZ, 32)

    def merge(cells, scale):
        out = cells[:NZ]
        for xi in range(1, 4):
            out = jnp.where(group == xi, cells[NZ * xi : NZ * (xi + 1)], out)
        return out * scale

    kinds = [merge(stack[:128], 1 / 128), merge(stack[128:256], 1 / 128)]
    kinds += [merge(sides[:, :128], 1 / 128), merge(sides[:, 128:], 1 / 128)]
    kinds += [merge(stack[256:384], 1 / 16), merge(stack[384:], 1 / 16)]
    head = [jnp.zeros((8, 128), F32)] * 3
    tail = [jnp.zeros((8, 128), F32)] * 3
    slot = iota((8, 128), 1) % 32 // 4
    for t, cells in enumerate(kinds):
        share2[pl.ds(t * NZ, NZ), :] = cells
        for zv in range(4):
            n = 4 * t + zv
            piece = cells[8 * zv : 8 * zv + 8]
            head[n // 8] = jnp.where(slot == n % 8, shift(piece, 4 * (n % 8), 1), head[n // 8])
            tail[n // 8] = jnp.where(slot == n % 8, shift(piece, 4 * (n % 8) + 4, 1), tail[n // 8])
    for n in range(3):
        y_head[pl.ds(STRIP + 8 * n, 8), :] = head[n]
        y_tail[pl.ds(STRIP + 8 * n, 8), :] = tail[n]

    group = lane_group(8, 8)
    for a, ref in enumerate((f, kappa, cx, cy, cz)):
        for half in range(2):
            for zo in range(2):
                head = jnp.zeros((8, 128), F32)
                tail = jnp.zeros((8, 128), F32)
                for zi in range(16):
                    cells = ref[pl.ds((zo * 16 + zi) * TX + 8 * half, 8), :]
                    cells = shift(cells, 8 * zi, 1)
                    head = jnp.where(group == zi, cells, head)
                    tail = jnp.where(group == (zi - 1) % 16, cells, tail)
                at = pl.ds(((half * 5 + a) * 2 + zo) * 8, 8)
                y_head[at, :] = head
                y_tail[at, :] = tail


def window2(tile, after, before, dest, first, iy, gy):
    lane = iota((NZ, 128), 1)
    first_after, first_before = jnp.where(iy < gy - 1, 36, 0), jnp.where(iy > 0, 124, 128)
    for xi in range(4):
        turned = (lane - 32 * xi + 128) % 128
        cells = jnp.where(turned < 32, tile, jnp.where(turned < first_after, after, jnp.where(turned >= first_before, before, 0.0)))
        dest[pl.ds(first + xi, NZ, stride=TX), :] = shift(cells, -32 * xi, 1)


def window_kernel(share2, xr, xl, yr, yl, cr, cl, x_face, y_face, inv, z_face, a, b, c, d, kappa, cz, diag):
    ix, iy = lax.axis_index("gx"), lax.axis_index("gy")
    gy = lax.axis_size("gy")
    nx, ny = lax.axis_size("gx") * 4, gy * 32
    refs = (a, b, c, d, kappa, cz)

    def unpack(ref, first, t, turn):
        pieces = []
        for zv in range(4):
            n = 4 * t + zv
            pieces.append(shift(ref[span(first + 8 * (n // 8), 8), :], turn - 4 * (n % 8), 1))
        return jnp.concatenate(pieces, axis=0)

    near, far = STRIP // 2, CORNER + STRIP // 2
    for t, dest in enumerate(refs):
        for first, tile, base, right, left, r_at, l_at in (
            (0, share2, 0, yr, yl, STRIP, STRIP),
            (4, xr, SLAB, cr, cr, far, near),
            (12, xl, SLAB, cl, cl, far, near),
        ):
            cells = tile[pl.ds(base + t * NZ, NZ), :]
            window2(cells, unpack(right, r_at, t, 32), unpack(left, l_at, t, 92), dest, first, iy, gy)
        for x in range(8, 12):
            dest[pl.ds(x, NZ, stride=TX), :] = jnp.zeros((NZ, 128), F32)
    mask = window_mask(TX, 128, 4, 32, 4, ix, iy, nx, ny)
    fields = [Field(ref, TX) for ref in (*refs, x_face, y_face, diag, inv)]
    a, b, c, d, kappa, cz, x_face, y_face, diag, inv = fields
    for k in range(NZ):
        x_k = a[k] + shift(b[k], 1, 0)
        y_k = c[k] + shift(d[k], 1, 1)
        x_face[k] = x_k
        y_face[k] = y_k
        diag[k] = base_diag(jnp.where(mask > 0, kappa[k], 1.0), x_k, y_k)
    z_face = Field(z_face, TX, 1, NZ + 1)
    z_faces(cz, z_face)
    factor(diag, z_face, 1, inv, None)


def assemble3(block, dest, gx, gy, rows):
    group = lane_group(8, 16)
    for ix in range(gx):
        blocks = [block(ix, iy) for iy in range(gy)]
        for zo in range(4):
            for xi in range(2):
                q = 2 * zo + xi
                cells = blocks[0]
                for iy in range(1, gy):
                    cells = jnp.where(group == (iy + q) % 8, blocks[iy], cells)
                dest[pl.ds(8 * zo * rows + 2 * ix + xi, 8, stride=rows), :] = shift(cells, -16 * q, 1)


def global_kernel(gx, gy, own, other, *refs):
    outs3, outs4 = refs[:5], refs[5:10]
    raw3, raw4, shares, sems = refs[10:18], refs[18:26], refs[26], refs[27]
    core = lax.axis_index("gx") % 2
    copies = [
        pltpu.make_async_copy(own, shares.at[:, core], sems.at[0]),
        pltpu.make_async_copy(other, shares.at[:, 1 - core], sems.at[1]),
    ]
    for copy in copies:
        copy.start()
    for copy in copies:
        copy.wait()
    rows, cols = 2 * gx, 16 * gy
    for t, n in enumerate((0, 1, 2, 4, 5)):
        block = lambda jx, jy: shares[jx // 2, jx % 2, pl.ds(jy * SHARE + 8 * t, 8), :]
        assemble3(block, raw3[n], gx, gy, rows)
    xl, xu, yl, yu = (Field(ref, rows) for ref in raw3[:4])
    x, y = iota((rows, 128), 0), iota((rows, 128), 1)
    odd_row, inside = x % 2 == 1, y < cols
    for k in range(NZ):
        half = jnp.where(inside, xu[k], 0.0)
        below = jnp.where(odd_row | (x < 2), 0.0, shift(half, 2, 0))
        x_k = jnp.where(inside, xl[k] + below, 0.0)
        xl[k] = x_k
        xu[k] = jnp.where(x == rows - 1, shift(half, 1, 0), shift(x_k, -1, 0))
        next_row = shift(half, -1, 0)
        below = jnp.where(odd_row, shift(half, 15, 1), shift(next_row, 16, 1))
        y_k = jnp.where(inside, yl[k] + jnp.where((y % 16 == 0) & (y > 0), below, 0.0), 0.0)
        yl[k] = y_k
        above = jnp.where(odd_row, shift(half, 14, 1), shift(next_row, 15, 1))
        yu[k] = jnp.where(y == cols - 1, above, jnp.where(inside, shift(y_k, -1, 1), 0.0))
    yy, jj = iota((128, 128), 0), iota((128, 128), 1)
    keep = yy // 2 == jj
    pair, even, odd = matrix(keep), matrix(keep & (yy % 2 == 0)), matrix(keep & (yy % 2 == 1))
    size = NZ * rows // 2
    lows = [Field(ref, rows) for ref in raw3]
    first = lambda n: lows[n].every_second(0, size, 0)
    second = lambda n: lows[n].every_second(0, size, 1)
    raw4[0][...] = 0.125 * mix(first(0), pair)
    raw4[1][...] = 0.125 * mix(second(1), pair)
    raw4[2][...] = 0.125 * mix(first(2) + second(2), even)
    raw4[3][...] = 0.125 * mix(first(3) + second(3), odd)
    raw4[4][...] = 0.25 * mix(first(4) + second(4), pair)
    raw4[5][...] = 0.25 * mix(first(5) + second(5), pair)
    for raw, outs in ((raw3, outs3), (raw4, outs4)):
        x, y = iota((rows, 128), 0), iota((rows, 128), 1)
        xl, xu, yl, yu, kappa, cz = (Field(ref, rows) for ref in raw[:6])
        z_face, diag = Field(raw[6], rows, 1, NZ + 1), Field(raw[7], rows)
        x_face, y_face, inv, g, c = (Field(ref, rows) for ref in outs)
        inside_x, inside_y = (x > 0).astype(F32), ((y > 0) & (y < cols)).astype(F32)
        for k in range(NZ):
            xl_k, yl_k = xl[k], yl[k]
            diag[k] = jnp.where(y < cols, kappa[k], 1.0) + (xl_k + xu[k]) + (yl_k + yu[k])
            x_face[k] = xl_k * inside_x
            y_face[k] = yl_k * inside_y
        z_faces(cz, z_face)
        factor(diag, z_face, 1, inv, None, g_out=g, c_out=c)
        rows, cols = rows // 2, cols // 2


def down_kernel(nx, ny, *refs):
    f, kappa, cx, cy, cz, yr, yl, corner_r, corner_l, xr_in, xl_in = refs[:11]
    sends, outs0, outs1 = refs[11], refs[12:18], refs[18:24]
    scratch = list(refs[24:-1])
    sems = refs[-1]
    take = lambda n: [scratch.pop(0) for _ in range(n)]
    ix, iy = lax.axis_index("gx"), lax.axis_index("gy")
    gx, gy = lax.axis_size("gx"), lax.axis_size("gy")
    xr, xl = take(2)
    fetches = [pltpu.make_async_copy(xr_in, xr, sems.at[12]), pltpu.make_async_copy(xl_in, xl, sems.at[13])]
    for fetch in fetches:
        fetch.start()
    rows, tiles = 2 * TX, 2
    whole = take(11)
    names = [Field(ref, rows, tiles) for ref in whole[:10]]
    x_face, y_face, inv, u, f0, kappa0, cz0, diag, kept, r = names
    z_face = Field(whole[10], rows, tiles, NZ + 1)
    group = lane_group(8, 8)

    def window(a, tile, z, after, before, turn):
        zo = z // 16
        slab = span(a * NZ * HALO + z * HALO, HALO)
        main = jnp.concatenate([tile[span(z * TX, TX), :], xr[slab, :], xl[slab, :]], axis=0)
        at = lambda first: span(first + (a * 2 + zo) * 8, 8)
        half = STRIP // 2
        sides = []
        for right, left in (
            (yr[at(0), :], yl[at(0), :]),
            (yr[at(half), :], yl[at(half), :]),
            (corner_r[at(CORNER), :], corner_r[at(0), :]),
            (corner_l[at(CORNER), :], corner_l[at(0), :]),
        ):
            cells = jnp.where(after, right, jnp.where(before, left, 0.0))
            sides.append(pltpu.roll(cells, turn, 1))
        return jnp.concatenate([main, jnp.concatenate(sides, axis=0)], axis=1)

    mask0 = window_mask(rows, 256, TX, TY, HALO, ix, iy, nx, ny)

    def prepare(z, cz_prev):
        zi = z % 16
        after, before = group == zi, group == (zi + 15) % 16
        turn = (128 - 8 * zi) % 128
        f_k, kappa_k, cx_k, cy_k, cz_k = (
            window(a, tile, z, after, before, turn) for a, tile in enumerate((f, kappa, cx, cy, cz))
        )
        f0[z] = f_k
        kappa0[z] = kappa_k
        cz0[z] = cz_k
        z_face[z] = 0.5 * (cz_k + cz_prev)
        x_k, y_k = 0.5 * (cx_k + shift(cx_k, 1, 0)), 0.5 * (cy_k + shift(cy_k, 1, 1))
        x_face[z] = x_k
        y_face[z] = y_k
        diag[z] = base_diag(jnp.where(mask0 > 0, kappa_k, 1.0), x_k, y_k)
        return cz_k

    for fetch in fetches:
        fetch.wait()
    last = loop(NZ, prepare, jnp.zeros((rows, 256), F32), 2)
    z_face[NZ] = 0.5 * last
    ends = factor(diag, z_face, tiles, inv, 4, f0, kept)
    sources = [x_face, y_face, inv, z_face, u, f0]
    copies = [pltpu.make_async_copy(s.ref, o, sems.at[n]) for n, (s, o) in enumerate(zip(sources, outs0))]
    for n in (0, 1, 2, 3, 5):
        copies[n].start()
    smooth_down(f0, x_face, y_face, Line(inv, z_face), ends, kept, u, r, 2)
    copies[4].start()

    fine = (r, kappa0, cz0, x_face, y_face)
    lanes, tile_x, tile_y, halo, outs = 256, TX, TY, HALO, outs1
    for level in (1, 2):
        rows, tile_x, tile_y, halo = rows // 2, tile_x // 2, tile_y // 2, halo // 2
        nx, ny = nx // 2, ny // 2
        whole = take(11)
        names = [Field(ref, rows) for ref in whole[:10]]
        x_face, y_face, inv, u, f1, kappa1, cz1, diag, kept, r = names
        z_face = Field(whole[10], rows, 1, NZ + 1)
        mask = window_mask(rows, 128, tile_x, tile_y, halo, ix, iy, nx, ny)
        y, j = iota((lanes, 128), 0), iota((lanes, 128), 1)
        if lanes == 128:
            j = jnp.where(j < 48, j, jnp.where(j >= 80, j - 64, -1))
        pair = matrix(y // 2 == j)
        even = (iota((1, lanes), 1) % 2 == 0).astype(F32)
        part = 128
        for at in range(0, NZ * rows, part):
            here = pl.ds(at, part)
            both = lambda n: fine[n].every_second(at, part, 0) + fine[n].every_second(at, part, 1)
            below = fine[3].every_second(at, part, 0)
            out = mix(jnp.concatenate([both(0), both(1), both(2), below, both(4) * even], axis=0), pair)
            for n, (dest, weight) in enumerate(((f1, 0.25), (kappa1, 0.25), (cz1, 0.25), (x_face, 0.125), (y_face, 0.125))):
                dest.ref[here, :] = weight * out[n * part : (n + 1) * part]
        for k in range(NZ):
            f1[k] = f1[k] * mask
            diag[k] = base_diag(jnp.where(mask > 0, kappa1[k], 1.0), x_face[k], y_face[k])
        z_faces(cz1, z_face)
        ends = factor(diag, z_face, 1, inv, None, f1, kept)
        smooth_down(f1, x_face, y_face, Line(inv, z_face), ends, kept, u, r, None)
        if level == 1:
            sources = [x_face, y_face, inv, z_face, u, f1]
            more = [pltpu.make_async_copy(s.ref, o, sems.at[6 + n]) for n, (s, o) in enumerate(zip(sources, outs1))]
            for copy in more:
                copy.start()
            copies += more
        fine, lanes = (r, kappa1, cz1, x_face, y_face), 128

    group = lane_group(NZ, 32)
    out = f1.row(0)
    for xi in range(1, 4):
        out = jnp.where(group == xi, shift(f1.row(xi), 32 * xi, 1), out)
    for n in range(gx * gy):
        sends[pl.ds(n * BLOCK, NZ), :] = out
    y, lane = iota((128, 128), 0), iota((128, 128), 1)
    total = jnp.zeros((NZ, 128), F32)
    for xi in range(2):
        place = (lane % 32 // 16 == xi) & (y // 2 == lane % 16) & (y < 32)
        total = total + mix(r.row(2 * xi) + r.row(2 * xi + 1), matrix(place, 0.25))
    total = fold_planes(total, 16 * iy)
    for n in range(gx * gy):
        sends[pl.ds(n * BLOCK + NZ, 8), :] = total
    for copy in copies:
        copy.wait()


def up_kernel(gx, gy, *refs):
    gathered, kappa, k3, k4 = refs[0], refs[1], refs[2:7], refs[7:12]
    saved2, saved0, saved1 = refs[12:16], refs[16:22], refs[22:28]
    solution_out, residual_out = refs[28:30]
    scratch = list(refs[30:-1])
    sems = refs[-1]
    take = lambda n: [scratch.pop(0) for _ in range(n)]
    ix, iy = lax.axis_index("gx"), lax.axis_index("gy")
    held0, held1, k2, whole3, blocks = take(6), take(6), take(4), take(1)[0], take(1)[0]
    fetch = pltpu.make_async_copy(gathered.at[:, pl.ds(NZ, 8), :], whole3, sems.at[25])
    fetch.start()
    fetches = []
    sides = [(dx, dy) for dx in (0, 1, -1) for dy in (0, 1, -1)]
    for n, (dx, dy) in enumerate(sides):
        device = jnp.clip(ix + dx, 0, gx - 1) * gy + jnp.clip(iy + dy, 0, gy - 1)
        source = gathered.at[device, pl.ds(0, NZ), :]
        fetches.append(pltpu.make_async_copy(source, blocks.at[n], sems.at[16 + n]))
        fetches[-1].start()
    copies = []
    for n, (source, dest) in enumerate(zip((*saved2, *saved1, *saved0), (*k2, *held1, *held0))):
        copies.append(pltpu.make_async_copy(source, dest, sems.at[n]))
        copies[-1].start()
    f2, u2, kept2, wide, e_ref, e0_ref, kept0, u3, f3, r3, f4, u4 = take(12)

    rows, cols = 2 * gx, 16 * gy
    fetch.wait()
    assemble3(lambda jx, jy: whole3[jx * gy + jy], f3, gx, gy, rows)
    f3, u3, r3 = (Field(ref, rows) for ref in (f3, u3, r3))
    y = iota((rows, 128), 1)
    x_face3, y_face3, inv3, g3, c3 = (Field(ref, rows) for ref in k3)
    line3 = StoredLine(inv3, g3, c3)
    clean = (y < cols).astype(F32)
    for k in range(NZ):
        f3[k] = f3[k] * clean
    zero = jnp.zeros((rows, 128), F32)
    ends = sweep_in(lambda k: f3[k], line3, r3, zero, None)
    smooth_down(f3, x_face3, y_face3, line3, ends, r3, u3, Field(e_ref, rows), None)
    fine = Field(e_ref, rows)
    rows, cols = rows // 2, cols // 2
    size = NZ * rows
    yy, jj = iota((128, 128), 0), iota((128, 128), 1)
    f4[...] = 0.25 * mix(fine.every_second(0, size, 0) + fine.every_second(0, size, 1), matrix(yy // 2 == jj))
    f4, u4 = Field(f4, rows), Field(u4, rows)
    x_face4, y_face4, inv4, g4, c4 = (Field(ref, rows) for ref in k4)
    line4 = StoredLine(inv4, g4, c4)
    zero = jnp.zeros((rows, 128), F32)

    def solve4(rhs, old):
        kept, out = {}, {}
        ends = sweep_in(rhs, line4, kept, zero, None)

        def emit(k, value):
            out[k] = OMEGA * value if old is None else (1.0 - OMEGA) * old[k] + OMEGA * value

        sweep_out(ends, kept, line4, emit, None)
        for k in range(NZ):
            u4[k] = out[k]

    solve4(lambda k: f4[k], None)

    def relax(sweep, carry):
        old = [u4[k] for k in range(NZ)]
        solve4(lambda k: f4[k] + neighbours(old[k], x_face4[k], y_face4[k]), old)
        return carry

    lax.fori_loop(0, COARSE_SWEEPS - 1, relax, 0)

    cells = u4.ref[...].reshape(NZ, rows, 128)
    x = iota((1, rows, 128), 1)
    before = jnp.where(x > 0, shift(cells, 1, 1), 0.0)
    after = jnp.where(x < rows - 1, shift(cells, -1, 1), 0.0)
    spread_rows(cells, before, after, wide, size)
    e_ref[...] = mix(wide[pl.ds(0, 2 * size), :], spread_matrix(iota((128, 128), 1), 0, cols), 3)
    rows, cols = 2 * rows, 2 * cols
    smooth_up(f3, x_face3, y_face3, line3, u3, Field(e_ref, rows), r3, None, None)

    def block(dx, dy):
        inside = ((ix + dx >= 0) & (ix + dx < gx)).astype(F32)
        return blocks[sides.index((dx, dy))] * inside

    for copy in fetches + copies[:4]:
        copy.wait()
    for first, dx in ((0, 0), (4, 1), (12, -1)):
        window2(block(dx, 0), shift(block(dx, 1), 32, 1), shift(block(dx, -1), 96, 1), f2, first, iy, gy)
    for x in range(8, 12):
        f2[pl.ds(x, NZ, stride=TX), :] = jnp.zeros((NZ, 128), F32)
    f2, u2, kept2 = (Field(ref, TX) for ref in (f2, u2, kept2))
    x_face2, y_face2, inv2 = (Field(ref, TX) for ref in k2[:3])
    line2 = Line(inv2, Field(k2[3], TX, 1, NZ + 1))
    zero = jnp.zeros((TX, 128), F32)
    ends = sweep_in(lambda k: f2[k], line2, kept2, zero, None)

    def emit2(k, value):
        u2[k] = OMEGA * value

    sweep_out(ends, kept2, line2, emit2, None)

    cells = pltpu.roll(u3.ref[...].reshape(NZ, rows, 128), (rows - 2 * ix) % rows, 1)
    x = iota((1, rows, 128), 1)
    place = 2 * ix + jnp.where(x < rows // 2, x, x - rows)
    cells = jnp.where((place >= 0) & (place < rows), cells, 0.0)
    ring = lambda v, first: jnp.where(iota((1, 8, 128), 1) < first, v[:, :8], v[:, rows - 8 :])
    spread_rows(ring(cells, 4), ring(shift(cells, 1, 1), 4), ring(shift(cells, -1, 1), 4), wide, NZ * 8)
    lane = iota((128, 128), 1)
    fine_y = jnp.where(lane < 80, lane, lane - 128) + 32 * iy
    e_ref[...] = mix(wide[pl.ds(0, NZ * TX), :], spread_matrix(fine_y, 0, cols), 3)
    mask2 = window_mask(TX, 128, 4, 32, 4, ix, iy, 4 * gx, 32 * gy)
    smooth_up(f2, x_face2, y_face2, line2, u2, Field(e_ref, TX), kept2, mask2, None)

    cells = u2.ref[...].reshape(NZ, TX, 128)
    ring = lambda v: jnp.where(iota((1, 8, 128), 1) < 6, v[:, :8], v[:, 8:])
    spread_rows(ring(cells), ring(shift(cells, 1, 1)), ring(shift(cells, -1, 1)), wide, NZ * 8)
    fine_y = jnp.where(lane < 96, lane, lane - 128)
    e_ref[...] = mix(wide[pl.ds(0, NZ * TX), :], spread_matrix(fine_y, 0, 0, circular=True), 3)
    for copy in copies[4:10]:
        copy.wait()
    x_face1, y_face1, inv1, z_face1, u1, f1 = held1
    x_face1, y_face1, inv1, u1, f1 = (Field(ref, TX) for ref in (x_face1, y_face1, inv1, u1, f1))
    line1 = Line(inv1, Field(z_face1, TX, 1, NZ + 1))
    mask1 = window_mask(TX, 128, 8, 64, 4, ix, iy, 8 * gx, 64 * gy)
    smooth_up(f1, x_face1, y_face1, line1, u1, Field(e_ref, TX), kept2, mask1, None)

    cells = u1.ref[...].reshape(NZ, TX, 128)
    spread_rows(cells, shift(cells, 1, 1), shift(cells, -1, 1), wide, NZ * TX)
    rows = 2 * TX
    weights = spread_matrix(iota((128, 256), 1), 0, 0, circular=True)
    e0 = Field(e0_ref, rows, 2)
    for k in range(0, NZ, 8):
        cells = mix(wide[pl.ds(k * rows, 8 * rows), :], weights, 3)
        for t in range(2):
            e0_ref[pl.ds(e0.base(t, k), 8 * rows), :] = cells[:, 128 * t : 128 * (t + 1)]
    for copy in copies[10:]:
        copy.wait()
    x_face0, y_face0, inv0, z_face0, u0, f0 = held0
    x_face0, y_face0, inv0, u0, f0 = (Field(ref, rows, 2) for ref in (x_face0, y_face0, inv0, u0, f0))
    z_face0 = Field(z_face0, rows, 2, NZ + 1)
    mask0 = window_mask(rows, 256, TX, TY, HALO, ix, iy, TX * gx, TY * gy)
    smooth_up(f0, x_face0, y_face0, Line(inv0, z_face0), u0, e0, Field(kept0, rows, 2), mask0, 2)

    kappa = Field(kappa, TX)

    def residual(k, carry):
        below, flux_z = carry
        column = u0.part(0, k)
        here = column[:TX]
        flux_x = (x_face0.part(0, k) * (column - shift(column, 1, 0)))[: TX + 8]
        row = u0[k][:TX]
        flux_y = y_face0[k][:TX] * (row - shift(row, 1, 1))
        side = (flux_x - shift(flux_x, -1, 0))[:TX] + (flux_y - shift(flux_y, -1, 1))[:, :TY]
        above = u0.part(0, k + 1)[:TX] if k is not NZ - 1 else jnp.zeros((TX, TY), F32)
        flux_up = z_face0.part(0, k + 1)[:TX] * (above - here)
        solution_out[span(k * TX, TX), :] = here
        out = f0.part(0, k)[:TX] - kappa[k] * here - side - flux_z + flux_up
        residual_out[span(k * TX, TX), :] = out
        return here, flux_up

    start = z_face0.part(0, 0)[:TX] * u0.part(0, 0)[:TX]
    carry = loop(NZ - 1, residual, (start, start), 4)
    residual(NZ - 1, carry)


COSTS = {
    "pack_y": 2 * 10**9, "pack_x": 2 * 10**9, "share": 10**9, "down": 10**10,
    "window_coeffs": 4 * 10**9, "global_coeffs": 4 * 10**9, "up": 12 * 10**9,
}


def call(kernel, name, outs, ins, scratch=(), in_specs=None, out_specs=None, aliases=None):
    shapes = [jax.ShapeDtypeStruct(s, F32) for s in outs]
    return pl.pallas_call(
        kernel,
        name=name,
        out_shape=shapes,
        in_specs=in_specs or [VMEM] * len(ins),
        out_specs=out_specs or [VMEM] * len(outs),
        scratch_shapes=list(scratch),
        input_output_aliases=aliases or {},
        compiler_params=pltpu.CompilerParams(vmem_limit_bytes=(32 if name in ("down", "up") else 16) * 1024 * 1024),
        cost_estimate=pl.CostEstimate(flops=COSTS[name], bytes_accessed=4 * sum(x.size for x in ins), transcendentals=0),
    )(*ins)


def body(right_side, kappa_sq, cond_x, cond_y, cond_z):
    gx, gy = lax.axis_size("gx"), lax.axis_size("gy")
    tiles = [v.reshape(NZ * TX, TY) for v in (right_side, kappa_sq, cond_x, cond_y, cond_z)]
    slab, strip = (SLAB + 6 * NZ, 128), (STRIP + 24, 128)
    vm = lambda *shape: pltpu.VMEM(shape, F32)
    dma = lambda n: pltpu.SemaphoreType.DMA((n,))
    devices = gx * gy
    up = lambda n: [(i, i + 1) for i in range(n - 1)]
    down = lambda n: [(i + 1, i) for i in range(n - 1)]
    y_head, y_tail, share2 = call(pack_y_kernel, "pack_y", [strip, strip, (6 * NZ, 128)], tiles)
    yr = lax.ppermute(y_head, "gy", down(gy))
    yl = lax.ppermute(y_tail, "gy", up(gy))
    x_head, x_tail = call(pack_x_kernel, "pack_x", [slab, slab], [*tiles, share2])
    xr = lax.ppermute(x_head, "gx", down(gx))
    xl = lax.ppermute(x_tail, "gx", up(gx))
    copies = call(functools.partial(share_kernel, devices // 2), "share", [(devices // 2 * SHARE, 128)], [share2])[0]
    half = STRIP // 2
    corner_r = lax.ppermute(jnp.concatenate([yl[:half], yl[STRIP:], yr[:half], yr[STRIP:]]), "gx", down(gx))
    corner_l = lax.ppermute(jnp.concatenate([yl[half:], yr[half:]]), "gx", up(gx))
    copies, corner_r, corner_l = lax.optimization_barrier((copies, corner_r, corner_l))
    cores = [[x * gy + y for x in range(core, gx, 2) for y in range(gy)] for core in range(2)]
    blocks = copies.reshape(devices // 2, SHARE, 128)
    own = lax.all_to_all(blocks, ("gx", "gy"), 0, 0, axis_index_groups=cores).reshape(gx // 2, gy * SHARE, 128)
    level = lambda rows, n: [vm(NZ * rows, 128)] * n
    faces = lambda rows, tiles: vm(tiles * (NZ + 1) * rows, 128)
    rows3, rows4 = 2 * gx, gx
    size, tall = (NZ * TX, 128), ((NZ + 1) * TX, 128)
    k2 = call(
        window_kernel, "window_coeffs", [size, size, size, tall], [share2, xr, xl, yr, yl, corner_r, corner_l], level(TX, 7)
    )
    big, big_z = (2 * NZ * 2 * TX, 128), (2 * (NZ + 1) * 2 * TX, 128)
    sends, *saved = call(
        functools.partial(down_kernel, gx * TX, gy * TY),
        "down",
        [(devices * BLOCK, 128), big, big, big, big_z, big, big, size, size, size, tall, size, size],
        [*tiles, yr, yl, corner_r, corner_l, xr, xl],
        [vm(*slab)] * 2 + [vm(*big)] * 10 + [vm(*big_z)] + level(TX, 10) + [faces(TX, 1)] + level(8, 10) + [faces(8, 1)]
        + [dma(14)],
        in_specs=[VMEM] * 9 + [ANY] * 2,
        out_specs=[VMEM] + [ANY] * 12,
    )
    sends, own = lax.optimization_barrier((sends, own))
    other = lax.ppermute(own, "gx", [(i, i ^ 1) for i in range(gx)])
    gathered = lax.all_to_all(sends.reshape(devices, BLOCK, 128), ("gx", "gy"), 0, 0)
    whole = call(
        functools.partial(global_kernel, gx, gy),
        "global_coeffs",
        [(NZ * rows3, 128)] * 5 + [(NZ * rows4, 128)] * 5,
        [own, other],
        level(rows3, 6) + [faces(rows3, 1)] + level(rows3, 1) + level(rows4, 6) + [faces(rows4, 1)] + level(rows4, 1)
        + [vm(gx // 2, 2, gy * SHARE, 128), dma(2)],
        in_specs=[ANY] * 2,
    )
    field, residual = call(
        functools.partial(up_kernel, gx, gy),
        "up",
        [(NZ * TX, TY)] * 2,
        [gathered, tiles[1], *whole, *k2, *saved],
        [vm(*big), vm(*big), vm(*big), vm(*big_z), vm(*big), vm(*big), vm(*size), vm(*size), vm(*size), vm(*tall), vm(*size), vm(*size)]
        + [vm(*size), vm(*size), vm(*size), vm(*tall), vm(devices, 8, 128), vm(9, NZ, 128)]
        + level(TX, 3) + [vm(NZ * 2 * TX, 128), vm(*size), vm(*big), vm(*big)]
        + level(rows3, 3) + level(rows4, 2) + [dma(26)],
        in_specs=[ANY] + [VMEM] * 11 + [ANY] * 16,
    )
    return field.reshape(right_side.shape), residual.reshape(right_side.shape)


def solution(mesh):
    spec = P(None, "gx", "gy")
    fits = (mesh.shape["gx"], mesh.shape["gy"]) == (8, 4)
    plan = body if fits else spread_body
    return jax.shard_map(plan, mesh=mesh, in_specs=(spec,) * 5, out_specs=(spec, spec), check_vma=False)
```

```python
import functools

import jax
import jax.numpy as jnp
from jax import lax
from jax.experimental import pallas as pl
from jax.experimental.pallas import tpu as pltpu
from jax.sharding import PartitionSpec as P

LEVELS = 4
COARSE_SWEEPS = 16


OMEGA = 0.8


def with_halo(cells, sides, width):
    for axis, dim in sides:
        count = lax.axis_size(axis)
        ends = count - 1
        head = lax.slice_in_dim(cells, 0, width, axis=dim)
        tail = lax.slice_in_dim(cells, cells.shape[dim] - width, cells.shape[dim], axis=dim)
        cells = jnp.concatenate(
            [
                lax.ppermute(tail, axis, [(i, (i + 1) % count) for i in range(ends)]),
                cells,
                lax.ppermute(head, axis, [((i + 1) % count, i) for i in range(ends)]),
            ],
            axis=dim,
        )
    return cells


def apply_op(field, padded, coeffs):
    kappa, x_up, x_low, y_up, y_low, z_up, z_low = coeffs
    zpad = jnp.pad(field, ((1, 1), (0, 0), (0, 0)))
    out = (
        kappa * field
        + x_up * (field - padded[:, 2:, 1:-1])
        + x_low * (field - padded[:, :-2, 1:-1])
    )
    out = out + y_up * (field - padded[:, 1:-1, 2:]) + y_low * (field - padded[:, 1:-1, :-2])
    return out + z_up * (field - zpad[2:]) + z_low * (field - zpad[:-2])


def face_pad(field):
    return with_halo(field, (("gx", 1), ("gy", 2)), 1)


def line_factors(coeffs):
    kappa, x_up, x_low, y_up, y_low, z_up, z_low = coeffs
    diag = kappa + x_up + x_low + y_up + y_low + z_up + z_low
    upper_src = z_up.at[-1].set(jnp.zeros_like(z_up[-1]))

    def factor_step(upper_prev, planes):
        diag_k, low_k, up_k = planes
        inv = 1.0 / (diag_k + low_k * upper_prev)
        upper = -up_k * inv
        return (upper, (inv, upper))

    start = jnp.zeros_like(diag[0])
    unused, stacked = lax.scan(factor_step, start, (diag, z_low, upper_src), unroll=True)
    return stacked


def line_solve(rhs, factors, z_low):
    inverses, uppers = factors

    def forward_step(prev, planes):
        rhs_k, low_k, inv_k = planes
        value = (rhs_k + low_k * prev) * inv_k
        return (value, value)

    start = jnp.zeros_like(rhs[0])
    unused, forward = lax.scan(forward_step, start, (rhs, z_low, inverses), unroll=True)

    def back_step(after, planes):
        fwd_k, up_k = planes
        value = fwd_k - up_k * after
        return (value, value)

    unused, result = lax.scan(back_step, start, (forward, uppers), reverse=True, unroll=True)
    return result


def mean_four(field):
    depth, rows, cols = field.shape
    return field.reshape(depth, rows // 2, 2, cols // 2, 2).mean(axis=(2, 4))


def coarsen(coeffs):
    kappa, x_up, x_low, y_up, y_low, z_up, z_low = coeffs
    depth, rows, cols = kappa.shape
    shape = (depth, rows // 2, 2, cols // 2, 2)
    xu_c = x_up.reshape(shape)[:, :, 1].mean(axis=-1) * 0.25
    xl_c = x_low.reshape(shape)[:, :, 0].mean(axis=-1) * 0.25
    yu_c = y_up.reshape(shape)[:, :, :, :, 1].mean(axis=2) * 0.25
    yl_c = y_low.reshape(shape)[:, :, :, :, 0].mean(axis=2) * 0.25
    return (mean_four(kappa), xu_c, xl_c, yu_c, yl_c, mean_four(z_up), mean_four(z_low))


def prolong(padded):
    depth = padded.shape[0]
    rows = padded.shape[1] - 2
    cols = padded.shape[2] - 2
    centre = padded[:, 1:-1, :]
    even = 0.75 * centre + 0.25 * padded[:, :-2, :]
    odd = 0.75 * centre + 0.25 * padded[:, 2:, :]
    spread = jnp.stack([even, odd], axis=2).reshape(depth, 2 * rows, cols + 2)
    centre = spread[:, :, 1:-1]
    even = 0.75 * centre + 0.25 * spread[:, :, :-2]
    odd = 0.75 * centre + 0.25 * spread[:, :, 2:]
    return jnp.stack([even, odd], axis=3).reshape(depth, 2 * rows, 2 * cols)


def coarse_solve(rhs, coeffs):
    factors = line_factors(coeffs)
    field = OMEGA * line_solve(rhs, factors, coeffs[6])

    def spread_sweep(sweep, current):
        padded = with_halo(current, (("gx", 1), ("gy", 2)), 1)
        defect = rhs - apply_op(current, padded, coeffs)
        return current + OMEGA * line_solve(defect, factors, coeffs[6])

    field = lax.fori_loop(0, COARSE_SWEEPS - 1, spread_sweep, field)
    return field


def cycle(rhs, coeffs, level):
    if level == LEVELS:
        return coarse_solve(rhs, coeffs)
    factors = line_factors(coeffs)
    field = OMEGA * line_solve(rhs, factors, coeffs[6])
    padded = face_pad(field)
    defect = rhs - apply_op(field, padded, coeffs)
    correction = cycle(mean_four(defect), coarsen(coeffs), level + 1)
    rimmed = with_halo(correction, (("gx", 1), ("gy", 2)), 1)
    field = field + prolong(rimmed)
    padded = face_pad(field)
    defect = rhs - apply_op(field, padded, coeffs)
    return field + OMEGA * line_solve(defect, factors, coeffs[6])


def spread_body(right_side, kappa_sq, cond_x, cond_y, cond_z):
    padded_x = with_halo(cond_x, (("gx", 1),), 1)
    padded_y = with_halo(cond_y, (("gy", 2),), 1)
    padded_z = jnp.pad(cond_z, ((1, 1), (0, 0), (0, 0)))
    x_up = 0.5 * (cond_x + padded_x[:, 2:, :])
    x_low = 0.5 * (cond_x + padded_x[:, :-2, :])
    y_up = 0.5 * (cond_y + padded_y[:, :, 2:])
    y_low = 0.5 * (cond_y + padded_y[:, :, :-2])
    z_up = 0.5 * (cond_z + padded_z[2:])
    z_low = 0.5 * (cond_z + padded_z[:-2])
    coeffs = (kappa_sq, x_up, x_low, y_up, y_low, z_up, z_low)
    solution_field = cycle(right_side, coeffs, 0)
    residual = right_side - apply_op(solution_field, face_pad(solution_field), coeffs)
    return (solution_field, residual)


F32 = jnp.float32
BF16 = jnp.bfloat16
NZ = 32
HALF = NZ // 2
TX, TY = 16, 128
HALO = 8
SLAB = 5 * NZ * HALO
STRIP = 160
CORNER = 104
SHARE = 40
BLOCK = NZ + 8
VMEM = pl.BlockSpec(memory_space=pltpu.VMEM)
ANY = pl.BlockSpec(memory_space=pl.ANY)
HBM = pl.BlockSpec(memory_space=pltpu.HBM)


def iota(shape, dim):
    return lax.broadcasted_iota(jnp.int32, shape, dim)


def shift(x, by, axis):
    by = by % x.shape[axis]
    return pltpu.roll(x, by, axis) if by else x


def mix(x, weights, parts=2):
    pieces = []
    for n in range(parts):
        piece = x.astype(BF16)
        pieces.append(piece)
        if n < parts - 1:
            x = x - piece.astype(F32)
    out = jnp.dot(jnp.concatenate(pieces, axis=0), weights, preferred_element_type=F32)
    rows = x.shape[0]
    return sum(out[n * rows : (n + 1) * rows] for n in reversed(range(parts)))


def matrix(mask, weight=1.0):
    return jnp.where(mask, weight, 0.0).astype(BF16)


def span(start, size):
    if not isinstance(start, int):
        start = pl.multiple_of(start, 8)
    return pl.ds(start, size)


class Field:
    def __init__(self, ref, rows, tiles=1, planes=NZ, start=0):
        self.ref, self.rows, self.tiles, self.planes, self.start = ref, rows, tiles, planes, start

    def base(self, tile, k):
        return self.start + tile * self.planes * self.rows + k * self.rows

    def part(self, tile, k):
        return self.ref[span(self.base(tile, k), self.rows), :]

    def __getitem__(self, k):
        parts = [self.part(t, k) for t in range(self.tiles)]
        return parts[0] if self.tiles == 1 else jnp.concatenate(parts, axis=1)

    def __setitem__(self, k, value):
        for t in range(self.tiles):
            self.put(t, k, value[:, 128 * t : 128 * (t + 1)])

    def put(self, tile, k, value):
        self.ref[span(self.base(tile, k), self.rows), :] = value

    def every_second(self, at, count, odd):
        parts = []
        for t in range(self.tiles):
            first = self.base(t, 0) + 2 * at + odd
            parts.append(self.ref[pl.ds(first, count, stride=2), :])
        return parts[0] if self.tiles == 1 else jnp.concatenate(parts, axis=1)

    def row(self, row):
        return self.ref[pl.ds(self.start + row, self.planes, stride=self.rows), :]


def stack_fields(ref, rows, count, tiles=1, z_face=True, start=0):
    size = tiles * NZ * rows
    out = [Field(ref, rows, tiles, NZ, start + n * size) for n in range(count)]
    return out + [Field(ref, rows, tiles, NZ + 1, start + count * size)] if z_face else out


def loop(count, step, carry, unroll=None):
    if unroll is None or unroll >= count:
        for i in range(count):
            carry = step(i, carry)
        return carry
    return lax.fori_loop(0, count, step, carry, unroll=unroll)


def neighbours(field, x_face, y_face):
    out = x_face * shift(field, 1, 0) + shift(x_face * field, -1, 0)
    return out + (y_face * shift(field, 1, 1) + shift(y_face * field, -1, 1))


class Line:
    def __init__(self, inv, z_face):
        self.inv, self.z_face = inv, z_face

    def inward(self, k, upper):
        return self.z_face[k + 1 if upper else k] * self.inv[k]

    def outward(self, k, upper):
        return self.z_face[k if upper else k + 1] * self.inv[k]


class StoredLine:
    def __init__(self, inv, g, c):
        self.inv, self.g, self.c = inv, g, c

    def inward(self, k, upper):
        return self.g[k]

    def outward(self, k, upper):
        return self.c[k]


def sweep_in(rhs, line, keep, start, unroll):
    def step(i, carry):
        low, high = carry
        k, m = i, NZ - 1 - i
        low = rhs(k) * line.inv[k] + line.inward(k, False) * low
        high = rhs(m) * line.inv[m] + line.inward(m, True) * high
        keep[k] = low
        keep[m] = high
        return low, high

    return loop(HALF, step, (start, start), unroll)


def sweep_out(ends, kept, line, emit, unroll):
    low, high = ends
    a, b = line.outward(HALF - 1, False), line.outward(HALF, True)
    low = (low + a * high) * (1.0 / (1.0 - a * b))
    high = high + b * low

    def step(i, carry):
        low, high = carry
        k, m = HALF - 1 - i, HALF + i
        emit(k, low)
        emit(m, high)
        low = kept[k - 1] + line.outward(k - 1, False) * low
        high = kept[m + 1] + line.outward(m + 1, True) * high
        return low, high

    low, high = loop(HALF - 1, step, (low, high), unroll)
    emit(0, low)
    emit(NZ - 1, high)


def factor(diag, z_face, tiles, inv_out, unroll, rhs=None, keep=None, g_out=None, c_out=None):
    ends = []
    for t in range(tiles):
        zero = diag.part(t, 0) * 0.0

        def one(k, upper, before, last, prev):
            below, above = z_face.part(t, k), z_face.part(t, k + 1)
            inner, outer = (above, below) if upper else (below, above)
            minor = (diag.part(t, k) + below + above) * last - (inner * inner) * before
            inv = last * (1.0 / minor)
            inv_out.put(t, k, inv)
            if g_out is not None:
                g_out.put(t, k, inner * inv)
                c_out.put(t, k, outer * inv)
            if rhs is not None:
                prev = rhs.part(t, k) * inv + (inner * inv) * prev
                keep.put(t, k, prev)
            return last, minor, prev

        def step(i, carry):
            low, high = carry
            return one(i, False, *low), one(NZ - 1 - i, True, *high)

        start = (zero, zero + 1.0, zero)
        low, high = loop(HALF, step, (start, start), unroll)
        ends.append((low[2], high[2]))
    join = lambda n: ends[0][n] if tiles == 1 else jnp.concatenate([e[n] for e in ends], axis=1)
    return join(0), join(1)


def z_faces(cz, out, tiles=1):
    for t in range(tiles):
        before = None
        for k in range(NZ + 1):
            here = cz.part(t, k) if k < NZ else None
            both = here if before is None else before if here is None else here + before
            out.put(t, k, 0.5 * both)
            before = here


def base_diag(kappa, x_face, y_face):
    return kappa + (x_face + shift(x_face, -1, 0)) + (y_face + shift(y_face, -1, 1))


def window_mask(rows, lanes, tile_x, tile_y, halo, ix, iy, nx, ny):
    x, y = iota((rows, lanes), 0), iota((rows, lanes), 1)
    x = jnp.where(x < (rows + tile_x) // 2, x, x - rows)
    y = jnp.where(y < (lanes + tile_y) // 2, y, y - lanes)
    valid = (y >= -halo) & (y < tile_y + halo) & (x >= -halo) & (x < tile_x + halo)
    x, y = x + ix * tile_x, y + iy * tile_y
    return (valid & (x >= 0) & (x < nx) & (y >= 0) & (y < ny)).astype(F32)


def smooth_down(f, x_face, y_face, line, ends, kept, u, r, unroll):
    def emit(k, value):
        field = OMEGA * value
        u[k] = field
        r[k] = (1.0 - OMEGA) * f[k] + neighbours(field, x_face[k], y_face[k])

    sweep_out(ends, kept, line, emit, unroll)


def smooth_up(f, x_face, y_face, line, u, e, kept, mask, unroll):
    masked = (lambda v: v) if mask is None else (lambda v: v * mask)

    def rhs(k):
        field = masked(u[k] + e[k])
        u[k] = field
        return masked(f[k] + neighbours(field, x_face[k], y_face[k]))

    def emit(k, value):
        u[k] = (1.0 - OMEGA) * u[k] + OMEGA * value

    zero = jnp.zeros((u.rows, 128 * u.tiles), F32)
    ends = sweep_in(rhs, line, kept, zero, unroll)
    sweep_out(ends, kept, line, emit, unroll)


def spread_rows(cells, before, after, dest, size):
    dest[pl.ds(0, size, stride=2), :] = (0.75 * cells + 0.25 * before).reshape(size, 128)
    dest[pl.ds(1, size, stride=2), :] = (0.75 * cells + 0.25 * after).reshape(size, 128)


def spread_matrix(fine, base, coarse_count, circular=False):
    j = iota((128, fine.shape[1]), 0) + base
    parent = (fine + 2048) // 2 - 1024
    partner = parent + 2 * ((fine + 2048) % 2) - 1
    if circular:
        j, parent, partner = j % 128, parent % 128, partner % 128
    weights = jnp.where(j == parent, 0.75, jnp.where(j == partner, 0.25, 0.0))
    if not circular:
        inside = (j >= 0) & (j < coarse_count) & (fine >= 0) & (fine < 2 * coarse_count)
        weights = jnp.where(inside, weights, 0.0)
    return weights.astype(BF16)


def lane_group(rows, width):
    return iota((rows, 128), 1) // width


def fold_planes(cells, turn):
    group = lane_group(8, 32)
    out = cells[:8]
    for n in range(1, 4):
        out = jnp.where(group == n, cells[8 * n : 8 * n + 8], out)
    return pltpu.roll(out, turn, 1)


def share_kernel(devices, share2, copies):
    iy = lax.axis_index("gy")
    y, lane = iota((128, 128), 0), iota((128, 128), 1)
    x_in, y_in = y // 32, y % 32
    x_out, y_out = lane % 32 // 16, lane % 16
    pair_y, pair_x = y_in // 2 == y_out, x_in // 2 == x_out
    a, b, c, d, kappa, cz = (share2[pl.ds(t * NZ, NZ), :] for t in range(6))
    eighth = lambda mask: matrix(mask, 0.125)
    blocks = [
        mix(a, eighth(pair_y & (x_in == 2 * x_out))) + mix(b, eighth(pair_y & (x_in == 1) & (x_out == 1))),
        mix(b, eighth(pair_y & (x_in == 3) & (x_out == 0)))
        + mix(d, eighth((x_out == 1) & (y_in == 31) & (x_in // 2 == y_out))),
        mix(c, eighth(pair_x & (y_in == 2 * y_out))) + mix(d, eighth(pair_x & (y_in == 2 * y_out - 1))),
        mix(kappa, matrix(pair_x & pair_y, 0.25)),
        mix(cz, matrix(pair_x & pair_y, 0.25)),
    ]
    for t, cells in enumerate(blocks):
        cells = fold_planes(cells, 16 * iy)
        for n in range(devices):
            copies[pl.ds(n * SHARE + 8 * t, 8), :] = cells


def fetch_all(sources, dests, sems, first=0):
    copies = [pltpu.make_async_copy(a, b, sems.at[first + n]) for n, (a, b) in enumerate(zip(sources, dests))]
    for copy in copies:
        copy.start()
    return copies


def pack_kernel(f_in, kappa_in, cx_in, cy_in, cz_in, x_near, x_far, y_near, y_far, share2, stack, sems):
    even_x, even_y = lax.axis_index("gx") % 2 == 0, lax.axis_index("gy") % 2 == 0
    tiles = [stack.at[pl.ds(a * NZ * TX, NZ * TX), :] for a in range(5)]
    for copy in fetch_all((f_in, kappa_in, cx_in, cy_in, cz_in), tiles, sems):
        copy.wait()
    f, kappa, cx, cy, cz = tiles
    for a, ref in enumerate(tiles):
        cells = ref[...].reshape(NZ, TX, TY)
        at = pl.ds(a * NZ * HALO, NZ * HALO)
        head = cells[:, :HALO].reshape(NZ * HALO, TY)
        tail = cells[:, TX - HALO :].reshape(NZ * HALO, TY)
        x_near[at, :] = jnp.where(even_x, tail, head)
        x_far[at, :] = jnp.where(even_x, head, tail)
    y, lane = iota((128, 128), 0), iota((128, 128), 1)
    fourth = y // 4 == lane % 32
    rows = lambda ref: [Field(ref, TX).row(r) for r in range(TX)]
    cx_rows, cy_rows, kappa_rows, cz_rows = rows(cx), rows(cy), rows(kappa), rows(cz)
    totals = lambda v: [(v[4 * i] + v[4 * i + 1]) + (v[4 * i + 2] + v[4 * i + 3]) for i in range(4)]
    stack = [cx_rows[4 * i] for i in range(4)] + [cx_rows[4 * i + 3] for i in range(4)]
    stack = mix(jnp.concatenate(stack + totals(kappa_rows) + totals(cz_rows), axis=0), matrix(fourth))
    ends = [matrix(fourth & (y % 4 == 0)), matrix(fourth & (y % 4 == 3))]
    sides = mix(jnp.concatenate(totals(cy_rows), axis=0), jnp.concatenate(ends, axis=1))
    group = lane_group(NZ, 32)

    def merge(cells, scale):
        out = cells[:NZ]
        for xi in range(1, 4):
            out = jnp.where(group == xi, cells[NZ * xi : NZ * (xi + 1)], out)
        return out * scale

    kinds = [merge(stack[:128], 1 / 128), merge(stack[128:256], 1 / 128)]
    kinds += [merge(sides[:, :128], 1 / 128), merge(sides[:, 128:], 1 / 128)]
    kinds += [merge(stack[256:384], 1 / 16), merge(stack[384:], 1 / 16)]
    head = [jnp.zeros((8, 128), F32)] * 3
    tail = [jnp.zeros((8, 128), F32)] * 3
    slot = iota((8, 128), 1) % 32 // 4
    for t, cells in enumerate(kinds):
        for dest, first in ((share2, 0), (x_near, SLAB), (x_far, SLAB)):
            dest[pl.ds(first + t * NZ, NZ), :] = cells
        for zv in range(4):
            n = 4 * t + zv
            piece = cells[8 * zv : 8 * zv + 8]
            head[n // 8] = jnp.where(slot == n % 8, shift(piece, 4 * (n % 8), 1), head[n // 8])
            tail[n // 8] = jnp.where(slot == n % 8, shift(piece, 4 * (n % 8) + 4, 1), tail[n // 8])
    for n in range(3):
        y_near[pl.ds(STRIP + 8 * n, 8), :] = jnp.where(even_y, tail[n], head[n])
        y_far[pl.ds(STRIP + 8 * n, 8), :] = jnp.where(even_y, head[n], tail[n])

    group = lane_group(8, 8)
    for a, ref in enumerate((f, kappa, cx, cy, cz)):
        for half in range(2):
            for zo in range(2):
                head = jnp.zeros((8, 128), F32)
                tail = jnp.zeros((8, 128), F32)
                for zi in range(16):
                    cells = ref[pl.ds((zo * 16 + zi) * TX + 8 * half, 8), :]
                    cells = shift(cells, 8 * zi, 1)
                    head = jnp.where(group == zi, cells, head)
                    tail = jnp.where(group == (zi - 1) % 16, cells, tail)
                at = pl.ds(((half * 5 + a) * 2 + zo) * 8, 8)
                y_near[at, :] = jnp.where(even_y, tail, head)
                y_far[at, :] = jnp.where(even_y, head, tail)


def window2(tile, after, before, dest, first, iy, gy):
    lane = iota((NZ, 128), 1)
    first_after, first_before = jnp.where(iy < gy - 1, 36, 0), jnp.where(iy > 0, 124, 128)
    for xi in range(4):
        turned = (lane - 32 * xi + 128) % 128
        cells = jnp.where(turned < 32, tile, jnp.where(turned < first_after, after, jnp.where(turned >= first_before, before, 0.0)))
        dest[pl.ds(first + xi, NZ, stride=TX), :] = shift(cells, -32 * xi, 1)


def window_kernel(share2, x_near, x_far, yr, yl, cr, cl, out, a, b, c, d, kappa, cz, diag):
    ix, iy = lax.axis_index("gx"), lax.axis_index("gy")
    gy = lax.axis_size("gy")
    nx, ny = lax.axis_size("gx") * 4, gy * 32
    refs = (a, b, c, d, kappa, cz)

    def unpack(ref, first, t, turn):
        pieces = []
        for zv in range(4):
            n = 4 * t + zv
            pieces.append(shift(ref[span(first + 8 * (n // 8), 8), :], turn - 4 * (n % 8), 1))
        return jnp.concatenate(pieces, axis=0)

    near, far = STRIP // 2, CORNER + STRIP // 2
    even_x = ix % 2 == 0
    for t, dest in enumerate(refs):
        beside = x_near[pl.ds(SLAB + t * NZ, NZ), :], x_far[pl.ds(SLAB + t * NZ, NZ), :]
        for first, cells, right, left, r_at, l_at in (
            (0, share2[pl.ds(t * NZ, NZ), :], yr, yl, STRIP, STRIP),
            (4, jnp.where(even_x, *beside), cr, cr, far, near),
            (12, jnp.where(even_x, *beside[::-1]), cl, cl, far, near),
        ):
            window2(cells, unpack(right, r_at, t, 32), unpack(left, l_at, t, 92), dest, first, iy, gy)
        for x in range(8, 12):
            dest[pl.ds(x, NZ, stride=TX), :] = jnp.zeros((NZ, 128), F32)
    mask = window_mask(TX, 128, 4, 32, 4, ix, iy, nx, ny)
    a, b, c, d, kappa, cz, diag = (Field(ref, TX) for ref in (*refs, diag))
    x_face, y_face, inv, z_face = stack_fields(out, TX, 3)
    for k in range(NZ):
        x_k = a[k] + shift(b[k], 1, 0)
        y_k = c[k] + shift(d[k], 1, 1)
        x_face[k] = x_k
        y_face[k] = y_k
        diag[k] = base_diag(jnp.where(mask > 0, kappa[k], 1.0), x_k, y_k)
    z_faces(cz, z_face)
    factor(diag, z_face, 1, inv, None)


def assemble3(block, dest, gx, gy, rows):
    group = lane_group(8, 16)
    for ix in range(gx):
        blocks = [block(ix, iy) for iy in range(gy)]
        for zo in range(4):
            for xi in range(2):
                q = 2 * zo + xi
                cells = blocks[0]
                for iy in range(1, gy):
                    cells = jnp.where(group == (iy + q) % 8, blocks[iy], cells)
                dest[pl.ds(8 * zo * rows + 2 * ix + xi, 8, stride=rows), :] = shift(cells, -16 * q, 1)


def global_kernel(gx, gy, own, other, *refs):
    out, raw3, raw4, shares, sems = refs[0], refs[1:9], refs[9:17], refs[17], refs[18]
    outs3 = stack_fields(out, 2 * gx, 5, z_face=False)
    outs4 = stack_fields(out, gx, 5, z_face=False, start=5 * NZ * 2 * gx)
    core = lax.axis_index("gx") % 2
    copies = [
        pltpu.make_async_copy(own, shares.at[:, core], sems.at[0]),
        pltpu.make_async_copy(other, shares.at[:, 1 - core], sems.at[1]),
    ]
    for copy in copies:
        copy.start()
    for copy in copies:
        copy.wait()
    rows, cols = 2 * gx, 16 * gy
    for t, n in enumerate((0, 1, 2, 4, 5)):
        block = lambda jx, jy: shares[jx // 2, jx % 2, pl.ds(jy * SHARE + 8 * t, 8), :]
        assemble3(block, raw3[n], gx, gy, rows)
    xl, xu, yl, yu = (Field(ref, rows) for ref in raw3[:4])
    x, y = iota((rows, 128), 0), iota((rows, 128), 1)
    odd_row, inside = x % 2 == 1, y < cols
    for k in range(NZ):
        half = jnp.where(inside, xu[k], 0.0)
        below = jnp.where(odd_row | (x < 2), 0.0, shift(half, 2, 0))
        x_k = jnp.where(inside, xl[k] + below, 0.0)
        xl[k] = x_k
        xu[k] = jnp.where(x == rows - 1, shift(half, 1, 0), shift(x_k, -1, 0))
        next_row = shift(half, -1, 0)
        below = jnp.where(odd_row, shift(half, 15, 1), shift(next_row, 16, 1))
        y_k = jnp.where(inside, yl[k] + jnp.where((y % 16 == 0) & (y > 0), below, 0.0), 0.0)
        yl[k] = y_k
        above = jnp.where(odd_row, shift(half, 14, 1), shift(next_row, 15, 1))
        yu[k] = jnp.where(y == cols - 1, above, jnp.where(inside, shift(y_k, -1, 1), 0.0))
    yy, jj = iota((128, 128), 0), iota((128, 128), 1)
    keep = yy // 2 == jj
    pair, even, odd = matrix(keep), matrix(keep & (yy % 2 == 0)), matrix(keep & (yy % 2 == 1))
    size = NZ * rows // 2
    lows = [Field(ref, rows) for ref in raw3]
    first = lambda n: lows[n].every_second(0, size, 0)
    second = lambda n: lows[n].every_second(0, size, 1)
    raw4[0][...] = 0.125 * mix(first(0), pair)
    raw4[1][...] = 0.125 * mix(second(1), pair)
    raw4[2][...] = 0.125 * mix(first(2) + second(2), even)
    raw4[3][...] = 0.125 * mix(first(3) + second(3), odd)
    raw4[4][...] = 0.25 * mix(first(4) + second(4), pair)
    raw4[5][...] = 0.25 * mix(first(5) + second(5), pair)
    for raw, outs in ((raw3, outs3), (raw4, outs4)):
        x, y = iota((rows, 128), 0), iota((rows, 128), 1)
        xl, xu, yl, yu, kappa, cz = (Field(ref, rows) for ref in raw[:6])
        z_face, diag = Field(raw[6], rows, 1, NZ + 1), Field(raw[7], rows)
        x_face, y_face, inv, g, c = outs
        inside_x, inside_y = (x > 0).astype(F32), ((y > 0) & (y < cols)).astype(F32)
        for k in range(NZ):
            xl_k, yl_k = xl[k], yl[k]
            diag[k] = jnp.where(y < cols, kappa[k], 1.0) + (xl_k + xu[k]) + (yl_k + yu[k])
            x_face[k] = xl_k * inside_x
            y_face[k] = yl_k * inside_y
        z_faces(cz, z_face)
        factor(diag, z_face, 1, inv, None, g_out=g, c_out=c)
        rows, cols = rows // 2, cols // 2


def down_kernel(nx, ny, *refs):
    stack, yr, yl, corner_r, corner_l, x_near, x_far = refs[:7]
    sends, saved = refs[7:9]
    scratch = list(refs[9:-1])
    sems = refs[-1]
    take = lambda n: [scratch.pop(0) for _ in range(n)]
    ix, iy = lax.axis_index("gx"), lax.axis_index("gy")
    gx, gy = lax.axis_size("gx"), lax.axis_size("gy")
    f, kappa, cx, cy, cz = (stack.at[pl.ds(a * NZ * TX, NZ * TX), :] for a in range(5))
    even_x = ix % 2 == 0
    rows, tiles = 2 * TX, 2
    whole = take(11)
    names = [Field(ref, rows, tiles) for ref in whole[:10]]
    x_face, y_face, inv, u, f0, kappa0, cz0, diag, kept, r = names
    z_face = Field(whole[10], rows, tiles, NZ + 1)
    group = lane_group(8, 8)

    def window(a, tile, z, after, before, turn):
        zo = z // 16
        slab = span(a * NZ * HALO + z * HALO, HALO)
        near, far = x_near[slab, :], x_far[slab, :]
        sides = [jnp.where(even_x, near, far), jnp.where(even_x, far, near)]
        main = jnp.concatenate([tile[span(z * TX, TX), :], *sides], axis=0)
        at = lambda first: span(first + (a * 2 + zo) * 8, 8)
        half = STRIP // 2
        sides = []
        for right, left in (
            (yr[at(0), :], yl[at(0), :]),
            (yr[at(half), :], yl[at(half), :]),
            (corner_r[at(CORNER), :], corner_r[at(0), :]),
            (corner_l[at(CORNER), :], corner_l[at(0), :]),
        ):
            cells = jnp.where(after, right, jnp.where(before, left, 0.0))
            sides.append(pltpu.roll(cells, turn, 1))
        return jnp.concatenate([main, jnp.concatenate(sides, axis=0)], axis=1)

    mask0 = window_mask(rows, 256, TX, TY, HALO, ix, iy, nx, ny)

    def prepare(z, cz_prev):
        zi = z % 16
        after, before = group == zi, group == (zi + 15) % 16
        turn = (128 - 8 * zi) % 128
        f_k, kappa_k, cx_k, cy_k, cz_k = (
            window(a, tile, z, after, before, turn) for a, tile in enumerate((f, kappa, cx, cy, cz))
        )
        f0[z] = f_k
        kappa0[z] = kappa_k
        cz0[z] = cz_k
        z_face[z] = 0.5 * (cz_k + cz_prev)
        x_k, y_k = 0.5 * (cx_k + shift(cx_k, 1, 0)), 0.5 * (cy_k + shift(cy_k, 1, 1))
        x_face[z] = x_k
        y_face[z] = y_k
        diag[z] = base_diag(jnp.where(mask0 > 0, kappa_k, 1.0), x_k, y_k)
        return cz_k

    last = loop(NZ, prepare, jnp.zeros((rows, 256), F32), 2)
    z_face[NZ] = 0.5 * last
    ends = factor(diag, z_face, tiles, inv, 4, f0, kept)
    copies = []

    def save(field):
        at = sum(copy[1] for copy in copies)
        count = field.ref.shape[0]
        copy = pltpu.make_async_copy(field.ref, saved.at[pl.ds(at, count), :], sems.at[len(copies)])
        copy.start()
        copies.append((copy, count))

    for field in (x_face, y_face, inv, f0):
        save(field)
    smooth_down(f0, x_face, y_face, Line(inv, z_face), ends, kept, u, r, 2)
    save(u)
    save(z_face)

    fine = (r, kappa0, cz0, x_face, y_face)
    lanes, tile_x, tile_y, halo = 256, TX, TY, HALO
    for level in (1, 2):
        rows, tile_x, tile_y, halo = rows // 2, tile_x // 2, tile_y // 2, halo // 2
        nx, ny = nx // 2, ny // 2
        whole = take(11)
        names = [Field(ref, rows) for ref in whole[:10]]
        x_face, y_face, inv, u, f1, kappa1, cz1, diag, kept, r = names
        z_face = Field(whole[10], rows, 1, NZ + 1)
        mask = window_mask(rows, 128, tile_x, tile_y, halo, ix, iy, nx, ny)
        y, j = iota((lanes, 128), 0), iota((lanes, 128), 1)
        if lanes == 128:
            j = jnp.where(j < 48, j, jnp.where(j >= 80, j - 64, -1))
        pair = matrix(y // 2 == j)
        even = (iota((1, lanes), 1) % 2 == 0).astype(F32)
        part = 128
        for at in range(0, NZ * rows, part):
            here = pl.ds(at, part)
            both = lambda n: fine[n].every_second(at, part, 0) + fine[n].every_second(at, part, 1)
            below = fine[3].every_second(at, part, 0)
            out = mix(jnp.concatenate([both(0), both(1), both(2), below, both(4) * even], axis=0), pair)
            for n, (dest, weight) in enumerate(((f1, 0.25), (kappa1, 0.25), (cz1, 0.25), (x_face, 0.125), (y_face, 0.125))):
                dest.ref[here, :] = weight * out[n * part : (n + 1) * part]
        for k in range(NZ):
            f1[k] = f1[k] * mask
            diag[k] = base_diag(jnp.where(mask > 0, kappa1[k], 1.0), x_face[k], y_face[k])
        z_faces(cz1, z_face)
        ends = factor(diag, z_face, 1, inv, None, f1, kept)
        smooth_down(f1, x_face, y_face, Line(inv, z_face), ends, kept, u, r, None)
        if level == 1:
            for field in (x_face, y_face, inv, f1, u, z_face):
                save(field)
        fine, lanes = (r, kappa1, cz1, x_face, y_face), 128

    group = lane_group(NZ, 32)
    out = f1.row(0)
    for xi in range(1, 4):
        out = jnp.where(group == xi, shift(f1.row(xi), 32 * xi, 1), out)
    for n in range(gx * gy):
        sends[pl.ds(n * BLOCK, NZ), :] = out
    y, lane = iota((128, 128), 0), iota((128, 128), 1)
    total = jnp.zeros((NZ, 128), F32)
    for xi in range(2):
        place = (lane % 32 // 16 == xi) & (y // 2 == lane % 16) & (y < 32)
        total = total + mix(r.row(2 * xi) + r.row(2 * xi + 1), matrix(place, 0.25))
    total = fold_planes(total, 16 * iy)
    for n in range(gx * gy):
        sends[pl.ds(n * BLOCK + NZ, 8), :] = total
    for copy, _ in copies:
        copy.wait()


def up_kernel(gx, gy, *refs):
    gathered, whole, k2, stack, saved, solution_out, residual_out = refs[:7]
    scratch = list(refs[7:-1])
    sems = refs[-1]
    take = lambda n: [scratch.pop(0) for _ in range(n)]
    ix, iy = lax.axis_index("gx"), lax.axis_index("gy")
    held0, held1 = take(2)
    split = held0.shape[0]
    parts = [saved.at[pl.ds(split, held1.shape[0]), :], saved.at[pl.ds(0, split), :]]
    copy1, copy0 = fetch_all(parts, (held1, held0), sems)
    f2, u2, kept2, wide, e_ref, e0_ref, kept0, u3, f3, r3, f4, u4 = take(12)

    rows, cols = 2 * gx, 16 * gy
    assemble3(lambda jx, jy: gathered[jx * gy + jy, pl.ds(NZ, 8), :], f3, gx, gy, rows)
    f3, u3, r3 = (Field(ref, rows) for ref in (f3, u3, r3))
    y = iota((rows, 128), 1)
    x_face3, y_face3, inv3, g3, c3 = stack_fields(whole, rows, 5, z_face=False)
    line3 = StoredLine(inv3, g3, c3)
    clean = (y < cols).astype(F32)
    for k in range(NZ):
        f3[k] = f3[k] * clean
    zero = jnp.zeros((rows, 128), F32)
    ends = sweep_in(lambda k: f3[k], line3, r3, zero, None)
    smooth_down(f3, x_face3, y_face3, line3, ends, r3, u3, Field(e_ref, rows), None)
    fine = Field(e_ref, rows)
    rows, cols = rows // 2, cols // 2
    size = NZ * rows
    yy, jj = iota((128, 128), 0), iota((128, 128), 1)
    f4[...] = 0.25 * mix(fine.every_second(0, size, 0) + fine.every_second(0, size, 1), matrix(yy // 2 == jj))
    f4, u4 = Field(f4, rows), Field(u4, rows)
    x_face4, y_face4, inv4, g4, c4 = stack_fields(whole, rows, 5, z_face=False, start=5 * NZ * 2 * rows)
    line4 = StoredLine(inv4, g4, c4)
    zero = jnp.zeros((rows, 128), F32)

    def solve4(rhs, old):
        kept, out = {}, {}
        ends = sweep_in(rhs, line4, kept, zero, None)

        def emit(k, value):
            out[k] = OMEGA * value if old is None else (1.0 - OMEGA) * old[k] + OMEGA * value

        sweep_out(ends, kept, line4, emit, None)
        for k in range(NZ):
            u4[k] = out[k]

    solve4(lambda k: f4[k], None)

    def relax(sweep, carry):
        old = [u4[k] for k in range(NZ)]
        solve4(lambda k: f4[k] + neighbours(old[k], x_face4[k], y_face4[k]), old)
        return carry

    lax.fori_loop(0, COARSE_SWEEPS - 1, relax, 0)

    cells = u4.ref[...].reshape(NZ, rows, 128)
    x = iota((1, rows, 128), 1)
    before = jnp.where(x > 0, shift(cells, 1, 1), 0.0)
    after = jnp.where(x < rows - 1, shift(cells, -1, 1), 0.0)
    spread_rows(cells, before, after, wide, size)
    e_ref[...] = mix(wide[pl.ds(0, 2 * size), :], spread_matrix(iota((128, 128), 1), 0, cols), 3)
    rows, cols = 2 * rows, 2 * cols
    smooth_up(f3, x_face3, y_face3, line3, u3, Field(e_ref, rows), r3, None, None)

    def block(dx, dy):
        inside = ((ix + dx >= 0) & (ix + dx < gx)).astype(F32)
        device = jnp.clip(ix + dx, 0, gx - 1) * gy + jnp.clip(iy + dy, 0, gy - 1)
        return gathered[device, pl.ds(0, NZ), :] * inside

    for first, dx in ((0, 0), (4, 1), (12, -1)):
        window2(block(dx, 0), shift(block(dx, 1), 32, 1), shift(block(dx, -1), 96, 1), f2, first, iy, gy)
    for x in range(8, 12):
        f2[pl.ds(x, NZ, stride=TX), :] = jnp.zeros((NZ, 128), F32)
    f2, u2, kept2 = (Field(ref, TX) for ref in (f2, u2, kept2))
    x_face2, y_face2, inv2, z_face2 = stack_fields(k2, TX, 3)
    line2 = Line(inv2, z_face2)
    zero = jnp.zeros((TX, 128), F32)
    ends = sweep_in(lambda k: f2[k], line2, kept2, zero, None)

    def emit2(k, value):
        u2[k] = OMEGA * value

    sweep_out(ends, kept2, line2, emit2, None)

    cells = pltpu.roll(u3.ref[...].reshape(NZ, rows, 128), (rows - 2 * ix) % rows, 1)
    x = iota((1, rows, 128), 1)
    place = 2 * ix + jnp.where(x < rows // 2, x, x - rows)
    cells = jnp.where((place >= 0) & (place < rows), cells, 0.0)
    ring = lambda v, first: jnp.where(iota((1, 8, 128), 1) < first, v[:, :8], v[:, rows - 8 :])
    spread_rows(ring(cells, 4), ring(shift(cells, 1, 1), 4), ring(shift(cells, -1, 1), 4), wide, NZ * 8)
    lane = iota((128, 128), 1)
    fine_y = jnp.where(lane < 80, lane, lane - 128) + 32 * iy
    e_ref[...] = mix(wide[pl.ds(0, NZ * TX), :], spread_matrix(fine_y, 0, cols), 3)
    mask2 = window_mask(TX, 128, 4, 32, 4, ix, iy, 4 * gx, 32 * gy)
    smooth_up(f2, x_face2, y_face2, line2, u2, Field(e_ref, TX), kept2, mask2, None)

    cells = u2.ref[...].reshape(NZ, TX, 128)
    ring = lambda v: jnp.where(iota((1, 8, 128), 1) < 6, v[:, :8], v[:, 8:])
    spread_rows(ring(cells), ring(shift(cells, 1, 1)), ring(shift(cells, -1, 1)), wide, NZ * 8)
    fine_y = jnp.where(lane < 96, lane, lane - 128)
    e_ref[...] = mix(wide[pl.ds(0, NZ * TX), :], spread_matrix(fine_y, 0, 0, circular=True), 3)
    copy1.wait()
    x_face1, y_face1, inv1, f1, u1, z_face1 = stack_fields(held1, TX, 5)
    line1 = Line(inv1, z_face1)
    mask1 = window_mask(TX, 128, 8, 64, 4, ix, iy, 8 * gx, 64 * gy)
    smooth_up(f1, x_face1, y_face1, line1, u1, Field(e_ref, TX), kept2, mask1, None)

    cells = held1[pl.ds(u1.start, NZ * TX), :].reshape(NZ, TX, 128)
    spread_rows(cells, shift(cells, 1, 1), shift(cells, -1, 1), wide, NZ * TX)
    rows = 2 * TX
    weights = spread_matrix(iota((128, 256), 1), 0, 0, circular=True)
    e0 = Field(e0_ref, rows, 2)
    for k in range(0, NZ, 8):
        cells = mix(wide[pl.ds(k * rows, 8 * rows), :], weights, 3)
        for t in range(2):
            e0_ref[pl.ds(e0.base(t, k), 8 * rows), :] = cells[:, 128 * t : 128 * (t + 1)]
    copy0.wait()
    x_face0, y_face0, inv0, f0, u0, z_face0 = stack_fields(held0, rows, 5, 2)
    mask0 = window_mask(rows, 256, TX, TY, HALO, ix, iy, TX * gx, TY * gy)
    smooth_up(f0, x_face0, y_face0, Line(inv0, z_face0), u0, e0, Field(kept0, rows, 2), mask0, 2)

    kappa = Field(stack, TX, start=NZ * TX)

    def residual(k, carry):
        below, flux_z = carry
        column = u0.part(0, k)
        here = column[:TX]
        flux_x = (x_face0.part(0, k) * (column - shift(column, 1, 0)))[: TX + 8]
        row = u0[k][:TX]
        flux_y = y_face0[k][:TX] * (row - shift(row, 1, 1))
        side = (flux_x - shift(flux_x, -1, 0))[:TX] + (flux_y - shift(flux_y, -1, 1))[:, :TY]
        above = u0.part(0, k + 1)[:TX] if k is not NZ - 1 else jnp.zeros((TX, TY), F32)
        flux_up = z_face0.part(0, k + 1)[:TX] * (above - here)
        solution_out[span(k * TX, TX), :] = here
        out = f0.part(0, k)[:TX] - kappa[k] * here - side - flux_z + flux_up
        residual_out[span(k * TX, TX), :] = out
        return here, flux_up

    start = z_face0.part(0, 0)[:TX] * u0.part(0, 0)[:TX]
    carry = loop(NZ - 1, residual, (start, start), 4)
    residual(NZ - 1, carry)


MEBIBYTES = {"pack": 56, "down": 32, "up": 32}
COSTS = {
    "pack": 3 * 10**9, "share": 10**9, "down": 10**10,
    "window_coeffs": 4 * 10**9, "global_coeffs": 4 * 10**9, "up": 12 * 10**9,
}


def call(kernel, name, outs, ins, scratch=(), in_specs=None, out_specs=None, aliases=None):
    shapes = [jax.ShapeDtypeStruct(s, F32) for s in outs]
    return pl.pallas_call(
        kernel,
        name=name,
        out_shape=shapes,
        in_specs=in_specs or [VMEM] * len(ins),
        out_specs=out_specs or [VMEM] * len(outs),
        scratch_shapes=list(scratch),
        input_output_aliases=aliases or {},
        compiler_params=pltpu.CompilerParams(vmem_limit_bytes=MEBIBYTES.get(name, 16) * 1024 * 1024),
        cost_estimate=pl.CostEstimate(flops=COSTS[name], bytes_accessed=4 * sum(x.size for x in ins), transcendentals=0),
    )(*ins)


def body(right_side, kappa_sq, cond_x, cond_y, cond_z):
    gx, gy = lax.axis_size("gx"), lax.axis_size("gy")
    tiles = [v.reshape(NZ * TX, TY) for v in (right_side, kappa_sq, cond_x, cond_y, cond_z)]
    slab, strip = (SLAB + 6 * NZ, 128), (STRIP + 24, 128)
    vm = lambda *shape: pltpu.VMEM(shape, F32)
    dma = lambda n: pltpu.SemaphoreType.DMA((n,))
    devices = gx * gy
    near = lambda n: [(i, i ^ 1) for i in range(n)]
    far = lambda n: [(i, (i + 1 ^ 1) - 1) for i in range(1, n - 1)]
    even_x, even_y = lax.axis_index("gx") % 2 == 0, lax.axis_index("gy") % 2 == 0
    x_near, x_far, y_near, y_far, share2, stack = call(
        pack_kernel, "pack", [slab, slab, strip, strip, (6 * NZ, 128), (5 * NZ * TX, TY)], tiles, [dma(5)], [HBM] * 5
    )
    y_near = lax.ppermute(y_near, "gy", near(gy))
    y_far = lax.ppermute(y_far, "gy", far(gy))
    x_near = lax.ppermute(x_near, "gx", near(gx))
    x_far = lax.ppermute(x_far, "gx", far(gx))
    yr, yl = jnp.where(even_y, y_near, y_far), jnp.where(even_y, y_far, y_near)
    copies = call(functools.partial(share_kernel, devices // 2), "share", [(devices // 2 * SHARE, 128)], [share2])[0]
    half = STRIP // 2
    head = jnp.concatenate([yl[:half], yl[STRIP:], yr[:half], yr[STRIP:]])
    tail = jnp.concatenate([yl[half:], yr[half:]])
    c_near = lax.ppermute(jnp.where(even_x, tail, head), "gx", near(gx))
    c_far = lax.ppermute(jnp.where(even_x, head, tail), "gx", far(gx))
    copies, c_near, c_far = lax.optimization_barrier((copies, c_near, c_far))
    corner_r, corner_l = jnp.where(even_x, c_near, c_far), jnp.where(even_x, c_far, c_near)
    cores = [[x * gy + y for x in range(core, gx, 2) for y in range(gy)] for core in range(2)]
    blocks = copies.reshape(devices // 2, SHARE, 128)
    own = lax.all_to_all(blocks, ("gx", "gy"), 0, 0, axis_index_groups=cores).reshape(gx // 2, gy * SHARE, 128)
    level = lambda rows, n: [vm(NZ * rows, 128)] * n
    faces = lambda rows, tiles: vm(tiles * (NZ + 1) * rows, 128)
    rows3, rows4 = 2 * gx, gx
    size, tall = (NZ * TX, 128), ((NZ + 1) * TX, 128)
    k2 = call(
        window_kernel, "window_coeffs", [(NZ * TX * 4 + TX, 128)], [share2, x_near, x_far, yr, yl, corner_r, corner_l], level(TX, 7)
    )[0]
    big, big_z = (2 * NZ * 2 * TX, 128), (2 * (NZ + 1) * 2 * TX, 128)
    total0, total1 = 2 * (NZ * 6 + 1) * 2 * TX, (NZ * 6 + 1) * TX
    sends, saved = call(
        functools.partial(down_kernel, gx * TX, gy * TY),
        "down",
        [(devices * BLOCK, 128), (total0 + total1, 128)],
        [stack, yr, yl, corner_r, corner_l, x_near, x_far],
        [vm(*big)] * 10 + [vm(*big_z)] + level(TX, 10) + [faces(TX, 1)] + level(8, 10) + [faces(8, 1)] + [dma(12)],
        out_specs=[VMEM, ANY],
    )
    sends, own = lax.optimization_barrier((sends, own))
    other = lax.ppermute(own, "gx", near(gx))
    gathered = lax.all_to_all(sends.reshape(devices, BLOCK, 128), ("gx", "gy"), 0, 0)
    whole = call(
        functools.partial(global_kernel, gx, gy),
        "global_coeffs",
        [(5 * NZ * (rows3 + rows4), 128)],
        [own, other],
        level(rows3, 6) + [faces(rows3, 1)] + level(rows3, 1) + level(rows4, 6) + [faces(rows4, 1)] + level(rows4, 1)
        + [vm(gx // 2, 2, gy * SHARE, 128), dma(2)],
        in_specs=[ANY] * 2,
    )[0]
    field, residual = call(
        functools.partial(up_kernel, gx, gy),
        "up",
        [(NZ * TX, TY)] * 2,
        [gathered, whole, k2, stack, saved],
        [vm(total0, 128), vm(total1, 128)] + level(TX, 3) + [vm(NZ * 2 * TX, 128), vm(*size), vm(*big), vm(*big)]
        + level(rows3, 3) + level(rows4, 2) + [dma(2)],
        in_specs=[VMEM] * 4 + [ANY],
    )
    return field.reshape(right_side.shape), residual.reshape(right_side.shape)


def solution(mesh):
    spec = P(None, "gx", "gy")
    fits = (mesh.shape["gx"], mesh.shape["gy"]) == (8, 4)
    plan = body if fits else spread_body
    return jax.shard_map(plan, mesh=mesh, in_specs=(spec,) * 5, out_specs=(spec, spec), check_vma=False)
```

```python
import functools

import jax
import jax.numpy as jnp
from jax import lax
from jax.experimental import pallas as pl
from jax.experimental.pallas import tpu as pltpu
from jax.sharding import PartitionSpec as P

LEVELS = 4
COARSE_SWEEPS = 16


OMEGA = 0.8


def with_halo(cells, sides, width):
    for axis, dim in sides:
        count = lax.axis_size(axis)
        ends = count - 1
        head = lax.slice_in_dim(cells, 0, width, axis=dim)
        tail = lax.slice_in_dim(cells, cells.shape[dim] - width, cells.shape[dim], axis=dim)
        cells = jnp.concatenate(
            [
                lax.ppermute(tail, axis, [(i, (i + 1) % count) for i in range(ends)]),
                cells,
                lax.ppermute(head, axis, [((i + 1) % count, i) for i in range(ends)]),
            ],
            axis=dim,
        )
    return cells


def apply_op(field, padded, coeffs):
    kappa, x_up, x_low, y_up, y_low, z_up, z_low = coeffs
    zpad = jnp.pad(field, ((1, 1), (0, 0), (0, 0)))
    out = (
        kappa * field
        + x_up * (field - padded[:, 2:, 1:-1])
        + x_low * (field - padded[:, :-2, 1:-1])
    )
    out = out + y_up * (field - padded[:, 1:-1, 2:]) + y_low * (field - padded[:, 1:-1, :-2])
    return out + z_up * (field - zpad[2:]) + z_low * (field - zpad[:-2])


def face_pad(field):
    return with_halo(field, (("gx", 1), ("gy", 2)), 1)


def line_factors(coeffs):
    kappa, x_up, x_low, y_up, y_low, z_up, z_low = coeffs
    diag = kappa + x_up + x_low + y_up + y_low + z_up + z_low
    upper_src = z_up.at[-1].set(jnp.zeros_like(z_up[-1]))

    def factor_step(upper_prev, planes):
        diag_k, low_k, up_k = planes
        inv = 1.0 / (diag_k + low_k * upper_prev)
        upper = -up_k * inv
        return (upper, (inv, upper))

    start = jnp.zeros_like(diag[0])
    unused, stacked = lax.scan(factor_step, start, (diag, z_low, upper_src), unroll=True)
    return stacked


def line_solve(rhs, factors, z_low):
    inverses, uppers = factors

    def forward_step(prev, planes):
        rhs_k, low_k, inv_k = planes
        value = (rhs_k + low_k * prev) * inv_k
        return (value, value)

    start = jnp.zeros_like(rhs[0])
    unused, forward = lax.scan(forward_step, start, (rhs, z_low, inverses), unroll=True)

    def back_step(after, planes):
        fwd_k, up_k = planes
        value = fwd_k - up_k * after
        return (value, value)

    unused, result = lax.scan(back_step, start, (forward, uppers), reverse=True, unroll=True)
    return result


def mean_four(field):
    depth, rows, cols = field.shape
    return field.reshape(depth, rows // 2, 2, cols // 2, 2).mean(axis=(2, 4))


def coarsen(coeffs):
    kappa, x_up, x_low, y_up, y_low, z_up, z_low = coeffs
    depth, rows, cols = kappa.shape
    shape = (depth, rows // 2, 2, cols // 2, 2)
    xu_c = x_up.reshape(shape)[:, :, 1].mean(axis=-1) * 0.25
    xl_c = x_low.reshape(shape)[:, :, 0].mean(axis=-1) * 0.25
    yu_c = y_up.reshape(shape)[:, :, :, :, 1].mean(axis=2) * 0.25
    yl_c = y_low.reshape(shape)[:, :, :, :, 0].mean(axis=2) * 0.25
    return (mean_four(kappa), xu_c, xl_c, yu_c, yl_c, mean_four(z_up), mean_four(z_low))


def prolong(padded):
    depth = padded.shape[0]
    rows = padded.shape[1] - 2
    cols = padded.shape[2] - 2
    centre = padded[:, 1:-1, :]
    even = 0.75 * centre + 0.25 * padded[:, :-2, :]
    odd = 0.75 * centre + 0.25 * padded[:, 2:, :]
    spread = jnp.stack([even, odd], axis=2).reshape(depth, 2 * rows, cols + 2)
    centre = spread[:, :, 1:-1]
    even = 0.75 * centre + 0.25 * spread[:, :, :-2]
    odd = 0.75 * centre + 0.25 * spread[:, :, 2:]
    return jnp.stack([even, odd], axis=3).reshape(depth, 2 * rows, 2 * cols)


def coarse_solve(rhs, coeffs):
    factors = line_factors(coeffs)
    field = OMEGA * line_solve(rhs, factors, coeffs[6])

    def spread_sweep(sweep, current):
        padded = with_halo(current, (("gx", 1), ("gy", 2)), 1)
        defect = rhs - apply_op(current, padded, coeffs)
        return current + OMEGA * line_solve(defect, factors, coeffs[6])

    field = lax.fori_loop(0, COARSE_SWEEPS - 1, spread_sweep, field)
    return field


def cycle(rhs, coeffs, level):
    if level == LEVELS:
        return coarse_solve(rhs, coeffs)
    factors = line_factors(coeffs)
    field = OMEGA * line_solve(rhs, factors, coeffs[6])
    padded = face_pad(field)
    defect = rhs - apply_op(field, padded, coeffs)
    correction = cycle(mean_four(defect), coarsen(coeffs), level + 1)
    rimmed = with_halo(correction, (("gx", 1), ("gy", 2)), 1)
    field = field + prolong(rimmed)
    padded = face_pad(field)
    defect = rhs - apply_op(field, padded, coeffs)
    return field + OMEGA * line_solve(defect, factors, coeffs[6])


def spread_body(right_side, kappa_sq, cond_x, cond_y, cond_z):
    padded_x = with_halo(cond_x, (("gx", 1),), 1)
    padded_y = with_halo(cond_y, (("gy", 2),), 1)
    padded_z = jnp.pad(cond_z, ((1, 1), (0, 0), (0, 0)))
    x_up = 0.5 * (cond_x + padded_x[:, 2:, :])
    x_low = 0.5 * (cond_x + padded_x[:, :-2, :])
    y_up = 0.5 * (cond_y + padded_y[:, :, 2:])
    y_low = 0.5 * (cond_y + padded_y[:, :, :-2])
    z_up = 0.5 * (cond_z + padded_z[2:])
    z_low = 0.5 * (cond_z + padded_z[:-2])
    coeffs = (kappa_sq, x_up, x_low, y_up, y_low, z_up, z_low)
    solution_field = cycle(right_side, coeffs, 0)
    residual = right_side - apply_op(solution_field, face_pad(solution_field), coeffs)
    return (solution_field, residual)


F32 = jnp.float32
BF16 = jnp.bfloat16
NZ = 32
HALF = NZ // 2
TX, TY = 16, 128
HALO = 8
SLAB = 5 * NZ * HALO
STRIP = 160
CORNER = 104
SHARE = 40
BLOCK = NZ + 8
VMEM = pl.BlockSpec(memory_space=pltpu.VMEM)
ANY = pl.BlockSpec(memory_space=pl.ANY)
HBM = pl.BlockSpec(memory_space=pltpu.HBM)


def iota(shape, dim):
    return lax.broadcasted_iota(jnp.int32, shape, dim)


def shift(x, by, axis):
    by = by % x.shape[axis]
    return pltpu.roll(x, by, axis) if by else x


def mix(x, weights, parts=2):
    pieces = []
    for n in range(parts):
        piece = x.astype(BF16)
        pieces.append(piece)
        if n < parts - 1:
            x = x - piece.astype(F32)
    out = jnp.dot(jnp.concatenate(pieces, axis=0), weights, preferred_element_type=F32)
    rows = x.shape[0]
    return sum(out[n * rows : (n + 1) * rows] for n in reversed(range(parts)))


def matrix(mask, weight=1.0):
    return jnp.where(mask, weight, 0.0).astype(BF16)


def span(start, size):
    if not isinstance(start, int):
        start = pl.multiple_of(start, 8)
    return pl.ds(start, size)


class Field:
    def __init__(self, ref, rows, tiles=1, planes=NZ, start=0):
        self.ref, self.rows, self.tiles, self.planes, self.start = ref, rows, tiles, planes, start

    def base(self, tile, k):
        return self.start + tile * self.planes * self.rows + k * self.rows

    def part(self, tile, k):
        return self.ref[span(self.base(tile, k), self.rows), :]

    def __getitem__(self, k):
        parts = [self.part(t, k) for t in range(self.tiles)]
        return parts[0] if self.tiles == 1 else jnp.concatenate(parts, axis=1)

    def __setitem__(self, k, value):
        for t in range(self.tiles):
            self.put(t, k, value[:, 128 * t : 128 * (t + 1)])

    def put(self, tile, k, value):
        self.ref[span(self.base(tile, k), self.rows), :] = value

    def every_second(self, at, count, odd):
        parts = []
        for t in range(self.tiles):
            first = self.base(t, 0) + 2 * at + odd
            parts.append(self.ref[pl.ds(first, count, stride=2), :])
        return parts[0] if self.tiles == 1 else jnp.concatenate(parts, axis=1)

    def row(self, row):
        return self.ref[pl.ds(self.start + row, self.planes, stride=self.rows), :]


def stack_fields(ref, rows, count, tiles=1, z_face=True, start=0):
    size = tiles * NZ * rows
    out = [Field(ref, rows, tiles, NZ, start + n * size) for n in range(count)]
    return out + [Field(ref, rows, tiles, NZ + 1, start + count * size)] if z_face else out


def loop(count, step, carry, unroll=None):
    if unroll is None or unroll >= count:
        for i in range(count):
            carry = step(i, carry)
        return carry
    return lax.fori_loop(0, count, step, carry, unroll=unroll)


def neighbours(field, x_face, y_face):
    out = x_face * shift(field, 1, 0) + shift(x_face * field, -1, 0)
    return out + (y_face * shift(field, 1, 1) + shift(y_face * field, -1, 1))


class Line:
    def __init__(self, inv, z_face):
        self.inv, self.z_face = inv, z_face

    def inward(self, k, upper):
        return self.z_face[k + 1 if upper else k] * self.inv[k]

    def outward(self, k, upper):
        return self.z_face[k if upper else k + 1] * self.inv[k]


class StoredLine:
    def __init__(self, inv, g, c):
        self.inv, self.g, self.c = inv, g, c

    def inward(self, k, upper):
        return self.g[k]

    def outward(self, k, upper):
        return self.c[k]


def sweep_in(rhs, line, keep, start, unroll):
    def step(i, carry):
        low, high = carry
        k, m = i, NZ - 1 - i
        low = rhs(k) * line.inv[k] + line.inward(k, False) * low
        high = rhs(m) * line.inv[m] + line.inward(m, True) * high
        keep[k] = low
        keep[m] = high
        return low, high

    return loop(HALF, step, (start, start), unroll)


def sweep_out(ends, kept, line, emit, unroll):
    low, high = ends
    a, b = line.outward(HALF - 1, False), line.outward(HALF, True)
    low = (low + a * high) * (1.0 / (1.0 - a * b))
    high = high + b * low

    def step(i, carry):
        low, high = carry
        k, m = HALF - 1 - i, HALF + i
        emit(k, low)
        emit(m, high)
        low = kept[k - 1] + line.outward(k - 1, False) * low
        high = kept[m + 1] + line.outward(m + 1, True) * high
        return low, high

    low, high = loop(HALF - 1, step, (low, high), unroll)
    emit(0, low)
    emit(NZ - 1, high)


def factor(diag, z_face, tiles, inv_out, unroll, rhs=None, keep=None, g_out=None, c_out=None):
    ends = []
    for t in range(tiles):
        zero = diag.part(t, 0) * 0.0

        def one(k, upper, before, last, prev):
            below, above = z_face.part(t, k), z_face.part(t, k + 1)
            inner, outer = (above, below) if upper else (below, above)
            minor = (diag.part(t, k) + below + above) * last - (inner * inner) * before
            inv = last * (1.0 / minor)
            inv_out.put(t, k, inv)
            if g_out is not None:
                g_out.put(t, k, inner * inv)
                c_out.put(t, k, outer * inv)
            if rhs is not None:
                prev = rhs.part(t, k) * inv + (inner * inv) * prev
                keep.put(t, k, prev)
            return last, minor, prev

        def step(i, carry):
            low, high = carry
            return one(i, False, *low), one(NZ - 1 - i, True, *high)

        start = (zero, zero + 1.0, zero)
        low, high = loop(HALF, step, (start, start), unroll)
        ends.append((low[2], high[2]))
    join = lambda n: ends[0][n] if tiles == 1 else jnp.concatenate([e[n] for e in ends], axis=1)
    return join(0), join(1)


def z_faces(cz, out, tiles=1):
    for t in range(tiles):
        before = None
        for k in range(NZ + 1):
            here = cz.part(t, k) if k < NZ else None
            both = here if before is None else before if here is None else here + before
            out.put(t, k, 0.5 * both)
            before = here


def base_diag(kappa, x_face, y_face):
    return kappa + (x_face + shift(x_face, -1, 0)) + (y_face + shift(y_face, -1, 1))


def window_mask(rows, lanes, tile_x, tile_y, halo, ix, iy, nx, ny):
    x, y = iota((rows, lanes), 0), iota((rows, lanes), 1)
    x = jnp.where(x < (rows + tile_x) // 2, x, x - rows)
    y = jnp.where(y < (lanes + tile_y) // 2, y, y - lanes)
    valid = (y >= -halo) & (y < tile_y + halo) & (x >= -halo) & (x < tile_x + halo)
    x, y = x + ix * tile_x, y + iy * tile_y
    return (valid & (x >= 0) & (x < nx) & (y >= 0) & (y < ny)).astype(F32)


def smooth_down(f, x_face, y_face, line, ends, kept, u, r, unroll):
    def emit(k, value):
        field = OMEGA * value
        u[k] = field
        r[k] = (1.0 - OMEGA) * f[k] + neighbours(field, x_face[k], y_face[k])

    sweep_out(ends, kept, line, emit, unroll)


def smooth_up(f, x_face, y_face, line, u, e, kept, mask, unroll):
    masked = (lambda v: v) if mask is None else (lambda v: v * mask)

    def rhs(k):
        field = masked(u[k] + e[k])
        u[k] = field
        return masked(f[k] + neighbours(field, x_face[k], y_face[k]))

    def emit(k, value):
        u[k] = (1.0 - OMEGA) * u[k] + OMEGA * value

    zero = jnp.zeros((u.rows, 128 * u.tiles), F32)
    ends = sweep_in(rhs, line, kept, zero, unroll)
    sweep_out(ends, kept, line, emit, unroll)


def spread_rows(cells, before, after, dest, size):
    dest[pl.ds(0, size, stride=2), :] = (0.75 * cells + 0.25 * before).reshape(size, 128)
    dest[pl.ds(1, size, stride=2), :] = (0.75 * cells + 0.25 * after).reshape(size, 128)


def spread_matrix(fine, base, coarse_count, circular=False):
    j = iota((128, fine.shape[1]), 0) + base
    parent = (fine + 2048) // 2 - 1024
    partner = parent + 2 * ((fine + 2048) % 2) - 1
    if circular:
        j, parent, partner = j % 128, parent % 128, partner % 128
    weights = jnp.where(j == parent, 0.75, jnp.where(j == partner, 0.25, 0.0))
    if not circular:
        inside = (j >= 0) & (j < coarse_count) & (fine >= 0) & (fine < 2 * coarse_count)
        weights = jnp.where(inside, weights, 0.0)
    return weights.astype(BF16)


def lane_group(rows, width):
    return iota((rows, 128), 1) // width


def fold_planes(cells, turn):
    group = lane_group(8, 32)
    out = cells[:8]
    for n in range(1, 4):
        out = jnp.where(group == n, cells[8 * n : 8 * n + 8], out)
    return pltpu.roll(out, turn, 1)


def share_kernel(devices, share2, copies):
    iy = lax.axis_index("gy")
    y, lane = iota((128, 128), 0), iota((128, 128), 1)
    x_in, y_in = y // 32, y % 32
    x_out, y_out = lane % 32 // 16, lane % 16
    pair_y, pair_x = y_in // 2 == y_out, x_in // 2 == x_out
    a, b, c, d, kappa, cz = (share2[pl.ds(t * NZ, NZ), :] for t in range(6))
    eighth = lambda mask: matrix(mask, 0.125)
    blocks = [
        mix(a, eighth(pair_y & (x_in == 2 * x_out))) + mix(b, eighth(pair_y & (x_in == 1) & (x_out == 1))),
        mix(b, eighth(pair_y & (x_in == 3) & (x_out == 0)))
        + mix(d, eighth((x_out == 1) & (y_in == 31) & (x_in // 2 == y_out))),
        mix(c, eighth(pair_x & (y_in == 2 * y_out))) + mix(d, eighth(pair_x & (y_in == 2 * y_out - 1))),
        mix(kappa, matrix(pair_x & pair_y, 0.25)),
        mix(cz, matrix(pair_x & pair_y, 0.25)),
    ]
    for t, cells in enumerate(blocks):
        cells = fold_planes(cells, 16 * iy)
        for n in range(devices):
            copies[pl.ds(n * SHARE + 8 * t, 8), :] = cells


def fetch_all(sources, dests, sems, first=0):
    copies = [pltpu.make_async_copy(a, b, sems.at[first + n]) for n, (a, b) in enumerate(zip(sources, dests))]
    for copy in copies:
        copy.start()
    return copies


def pack_kernel(f_in, kappa_in, cx_in, cy_in, cz_in, x_near, x_far, y_near, y_far, share2, stack, sems):
    even_x, even_y = lax.axis_index("gx") % 2 == 0, lax.axis_index("gy") % 2 == 0
    tiles = [stack.at[pl.ds(a * NZ * TX, NZ * TX), :] for a in range(5)]
    for copy in fetch_all((f_in, kappa_in, cx_in, cy_in, cz_in), tiles, sems):
        copy.wait()
    f, kappa, cx, cy, cz = tiles
    for a, ref in enumerate(tiles):
        cells = ref[...].reshape(NZ, TX, TY)
        at = pl.ds(a * NZ * HALO, NZ * HALO)
        head = cells[:, :HALO].reshape(NZ * HALO, TY)
        tail = cells[:, TX - HALO :].reshape(NZ * HALO, TY)
        x_near[at, :] = jnp.where(even_x, tail, head)
        x_far[at, :] = jnp.where(even_x, head, tail)
    y, lane = iota((128, 128), 0), iota((128, 128), 1)
    fourth = y // 4 == lane % 32
    rows = lambda ref: [Field(ref, TX).row(r) for r in range(TX)]
    cx_rows, cy_rows, kappa_rows, cz_rows = rows(cx), rows(cy), rows(kappa), rows(cz)
    totals = lambda v: [(v[4 * i] + v[4 * i + 1]) + (v[4 * i + 2] + v[4 * i + 3]) for i in range(4)]
    stack = [cx_rows[4 * i] for i in range(4)] + [cx_rows[4 * i + 3] for i in range(4)]
    stack = mix(jnp.concatenate(stack + totals(kappa_rows) + totals(cz_rows), axis=0), matrix(fourth))
    ends = [matrix(fourth & (y % 4 == 0)), matrix(fourth & (y % 4 == 3))]
    sides = mix(jnp.concatenate(totals(cy_rows), axis=0), jnp.concatenate(ends, axis=1))
    group = lane_group(NZ, 32)

    def merge(cells, scale):
        out = cells[:NZ]
        for xi in range(1, 4):
            out = jnp.where(group == xi, cells[NZ * xi : NZ * (xi + 1)], out)
        return out * scale

    kinds = [merge(stack[:128], 1 / 128), merge(stack[128:256], 1 / 128)]
    kinds += [merge(sides[:, :128], 1 / 128), merge(sides[:, 128:], 1 / 128)]
    kinds += [merge(stack[256:384], 1 / 16), merge(stack[384:], 1 / 16)]
    head = [jnp.zeros((8, 128), F32)] * 3
    tail = [jnp.zeros((8, 128), F32)] * 3
    slot = iota((8, 128), 1) % 32 // 4
    for t, cells in enumerate(kinds):
        for dest, first in ((share2, 0), (x_near, SLAB), (x_far, SLAB)):
            dest[pl.ds(first + t * NZ, NZ), :] = cells
        for zv in range(4):
            n = 4 * t + zv
            piece = cells[8 * zv : 8 * zv + 8]
            head[n // 8] = jnp.where(slot == n % 8, shift(piece, 4 * (n % 8), 1), head[n // 8])
            tail[n // 8] = jnp.where(slot == n % 8, shift(piece, 4 * (n % 8) + 4, 1), tail[n // 8])
    for n in range(3):
        y_near[pl.ds(STRIP + 8 * n, 8), :] = jnp.where(even_y, tail[n], head[n])
        y_far[pl.ds(STRIP + 8 * n, 8), :] = jnp.where(even_y, head[n], tail[n])

    group = lane_group(8, 8)
    for a, ref in enumerate((f, kappa, cx, cy, cz)):
        for half in range(2):
            for zo in range(2):
                head = jnp.zeros((8, 128), F32)
                tail = jnp.zeros((8, 128), F32)
                for zi in range(16):
                    cells = ref[pl.ds((zo * 16 + zi) * TX + 8 * half, 8), :]
                    cells = shift(cells, 8 * zi, 1)
                    head = jnp.where(group == zi, cells, head)
                    tail = jnp.where(group == (zi - 1) % 16, cells, tail)
                at = pl.ds(((half * 5 + a) * 2 + zo) * 8, 8)
                y_near[at, :] = jnp.where(even_y, tail, head)
                y_far[at, :] = jnp.where(even_y, head, tail)


def window2(tile, after, before, dest, first, iy, gy):
    lane = iota((NZ, 128), 1)
    first_after, first_before = jnp.where(iy < gy - 1, 36, 0), jnp.where(iy > 0, 124, 128)
    for xi in range(4):
        turned = (lane - 32 * xi + 128) % 128
        cells = jnp.where(turned < 32, tile, jnp.where(turned < first_after, after, jnp.where(turned >= first_before, before, 0.0)))
        dest[pl.ds(first + xi, NZ, stride=TX), :] = shift(cells, -32 * xi, 1)


def window_kernel(share2, x_near, x_far, yr, yl, cr, cl, out, a, b, c, d, kappa, cz, diag):
    ix, iy = lax.axis_index("gx"), lax.axis_index("gy")
    gy = lax.axis_size("gy")
    nx, ny = lax.axis_size("gx") * 4, gy * 32
    refs = (a, b, c, d, kappa, cz)

    def unpack(ref, first, t, turn):
        pieces = []
        for zv in range(4):
            n = 4 * t + zv
            pieces.append(shift(ref[span(first + 8 * (n // 8), 8), :], turn - 4 * (n % 8), 1))
        return jnp.concatenate(pieces, axis=0)

    near, far = STRIP // 2, CORNER + STRIP // 2
    even_x = ix % 2 == 0
    for t, dest in enumerate(refs):
        beside = x_near[pl.ds(SLAB + t * NZ, NZ), :], x_far[pl.ds(SLAB + t * NZ, NZ), :]
        for first, cells, right, left, r_at, l_at in (
            (0, share2[pl.ds(t * NZ, NZ), :], yr, yl, STRIP, STRIP),
            (4, jnp.where(even_x, *beside), cr, cr, far, near),
            (12, jnp.where(even_x, *beside[::-1]), cl, cl, far, near),
        ):
            window2(cells, unpack(right, r_at, t, 32), unpack(left, l_at, t, 92), dest, first, iy, gy)
        for x in range(8, 12):
            dest[pl.ds(x, NZ, stride=TX), :] = jnp.zeros((NZ, 128), F32)
    mask = window_mask(TX, 128, 4, 32, 4, ix, iy, nx, ny)
    a, b, c, d, kappa, cz, diag = (Field(ref, TX) for ref in (*refs, diag))
    x_face, y_face, inv, z_face = stack_fields(out, TX, 3)
    for k in range(NZ):
        x_k = a[k] + shift(b[k], 1, 0)
        y_k = c[k] + shift(d[k], 1, 1)
        x_face[k] = x_k
        y_face[k] = y_k
        diag[k] = base_diag(jnp.where(mask > 0, kappa[k], 1.0), x_k, y_k)
    z_faces(cz, z_face)
    factor(diag, z_face, 1, inv, None)


def assemble3(block, dest, gx, gy, rows):
    group = lane_group(8, 16)
    for ix in range(gx):
        blocks = [block(ix, iy) for iy in range(gy)]
        for zo in range(4):
            for xi in range(2):
                q = 2 * zo + xi
                cells = blocks[0]
                for iy in range(1, gy):
                    cells = jnp.where(group == (iy + q) % 8, blocks[iy], cells)
                dest[pl.ds(8 * zo * rows + 2 * ix + xi, 8, stride=rows), :] = shift(cells, -16 * q, 1)


def global_kernel(gx, gy, own, other, *refs):
    out, raw3, raw4, shares, sems = refs[0], refs[1:9], refs[9:17], refs[17], refs[18]
    outs3 = stack_fields(out, 2 * gx, 5, z_face=False)
    outs4 = stack_fields(out, gx, 5, z_face=False, start=5 * NZ * 2 * gx)
    core = lax.axis_index("gx") % 2
    copies = [
        pltpu.make_async_copy(own, shares.at[:, core], sems.at[0]),
        pltpu.make_async_copy(other, shares.at[:, 1 - core], sems.at[1]),
    ]
    for copy in copies:
        copy.start()
    for copy in copies:
        copy.wait()
    rows, cols = 2 * gx, 16 * gy
    for t, n in enumerate((0, 1, 2, 4, 5)):
        block = lambda jx, jy: shares[jx // 2, jx % 2, pl.ds(jy * SHARE + 8 * t, 8), :]
        assemble3(block, raw3[n], gx, gy, rows)
    xl, xu, yl, yu = (Field(ref, rows) for ref in raw3[:4])
    x, y = iota((rows, 128), 0), iota((rows, 128), 1)
    odd_row, inside = x % 2 == 1, y < cols
    for k in range(NZ):
        half = jnp.where(inside, xu[k], 0.0)
        below = jnp.where(odd_row | (x < 2), 0.0, shift(half, 2, 0))
        x_k = jnp.where(inside, xl[k] + below, 0.0)
        xl[k] = x_k
        xu[k] = jnp.where(x == rows - 1, shift(half, 1, 0), shift(x_k, -1, 0))
        next_row = shift(half, -1, 0)
        below = jnp.where(odd_row, shift(half, 15, 1), shift(next_row, 16, 1))
        y_k = jnp.where(inside, yl[k] + jnp.where((y % 16 == 0) & (y > 0), below, 0.0), 0.0)
        yl[k] = y_k
        above = jnp.where(odd_row, shift(half, 14, 1), shift(next_row, 15, 1))
        yu[k] = jnp.where(y == cols - 1, above, jnp.where(inside, shift(y_k, -1, 1), 0.0))
    yy, jj = iota((128, 128), 0), iota((128, 128), 1)
    keep = yy // 2 == jj
    pair, even, odd = matrix(keep), matrix(keep & (yy % 2 == 0)), matrix(keep & (yy % 2 == 1))
    size = NZ * rows // 2
    lows = [Field(ref, rows) for ref in raw3]
    first = lambda n: lows[n].every_second(0, size, 0)
    second = lambda n: lows[n].every_second(0, size, 1)
    raw4[0][...] = 0.125 * mix(first(0), pair)
    raw4[1][...] = 0.125 * mix(second(1), pair)
    raw4[2][...] = 0.125 * mix(first(2) + second(2), even)
    raw4[3][...] = 0.125 * mix(first(3) + second(3), odd)
    raw4[4][...] = 0.25 * mix(first(4) + second(4), pair)
    raw4[5][...] = 0.25 * mix(first(5) + second(5), pair)
    for raw, outs in ((raw3, outs3), (raw4, outs4)):
        x, y = iota((rows, 128), 0), iota((rows, 128), 1)
        xl, xu, yl, yu, kappa, cz = (Field(ref, rows) for ref in raw[:6])
        z_face, diag = Field(raw[6], rows, 1, NZ + 1), Field(raw[7], rows)
        x_face, y_face, inv, g, c = outs
        inside_x, inside_y = (x > 0).astype(F32), ((y > 0) & (y < cols)).astype(F32)
        for k in range(NZ):
            xl_k, yl_k = xl[k], yl[k]
            diag[k] = jnp.where(y < cols, kappa[k], 1.0) + (xl_k + xu[k]) + (yl_k + yu[k])
            x_face[k] = xl_k * inside_x
            y_face[k] = yl_k * inside_y
        z_faces(cz, z_face)
        factor(diag, z_face, 1, inv, None, g_out=g, c_out=c)
        rows, cols = rows // 2, cols // 2


def down_kernel(nx, ny, *refs):
    stack, yr, yl, corner_r, corner_l, x_near, x_far = refs[:7]
    sends, saved = refs[7:9]
    scratch = list(refs[9:-1])
    sems = refs[-1]
    take = lambda n: [scratch.pop(0) for _ in range(n)]
    ix, iy = lax.axis_index("gx"), lax.axis_index("gy")
    gx, gy = lax.axis_size("gx"), lax.axis_size("gy")
    f, kappa, cx, cy, cz = (stack.at[pl.ds(a * NZ * TX, NZ * TX), :] for a in range(5))
    even_x = ix % 2 == 0
    rows, tiles = 2 * TX, 2
    whole = take(11)
    names = [Field(ref, rows, tiles) for ref in whole[:10]]
    x_face, y_face, inv, u, f0, kappa0, cz0, diag, kept, r = names
    z_face = Field(whole[10], rows, tiles, NZ + 1)
    group = lane_group(8, 8)

    def window(a, tile, z, after, before, turn):
        zo = z // 16
        slab = span(a * NZ * HALO + z * HALO, HALO)
        near, far = x_near[slab, :], x_far[slab, :]
        sides = [jnp.where(even_x, near, far), jnp.where(even_x, far, near)]
        main = jnp.concatenate([tile[span(z * TX, TX), :], *sides], axis=0)
        at = lambda first: span(first + (a * 2 + zo) * 8, 8)
        half = STRIP // 2
        sides = []
        for right, left in (
            (yr[at(0), :], yl[at(0), :]),
            (yr[at(half), :], yl[at(half), :]),
            (corner_r[at(CORNER), :], corner_r[at(0), :]),
            (corner_l[at(CORNER), :], corner_l[at(0), :]),
        ):
            cells = jnp.where(after, right, jnp.where(before, left, 0.0))
            sides.append(pltpu.roll(cells, turn, 1))
        return jnp.concatenate([main, jnp.concatenate(sides, axis=0)], axis=1)

    mask0 = window_mask(rows, 256, TX, TY, HALO, ix, iy, nx, ny)

    def prepare(z, cz_prev):
        zi = z % 16
        after, before = group == zi, group == (zi + 15) % 16
        turn = (128 - 8 * zi) % 128
        f_k, kappa_k, cx_k, cy_k, cz_k = (
            window(a, tile, z, after, before, turn) for a, tile in enumerate((f, kappa, cx, cy, cz))
        )
        f0[z] = f_k
        kappa0[z] = kappa_k
        cz0[z] = cz_k
        z_face[z] = 0.5 * (cz_k + cz_prev)
        x_k, y_k = 0.5 * (cx_k + shift(cx_k, 1, 0)), 0.5 * (cy_k + shift(cy_k, 1, 1))
        x_face[z] = x_k
        y_face[z] = y_k
        diag[z] = base_diag(jnp.where(mask0 > 0, kappa_k, 1.0), x_k, y_k)
        return cz_k

    last = loop(NZ, prepare, jnp.zeros((rows, 256), F32), 2)
    z_face[NZ] = 0.5 * last
    ends = factor(diag, z_face, tiles, inv, 4, f0, kept)
    copies = []

    def save(field):
        at = sum(copy[1] for copy in copies)
        count = field.ref.shape[0]
        copy = pltpu.make_async_copy(field.ref, saved.at[pl.ds(at, count), :], sems.at[len(copies)])
        copy.start()
        copies.append((copy, count))

    for field in (x_face, y_face, inv, f0):
        save(field)
    smooth_down(f0, x_face, y_face, Line(inv, z_face), ends, kept, u, r, 2)
    save(u)
    save(z_face)

    fine = (r, kappa0, cz0, x_face, y_face)
    lanes, tile_x, tile_y, halo = 256, TX, TY, HALO
    for level in (1, 2):
        rows, tile_x, tile_y, halo = rows // 2, tile_x // 2, tile_y // 2, halo // 2
        nx, ny = nx // 2, ny // 2
        whole = take(11)
        names = [Field(ref, rows) for ref in whole[:10]]
        x_face, y_face, inv, u, f1, kappa1, cz1, diag, kept, r = names
        z_face = Field(whole[10], rows, 1, NZ + 1)
        mask = window_mask(rows, 128, tile_x, tile_y, halo, ix, iy, nx, ny)
        y, j = iota((lanes, 128), 0), iota((lanes, 128), 1)
        if lanes == 128:
            j = jnp.where(j < 48, j, jnp.where(j >= 80, j - 64, -1))
        pair = matrix(y // 2 == j)
        even = (iota((1, lanes), 1) % 2 == 0).astype(F32)
        part = 128
        for at in range(0, NZ * rows, part):
            here = pl.ds(at, part)
            both = lambda n: fine[n].every_second(at, part, 0) + fine[n].every_second(at, part, 1)
            below = fine[3].every_second(at, part, 0)
            out = mix(jnp.concatenate([both(0), both(1), both(2), below, both(4) * even], axis=0), pair)
            for n, (dest, weight) in enumerate(((f1, 0.25), (kappa1, 0.25), (cz1, 0.25), (x_face, 0.125), (y_face, 0.125))):
                dest.ref[here, :] = weight * out[n * part : (n + 1) * part]
        for k in range(NZ):
            f1[k] = f1[k] * mask
            diag[k] = base_diag(jnp.where(mask > 0, kappa1[k], 1.0), x_face[k], y_face[k])
        z_faces(cz1, z_face)
        ends = factor(diag, z_face, 1, inv, None, f1, kept)
        smooth_down(f1, x_face, y_face, Line(inv, z_face), ends, kept, u, r, None)
        if level == 1:
            for field in (x_face, y_face, inv, f1, u, z_face):
                save(field)
        fine, lanes = (r, kappa1, cz1, x_face, y_face), 128

    group = lane_group(NZ, 32)
    out = f1.row(0)
    for xi in range(1, 4):
        out = jnp.where(group == xi, shift(f1.row(xi), 32 * xi, 1), out)
    for n in range(gx * gy // 2):
        sends[pl.ds(n * BLOCK, NZ), :] = out
    y, lane = iota((128, 128), 0), iota((128, 128), 1)
    total = jnp.zeros((NZ, 128), F32)
    for xi in range(2):
        place = (lane % 32 // 16 == xi) & (y // 2 == lane % 16) & (y < 32)
        total = total + mix(r.row(2 * xi) + r.row(2 * xi + 1), matrix(place, 0.25))
    total = fold_planes(total, 16 * iy)
    for n in range(gx * gy // 2):
        sends[pl.ds(n * BLOCK + NZ, 8), :] = total
    for copy, _ in copies:
        copy.wait()


def up_kernel(gx, gy, *refs):
    own, other, whole, k2, stack, saved, solution_out, residual_out = refs[:8]
    scratch = list(refs[8:-1])
    sems = refs[-1]
    take = lambda n: [scratch.pop(0) for _ in range(n)]
    ix, iy = lax.axis_index("gx"), lax.axis_index("gy")
    held0, held1 = take(2)
    split = held0.shape[0]
    parts = [saved.at[pl.ds(split, held1.shape[0]), :], saved.at[pl.ds(0, split), :]]
    fetched = fetch_all(parts, (held1, held0), sems)
    core = ix % 2

    def gathered(jx, jy, at):
        if isinstance(jx, int):
            same = core == jx % 2
            return jnp.where(same, own[jx // 2 * gy + jy, at, :], other[jx // 2 * gy + jy, at, :])
        return jx[1][jx[0] // 2 * gy + jy, at, :]
    f2, u2, kept2, wide, e_ref, e0_ref, kept0, u3, f3, r3, f4, u4 = take(12)

    rows, cols = 2 * gx, 16 * gy
    assemble3(lambda jx, jy: gathered(jx, jy, pl.ds(NZ, 8)), f3, gx, gy, rows)
    f3, u3, r3 = (Field(ref, rows) for ref in (f3, u3, r3))
    y = iota((rows, 128), 1)
    x_face3, y_face3, inv3, g3, c3 = stack_fields(whole, rows, 5, z_face=False)
    line3 = StoredLine(inv3, g3, c3)
    clean = (y < cols).astype(F32)
    for k in range(NZ):
        f3[k] = f3[k] * clean
    zero = jnp.zeros((rows, 128), F32)
    ends = sweep_in(lambda k: f3[k], line3, r3, zero, None)
    smooth_down(f3, x_face3, y_face3, line3, ends, r3, u3, Field(e_ref, rows), None)
    fine = Field(e_ref, rows)
    rows, cols = rows // 2, cols // 2
    size = NZ * rows
    yy, jj = iota((128, 128), 0), iota((128, 128), 1)
    f4[...] = 0.25 * mix(fine.every_second(0, size, 0) + fine.every_second(0, size, 1), matrix(yy // 2 == jj))
    f4, u4 = Field(f4, rows), Field(u4, rows)
    x_face4, y_face4, inv4, g4, c4 = stack_fields(whole, rows, 5, z_face=False, start=5 * NZ * 2 * rows)
    line4 = StoredLine(inv4, g4, c4)
    zero = jnp.zeros((rows, 128), F32)

    def solve4(rhs, old):
        kept, out = {}, {}
        ends = sweep_in(rhs, line4, kept, zero, None)

        def emit(k, value):
            out[k] = OMEGA * value if old is None else (1.0 - OMEGA) * old[k] + OMEGA * value

        sweep_out(ends, kept, line4, emit, None)
        for k in range(NZ):
            u4[k] = out[k]

    solve4(lambda k: f4[k], None)

    def relax(sweep, carry):
        old = [u4[k] for k in range(NZ)]
        solve4(lambda k: f4[k] + neighbours(old[k], x_face4[k], y_face4[k]), old)
        return carry

    lax.fori_loop(0, COARSE_SWEEPS - 1, relax, 0)

    cells = u4.ref[...].reshape(NZ, rows, 128)
    x = iota((1, rows, 128), 1)
    before = jnp.where(x > 0, shift(cells, 1, 1), 0.0)
    after = jnp.where(x < rows - 1, shift(cells, -1, 1), 0.0)
    spread_rows(cells, before, after, wide, size)
    e_ref[...] = mix(wide[pl.ds(0, 2 * size), :], spread_matrix(iota((128, 128), 1), 0, cols), 3)
    rows, cols = 2 * rows, 2 * cols
    smooth_up(f3, x_face3, y_face3, line3, u3, Field(e_ref, rows), r3, None, None)

    def block(dx, dy):
        inside = ((ix + dx >= 0) & (ix + dx < gx)).astype(F32)
        jx, jy = jnp.clip(ix + dx, 0, gx - 1), jnp.clip(iy + dy, 0, gy - 1)
        return gathered((jx, other if dx else own), jy, pl.ds(0, NZ)) * inside

    for first, dx in ((0, 0), (4, 1), (12, -1)):
        window2(block(dx, 0), shift(block(dx, 1), 32, 1), shift(block(dx, -1), 96, 1), f2, first, iy, gy)
    for x in range(8, 12):
        f2[pl.ds(x, NZ, stride=TX), :] = jnp.zeros((NZ, 128), F32)
    f2, u2, kept2 = (Field(ref, TX) for ref in (f2, u2, kept2))
    x_face2, y_face2, inv2, z_face2 = stack_fields(k2, TX, 3)
    line2 = Line(inv2, z_face2)
    zero = jnp.zeros((TX, 128), F32)
    ends = sweep_in(lambda k: f2[k], line2, kept2, zero, None)

    def emit2(k, value):
        u2[k] = OMEGA * value

    sweep_out(ends, kept2, line2, emit2, None)

    cells = pltpu.roll(u3.ref[...].reshape(NZ, rows, 128), (rows - 2 * ix) % rows, 1)
    x = iota((1, rows, 128), 1)
    place = 2 * ix + jnp.where(x < rows // 2, x, x - rows)
    cells = jnp.where((place >= 0) & (place < rows), cells, 0.0)
    ring = lambda v, first: jnp.where(iota((1, 8, 128), 1) < first, v[:, :8], v[:, rows - 8 :])
    spread_rows(ring(cells, 4), ring(shift(cells, 1, 1), 4), ring(shift(cells, -1, 1), 4), wide, NZ * 8)
    lane = iota((128, 128), 1)
    fine_y = jnp.where(lane < 80, lane, lane - 128) + 32 * iy
    e_ref[...] = mix(wide[pl.ds(0, NZ * TX), :], spread_matrix(fine_y, 0, cols), 3)
    mask2 = window_mask(TX, 128, 4, 32, 4, ix, iy, 4 * gx, 32 * gy)
    smooth_up(f2, x_face2, y_face2, line2, u2, Field(e_ref, TX), kept2, mask2, None)

    cells = u2.ref[...].reshape(NZ, TX, 128)
    ring = lambda v: jnp.where(iota((1, 8, 128), 1) < 6, v[:, :8], v[:, 8:])
    spread_rows(ring(cells), ring(shift(cells, 1, 1)), ring(shift(cells, -1, 1)), wide, NZ * 8)
    fine_y = jnp.where(lane < 96, lane, lane - 128)
    e_ref[...] = mix(wide[pl.ds(0, NZ * TX), :], spread_matrix(fine_y, 0, 0, circular=True), 3)
    fetched[0].wait()
    x_face1, y_face1, inv1, f1, u1, z_face1 = stack_fields(held1, TX, 5)
    line1 = Line(inv1, z_face1)
    mask1 = window_mask(TX, 128, 8, 64, 4, ix, iy, 8 * gx, 64 * gy)
    smooth_up(f1, x_face1, y_face1, line1, u1, Field(e_ref, TX), kept2, mask1, None)

    cells = held1[pl.ds(u1.start, NZ * TX), :].reshape(NZ, TX, 128)
    spread_rows(cells, shift(cells, 1, 1), shift(cells, -1, 1), wide, NZ * TX)
    rows = 2 * TX
    weights = spread_matrix(iota((128, 256), 1), 0, 0, circular=True)
    e0 = Field(e0_ref, rows, 2)
    for k in range(0, NZ, 8):
        cells = mix(wide[pl.ds(k * rows, 8 * rows), :], weights, 3)
        for t in range(2):
            e0_ref[pl.ds(e0.base(t, k), 8 * rows), :] = cells[:, 128 * t : 128 * (t + 1)]
    fetched[1].wait()
    x_face0, y_face0, inv0, f0, u0, z_face0 = stack_fields(held0, rows, 5, 2)
    mask0 = window_mask(rows, 256, TX, TY, HALO, ix, iy, TX * gx, TY * gy)
    smooth_up(f0, x_face0, y_face0, Line(inv0, z_face0), u0, e0, Field(kept0, rows, 2), mask0, 2)

    kappa = Field(stack, TX, start=NZ * TX)

    def residual(k, carry):
        below, flux_z = carry
        column = u0.part(0, k)
        here = column[:TX]
        flux_x = (x_face0.part(0, k) * (column - shift(column, 1, 0)))[: TX + 8]
        row = u0[k][:TX]
        flux_y = y_face0[k][:TX] * (row - shift(row, 1, 1))
        side = (flux_x - shift(flux_x, -1, 0))[:TX] + (flux_y - shift(flux_y, -1, 1))[:, :TY]
        above = u0.part(0, k + 1)[:TX] if k is not NZ - 1 else jnp.zeros((TX, TY), F32)
        flux_up = z_face0.part(0, k + 1)[:TX] * (above - here)
        solution_out[span(k * TX, TX), :] = here
        out = f0.part(0, k)[:TX] - kappa[k] * here - side - flux_z + flux_up
        residual_out[span(k * TX, TX), :] = out
        return here, flux_up

    start = z_face0.part(0, 0)[:TX] * u0.part(0, 0)[:TX]
    carry = loop(NZ - 1, residual, (start, start), 4)
    residual(NZ - 1, carry)


SAVED_ROWS = 72 * 1024
MEBIBYTES = {"pack": 56}
COSTS = {
    "pack": 3 * 10**9, "share": 10**9, "down": 10**10,
    "window_coeffs": 4 * 10**9, "global_coeffs": 4 * 10**9, "up": 12 * 10**9,
}


def call(kernel, name, outs, ins, scratch=(), in_specs=None, out_specs=None, aliases=None):
    shapes = [jax.ShapeDtypeStruct(s, F32) for s in outs]
    return pl.pallas_call(
        kernel,
        name=name,
        out_shape=shapes,
        in_specs=in_specs or [VMEM] * len(ins),
        out_specs=out_specs or [VMEM] * len(outs),
        scratch_shapes=list(scratch),
        input_output_aliases=aliases or {},
        compiler_params=pltpu.CompilerParams(vmem_limit_bytes=MEBIBYTES.get(name, 32) * 1024 * 1024),
        cost_estimate=pl.CostEstimate(flops=COSTS[name], bytes_accessed=4 * sum(x.size for x in ins), transcendentals=0),
    )(*ins)


def body(right_side, kappa_sq, cond_x, cond_y, cond_z):
    gx, gy = lax.axis_size("gx"), lax.axis_size("gy")
    tiles = [v.reshape(NZ * TX, TY) for v in (right_side, kappa_sq, cond_x, cond_y, cond_z)]
    slab, strip = (SLAB + 6 * NZ, 128), (STRIP + 24, 128)
    vm = lambda *shape: pltpu.VMEM(shape, F32)
    dma = lambda n: pltpu.SemaphoreType.DMA((n,))
    devices = gx * gy
    near = lambda n: [(i, i ^ 1) for i in range(n)]
    far = lambda n: [(i, (i + 1 ^ 1) - 1) for i in range(1, n - 1)]
    even_x, even_y = lax.axis_index("gx") % 2 == 0, lax.axis_index("gy") % 2 == 0
    x_near, x_far, y_near, y_far, share2, stack = call(
        pack_kernel, "pack", [slab, slab, strip, strip, (6 * NZ, 128), (5 * NZ * TX, TY)], tiles, [dma(5)], [HBM] * 5
    )
    y_near = lax.ppermute(y_near, "gy", near(gy))
    y_far = lax.ppermute(y_far, "gy", far(gy))
    x_near = lax.ppermute(x_near, "gx", near(gx))
    x_far = lax.ppermute(x_far, "gx", far(gx))
    yr, yl = jnp.where(even_y, y_near, y_far), jnp.where(even_y, y_far, y_near)
    copies = call(functools.partial(share_kernel, devices // 2), "share", [(devices // 2 * SHARE, 128)], [share2])[0]
    half = STRIP // 2
    head = jnp.concatenate([yl[:half], yl[STRIP:], yr[:half], yr[STRIP:]])
    tail = jnp.concatenate([yl[half:], yr[half:]])
    c_near = lax.ppermute(jnp.where(even_x, tail, head), "gx", near(gx))
    c_far = lax.ppermute(jnp.where(even_x, head, tail), "gx", far(gx))
    copies, c_near, c_far = lax.optimization_barrier((copies, c_near, c_far))
    corner_r, corner_l = jnp.where(even_x, c_near, c_far), jnp.where(even_x, c_far, c_near)
    cores = [[x * gy + y for x in range(core, gx, 2) for y in range(gy)] for core in range(2)]
    blocks = copies.reshape(devices // 2, SHARE, 128)
    own = lax.all_to_all(blocks, ("gx", "gy"), 0, 0, axis_index_groups=cores).reshape(gx // 2, gy * SHARE, 128)
    level = lambda rows, n: [vm(NZ * rows, 128)] * n
    faces = lambda rows, tiles: vm(tiles * (NZ + 1) * rows, 128)
    rows3, rows4 = 2 * gx, gx
    size, tall = (NZ * TX, 128), ((NZ + 1) * TX, 128)
    k2 = call(
        window_kernel, "window_coeffs", [(NZ * TX * 4 + TX, 128)], [share2, x_near, x_far, yr, yl, corner_r, corner_l], level(TX, 7)
    )[0]
    big, big_z = (2 * NZ * 2 * TX, 128), (2 * (NZ + 1) * 2 * TX, 128)
    total0, total1 = 2 * (NZ * 6 + 1) * 2 * TX, (NZ * 6 + 1) * TX
    sends, saved = call(
        functools.partial(down_kernel, gx * TX, gy * TY),
        "down",
        [(devices // 2 * BLOCK, 128), (max(total0 + total1, SAVED_ROWS), 128)],
        [stack, yr, yl, corner_r, corner_l, x_near, x_far],
        [vm(*big)] * 10 + [vm(*big_z)] + level(TX, 10) + [faces(TX, 1)] + level(8, 10) + [faces(8, 1)] + [dma(12)],
        out_specs=[VMEM, ANY],
    )
    sends, own = lax.optimization_barrier((sends, own))
    other = lax.ppermute(own, "gx", near(gx))
    blocks = sends.reshape(devices // 2, BLOCK, 128)
    own_blocks = lax.all_to_all(blocks, ("gx", "gy"), 0, 0, axis_index_groups=cores)
    other_blocks = lax.ppermute(own_blocks, "gx", near(gx))
    whole = call(
        functools.partial(global_kernel, gx, gy),
        "global_coeffs",
        [(5 * NZ * (rows3 + rows4), 128)],
        [own, other],
        level(rows3, 6) + [faces(rows3, 1)] + level(rows3, 1) + level(rows4, 6) + [faces(rows4, 1)] + level(rows4, 1)
        + [vm(gx // 2, 2, gy * SHARE, 128), dma(2)],
        in_specs=[ANY] * 2,
    )[0]
    field, residual = call(
        functools.partial(up_kernel, gx, gy),
        "up",
        [(NZ * TX, TY)] * 2,
        [own_blocks, other_blocks, whole, k2, stack, saved],
        [vm(total0, 128), vm(total1, 128)] + level(TX, 3) + [vm(NZ * 2 * TX, 128), vm(*size), vm(*big), vm(*big)]
        + level(rows3, 3) + level(rows4, 2) + [dma(2)],
        in_specs=[VMEM] * 5 + [ANY],
    )
    return field.reshape(right_side.shape), residual.reshape(right_side.shape)


def solution(mesh):
    spec = P(None, "gx", "gy")
    fits = (mesh.shape["gx"], mesh.shape["gy"]) == (8, 4)
    plan = body if fits else spread_body
    return jax.shard_map(plan, mesh=mesh, in_specs=(spec,) * 5, out_specs=(spec, spec), check_vma=False)
```

```python
import functools

import jax
import jax.numpy as jnp
from jax import lax
from jax.experimental import pallas as pl
from jax.experimental.pallas import tpu as pltpu
from jax.sharding import PartitionSpec as P

LEVELS = 4
COARSE_SWEEPS = 16


OMEGA = 0.8


def with_halo(cells, sides, width):
    for axis, dim in sides:
        count = lax.axis_size(axis)
        ends = count - 1
        head = lax.slice_in_dim(cells, 0, width, axis=dim)
        tail = lax.slice_in_dim(cells, cells.shape[dim] - width, cells.shape[dim], axis=dim)
        cells = jnp.concatenate(
            [
                lax.ppermute(tail, axis, [(i, (i + 1) % count) for i in range(ends)]),
                cells,
                lax.ppermute(head, axis, [((i + 1) % count, i) for i in range(ends)]),
            ],
            axis=dim,
        )
    return cells


def apply_op(field, padded, coeffs):
    kappa, x_up, x_low, y_up, y_low, z_up, z_low = coeffs
    zpad = jnp.pad(field, ((1, 1), (0, 0), (0, 0)))
    out = (
        kappa * field
        + x_up * (field - padded[:, 2:, 1:-1])
        + x_low * (field - padded[:, :-2, 1:-1])
    )
    out = out + y_up * (field - padded[:, 1:-1, 2:]) + y_low * (field - padded[:, 1:-1, :-2])
    return out + z_up * (field - zpad[2:]) + z_low * (field - zpad[:-2])


def face_pad(field):
    return with_halo(field, (("gx", 1), ("gy", 2)), 1)


def line_factors(coeffs):
    kappa, x_up, x_low, y_up, y_low, z_up, z_low = coeffs
    diag = kappa + x_up + x_low + y_up + y_low + z_up + z_low
    upper_src = z_up.at[-1].set(jnp.zeros_like(z_up[-1]))

    def factor_step(upper_prev, planes):
        diag_k, low_k, up_k = planes
        inv = 1.0 / (diag_k + low_k * upper_prev)
        upper = -up_k * inv
        return (upper, (inv, upper))

    start = jnp.zeros_like(diag[0])
    unused, stacked = lax.scan(factor_step, start, (diag, z_low, upper_src), unroll=True)
    return stacked


def line_solve(rhs, factors, z_low):
    inverses, uppers = factors

    def forward_step(prev, planes):
        rhs_k, low_k, inv_k = planes
        value = (rhs_k + low_k * prev) * inv_k
        return (value, value)

    start = jnp.zeros_like(rhs[0])
    unused, forward = lax.scan(forward_step, start, (rhs, z_low, inverses), unroll=True)

    def back_step(after, planes):
        fwd_k, up_k = planes
        value = fwd_k - up_k * after
        return (value, value)

    unused, result = lax.scan(back_step, start, (forward, uppers), reverse=True, unroll=True)
    return result


def mean_four(field):
    depth, rows, cols = field.shape
    return field.reshape(depth, rows // 2, 2, cols // 2, 2).mean(axis=(2, 4))


def coarsen(coeffs):
    kappa, x_up, x_low, y_up, y_low, z_up, z_low = coeffs
    depth, rows, cols = kappa.shape
    shape = (depth, rows // 2, 2, cols // 2, 2)
    xu_c = x_up.reshape(shape)[:, :, 1].mean(axis=-1) * 0.25
    xl_c = x_low.reshape(shape)[:, :, 0].mean(axis=-1) * 0.25
    yu_c = y_up.reshape(shape)[:, :, :, :, 1].mean(axis=2) * 0.25
    yl_c = y_low.reshape(shape)[:, :, :, :, 0].mean(axis=2) * 0.25
    return (mean_four(kappa), xu_c, xl_c, yu_c, yl_c, mean_four(z_up), mean_four(z_low))


def prolong(padded):
    depth = padded.shape[0]
    rows = padded.shape[1] - 2
    cols = padded.shape[2] - 2
    centre = padded[:, 1:-1, :]
    even = 0.75 * centre + 0.25 * padded[:, :-2, :]
    odd = 0.75 * centre + 0.25 * padded[:, 2:, :]
    spread = jnp.stack([even, odd], axis=2).reshape(depth, 2 * rows, cols + 2)
    centre = spread[:, :, 1:-1]
    even = 0.75 * centre + 0.25 * spread[:, :, :-2]
    odd = 0.75 * centre + 0.25 * spread[:, :, 2:]
    return jnp.stack([even, odd], axis=3).reshape(depth, 2 * rows, 2 * cols)


def coarse_solve(rhs, coeffs):
    factors = line_factors(coeffs)
    field = OMEGA * line_solve(rhs, factors, coeffs[6])

    def spread_sweep(sweep, current):
        padded = with_halo(current, (("gx", 1), ("gy", 2)), 1)
        defect = rhs - apply_op(current, padded, coeffs)
        return current + OMEGA * line_solve(defect, factors, coeffs[6])

    field = lax.fori_loop(0, COARSE_SWEEPS - 1, spread_sweep, field)
    return field


def cycle(rhs, coeffs, level):
    if level == LEVELS:
        return coarse_solve(rhs, coeffs)
    factors = line_factors(coeffs)
    field = OMEGA * line_solve(rhs, factors, coeffs[6])
    padded = face_pad(field)
    defect = rhs - apply_op(field, padded, coeffs)
    correction = cycle(mean_four(defect), coarsen(coeffs), level + 1)
    rimmed = with_halo(correction, (("gx", 1), ("gy", 2)), 1)
    field = field + prolong(rimmed)
    padded = face_pad(field)
    defect = rhs - apply_op(field, padded, coeffs)
    return field + OMEGA * line_solve(defect, factors, coeffs[6])


def spread_body(right_side, kappa_sq, cond_x, cond_y, cond_z):
    padded_x = with_halo(cond_x, (("gx", 1),), 1)
    padded_y = with_halo(cond_y, (("gy", 2),), 1)
    padded_z = jnp.pad(cond_z, ((1, 1), (0, 0), (0, 0)))
    x_up = 0.5 * (cond_x + padded_x[:, 2:, :])
    x_low = 0.5 * (cond_x + padded_x[:, :-2, :])
    y_up = 0.5 * (cond_y + padded_y[:, :, 2:])
    y_low = 0.5 * (cond_y + padded_y[:, :, :-2])
    z_up = 0.5 * (cond_z + padded_z[2:])
    z_low = 0.5 * (cond_z + padded_z[:-2])
    coeffs = (kappa_sq, x_up, x_low, y_up, y_low, z_up, z_low)
    solution_field = cycle(right_side, coeffs, 0)
    residual = right_side - apply_op(solution_field, face_pad(solution_field), coeffs)
    return (solution_field, residual)


F32 = jnp.float32
BF16 = jnp.bfloat16
NZ = 32
HALF = NZ // 2
TX, TY = 16, 128
HALO = 8
SLAB = 5 * NZ * HALO
STRIP = 160
CORNER = 104
SHARE = 40
BLOCK = NZ + 8
VMEM = pl.BlockSpec(memory_space=pltpu.VMEM)
ANY = pl.BlockSpec(memory_space=pl.ANY)
HBM = pl.BlockSpec(memory_space=pltpu.HBM)


def iota(shape, dim):
    return lax.broadcasted_iota(jnp.int32, shape, dim)


def shift(x, by, axis):
    by = by % x.shape[axis]
    return pltpu.roll(x, by, axis) if by else x


def mix(x, weights, parts=2):
    pieces = []
    for n in range(parts):
        piece = x.astype(BF16)
        pieces.append(piece)
        if n < parts - 1:
            x = x - piece.astype(F32)
    out = jnp.dot(jnp.concatenate(pieces, axis=0), weights, preferred_element_type=F32)
    rows = x.shape[0]
    return sum(out[n * rows : (n + 1) * rows] for n in reversed(range(parts)))


def matrix(mask, weight=1.0):
    return jnp.where(mask, weight, 0.0).astype(BF16)


def span(start, size):
    if not isinstance(start, int):
        start = pl.multiple_of(start, 8)
    return pl.ds(start, size)


class Field:
    def __init__(self, ref, rows, tiles=1, planes=NZ, start=0):
        self.ref, self.rows, self.tiles, self.planes, self.start = ref, rows, tiles, planes, start

    def base(self, tile, k):
        return self.start + tile * self.planes * self.rows + k * self.rows

    def part(self, tile, k):
        return self.ref[span(self.base(tile, k), self.rows), :]

    def __getitem__(self, k):
        parts = [self.part(t, k) for t in range(self.tiles)]
        return parts[0] if self.tiles == 1 else jnp.concatenate(parts, axis=1)

    def __setitem__(self, k, value):
        for t in range(self.tiles):
            self.put(t, k, value[:, 128 * t : 128 * (t + 1)])

    def put(self, tile, k, value):
        self.ref[span(self.base(tile, k), self.rows), :] = value

    def every_second(self, at, count, odd):
        parts = []
        for t in range(self.tiles):
            first = self.base(t, 0) + 2 * at + odd
            parts.append(self.ref[pl.ds(first, count, stride=2), :])
        return parts[0] if self.tiles == 1 else jnp.concatenate(parts, axis=1)

    def row(self, row):
        return self.ref[pl.ds(self.start + row, self.planes, stride=self.rows), :]


def stack_fields(ref, rows, count, tiles=1, z_face=True, start=0):
    size = tiles * NZ * rows
    out = [Field(ref, rows, tiles, NZ, start + n * size) for n in range(count)]
    return out + [Field(ref, rows, tiles, NZ + 1, start + count * size)] if z_face else out


def loop(count, step, carry, unroll=None):
    if unroll is None or unroll >= count:
        for i in range(count):
            carry = step(i, carry)
        return carry
    return lax.fori_loop(0, count, step, carry, unroll=unroll)


def neighbours(field, x_face, y_face):
    out = x_face * shift(field, 1, 0) + shift(x_face * field, -1, 0)
    return out + (y_face * shift(field, 1, 1) + shift(y_face * field, -1, 1))


class Line:
    def __init__(self, inv, z_face):
        self.inv, self.z_face = inv, z_face

    def inward(self, k, upper):
        return self.z_face[k + 1 if upper else k] * self.inv[k]

    def outward(self, k, upper):
        return self.z_face[k if upper else k + 1] * self.inv[k]


class StoredLine:
    def __init__(self, inv, g, c):
        self.inv, self.g, self.c = inv, g, c

    def inward(self, k, upper):
        return self.g[k]

    def outward(self, k, upper):
        return self.c[k]


def sweep_in(rhs, line, keep, start, unroll):
    def step(i, carry):
        low, high = carry
        k, m = i, NZ - 1 - i
        low = rhs(k) * line.inv[k] + line.inward(k, False) * low
        high = rhs(m) * line.inv[m] + line.inward(m, True) * high
        keep[k] = low
        keep[m] = high
        return low, high

    return loop(HALF, step, (start, start), unroll)


def sweep_out(ends, kept, line, emit, unroll):
    low, high = ends
    a, b = line.outward(HALF - 1, False), line.outward(HALF, True)
    low = (low + a * high) * (1.0 / (1.0 - a * b))
    high = high + b * low

    def step(i, carry):
        low, high = carry
        k, m = HALF - 1 - i, HALF + i
        emit(k, low)
        emit(m, high)
        low = kept[k - 1] + line.outward(k - 1, False) * low
        high = kept[m + 1] + line.outward(m + 1, True) * high
        return low, high

    low, high = loop(HALF - 1, step, (low, high), unroll)
    emit(0, low)
    emit(NZ - 1, high)


def factor(diag, z_face, tiles, inv_out, unroll, rhs=None, keep=None, g_out=None, c_out=None):
    ends = []
    for t in range(tiles):
        zero = diag.part(t, 0) * 0.0

        def one(k, upper, before, last, prev):
            below, above = z_face.part(t, k), z_face.part(t, k + 1)
            inner, outer = (above, below) if upper else (below, above)
            minor = (diag.part(t, k) + below + above) * last - (inner * inner) * before
            inv = last * (1.0 / minor)
            inv_out.put(t, k, inv)
            if g_out is not None:
                g_out.put(t, k, inner * inv)
                c_out.put(t, k, outer * inv)
            if rhs is not None:
                prev = rhs.part(t, k) * inv + (inner * inv) * prev
                keep.put(t, k, prev)
            return last, minor, prev

        def step(i, carry):
            low, high = carry
            return one(i, False, *low), one(NZ - 1 - i, True, *high)

        start = (zero, zero + 1.0, zero)
        low, high = loop(HALF, step, (start, start), unroll)
        ends.append((low[2], high[2]))
    join = lambda n: ends[0][n] if tiles == 1 else jnp.concatenate([e[n] for e in ends], axis=1)
    return join(0), join(1)


def z_faces(cz, out, tiles=1):
    for t in range(tiles):
        before = None
        for k in range(NZ + 1):
            here = cz.part(t, k) if k < NZ else None
            both = here if before is None else before if here is None else here + before
            out.put(t, k, 0.5 * both)
            before = here


def base_diag(kappa, x_face, y_face):
    return kappa + (x_face + shift(x_face, -1, 0)) + (y_face + shift(y_face, -1, 1))


def window_mask(rows, lanes, tile_x, tile_y, halo, ix, iy, nx, ny):
    x, y = iota((rows, lanes), 0), iota((rows, lanes), 1)
    x = jnp.where(x < (rows + tile_x) // 2, x, x - rows)
    y = jnp.where(y < (lanes + tile_y) // 2, y, y - lanes)
    valid = (y >= -halo) & (y < tile_y + halo) & (x >= -halo) & (x < tile_x + halo)
    x, y = x + ix * tile_x, y + iy * tile_y
    return (valid & (x >= 0) & (x < nx) & (y >= 0) & (y < ny)).astype(F32)


def smooth_down(f, x_face, y_face, line, ends, kept, u, r, unroll):
    def emit(k, value):
        field = OMEGA * value
        u[k] = field
        r[k] = (1.0 - OMEGA) * f[k] + neighbours(field, x_face[k], y_face[k])

    sweep_out(ends, kept, line, emit, unroll)


def smooth_up(f, x_face, y_face, line, u, e, kept, mask, unroll):
    masked = (lambda v: v) if mask is None else (lambda v: v * mask)

    def rhs(k):
        field = masked(u[k] + e[k])
        u[k] = field
        return masked(f[k] + neighbours(field, x_face[k], y_face[k]))

    def emit(k, value):
        u[k] = (1.0 - OMEGA) * u[k] + OMEGA * value

    zero = jnp.zeros((u.rows, 128 * u.tiles), F32)
    ends = sweep_in(rhs, line, kept, zero, unroll)
    sweep_out(ends, kept, line, emit, unroll)


def spread_rows(cells, before, after, dest, size):
    dest[pl.ds(0, size, stride=2), :] = (0.75 * cells + 0.25 * before).reshape(size, 128)
    dest[pl.ds(1, size, stride=2), :] = (0.75 * cells + 0.25 * after).reshape(size, 128)


def spread_matrix(fine, base, coarse_count, circular=False):
    j = iota((128, fine.shape[1]), 0) + base
    parent = (fine + 2048) // 2 - 1024
    partner = parent + 2 * ((fine + 2048) % 2) - 1
    if circular:
        j, parent, partner = j % 128, parent % 128, partner % 128
    weights = jnp.where(j == parent, 0.75, jnp.where(j == partner, 0.25, 0.0))
    if not circular:
        inside = (j >= 0) & (j < coarse_count) & (fine >= 0) & (fine < 2 * coarse_count)
        weights = jnp.where(inside, weights, 0.0)
    return weights.astype(BF16)


def lane_group(rows, width):
    return iota((rows, 128), 1) // width


def fold_planes(cells, turn):
    group = lane_group(8, 32)
    out = cells[:8]
    for n in range(1, 4):
        out = jnp.where(group == n, cells[8 * n : 8 * n + 8], out)
    return pltpu.roll(out, turn, 1)


def share_kernel(devices, share2, stack, copies):
    iy = lax.axis_index("gy")
    y, lane = iota((128, 128), 0), iota((128, 128), 1)
    x_in, y_in = y // 32, y % 32
    x_out, y_out = lane % 32 // 16, lane % 16
    pair_y, pair_x = y_in // 2 == y_out, x_in // 2 == x_out
    a, b, c, d, kappa, cz = (share2[pl.ds(t * NZ, NZ), :] for t in range(6))
    eighth = lambda mask: matrix(mask, 0.125)
    blocks = [
        mix(a, eighth(pair_y & (x_in == 2 * x_out))) + mix(b, eighth(pair_y & (x_in == 1) & (x_out == 1))),
        mix(b, eighth(pair_y & (x_in == 3) & (x_out == 0)))
        + mix(d, eighth((x_out == 1) & (y_in == 31) & (x_in // 2 == y_out))),
        mix(c, eighth(pair_x & (y_in == 2 * y_out))) + mix(d, eighth(pair_x & (y_in == 2 * y_out - 1))),
        mix(kappa, matrix(pair_x & pair_y, 0.25)),
        mix(cz, matrix(pair_x & pair_y, 0.25)),
    ]
    for t, cells in enumerate(blocks):
        cells = fold_planes(cells, 16 * iy)
        for n in range(devices):
            copies[pl.ds(n * SHARE + 8 * t, 8), :] = cells


def fetch_all(sources, dests, sems, first=0):
    copies = [pltpu.make_async_copy(a, b, sems.at[first + n]) for n, (a, b) in enumerate(zip(sources, dests))]
    for copy in copies:
        copy.start()
    return copies


def pack_kernel(f_in, kappa_in, cx_in, cy_in, cz_in, x_near, x_far, y_near, y_far, share2, stack, sems):
    even_x, even_y = lax.axis_index("gx") % 2 == 0, lax.axis_index("gy") % 2 == 0
    tiles = [stack.at[pl.ds(a * NZ * TX, NZ * TX), :] for a in range(5)]
    for copy in fetch_all((f_in, kappa_in, cx_in, cy_in, cz_in), tiles, sems):
        copy.wait()
    f, kappa, cx, cy, cz = tiles
    for a, ref in enumerate(tiles):
        cells = ref[...].reshape(NZ, TX, TY)
        at = pl.ds(a * NZ * HALO, NZ * HALO)
        head = cells[:, :HALO].reshape(NZ * HALO, TY)
        tail = cells[:, TX - HALO :].reshape(NZ * HALO, TY)
        x_near[at, :] = jnp.where(even_x, tail, head)
        x_far[at, :] = jnp.where(even_x, head, tail)
    y, lane = iota((128, 128), 0), iota((128, 128), 1)
    fourth = y // 4 == lane % 32
    rows = lambda ref: [Field(ref, TX).row(r) for r in range(TX)]
    cx_rows, cy_rows, kappa_rows, cz_rows = rows(cx), rows(cy), rows(kappa), rows(cz)
    totals = lambda v: [(v[4 * i] + v[4 * i + 1]) + (v[4 * i + 2] + v[4 * i + 3]) for i in range(4)]
    stack = [cx_rows[4 * i] for i in range(4)] + [cx_rows[4 * i + 3] for i in range(4)]
    stack = mix(jnp.concatenate(stack + totals(kappa_rows) + totals(cz_rows), axis=0), matrix(fourth))
    ends = [matrix(fourth & (y % 4 == 0)), matrix(fourth & (y % 4 == 3))]
    sides = mix(jnp.concatenate(totals(cy_rows), axis=0), jnp.concatenate(ends, axis=1))
    group = lane_group(NZ, 32)

    def merge(cells, scale):
        out = cells[:NZ]
        for xi in range(1, 4):
            out = jnp.where(group == xi, cells[NZ * xi : NZ * (xi + 1)], out)
        return out * scale

    kinds = [merge(stack[:128], 1 / 128), merge(stack[128:256], 1 / 128)]
    kinds += [merge(sides[:, :128], 1 / 128), merge(sides[:, 128:], 1 / 128)]
    kinds += [merge(stack[256:384], 1 / 16), merge(stack[384:], 1 / 16)]
    head = [jnp.zeros((8, 128), F32)] * 3
    tail = [jnp.zeros((8, 128), F32)] * 3
    slot = iota((8, 128), 1) % 32 // 4
    for t, cells in enumerate(kinds):
        for dest, first in ((share2, 0), (x_near, SLAB), (x_far, SLAB)):
            dest[pl.ds(first + t * NZ, NZ), :] = cells
        for zv in range(4):
            n = 4 * t + zv
            piece = cells[8 * zv : 8 * zv + 8]
            head[n // 8] = jnp.where(slot == n % 8, shift(piece, 4 * (n % 8), 1), head[n // 8])
            tail[n // 8] = jnp.where(slot == n % 8, shift(piece, 4 * (n % 8) + 4, 1), tail[n // 8])
    for n in range(3):
        y_near[pl.ds(STRIP + 8 * n, 8), :] = jnp.where(even_y, tail[n], head[n])
        y_far[pl.ds(STRIP + 8 * n, 8), :] = jnp.where(even_y, head[n], tail[n])

    group = lane_group(8, 8)
    for a, ref in enumerate((f, kappa, cx, cy, cz)):
        for half in range(2):
            for zo in range(2):
                head = jnp.zeros((8, 128), F32)
                tail = jnp.zeros((8, 128), F32)
                for zi in range(16):
                    cells = ref[pl.ds((zo * 16 + zi) * TX + 8 * half, 8), :]
                    cells = shift(cells, 8 * zi, 1)
                    head = jnp.where(group == zi, cells, head)
                    tail = jnp.where(group == (zi - 1) % 16, cells, tail)
                at = pl.ds(((half * 5 + a) * 2 + zo) * 8, 8)
                y_near[at, :] = jnp.where(even_y, tail, head)
                y_far[at, :] = jnp.where(even_y, head, tail)


def window2(tile, after, before, dest, first, iy, gy):
    lane = iota((NZ, 128), 1)
    first_after, first_before = jnp.where(iy < gy - 1, 36, 0), jnp.where(iy > 0, 124, 128)
    for xi in range(4):
        turned = (lane - 32 * xi + 128) % 128
        cells = jnp.where(turned < 32, tile, jnp.where(turned < first_after, after, jnp.where(turned >= first_before, before, 0.0)))
        dest[pl.ds(first + xi, NZ, stride=TX), :] = shift(cells, -32 * xi, 1)


def window_kernel(share2, x_near, x_far, yr, yl, cr, cl, out, a, b, c, d, kappa, cz, diag):
    ix, iy = lax.axis_index("gx"), lax.axis_index("gy")
    gy = lax.axis_size("gy")
    nx, ny = lax.axis_size("gx") * 4, gy * 32
    refs = (a, b, c, d, kappa, cz)

    def unpack(ref, first, t, turn):
        pieces = []
        for zv in range(4):
            n = 4 * t + zv
            pieces.append(shift(ref[span(first + 8 * (n // 8), 8), :], turn - 4 * (n % 8), 1))
        return jnp.concatenate(pieces, axis=0)

    near, far = STRIP // 2, CORNER + STRIP // 2
    even_x = ix % 2 == 0
    for t, dest in enumerate(refs):
        beside = x_near[pl.ds(SLAB + t * NZ, NZ), :], x_far[pl.ds(SLAB + t * NZ, NZ), :]
        for first, cells, right, left, r_at, l_at in (
            (0, share2[pl.ds(t * NZ, NZ), :], yr, yl, STRIP, STRIP),
            (4, jnp.where(even_x, *beside), cr, cr, far, near),
            (12, jnp.where(even_x, *beside[::-1]), cl, cl, far, near),
        ):
            window2(cells, unpack(right, r_at, t, 32), unpack(left, l_at, t, 92), dest, first, iy, gy)
        for x in range(8, 12):
            dest[pl.ds(x, NZ, stride=TX), :] = jnp.zeros((NZ, 128), F32)
    mask = window_mask(TX, 128, 4, 32, 4, ix, iy, nx, ny)
    a, b, c, d, kappa, cz, diag = (Field(ref, TX) for ref in (*refs, diag))
    x_face, y_face, inv, z_face = stack_fields(out, TX, 3)
    for k in range(NZ):
        x_k = a[k] + shift(b[k], 1, 0)
        y_k = c[k] + shift(d[k], 1, 1)
        x_face[k] = x_k
        y_face[k] = y_k
        diag[k] = base_diag(jnp.where(mask > 0, kappa[k], 1.0), x_k, y_k)
    z_faces(cz, z_face)
    factor(diag, z_face, 1, inv, None)


def assemble3(block, dest, gx, gy, rows):
    group = lane_group(8, 16)
    for ix in range(gx):
        blocks = [block(ix, iy) for iy in range(gy)]
        for zo in range(4):
            for xi in range(2):
                q = 2 * zo + xi
                cells = blocks[0]
                for iy in range(1, gy):
                    cells = jnp.where(group == (iy + q) % 8, blocks[iy], cells)
                dest[pl.ds(8 * zo * rows + 2 * ix + xi, 8, stride=rows), :] = shift(cells, -16 * q, 1)


def global_kernel(gx, gy, own, other, *refs):
    out, raw3, raw4, shares, sems = refs[0], refs[1:9], refs[9:17], refs[17], refs[18]
    outs3 = stack_fields(out, 2 * gx, 5, z_face=False)
    outs4 = stack_fields(out, gx, 5, z_face=False, start=5 * NZ * 2 * gx)
    core = lax.axis_index("gx") % 2
    copies = [
        pltpu.make_async_copy(own, shares.at[:, core], sems.at[0]),
        pltpu.make_async_copy(other, shares.at[:, 1 - core], sems.at[1]),
    ]
    for copy in copies:
        copy.start()
    for copy in copies:
        copy.wait()
    rows, cols = 2 * gx, 16 * gy
    for t, n in enumerate((0, 1, 2, 4, 5)):
        block = lambda jx, jy: shares[jx // 2, jx % 2, pl.ds(jy * SHARE + 8 * t, 8), :]
        assemble3(block, raw3[n], gx, gy, rows)
    xl, xu, yl, yu = (Field(ref, rows) for ref in raw3[:4])
    x, y = iota((rows, 128), 0), iota((rows, 128), 1)
    odd_row, inside = x % 2 == 1, y < cols
    for k in range(NZ):
        half = jnp.where(inside, xu[k], 0.0)
        below = jnp.where(odd_row | (x < 2), 0.0, shift(half, 2, 0))
        x_k = jnp.where(inside, xl[k] + below, 0.0)
        xl[k] = x_k
        xu[k] = jnp.where(x == rows - 1, shift(half, 1, 0), shift(x_k, -1, 0))
        next_row = shift(half, -1, 0)
        below = jnp.where(odd_row, shift(half, 15, 1), shift(next_row, 16, 1))
        y_k = jnp.where(inside, yl[k] + jnp.where((y % 16 == 0) & (y > 0), below, 0.0), 0.0)
        yl[k] = y_k
        above = jnp.where(odd_row, shift(half, 14, 1), shift(next_row, 15, 1))
        yu[k] = jnp.where(y == cols - 1, above, jnp.where(inside, shift(y_k, -1, 1), 0.0))
    yy, jj = iota((128, 128), 0), iota((128, 128), 1)
    keep = yy // 2 == jj
    pair, even, odd = matrix(keep), matrix(keep & (yy % 2 == 0)), matrix(keep & (yy % 2 == 1))
    size = NZ * rows // 2
    lows = [Field(ref, rows) for ref in raw3]
    first = lambda n: lows[n].every_second(0, size, 0)
    second = lambda n: lows[n].every_second(0, size, 1)
    raw4[0][...] = 0.125 * mix(first(0), pair)
    raw4[1][...] = 0.125 * mix(second(1), pair)
    raw4[2][...] = 0.125 * mix(first(2) + second(2), even)
    raw4[3][...] = 0.125 * mix(first(3) + second(3), odd)
    raw4[4][...] = 0.25 * mix(first(4) + second(4), pair)
    raw4[5][...] = 0.25 * mix(first(5) + second(5), pair)
    for raw, outs in ((raw3, outs3), (raw4, outs4)):
        x, y = iota((rows, 128), 0), iota((rows, 128), 1)
        xl, xu, yl, yu, kappa, cz = (Field(ref, rows) for ref in raw[:6])
        z_face, diag = Field(raw[6], rows, 1, NZ + 1), Field(raw[7], rows)
        x_face, y_face, inv, g, c = outs
        inside_x, inside_y = (x > 0).astype(F32), ((y > 0) & (y < cols)).astype(F32)
        for k in range(NZ):
            xl_k, yl_k = xl[k], yl[k]
            diag[k] = jnp.where(y < cols, kappa[k], 1.0) + (xl_k + xu[k]) + (yl_k + yu[k])
            x_face[k] = xl_k * inside_x
            y_face[k] = yl_k * inside_y
        z_faces(cz, z_face)
        factor(diag, z_face, 1, inv, None, g_out=g, c_out=c)
        rows, cols = rows // 2, cols // 2


def down_kernel(nx, ny, *refs):
    stack, yr, yl, corner_r, corner_l, x_near, x_far = refs[:7]
    sends, saved = refs[7:9]
    scratch = list(refs[9:-1])
    sems = refs[-1]
    take = lambda n: [scratch.pop(0) for _ in range(n)]
    ix, iy = lax.axis_index("gx"), lax.axis_index("gy")
    gx, gy = lax.axis_size("gx"), lax.axis_size("gy")
    f, kappa, cx, cy, cz = (stack.at[pl.ds(a * NZ * TX, NZ * TX), :] for a in range(5))
    even_x = ix % 2 == 0
    rows, tiles = 2 * TX, 2
    whole = take(11)
    names = [Field(ref, rows, tiles) for ref in whole[:10]]
    x_face, y_face, inv, u, f0, kappa0, cz0, diag, kept, r = names
    z_face = Field(whole[10], rows, tiles, NZ + 1)
    group = lane_group(8, 8)

    def window(a, tile, z, after, before, turn):
        zo = z // 16
        slab = span(a * NZ * HALO + z * HALO, HALO)
        near, far = x_near[slab, :], x_far[slab, :]
        sides = [jnp.where(even_x, near, far), jnp.where(even_x, far, near)]
        main = jnp.concatenate([tile[span(z * TX, TX), :], *sides], axis=0)
        at = lambda first: span(first + (a * 2 + zo) * 8, 8)
        half = STRIP // 2
        sides = []
        for right, left in (
            (yr[at(0), :], yl[at(0), :]),
            (yr[at(half), :], yl[at(half), :]),
            (corner_r[at(CORNER), :], corner_r[at(0), :]),
            (corner_l[at(CORNER), :], corner_l[at(0), :]),
        ):
            cells = jnp.where(after, right, jnp.where(before, left, 0.0))
            sides.append(pltpu.roll(cells, turn, 1))
        return jnp.concatenate([main, jnp.concatenate(sides, axis=0)], axis=1)

    mask0 = window_mask(rows, 256, TX, TY, HALO, ix, iy, nx, ny)

    def prepare(z, cz_prev):
        zi = z % 16
        after, before = group == zi, group == (zi + 15) % 16
        turn = (128 - 8 * zi) % 128
        f_k, kappa_k, cx_k, cy_k, cz_k = (
            window(a, tile, z, after, before, turn) for a, tile in enumerate((f, kappa, cx, cy, cz))
        )
        f0[z] = f_k
        kappa0[z] = kappa_k
        cz0[z] = cz_k
        z_face[z] = 0.5 * (cz_k + cz_prev)
        x_k, y_k = 0.5 * (cx_k + shift(cx_k, 1, 0)), 0.5 * (cy_k + shift(cy_k, 1, 1))
        x_face[z] = x_k
        y_face[z] = y_k
        diag[z] = base_diag(jnp.where(mask0 > 0, kappa_k, 1.0), x_k, y_k)
        return cz_k

    last = loop(NZ, prepare, jnp.zeros((rows, 256), F32), 2)
    z_face[NZ] = 0.5 * last
    ends = factor(diag, z_face, tiles, inv, 4, f0, kept)
    copies = []

    def save(field):
        at = sum(copy[1] for copy in copies)
        count = field.ref.shape[0]
        copy = pltpu.make_async_copy(field.ref, saved.at[pl.ds(at, count), :], sems.at[len(copies)])
        copy.start()
        copies.append((copy, count))

    for field in (x_face, y_face, inv, f0):
        save(field)
    smooth_down(f0, x_face, y_face, Line(inv, z_face), ends, kept, u, r, 2)
    save(u)
    save(z_face)

    fine = (r, kappa0, cz0, x_face, y_face)
    lanes, tile_x, tile_y, halo = 256, TX, TY, HALO
    for level in (1, 2):
        rows, tile_x, tile_y, halo = rows // 2, tile_x // 2, tile_y // 2, halo // 2
        nx, ny = nx // 2, ny // 2
        whole = take(11)
        names = [Field(ref, rows) for ref in whole[:10]]
        x_face, y_face, inv, u, f1, kappa1, cz1, diag, kept, r = names
        z_face = Field(whole[10], rows, 1, NZ + 1)
        mask = window_mask(rows, 128, tile_x, tile_y, halo, ix, iy, nx, ny)
        y, j = iota((lanes, 128), 0), iota((lanes, 128), 1)
        if lanes == 128:
            j = jnp.where(j < 48, j, jnp.where(j >= 80, j - 64, -1))
        pair = matrix(y // 2 == j)
        even = (iota((1, lanes), 1) % 2 == 0).astype(F32)
        part = 128
        for at in range(0, NZ * rows, part):
            here = pl.ds(at, part)
            both = lambda n: fine[n].every_second(at, part, 0) + fine[n].every_second(at, part, 1)
            below = fine[3].every_second(at, part, 0)
            out = mix(jnp.concatenate([both(0), both(1), both(2), below, both(4) * even], axis=0), pair)
            for n, (dest, weight) in enumerate(((f1, 0.25), (kappa1, 0.25), (cz1, 0.25), (x_face, 0.125), (y_face, 0.125))):
                dest.ref[here, :] = weight * out[n * part : (n + 1) * part]
        for k in range(NZ):
            f1[k] = f1[k] * mask
            diag[k] = base_diag(jnp.where(mask > 0, kappa1[k], 1.0), x_face[k], y_face[k])
        z_faces(cz1, z_face)
        ends = factor(diag, z_face, 1, inv, None, f1, kept)
        smooth_down(f1, x_face, y_face, Line(inv, z_face), ends, kept, u, r, None)
        if level == 1:
            for field in (x_face, y_face, inv, f1, u, z_face):
                save(field)
        fine, lanes = (r, kappa1, cz1, x_face, y_face), 128

    group = lane_group(NZ, 32)
    out = f1.row(0)
    for xi in range(1, 4):
        out = jnp.where(group == xi, shift(f1.row(xi), 32 * xi, 1), out)
    for n in range(gx * gy // 2):
        sends[pl.ds(n * BLOCK, NZ), :] = out
    y, lane = iota((128, 128), 0), iota((128, 128), 1)
    total = jnp.zeros((NZ, 128), F32)
    for xi in range(2):
        place = (lane % 32 // 16 == xi) & (y // 2 == lane % 16) & (y < 32)
        total = total + mix(r.row(2 * xi) + r.row(2 * xi + 1), matrix(place, 0.25))
    total = fold_planes(total, 16 * iy)
    for n in range(gx * gy // 2):
        sends[pl.ds(n * BLOCK + NZ, 8), :] = total
    for copy, _ in copies:
        copy.wait()


def up_kernel(gx, gy, *refs):
    own, other, whole, k2, stack, saved, solution_out, residual_out = refs[:8]
    scratch = list(refs[8:-1])
    sems = refs[-1]
    take = lambda n: [scratch.pop(0) for _ in range(n)]
    ix, iy = lax.axis_index("gx"), lax.axis_index("gy")
    held0, held1 = take(2)
    split = held0.shape[0]
    parts = [saved.at[pl.ds(split, held1.shape[0]), :], saved.at[pl.ds(0, split), :]]
    fetched = fetch_all(parts, (held1, held0), sems)
    core = ix % 2

    def gathered(jx, jy, at):
        if isinstance(jx, int):
            same = core == jx % 2
            return jnp.where(same, own[jx // 2 * gy + jy, at, :], other[jx // 2 * gy + jy, at, :])
        return jx[1][jx[0] // 2 * gy + jy, at, :]
    f2, u2, kept2, wide, e_ref, e0_ref, kept0, u3, f3, r3, f4, u4 = take(12)

    rows, cols = 2 * gx, 16 * gy
    assemble3(lambda jx, jy: gathered(jx, jy, pl.ds(NZ, 8)), f3, gx, gy, rows)
    f3, u3, r3 = (Field(ref, rows) for ref in (f3, u3, r3))
    y = iota((rows, 128), 1)
    x_face3, y_face3, inv3, g3, c3 = stack_fields(whole, rows, 5, z_face=False)
    line3 = StoredLine(inv3, g3, c3)
    clean = (y < cols).astype(F32)
    for k in range(NZ):
        f3[k] = f3[k] * clean
    zero = jnp.zeros((rows, 128), F32)
    ends = sweep_in(lambda k: f3[k], line3, r3, zero, None)
    smooth_down(f3, x_face3, y_face3, line3, ends, r3, u3, Field(e_ref, rows), None)
    fine = Field(e_ref, rows)
    rows, cols = rows // 2, cols // 2
    size = NZ * rows
    yy, jj = iota((128, 128), 0), iota((128, 128), 1)
    f4[...] = 0.25 * mix(fine.every_second(0, size, 0) + fine.every_second(0, size, 1), matrix(yy // 2 == jj))
    f4, u4 = Field(f4, rows), Field(u4, rows)
    x_face4, y_face4, inv4, g4, c4 = stack_fields(whole, rows, 5, z_face=False, start=5 * NZ * 2 * rows)
    line4 = StoredLine(inv4, g4, c4)
    zero = jnp.zeros((rows, 128), F32)

    def solve4(rhs, old):
        kept, out = {}, {}
        ends = sweep_in(rhs, line4, kept, zero, None)

        def emit(k, value):
            out[k] = OMEGA * value if old is None else (1.0 - OMEGA) * old[k] + OMEGA * value

        sweep_out(ends, kept, line4, emit, None)
        for k in range(NZ):
            u4[k] = out[k]

    solve4(lambda k: f4[k], None)

    def relax(sweep, carry):
        old = [u4[k] for k in range(NZ)]
        solve4(lambda k: f4[k] + neighbours(old[k], x_face4[k], y_face4[k]), old)
        return carry

    lax.fori_loop(0, COARSE_SWEEPS - 1, relax, 0)

    cells = u4.ref[...].reshape(NZ, rows, 128)
    x = iota((1, rows, 128), 1)
    before = jnp.where(x > 0, shift(cells, 1, 1), 0.0)
    after = jnp.where(x < rows - 1, shift(cells, -1, 1), 0.0)
    spread_rows(cells, before, after, wide, size)
    e_ref[...] = mix(wide[pl.ds(0, 2 * size), :], spread_matrix(iota((128, 128), 1), 0, cols), 3)
    rows, cols = 2 * rows, 2 * cols
    smooth_up(f3, x_face3, y_face3, line3, u3, Field(e_ref, rows), r3, None, None)

    def block(dx, dy):
        inside = ((ix + dx >= 0) & (ix + dx < gx)).astype(F32)
        jx, jy = jnp.clip(ix + dx, 0, gx - 1), jnp.clip(iy + dy, 0, gy - 1)
        return gathered((jx, other if dx else own), jy, pl.ds(0, NZ)) * inside

    for first, dx in ((0, 0), (4, 1), (12, -1)):
        window2(block(dx, 0), shift(block(dx, 1), 32, 1), shift(block(dx, -1), 96, 1), f2, first, iy, gy)
    for x in range(8, 12):
        f2[pl.ds(x, NZ, stride=TX), :] = jnp.zeros((NZ, 128), F32)
    f2, u2, kept2 = (Field(ref, TX) for ref in (f2, u2, kept2))
    x_face2, y_face2, inv2, z_face2 = stack_fields(k2, TX, 3)
    line2 = Line(inv2, z_face2)
    zero = jnp.zeros((TX, 128), F32)
    ends = sweep_in(lambda k: f2[k], line2, kept2, zero, None)

    def emit2(k, value):
        u2[k] = OMEGA * value

    sweep_out(ends, kept2, line2, emit2, None)

    cells = pltpu.roll(u3.ref[...].reshape(NZ, rows, 128), (rows - 2 * ix) % rows, 1)
    x = iota((1, rows, 128), 1)
    place = 2 * ix + jnp.where(x < rows // 2, x, x - rows)
    cells = jnp.where((place >= 0) & (place < rows), cells, 0.0)
    ring = lambda v, first: jnp.where(iota((1, 8, 128), 1) < first, v[:, :8], v[:, rows - 8 :])
    spread_rows(ring(cells, 4), ring(shift(cells, 1, 1), 4), ring(shift(cells, -1, 1), 4), wide, NZ * 8)
    lane = iota((128, 128), 1)
    fine_y = jnp.where(lane < 80, lane, lane - 128) + 32 * iy
    e_ref[...] = mix(wide[pl.ds(0, NZ * TX), :], spread_matrix(fine_y, 0, cols), 3)
    mask2 = window_mask(TX, 128, 4, 32, 4, ix, iy, 4 * gx, 32 * gy)
    smooth_up(f2, x_face2, y_face2, line2, u2, Field(e_ref, TX), kept2, mask2, None)

    cells = u2.ref[...].reshape(NZ, TX, 128)
    ring = lambda v: jnp.where(iota((1, 8, 128), 1) < 6, v[:, :8], v[:, 8:])
    spread_rows(ring(cells), ring(shift(cells, 1, 1)), ring(shift(cells, -1, 1)), wide, NZ * 8)
    fine_y = jnp.where(lane < 96, lane, lane - 128)
    e_ref[...] = mix(wide[pl.ds(0, NZ * TX), :], spread_matrix(fine_y, 0, 0, circular=True), 3)
    fetched[0].wait()
    x_face1, y_face1, inv1, f1, u1, z_face1 = stack_fields(held1, TX, 5)
    line1 = Line(inv1, z_face1)
    mask1 = window_mask(TX, 128, 8, 64, 4, ix, iy, 8 * gx, 64 * gy)
    smooth_up(f1, x_face1, y_face1, line1, u1, Field(e_ref, TX), kept2, mask1, None)

    cells = held1[pl.ds(u1.start, NZ * TX), :].reshape(NZ, TX, 128)
    spread_rows(cells, shift(cells, 1, 1), shift(cells, -1, 1), wide, NZ * TX)
    rows = 2 * TX
    weights = spread_matrix(iota((128, 256), 1), 0, 0, circular=True)
    e0 = Field(e0_ref, rows, 2)
    for k in range(0, NZ, 8):
        cells = mix(wide[pl.ds(k * rows, 8 * rows), :], weights, 3)
        for t in range(2):
            e0_ref[pl.ds(e0.base(t, k), 8 * rows), :] = cells[:, 128 * t : 128 * (t + 1)]
    fetched[1].wait()
    x_face0, y_face0, inv0, f0, u0, z_face0 = stack_fields(held0, rows, 5, 2)
    mask0 = window_mask(rows, 256, TX, TY, HALO, ix, iy, TX * gx, TY * gy)
    smooth_up(f0, x_face0, y_face0, Line(inv0, z_face0), u0, e0, Field(kept0, rows, 2), mask0, 2)

    kappa = Field(stack, TX, start=NZ * TX)

    def residual(k, carry):
        below, flux_z = carry
        column = u0.part(0, k)
        here = column[:TX]
        flux_x = (x_face0.part(0, k) * (column - shift(column, 1, 0)))[: TX + 8]
        row = u0[k][:TX]
        flux_y = y_face0[k][:TX] * (row - shift(row, 1, 1))
        side = (flux_x - shift(flux_x, -1, 0))[:TX] + (flux_y - shift(flux_y, -1, 1))[:, :TY]
        above = u0.part(0, k + 1)[:TX] if k is not NZ - 1 else jnp.zeros((TX, TY), F32)
        flux_up = z_face0.part(0, k + 1)[:TX] * (above - here)
        solution_out[span(k * TX, TX), :] = here
        out = f0.part(0, k)[:TX] - kappa[k] * here - side - flux_z + flux_up
        residual_out[span(k * TX, TX), :] = out
        return here, flux_up

    start = z_face0.part(0, 0)[:TX] * u0.part(0, 0)[:TX]
    carry = loop(NZ - 1, residual, (start, start), 4)
    residual(NZ - 1, carry)


SAVED_ROWS = 72 * 1024
MEBIBYTES = {"pack": 56}
COSTS = {
    "pack": 3 * 10**9, "share": 10**9, "down": 10**10,
    "window_coeffs": 4 * 10**9, "global_coeffs": 4 * 10**9, "up": 12 * 10**9,
}


def call(kernel, name, outs, ins, scratch=(), in_specs=None, out_specs=None, aliases=None):
    shapes = [jax.ShapeDtypeStruct(s, F32) for s in outs]
    return pl.pallas_call(
        kernel,
        name=name,
        out_shape=shapes,
        in_specs=in_specs or [VMEM] * len(ins),
        out_specs=out_specs or [VMEM] * len(outs),
        scratch_shapes=list(scratch),
        input_output_aliases=aliases or {},
        compiler_params=pltpu.CompilerParams(vmem_limit_bytes=MEBIBYTES.get(name, 32) * 1024 * 1024),
        cost_estimate=pl.CostEstimate(flops=COSTS[name], bytes_accessed=4 * sum(x.size for x in ins), transcendentals=0),
    )(*ins)


def body(right_side, kappa_sq, cond_x, cond_y, cond_z):
    gx, gy = lax.axis_size("gx"), lax.axis_size("gy")
    tiles = [v.reshape(NZ * TX, TY) for v in (right_side, kappa_sq, cond_x, cond_y, cond_z)]
    slab, strip = (SLAB + 6 * NZ, 128), (STRIP + 24, 128)
    vm = lambda *shape: pltpu.VMEM(shape, F32)
    dma = lambda n: pltpu.SemaphoreType.DMA((n,))
    devices = gx * gy
    near = lambda n: [(i, i ^ 1) for i in range(n)]
    far = lambda n: [(i, (i + 1 ^ 1) - 1) for i in range(1, n - 1)]
    even_x, even_y = lax.axis_index("gx") % 2 == 0, lax.axis_index("gy") % 2 == 0
    x_near, x_far, y_near, y_far, share2, stack = call(
        pack_kernel, "pack", [slab, slab, strip, strip, (6 * NZ, 128), (5 * NZ * TX, TY)], tiles, [dma(5)], [HBM] * 5
    )
    y_near = lax.ppermute(y_near, "gy", near(gy))
    y_far = lax.ppermute(y_far, "gy", far(gy))
    x_near = lax.ppermute(x_near, "gx", near(gx))
    x_far = lax.ppermute(x_far, "gx", far(gx))
    yr, yl = jnp.where(even_y, y_near, y_far), jnp.where(even_y, y_far, y_near)
    copies = call(functools.partial(share_kernel, devices // 2), "share", [(devices // 2 * SHARE, 128)], [share2, stack])[0]
    half = STRIP // 2
    head = jnp.concatenate([yl[:half], yl[STRIP:], yr[:half], yr[STRIP:]])
    tail = jnp.concatenate([yl[half:], yr[half:]])
    c_near = lax.ppermute(jnp.where(even_x, tail, head), "gx", near(gx))
    c_far = lax.ppermute(jnp.where(even_x, head, tail), "gx", far(gx))
    copies, c_near = lax.optimization_barrier((copies, c_near))
    corner_r, corner_l = jnp.where(even_x, c_near, c_far), jnp.where(even_x, c_far, c_near)
    cores = [[x * gy + y for x in range(core, gx, 2) for y in range(gy)] for core in range(2)]
    blocks = copies.reshape(devices // 2, SHARE, 128)
    own = lax.all_to_all(blocks, ("gx", "gy"), 0, 0, axis_index_groups=cores).reshape(gx // 2, gy * SHARE, 128)
    level = lambda rows, n: [vm(NZ * rows, 128)] * n
    faces = lambda rows, tiles: vm(tiles * (NZ + 1) * rows, 128)
    rows3, rows4 = 2 * gx, gx
    size, tall = (NZ * TX, 128), ((NZ + 1) * TX, 128)
    k2 = call(
        window_kernel, "window_coeffs", [(NZ * TX * 4 + TX, 128)], [share2, x_near, x_far, yr, yl, corner_r, corner_l], level(TX, 7)
    )[0]
    big, big_z = (2 * NZ * 2 * TX, 128), (2 * (NZ + 1) * 2 * TX, 128)
    total0, total1 = 2 * (NZ * 6 + 1) * 2 * TX, (NZ * 6 + 1) * TX
    sends, saved = call(
        functools.partial(down_kernel, gx * TX, gy * TY),
        "down",
        [(devices // 2 * BLOCK, 128), (max(total0 + total1, SAVED_ROWS), 128)],
        [stack, yr, yl, corner_r, corner_l, x_near, x_far],
        [vm(*big)] * 10 + [vm(*big_z)] + level(TX, 10) + [faces(TX, 1)] + level(8, 10) + [faces(8, 1)] + [dma(12)],
        out_specs=[VMEM, ANY],
    )
    sends, own = lax.optimization_barrier((sends, own))
    other = lax.ppermute(own, "gx", near(gx))
    blocks = sends.reshape(devices // 2, BLOCK, 128)
    own_blocks = lax.all_to_all(blocks, ("gx", "gy"), 0, 0, axis_index_groups=cores)
    other_blocks = lax.ppermute(own_blocks, "gx", near(gx))
    whole = call(
        functools.partial(global_kernel, gx, gy),
        "global_coeffs",
        [(5 * NZ * (rows3 + rows4), 128)],
        [own, other],
        level(rows3, 6) + [faces(rows3, 1)] + level(rows3, 1) + level(rows4, 6) + [faces(rows4, 1)] + level(rows4, 1)
        + [vm(gx // 2, 2, gy * SHARE, 128), dma(2)],
        in_specs=[ANY] * 2,
    )[0]
    field, residual = call(
        functools.partial(up_kernel, gx, gy),
        "up",
        [(NZ * TX, TY)] * 2,
        [own_blocks, other_blocks, whole, k2, stack, saved],
        [vm(total0, 128), vm(total1, 128)] + level(TX, 3) + [vm(NZ * 2 * TX, 128), vm(*size), vm(*big), vm(*big)]
        + level(rows3, 3) + level(rows4, 2) + [dma(2)],
        in_specs=[VMEM] * 5 + [ANY],
    )
    return field.reshape(right_side.shape), residual.reshape(right_side.shape)


def solution(mesh):
    spec = P(None, "gx", "gy")
    fits = (mesh.shape["gx"], mesh.shape["gy"]) == (8, 4)
    plan = body if fits else spread_body
    return jax.shard_map(plan, mesh=mesh, in_specs=(spec,) * 5, out_specs=(spec, spec), check_vma=False)
```

```python
import functools

import jax
import jax.numpy as jnp
from jax import lax
from jax.experimental import pallas as pl
from jax.experimental.pallas import tpu as pltpu
from jax.sharding import PartitionSpec as P

LEVELS = 4
COARSE_SWEEPS = 16


OMEGA = 0.8


def with_halo(cells, sides, width):
    for axis, dim in sides:
        count = lax.axis_size(axis)
        ends = count - 1
        head = lax.slice_in_dim(cells, 0, width, axis=dim)
        tail = lax.slice_in_dim(cells, cells.shape[dim] - width, cells.shape[dim], axis=dim)
        cells = jnp.concatenate(
            [
                lax.ppermute(tail, axis, [(i, (i + 1) % count) for i in range(ends)]),
                cells,
                lax.ppermute(head, axis, [((i + 1) % count, i) for i in range(ends)]),
            ],
            axis=dim,
        )
    return cells


def apply_op(field, padded, coeffs):
    kappa, x_up, x_low, y_up, y_low, z_up, z_low = coeffs
    zpad = jnp.pad(field, ((1, 1), (0, 0), (0, 0)))
    out = (
        kappa * field
        + x_up * (field - padded[:, 2:, 1:-1])
        + x_low * (field - padded[:, :-2, 1:-1])
    )
    out = out + y_up * (field - padded[:, 1:-1, 2:]) + y_low * (field - padded[:, 1:-1, :-2])
    return out + z_up * (field - zpad[2:]) + z_low * (field - zpad[:-2])


def face_pad(field):
    return with_halo(field, (("gx", 1), ("gy", 2)), 1)


def line_factors(coeffs):
    kappa, x_up, x_low, y_up, y_low, z_up, z_low = coeffs
    diag = kappa + x_up + x_low + y_up + y_low + z_up + z_low
    upper_src = z_up.at[-1].set(jnp.zeros_like(z_up[-1]))

    def factor_step(upper_prev, planes):
        diag_k, low_k, up_k = planes
        inv = 1.0 / (diag_k + low_k * upper_prev)
        upper = -up_k * inv
        return (upper, (inv, upper))

    start = jnp.zeros_like(diag[0])
    unused, stacked = lax.scan(factor_step, start, (diag, z_low, upper_src), unroll=True)
    return stacked


def line_solve(rhs, factors, z_low):
    inverses, uppers = factors

    def forward_step(prev, planes):
        rhs_k, low_k, inv_k = planes
        value = (rhs_k + low_k * prev) * inv_k
        return (value, value)

    start = jnp.zeros_like(rhs[0])
    unused, forward = lax.scan(forward_step, start, (rhs, z_low, inverses), unroll=True)

    def back_step(after, planes):
        fwd_k, up_k = planes
        value = fwd_k - up_k * after
        return (value, value)

    unused, result = lax.scan(back_step, start, (forward, uppers), reverse=True, unroll=True)
    return result


def mean_four(field):
    depth, rows, cols = field.shape
    return field.reshape(depth, rows // 2, 2, cols // 2, 2).mean(axis=(2, 4))


def coarsen(coeffs):
    kappa, x_up, x_low, y_up, y_low, z_up, z_low = coeffs
    depth, rows, cols = kappa.shape
    shape = (depth, rows // 2, 2, cols // 2, 2)
    xu_c = x_up.reshape(shape)[:, :, 1].mean(axis=-1) * 0.25
    xl_c = x_low.reshape(shape)[:, :, 0].mean(axis=-1) * 0.25
    yu_c = y_up.reshape(shape)[:, :, :, :, 1].mean(axis=2) * 0.25
    yl_c = y_low.reshape(shape)[:, :, :, :, 0].mean(axis=2) * 0.25
    return (mean_four(kappa), xu_c, xl_c, yu_c, yl_c, mean_four(z_up), mean_four(z_low))


def prolong(padded):
    depth = padded.shape[0]
    rows = padded.shape[1] - 2
    cols = padded.shape[2] - 2
    centre = padded[:, 1:-1, :]
    even = 0.75 * centre + 0.25 * padded[:, :-2, :]
    odd = 0.75 * centre + 0.25 * padded[:, 2:, :]
    spread = jnp.stack([even, odd], axis=2).reshape(depth, 2 * rows, cols + 2)
    centre = spread[:, :, 1:-1]
    even = 0.75 * centre + 0.25 * spread[:, :, :-2]
    odd = 0.75 * centre + 0.25 * spread[:, :, 2:]
    return jnp.stack([even, odd], axis=3).reshape(depth, 2 * rows, 2 * cols)


def coarse_solve(rhs, coeffs):
    factors = line_factors(coeffs)
    field = OMEGA * line_solve(rhs, factors, coeffs[6])

    def spread_sweep(sweep, current):
        padded = with_halo(current, (("gx", 1), ("gy", 2)), 1)
        defect = rhs - apply_op(current, padded, coeffs)
        return current + OMEGA * line_solve(defect, factors, coeffs[6])

    field = lax.fori_loop(0, COARSE_SWEEPS - 1, spread_sweep, field)
    return field


def cycle(rhs, coeffs, level):
    if level == LEVELS:
        return coarse_solve(rhs, coeffs)
    factors = line_factors(coeffs)
    field = OMEGA * line_solve(rhs, factors, coeffs[6])
    padded = face_pad(field)
    defect = rhs - apply_op(field, padded, coeffs)
    correction = cycle(mean_four(defect), coarsen(coeffs), level + 1)
    rimmed = with_halo(correction, (("gx", 1), ("gy", 2)), 1)
    field = field + prolong(rimmed)
    padded = face_pad(field)
    defect = rhs - apply_op(field, padded, coeffs)
    return field + OMEGA * line_solve(defect, factors, coeffs[6])


def spread_body(right_side, kappa_sq, cond_x, cond_y, cond_z):
    padded_x = with_halo(cond_x, (("gx", 1),), 1)
    padded_y = with_halo(cond_y, (("gy", 2),), 1)
    padded_z = jnp.pad(cond_z, ((1, 1), (0, 0), (0, 0)))
    x_up = 0.5 * (cond_x + padded_x[:, 2:, :])
    x_low = 0.5 * (cond_x + padded_x[:, :-2, :])
    y_up = 0.5 * (cond_y + padded_y[:, :, 2:])
    y_low = 0.5 * (cond_y + padded_y[:, :, :-2])
    z_up = 0.5 * (cond_z + padded_z[2:])
    z_low = 0.5 * (cond_z + padded_z[:-2])
    coeffs = (kappa_sq, x_up, x_low, y_up, y_low, z_up, z_low)
    solution_field = cycle(right_side, coeffs, 0)
    residual = right_side - apply_op(solution_field, face_pad(solution_field), coeffs)
    return (solution_field, residual)


F32 = jnp.float32
BF16 = jnp.bfloat16
NZ = 32
HALF = NZ // 2
TX, TY = 16, 128
HALO = 8
SLAB = 5 * NZ * HALO
STRIP = 160
CORNER = 104
SHARE = 40
BLOCK = NZ + 8
VMEM = pl.BlockSpec(memory_space=pltpu.VMEM)
ANY = pl.BlockSpec(memory_space=pl.ANY)
HBM = pl.BlockSpec(memory_space=pltpu.HBM)


def iota(shape, dim):
    return lax.broadcasted_iota(jnp.int32, shape, dim)


def shift(x, by, axis):
    by = by % x.shape[axis]
    return pltpu.roll(x, by, axis) if by else x


def mix(x, weights, parts=2):
    pieces = []
    for n in range(parts):
        piece = x.astype(BF16)
        pieces.append(piece)
        if n < parts - 1:
            x = x - piece.astype(F32)
    out = jnp.dot(jnp.concatenate(pieces, axis=0), weights, preferred_element_type=F32)
    rows = x.shape[0]
    return sum(out[n * rows : (n + 1) * rows] for n in reversed(range(parts)))


def matrix(mask, weight=1.0):
    return jnp.where(mask, weight, 0.0).astype(BF16)


def span(start, size):
    if not isinstance(start, int):
        start = pl.multiple_of(start, 8)
    return pl.ds(start, size)


class Field:
    def __init__(self, ref, rows, tiles=1, planes=NZ, start=0):
        self.ref, self.rows, self.tiles, self.planes, self.start = ref, rows, tiles, planes, start

    def base(self, tile, k):
        return self.start + tile * self.planes * self.rows + k * self.rows

    def part(self, tile, k):
        return self.ref[span(self.base(tile, k), self.rows), :]

    def __getitem__(self, k):
        parts = [self.part(t, k) for t in range(self.tiles)]
        return parts[0] if self.tiles == 1 else jnp.concatenate(parts, axis=1)

    def __setitem__(self, k, value):
        for t in range(self.tiles):
            self.put(t, k, value[:, 128 * t : 128 * (t + 1)])

    def put(self, tile, k, value):
        self.ref[span(self.base(tile, k), self.rows), :] = value

    def every_second(self, at, count, odd):
        parts = []
        for t in range(self.tiles):
            first = self.base(t, 0) + 2 * at + odd
            parts.append(self.ref[pl.ds(first, count, stride=2), :])
        return parts[0] if self.tiles == 1 else jnp.concatenate(parts, axis=1)

    def row(self, row):
        return self.ref[pl.ds(self.start + row, self.planes, stride=self.rows), :]


def stack_fields(ref, rows, count, tiles=1, z_face=True, start=0):
    size = tiles * NZ * rows
    out = [Field(ref, rows, tiles, NZ, start + n * size) for n in range(count)]
    return out + [Field(ref, rows, tiles, NZ + 1, start + count * size)] if z_face else out


def loop(count, step, carry, unroll=None):
    if unroll is None or unroll >= count:
        for i in range(count):
            carry = step(i, carry)
        return carry
    return lax.fori_loop(0, count, step, carry, unroll=unroll)


def neighbours(field, x_face, y_face):
    out = x_face * shift(field, 1, 0) + shift(x_face * field, -1, 0)
    return out + (y_face * shift(field, 1, 1) + shift(y_face * field, -1, 1))


class Line:
    def __init__(self, inv, z_face):
        self.inv, self.z_face = inv, z_face

    def inward(self, k, upper):
        return self.z_face[k + 1 if upper else k] * self.inv[k]

    def outward(self, k, upper):
        return self.z_face[k if upper else k + 1] * self.inv[k]


class StoredLine:
    def __init__(self, inv, g, c):
        self.inv, self.g, self.c = inv, g, c

    def inward(self, k, upper):
        return self.g[k]

    def outward(self, k, upper):
        return self.c[k]


def sweep_in(rhs, line, keep, start, unroll):
    def step(i, carry):
        low, high = carry
        k, m = i, NZ - 1 - i
        low = rhs(k) * line.inv[k] + line.inward(k, False) * low
        high = rhs(m) * line.inv[m] + line.inward(m, True) * high
        keep[k] = low
        keep[m] = high
        return low, high

    return loop(HALF, step, (start, start), unroll)


def sweep_out(ends, kept, line, emit, unroll):
    low, high = ends
    a, b = line.outward(HALF - 1, False), line.outward(HALF, True)
    low = (low + a * high) * (1.0 / (1.0 - a * b))
    high = high + b * low

    def step(i, carry):
        low, high = carry
        k, m = HALF - 1 - i, HALF + i
        emit(k, low)
        emit(m, high)
        low = kept[k - 1] + line.outward(k - 1, False) * low
        high = kept[m + 1] + line.outward(m + 1, True) * high
        return low, high

    low, high = loop(HALF - 1, step, (low, high), unroll)
    emit(0, low)
    emit(NZ - 1, high)


def factor(diag, z_face, tiles, inv_out, unroll, rhs=None, keep=None, g_out=None, c_out=None):
    ends = []
    for t in range(tiles):
        zero = diag.part(t, 0) * 0.0

        def one(k, upper, before, last, prev):
            below, above = z_face.part(t, k), z_face.part(t, k + 1)
            inner, outer = (above, below) if upper else (below, above)
            minor = (diag.part(t, k) + below + above) * last - (inner * inner) * before
            inv = last * (1.0 / minor)
            inv_out.put(t, k, inv)
            if g_out is not None:
                g_out.put(t, k, inner * inv)
                c_out.put(t, k, outer * inv)
            if rhs is not None:
                prev = rhs.part(t, k) * inv + (inner * inv) * prev
                keep.put(t, k, prev)
            return last, minor, prev

        def step(i, carry):
            low, high = carry
            return one(i, False, *low), one(NZ - 1 - i, True, *high)

        start = (zero, zero + 1.0, zero)
        low, high = loop(HALF, step, (start, start), unroll)
        ends.append((low[2], high[2]))
    join = lambda n: ends[0][n] if tiles == 1 else jnp.concatenate([e[n] for e in ends], axis=1)
    return join(0), join(1)


def z_faces(cz, out, tiles=1):
    for t in range(tiles):
        before = None
        for k in range(NZ + 1):
            here = cz.part(t, k) if k < NZ else None
            both = here if before is None else before if here is None else here + before
            out.put(t, k, 0.5 * both)
            before = here


def base_diag(kappa, x_face, y_face):
    return kappa + (x_face + shift(x_face, -1, 0)) + (y_face + shift(y_face, -1, 1))


def window_mask(rows, lanes, tile_x, tile_y, halo, ix, iy, nx, ny):
    x, y = iota((rows, lanes), 0), iota((rows, lanes), 1)
    x = jnp.where(x < (rows + tile_x) // 2, x, x - rows)
    y = jnp.where(y < (lanes + tile_y) // 2, y, y - lanes)
    valid = (y >= -halo) & (y < tile_y + halo) & (x >= -halo) & (x < tile_x + halo)
    x, y = x + ix * tile_x, y + iy * tile_y
    return (valid & (x >= 0) & (x < nx) & (y >= 0) & (y < ny)).astype(F32)


def smooth_down(f, x_face, y_face, line, ends, kept, u, r, unroll):
    def emit(k, value):
        field = OMEGA * value
        u[k] = field
        r[k] = (1.0 - OMEGA) * f[k] + neighbours(field, x_face[k], y_face[k])

    sweep_out(ends, kept, line, emit, unroll)


def smooth_up(f, x_face, y_face, line, u, e, kept, mask, unroll):
    masked = (lambda v: v) if mask is None else (lambda v: v * mask)

    def rhs(k):
        field = masked(u[k] + e[k])
        u[k] = field
        return masked(f[k] + neighbours(field, x_face[k], y_face[k]))

    def emit(k, value):
        u[k] = (1.0 - OMEGA) * u[k] + OMEGA * value

    zero = jnp.zeros((u.rows, 128 * u.tiles), F32)
    ends = sweep_in(rhs, line, kept, zero, unroll)
    sweep_out(ends, kept, line, emit, unroll)


def spread_rows(cells, before, after, dest, size):
    dest[pl.ds(0, size, stride=2), :] = (0.75 * cells + 0.25 * before).reshape(size, 128)
    dest[pl.ds(1, size, stride=2), :] = (0.75 * cells + 0.25 * after).reshape(size, 128)


def spread_matrix(fine, base, coarse_count, circular=False):
    j = iota((128, fine.shape[1]), 0) + base
    parent = (fine + 2048) // 2 - 1024
    partner = parent + 2 * ((fine + 2048) % 2) - 1
    if circular:
        j, parent, partner = j % 128, parent % 128, partner % 128
    weights = jnp.where(j == parent, 0.75, jnp.where(j == partner, 0.25, 0.0))
    if not circular:
        inside = (j >= 0) & (j < coarse_count) & (fine >= 0) & (fine < 2 * coarse_count)
        weights = jnp.where(inside, weights, 0.0)
    return weights.astype(BF16)


def lane_group(rows, width):
    return iota((rows, 128), 1) // width


def fold_planes(cells, turn):
    group = lane_group(8, 32)
    out = cells[:8]
    for n in range(1, 4):
        out = jnp.where(group == n, cells[8 * n : 8 * n + 8], out)
    return pltpu.roll(out, turn, 1)


def share_blocks(kinds):
    iy = lax.axis_index("gy")
    y, lane = iota((128, 128), 0), iota((128, 128), 1)
    x_in, y_in = y // 32, y % 32
    x_out, y_out = lane % 32 // 16, lane % 16
    pair_y, pair_x = y_in // 2 == y_out, x_in // 2 == x_out
    a, b, c, d, kappa, cz = kinds
    eighth = lambda mask: matrix(mask, 0.125)
    blocks = [
        mix(a, eighth(pair_y & (x_in == 2 * x_out))) + mix(b, eighth(pair_y & (x_in == 1) & (x_out == 1))),
        mix(b, eighth(pair_y & (x_in == 3) & (x_out == 0)))
        + mix(d, eighth((x_out == 1) & (y_in == 31) & (x_in // 2 == y_out))),
        mix(c, eighth(pair_x & (y_in == 2 * y_out))) + mix(d, eighth(pair_x & (y_in == 2 * y_out - 1))),
        mix(kappa, matrix(pair_x & pair_y, 0.25)),
        mix(cz, matrix(pair_x & pair_y, 0.25)),
    ]
    return [fold_planes(cells, 16 * iy) for cells in blocks]


def fetch_all(sources, dests, sems, first=0):
    copies = [pltpu.make_async_copy(a, b, sems.at[first + n]) for n, (a, b) in enumerate(zip(sources, dests))]
    for copy in copies:
        copy.start()
    return copies


def pack_kernel(devices, f_in, kappa_in, cx_in, cy_in, cz_in, x_near, x_far, y_near, y_far, share2, stack, copies, sems):
    even_x, even_y = lax.axis_index("gx") % 2 == 0, lax.axis_index("gy") % 2 == 0
    tiles = [stack.at[pl.ds(a * NZ * TX, NZ * TX), :] for a in range(5)]
    for copy in fetch_all((f_in, kappa_in, cx_in, cy_in, cz_in), tiles, sems):
        copy.wait()
    f, kappa, cx, cy, cz = tiles
    for a, ref in enumerate(tiles):
        cells = ref[...].reshape(NZ, TX, TY)
        at = pl.ds(a * NZ * HALO, NZ * HALO)
        head = cells[:, :HALO].reshape(NZ * HALO, TY)
        tail = cells[:, TX - HALO :].reshape(NZ * HALO, TY)
        x_near[at, :] = jnp.where(even_x, tail, head)
        x_far[at, :] = jnp.where(even_x, head, tail)
    y, lane = iota((128, 128), 0), iota((128, 128), 1)
    fourth = y // 4 == lane % 32
    rows = lambda ref: [Field(ref, TX).row(r) for r in range(TX)]
    cx_rows, cy_rows, kappa_rows, cz_rows = rows(cx), rows(cy), rows(kappa), rows(cz)
    totals = lambda v: [(v[4 * i] + v[4 * i + 1]) + (v[4 * i + 2] + v[4 * i + 3]) for i in range(4)]
    stack = [cx_rows[4 * i] for i in range(4)] + [cx_rows[4 * i + 3] for i in range(4)]
    stack = mix(jnp.concatenate(stack + totals(kappa_rows) + totals(cz_rows), axis=0), matrix(fourth))
    ends = [matrix(fourth & (y % 4 == 0)), matrix(fourth & (y % 4 == 3))]
    sides = mix(jnp.concatenate(totals(cy_rows), axis=0), jnp.concatenate(ends, axis=1))
    group = lane_group(NZ, 32)

    def merge(cells, scale):
        out = cells[:NZ]
        for xi in range(1, 4):
            out = jnp.where(group == xi, cells[NZ * xi : NZ * (xi + 1)], out)
        return out * scale

    kinds = [merge(stack[:128], 1 / 128), merge(stack[128:256], 1 / 128)]
    kinds += [merge(sides[:, :128], 1 / 128), merge(sides[:, 128:], 1 / 128)]
    kinds += [merge(stack[256:384], 1 / 16), merge(stack[384:], 1 / 16)]
    for t, cells in enumerate(share_blocks(kinds)):
        for n in range(devices):
            copies[pl.ds(n * SHARE + 8 * t, 8), :] = cells
    head = [jnp.zeros((8, 128), F32)] * 3
    tail = [jnp.zeros((8, 128), F32)] * 3
    slot = iota((8, 128), 1) % 32 // 4
    for t, cells in enumerate(kinds):
        for dest, first in ((share2, 0), (x_near, SLAB), (x_far, SLAB)):
            dest[pl.ds(first + t * NZ, NZ), :] = cells
        for zv in range(4):
            n = 4 * t + zv
            piece = cells[8 * zv : 8 * zv + 8]
            head[n // 8] = jnp.where(slot == n % 8, shift(piece, 4 * (n % 8), 1), head[n // 8])
            tail[n // 8] = jnp.where(slot == n % 8, shift(piece, 4 * (n % 8) + 4, 1), tail[n // 8])
    for n in range(3):
        y_near[pl.ds(STRIP + 8 * n, 8), :] = jnp.where(even_y, tail[n], head[n])
        y_far[pl.ds(STRIP + 8 * n, 8), :] = jnp.where(even_y, head[n], tail[n])

    group = lane_group(8, 8)
    for a, ref in enumerate((f, kappa, cx, cy, cz)):
        for half in range(2):
            for zo in range(2):
                head = jnp.zeros((8, 128), F32)
                tail = jnp.zeros((8, 128), F32)
                for zi in range(16):
                    cells = ref[pl.ds((zo * 16 + zi) * TX + 8 * half, 8), :]
                    cells = shift(cells, 8 * zi, 1)
                    head = jnp.where(group == zi, cells, head)
                    tail = jnp.where(group == (zi - 1) % 16, cells, tail)
                at = pl.ds(((half * 5 + a) * 2 + zo) * 8, 8)
                y_near[at, :] = jnp.where(even_y, tail, head)
                y_far[at, :] = jnp.where(even_y, head, tail)


def window2(tile, after, before, dest, first, iy, gy):
    lane = iota((NZ, 128), 1)
    first_after, first_before = jnp.where(iy < gy - 1, 36, 0), jnp.where(iy > 0, 124, 128)
    for xi in range(4):
        turned = (lane - 32 * xi + 128) % 128
        cells = jnp.where(turned < 32, tile, jnp.where(turned < first_after, after, jnp.where(turned >= first_before, before, 0.0)))
        dest[pl.ds(first + xi, NZ, stride=TX), :] = shift(cells, -32 * xi, 1)


def window_kernel(share2, x_near, x_far, yr, yl, cr, cl, out, a, b, c, d, kappa, cz, diag):
    ix, iy = lax.axis_index("gx"), lax.axis_index("gy")
    gy = lax.axis_size("gy")
    nx, ny = lax.axis_size("gx") * 4, gy * 32
    refs = (a, b, c, d, kappa, cz)

    def unpack(ref, first, t, turn):
        pieces = []
        for zv in range(4):
            n = 4 * t + zv
            pieces.append(shift(ref[span(first + 8 * (n // 8), 8), :], turn - 4 * (n % 8), 1))
        return jnp.concatenate(pieces, axis=0)

    near, far = STRIP // 2, CORNER + STRIP // 2
    even_x = ix % 2 == 0
    for t, dest in enumerate(refs):
        beside = x_near[pl.ds(SLAB + t * NZ, NZ), :], x_far[pl.ds(SLAB + t * NZ, NZ), :]
        for first, cells, right, left, r_at, l_at in (
            (0, share2[pl.ds(t * NZ, NZ), :], yr, yl, STRIP, STRIP),
            (4, jnp.where(even_x, *beside), cr, cr, far, near),
            (12, jnp.where(even_x, *beside[::-1]), cl, cl, far, near),
        ):
            window2(cells, unpack(right, r_at, t, 32), unpack(left, l_at, t, 92), dest, first, iy, gy)
        for x in range(8, 12):
            dest[pl.ds(x, NZ, stride=TX), :] = jnp.zeros((NZ, 128), F32)
    mask = window_mask(TX, 128, 4, 32, 4, ix, iy, nx, ny)
    a, b, c, d, kappa, cz, diag = (Field(ref, TX) for ref in (*refs, diag))
    x_face, y_face, inv, z_face = stack_fields(out, TX, 3)
    for k in range(NZ):
        x_k = a[k] + shift(b[k], 1, 0)
        y_k = c[k] + shift(d[k], 1, 1)
        x_face[k] = x_k
        y_face[k] = y_k
        diag[k] = base_diag(jnp.where(mask > 0, kappa[k], 1.0), x_k, y_k)
    z_faces(cz, z_face)
    factor(diag, z_face, 1, inv, None)


def assemble3(block, dest, gx, gy, rows):
    group = lane_group(8, 16)
    for ix in range(gx):
        blocks = [block(ix, iy) for iy in range(gy)]
        for zo in range(4):
            for xi in range(2):
                q = 2 * zo + xi
                cells = blocks[0]
                for iy in range(1, gy):
                    cells = jnp.where(group == (iy + q) % 8, blocks[iy], cells)
                dest[pl.ds(8 * zo * rows + 2 * ix + xi, 8, stride=rows), :] = shift(cells, -16 * q, 1)


def global_kernel(gx, gy, own, other, *refs):
    out, raw3, raw4, shares, sems = refs[0], refs[1:9], refs[9:17], refs[17], refs[18]
    outs3 = stack_fields(out, 2 * gx, 5, z_face=False)
    outs4 = stack_fields(out, gx, 5, z_face=False, start=5 * NZ * 2 * gx)
    core = lax.axis_index("gx") % 2
    copies = [
        pltpu.make_async_copy(own, shares.at[:, core], sems.at[0]),
        pltpu.make_async_copy(other, shares.at[:, 1 - core], sems.at[1]),
    ]
    for copy in copies:
        copy.start()
    for copy in copies:
        copy.wait()
    rows, cols = 2 * gx, 16 * gy
    for t, n in enumerate((0, 1, 2, 4, 5)):
        block = lambda jx, jy: shares[jx // 2, jx % 2, pl.ds(jy * SHARE + 8 * t, 8), :]
        assemble3(block, raw3[n], gx, gy, rows)
    xl, xu, yl, yu = (Field(ref, rows) for ref in raw3[:4])
    x, y = iota((rows, 128), 0), iota((rows, 128), 1)
    odd_row, inside = x % 2 == 1, y < cols
    for k in range(NZ):
        half = jnp.where(inside, xu[k], 0.0)
        below = jnp.where(odd_row | (x < 2), 0.0, shift(half, 2, 0))
        x_k = jnp.where(inside, xl[k] + below, 0.0)
        xl[k] = x_k
        xu[k] = jnp.where(x == rows - 1, shift(half, 1, 0), shift(x_k, -1, 0))
        next_row = shift(half, -1, 0)
        below = jnp.where(odd_row, shift(half, 15, 1), shift(next_row, 16, 1))
        y_k = jnp.where(inside, yl[k] + jnp.where((y % 16 == 0) & (y > 0), below, 0.0), 0.0)
        yl[k] = y_k
        above = jnp.where(odd_row, shift(half, 14, 1), shift(next_row, 15, 1))
        yu[k] = jnp.where(y == cols - 1, above, jnp.where(inside, shift(y_k, -1, 1), 0.0))
    yy, jj = iota((128, 128), 0), iota((128, 128), 1)
    keep = yy // 2 == jj
    pair, even, odd = matrix(keep), matrix(keep & (yy % 2 == 0)), matrix(keep & (yy % 2 == 1))
    size = NZ * rows // 2
    lows = [Field(ref, rows) for ref in raw3]
    first = lambda n: lows[n].every_second(0, size, 0)
    second = lambda n: lows[n].every_second(0, size, 1)
    raw4[0][...] = 0.125 * mix(first(0), pair)
    raw4[1][...] = 0.125 * mix(second(1), pair)
    raw4[2][...] = 0.125 * mix(first(2) + second(2), even)
    raw4[3][...] = 0.125 * mix(first(3) + second(3), odd)
    raw4[4][...] = 0.25 * mix(first(4) + second(4), pair)
    raw4[5][...] = 0.25 * mix(first(5) + second(5), pair)
    for raw, outs in ((raw3, outs3), (raw4, outs4)):
        x, y = iota((rows, 128), 0), iota((rows, 128), 1)
        xl, xu, yl, yu, kappa, cz = (Field(ref, rows) for ref in raw[:6])
        z_face, diag = Field(raw[6], rows, 1, NZ + 1), Field(raw[7], rows)
        x_face, y_face, inv, g, c = outs
        inside_x, inside_y = (x > 0).astype(F32), ((y > 0) & (y < cols)).astype(F32)
        for k in range(NZ):
            xl_k, yl_k = xl[k], yl[k]
            diag[k] = jnp.where(y < cols, kappa[k], 1.0) + (xl_k + xu[k]) + (yl_k + yu[k])
            x_face[k] = xl_k * inside_x
            y_face[k] = yl_k * inside_y
        z_faces(cz, z_face)
        factor(diag, z_face, 1, inv, None, g_out=g, c_out=c)
        rows, cols = rows // 2, cols // 2


def down_kernel(nx, ny, *refs):
    stack, yr, yl, corner_r, corner_l, x_near, x_far = refs[:7]
    sends, saved = refs[7:9]
    scratch = list(refs[9:-1])
    sems = refs[-1]
    take = lambda n: [scratch.pop(0) for _ in range(n)]
    ix, iy = lax.axis_index("gx"), lax.axis_index("gy")
    gx, gy = lax.axis_size("gx"), lax.axis_size("gy")
    f, kappa, cx, cy, cz = (stack.at[pl.ds(a * NZ * TX, NZ * TX), :] for a in range(5))
    even_x = ix % 2 == 0
    rows, tiles = 2 * TX, 2
    whole = take(11)
    names = [Field(ref, rows, tiles) for ref in whole[:10]]
    x_face, y_face, inv, u, f0, kappa0, cz0, diag, kept, r = names
    z_face = Field(whole[10], rows, tiles, NZ + 1)
    group = lane_group(8, 8)

    def window(a, tile, z, after, before, turn):
        zo = z // 16
        slab = span(a * NZ * HALO + z * HALO, HALO)
        near, far = x_near[slab, :], x_far[slab, :]
        sides = [jnp.where(even_x, near, far), jnp.where(even_x, far, near)]
        main = jnp.concatenate([tile[span(z * TX, TX), :], *sides], axis=0)
        at = lambda first: span(first + (a * 2 + zo) * 8, 8)
        half = STRIP // 2
        sides = []
        for right, left in (
            (yr[at(0), :], yl[at(0), :]),
            (yr[at(half), :], yl[at(half), :]),
            (corner_r[at(CORNER), :], corner_r[at(0), :]),
            (corner_l[at(CORNER), :], corner_l[at(0), :]),
        ):
            cells = jnp.where(after, right, jnp.where(before, left, 0.0))
            sides.append(pltpu.roll(cells, turn, 1))
        return jnp.concatenate([main, jnp.concatenate(sides, axis=0)], axis=1)

    mask0 = window_mask(rows, 256, TX, TY, HALO, ix, iy, nx, ny)

    def prepare(z, cz_prev):
        zi = z % 16
        after, before = group == zi, group == (zi + 15) % 16
        turn = (128 - 8 * zi) % 128
        f_k, kappa_k, cx_k, cy_k, cz_k = (
            window(a, tile, z, after, before, turn) for a, tile in enumerate((f, kappa, cx, cy, cz))
        )
        f0[z] = f_k
        kappa0[z] = kappa_k
        cz0[z] = cz_k
        z_face[z] = 0.5 * (cz_k + cz_prev)
        x_k, y_k = 0.5 * (cx_k + shift(cx_k, 1, 0)), 0.5 * (cy_k + shift(cy_k, 1, 1))
        x_face[z] = x_k
        y_face[z] = y_k
        diag[z] = base_diag(jnp.where(mask0 > 0, kappa_k, 1.0), x_k, y_k)
        return cz_k

    last = loop(NZ, prepare, jnp.zeros((rows, 256), F32), 2)
    z_face[NZ] = 0.5 * last
    ends = factor(diag, z_face, tiles, inv, 4, f0, kept)
    copies = []

    def save(field):
        at = sum(copy[1] for copy in copies)
        count = field.ref.shape[0]
        copy = pltpu.make_async_copy(field.ref, saved.at[pl.ds(at, count), :], sems.at[len(copies)])
        copy.start()
        copies.append((copy, count))

    for field in (x_face, y_face, inv, f0):
        save(field)
    smooth_down(f0, x_face, y_face, Line(inv, z_face), ends, kept, u, r, 2)
    save(u)
    save(z_face)

    fine = (r, kappa0, cz0, x_face, y_face)
    lanes, tile_x, tile_y, halo = 256, TX, TY, HALO
    for level in (1, 2):
        rows, tile_x, tile_y, halo = rows // 2, tile_x // 2, tile_y // 2, halo // 2
        nx, ny = nx // 2, ny // 2
        whole = take(11)
        names = [Field(ref, rows) for ref in whole[:10]]
        x_face, y_face, inv, u, f1, kappa1, cz1, diag, kept, r = names
        z_face = Field(whole[10], rows, 1, NZ + 1)
        mask = window_mask(rows, 128, tile_x, tile_y, halo, ix, iy, nx, ny)
        y, j = iota((lanes, 128), 0), iota((lanes, 128), 1)
        if lanes == 128:
            j = jnp.where(j < 48, j, jnp.where(j >= 80, j - 64, -1))
        pair = matrix(y // 2 == j)
        even = (iota((1, lanes), 1) % 2 == 0).astype(F32)
        part = 128
        for at in range(0, NZ * rows, part):
            here = pl.ds(at, part)
            both = lambda n: fine[n].every_second(at, part, 0) + fine[n].every_second(at, part, 1)
            below = fine[3].every_second(at, part, 0)
            out = mix(jnp.concatenate([both(0), both(1), both(2), below, both(4) * even], axis=0), pair)
            for n, (dest, weight) in enumerate(((f1, 0.25), (kappa1, 0.25), (cz1, 0.25), (x_face, 0.125), (y_face, 0.125))):
                dest.ref[here, :] = weight * out[n * part : (n + 1) * part]
        for k in range(NZ):
            f1[k] = f1[k] * mask
            diag[k] = base_diag(jnp.where(mask > 0, kappa1[k], 1.0), x_face[k], y_face[k])
        z_faces(cz1, z_face)
        ends = factor(diag, z_face, 1, inv, None, f1, kept)
        smooth_down(f1, x_face, y_face, Line(inv, z_face), ends, kept, u, r, None)
        if level == 1:
            for field in (x_face, y_face, inv, f1, u, z_face):
                save(field)
        fine, lanes = (r, kappa1, cz1, x_face, y_face), 128

    group = lane_group(NZ, 32)
    out = f1.row(0)
    for xi in range(1, 4):
        out = jnp.where(group == xi, shift(f1.row(xi), 32 * xi, 1), out)
    for n in range(gx * gy // 2):
        sends[pl.ds(n * BLOCK, NZ), :] = out
    y, lane = iota((128, 128), 0), iota((128, 128), 1)
    total = jnp.zeros((NZ, 128), F32)
    for xi in range(2):
        place = (lane % 32 // 16 == xi) & (y // 2 == lane % 16) & (y < 32)
        total = total + mix(r.row(2 * xi) + r.row(2 * xi + 1), matrix(place, 0.25))
    total = fold_planes(total, 16 * iy)
    for n in range(gx * gy // 2):
        sends[pl.ds(n * BLOCK + NZ, 8), :] = total
    for copy, _ in copies:
        copy.wait()


def up_kernel(gx, gy, *refs):
    own, other, whole, k2, stack, saved, solution_out, residual_out = refs[:8]
    scratch = list(refs[8:-1])
    sems = refs[-1]
    take = lambda n: [scratch.pop(0) for _ in range(n)]
    ix, iy = lax.axis_index("gx"), lax.axis_index("gy")
    held0, held1 = take(2)
    split = held0.shape[0]
    parts = [saved.at[pl.ds(split, held1.shape[0]), :], saved.at[pl.ds(0, split), :]]
    fetched = fetch_all(parts, (held1, held0), sems)
    core = ix % 2

    def gathered(jx, jy, at):
        if isinstance(jx, int):
            same = core == jx % 2
            return jnp.where(same, own[jx // 2 * gy + jy, at, :], other[jx // 2 * gy + jy, at, :])
        return jx[1][jx[0] // 2 * gy + jy, at, :]
    f2, u2, kept2, wide, e_ref, e0_ref, kept0, u3, f3, r3, f4, u4, pairs4 = take(13)

    rows, cols = 2 * gx, 16 * gy
    assemble3(lambda jx, jy: gathered(jx, jy, pl.ds(NZ, 8)), f3, gx, gy, rows)
    f3, u3, r3 = (Field(ref, rows) for ref in (f3, u3, r3))
    y = iota((rows, 128), 1)
    x_face3, y_face3, inv3, g3, c3 = stack_fields(whole, rows, 5, z_face=False)
    line3 = StoredLine(inv3, g3, c3)
    clean = (y < cols).astype(F32)
    for k in range(NZ):
        f3[k] = f3[k] * clean
    zero = jnp.zeros((rows, 128), F32)
    ends = sweep_in(lambda k: f3[k], line3, r3, zero, None)
    smooth_down(f3, x_face3, y_face3, line3, ends, r3, u3, Field(e_ref, rows), None)
    fine = Field(e_ref, rows)
    rows, cols = rows // 2, cols // 2
    size = NZ * rows
    yy, jj = iota((128, 128), 0), iota((128, 128), 1)
    f4[...] = 0.25 * mix(fine.every_second(0, size, 0) + fine.every_second(0, size, 1), matrix(yy // 2 == jj))
    f4, u4 = Field(f4, rows), Field(u4, rows)
    first = iota((rows, 128), 1) < 64
    fields = (f4, *stack_fields(whole, rows, 5, z_face=False, start=5 * NZ * 2 * rows))
    pairs = [Field(pairs4, rows, 1, HALF, n * HALF * rows) for n in range(7)]
    for field, pair in zip(fields, pairs):
        for k in range(HALF):
            pair[k] = jnp.where(first, field[k], shift(field[NZ - 1 - k], 64, 1))
    fp, x_facep, y_facep, invp, gp, cp, up4 = pairs
    middle = cp[HALF - 1]
    scale = 1.0 / (1.0 - middle * shift(middle, 64, 1))

    def solve4(rhs, old):
        value = rhs(0) * invp[0]
        kept = [value]
        for k in range(1, HALF):
            value = rhs(k) * invp[k] + gp[k] * value
            kept.append(value)
        value = (value + middle * shift(value, 64, 1)) * scale
        for k in reversed(range(HALF)):
            up4[k] = OMEGA * value if old is None else (1.0 - OMEGA) * old[k] + OMEGA * value
            if k:
                value = kept[k - 1] + cp[k - 1] * value

    solve4(lambda k: fp[k], None)

    def relax(sweep, carry):
        old = [up4[k] for k in range(HALF)]
        solve4(lambda k: fp[k] + neighbours(old[k], x_facep[k], y_facep[k]), old)
        return carry

    lax.fori_loop(0, COARSE_SWEEPS - 1, relax, 0)
    for k in range(HALF):
        both = up4[k]
        u4[k] = jnp.where(first, both, 0.0)
        u4[NZ - 1 - k] = jnp.where(first, shift(both, 64, 1), 0.0)

    cells = u4.ref[...].reshape(NZ, rows, 128)
    x = iota((1, rows, 128), 1)
    before = jnp.where(x > 0, shift(cells, 1, 1), 0.0)
    after = jnp.where(x < rows - 1, shift(cells, -1, 1), 0.0)
    spread_rows(cells, before, after, wide, size)
    e_ref[...] = mix(wide[pl.ds(0, 2 * size), :], spread_matrix(iota((128, 128), 1), 0, cols), 3)
    rows, cols = 2 * rows, 2 * cols
    smooth_up(f3, x_face3, y_face3, line3, u3, Field(e_ref, rows), r3, None, None)

    def block(dx, dy):
        inside = ((ix + dx >= 0) & (ix + dx < gx)).astype(F32)
        jx, jy = jnp.clip(ix + dx, 0, gx - 1), jnp.clip(iy + dy, 0, gy - 1)
        return gathered((jx, other if dx else own), jy, pl.ds(0, NZ)) * inside

    for first, dx in ((0, 0), (4, 1), (12, -1)):
        window2(block(dx, 0), shift(block(dx, 1), 32, 1), shift(block(dx, -1), 96, 1), f2, first, iy, gy)
    for x in range(8, 12):
        f2[pl.ds(x, NZ, stride=TX), :] = jnp.zeros((NZ, 128), F32)
    f2, u2, kept2 = (Field(ref, TX) for ref in (f2, u2, kept2))
    x_face2, y_face2, inv2, z_face2 = stack_fields(k2, TX, 3)
    line2 = Line(inv2, z_face2)
    zero = jnp.zeros((TX, 128), F32)
    ends = sweep_in(lambda k: f2[k], line2, kept2, zero, None)

    def emit2(k, value):
        u2[k] = OMEGA * value

    sweep_out(ends, kept2, line2, emit2, None)

    cells = pltpu.roll(u3.ref[...].reshape(NZ, rows, 128), (rows - 2 * ix) % rows, 1)
    x = iota((1, rows, 128), 1)
    place = 2 * ix + jnp.where(x < rows // 2, x, x - rows)
    cells = jnp.where((place >= 0) & (place < rows), cells, 0.0)
    ring = lambda v, first: jnp.where(iota((1, 8, 128), 1) < first, v[:, :8], v[:, rows - 8 :])
    spread_rows(ring(cells, 4), ring(shift(cells, 1, 1), 4), ring(shift(cells, -1, 1), 4), wide, NZ * 8)
    lane = iota((128, 128), 1)
    fine_y = jnp.where(lane < 80, lane, lane - 128) + 32 * iy
    e_ref[...] = mix(wide[pl.ds(0, NZ * TX), :], spread_matrix(fine_y, 0, cols), 3)
    mask2 = window_mask(TX, 128, 4, 32, 4, ix, iy, 4 * gx, 32 * gy)
    smooth_up(f2, x_face2, y_face2, line2, u2, Field(e_ref, TX), kept2, mask2, None)

    cells = u2.ref[...].reshape(NZ, TX, 128)
    ring = lambda v: jnp.where(iota((1, 8, 128), 1) < 6, v[:, :8], v[:, 8:])
    spread_rows(ring(cells), ring(shift(cells, 1, 1)), ring(shift(cells, -1, 1)), wide, NZ * 8)
    fine_y = jnp.where(lane < 96, lane, lane - 128)
    e_ref[...] = mix(wide[pl.ds(0, NZ * TX), :], spread_matrix(fine_y, 0, 0, circular=True), 3)
    fetched[0].wait()
    x_face1, y_face1, inv1, f1, u1, z_face1 = stack_fields(held1, TX, 5)
    line1 = Line(inv1, z_face1)
    mask1 = window_mask(TX, 128, 8, 64, 4, ix, iy, 8 * gx, 64 * gy)
    smooth_up(f1, x_face1, y_face1, line1, u1, Field(e_ref, TX), kept2, mask1, None)

    cells = held1[pl.ds(u1.start, NZ * TX), :].reshape(NZ, TX, 128)
    spread_rows(cells, shift(cells, 1, 1), shift(cells, -1, 1), wide, NZ * TX)
    rows = 2 * TX
    weights = spread_matrix(iota((128, 256), 1), 0, 0, circular=True)
    e0 = Field(e0_ref, rows, 2)
    for k in range(0, NZ, 8):
        cells = mix(wide[pl.ds(k * rows, 8 * rows), :], weights, 3)
        for t in range(2):
            e0_ref[pl.ds(e0.base(t, k), 8 * rows), :] = cells[:, 128 * t : 128 * (t + 1)]
    fetched[1].wait()
    x_face0, y_face0, inv0, f0, u0, z_face0 = stack_fields(held0, rows, 5, 2)
    mask0 = window_mask(rows, 256, TX, TY, HALO, ix, iy, TX * gx, TY * gy)
    smooth_up(f0, x_face0, y_face0, Line(inv0, z_face0), u0, e0, Field(kept0, rows, 2), mask0, 2)

    kappa = Field(stack, TX, start=NZ * TX)

    def residual(k, carry):
        below, flux_z = carry
        column = u0.part(0, k)
        here = column[:TX]
        flux_x = (x_face0.part(0, k) * (column - shift(column, 1, 0)))[: TX + 8]
        row = u0[k][:TX]
        flux_y = y_face0[k][:TX] * (row - shift(row, 1, 1))
        side = (flux_x - shift(flux_x, -1, 0))[:TX] + (flux_y - shift(flux_y, -1, 1))[:, :TY]
        above = u0.part(0, k + 1)[:TX] if k is not NZ - 1 else jnp.zeros((TX, TY), F32)
        flux_up = z_face0.part(0, k + 1)[:TX] * (above - here)
        solution_out[span(k * TX, TX), :] = here
        out = f0.part(0, k)[:TX] - kappa[k] * here - side - flux_z + flux_up
        residual_out[span(k * TX, TX), :] = out
        return here, flux_up

    start = z_face0.part(0, 0)[:TX] * u0.part(0, 0)[:TX]
    carry = loop(NZ - 1, residual, (start, start), 4)
    residual(NZ - 1, carry)


SAVED_ROWS = 72 * 1024
MEBIBYTES = {"pack": 56}
COSTS = {
    "pack": 3 * 10**9, "down": 10**10,
    "window_coeffs": 4 * 10**9, "global_coeffs": 4 * 10**9, "up": 12 * 10**9,
}


def call(kernel, name, outs, ins, scratch=(), in_specs=None, out_specs=None, aliases=None):
    shapes = [jax.ShapeDtypeStruct(s, F32) for s in outs]
    return pl.pallas_call(
        kernel,
        name=name,
        out_shape=shapes,
        in_specs=in_specs or [VMEM] * len(ins),
        out_specs=out_specs or [VMEM] * len(outs),
        scratch_shapes=list(scratch),
        input_output_aliases=aliases or {},
        compiler_params=pltpu.CompilerParams(vmem_limit_bytes=MEBIBYTES.get(name, 32) * 1024 * 1024),
        cost_estimate=pl.CostEstimate(flops=COSTS[name], bytes_accessed=4 * sum(x.size for x in ins), transcendentals=0),
    )(*ins)


def body(right_side, kappa_sq, cond_x, cond_y, cond_z):
    gx, gy = lax.axis_size("gx"), lax.axis_size("gy")
    tiles = [v.reshape(NZ * TX, TY) for v in (right_side, kappa_sq, cond_x, cond_y, cond_z)]
    slab, strip = (SLAB + 6 * NZ, 128), (STRIP + 24, 128)
    vm = lambda *shape: pltpu.VMEM(shape, F32)
    dma = lambda n: pltpu.SemaphoreType.DMA((n,))
    devices = gx * gy
    near = lambda n: [(i, i ^ 1) for i in range(n)]
    far = lambda n: [(i, (i + 1 ^ 1) - 1) for i in range(1, n - 1)]
    even_x, even_y = lax.axis_index("gx") % 2 == 0, lax.axis_index("gy") % 2 == 0
    x_near, x_far, y_near, y_far, share2, stack, copies = call(
        functools.partial(pack_kernel, devices // 2),
        "pack",
        [slab, slab, strip, strip, (6 * NZ, 128), (5 * NZ * TX, TY), (devices // 2 * SHARE, 128)],
        tiles,
        [dma(5)],
        [HBM] * 5,
    )
    y_near = lax.ppermute(y_near, "gy", near(gy))
    y_far = lax.ppermute(y_far, "gy", far(gy))
    x_near = lax.ppermute(x_near, "gx", near(gx))
    x_far = lax.ppermute(x_far, "gx", far(gx))
    yr, yl = jnp.where(even_y, y_near, y_far), jnp.where(even_y, y_far, y_near)
    half = STRIP // 2
    head = jnp.concatenate([yl[:half], yl[STRIP:], yr[:half], yr[STRIP:]])
    tail = jnp.concatenate([yl[half:], yr[half:]])
    c_near = lax.ppermute(jnp.where(even_x, tail, head), "gx", near(gx))
    c_far = lax.ppermute(jnp.where(even_x, head, tail), "gx", far(gx))
    copies, c_near = lax.optimization_barrier((copies, c_near))
    corner_r, corner_l = jnp.where(even_x, c_near, c_far), jnp.where(even_x, c_far, c_near)
    cores = [[x * gy + y for x in range(core, gx, 2) for y in range(gy)] for core in range(2)]
    blocks = copies.reshape(devices // 2, SHARE, 128)
    own = lax.all_to_all(blocks, ("gx", "gy"), 0, 0, axis_index_groups=cores).reshape(gx // 2, gy * SHARE, 128)
    level = lambda rows, n: [vm(NZ * rows, 128)] * n
    faces = lambda rows, tiles: vm(tiles * (NZ + 1) * rows, 128)
    rows3, rows4 = 2 * gx, gx
    size, tall = (NZ * TX, 128), ((NZ + 1) * TX, 128)
    k2 = call(
        window_kernel, "window_coeffs", [(NZ * TX * 4 + TX, 128)], [share2, x_near, x_far, yr, yl, corner_r, corner_l], level(TX, 7)
    )[0]
    big, big_z = (2 * NZ * 2 * TX, 128), (2 * (NZ + 1) * 2 * TX, 128)
    total0, total1 = 2 * (NZ * 6 + 1) * 2 * TX, (NZ * 6 + 1) * TX
    sends, saved = call(
        functools.partial(down_kernel, gx * TX, gy * TY),
        "down",
        [(devices // 2 * BLOCK, 128), (max(total0 + total1, SAVED_ROWS), 128)],
        [stack, yr, yl, corner_r, corner_l, x_near, x_far],
        [vm(*big)] * 10 + [vm(*big_z)] + level(TX, 10) + [faces(TX, 1)] + level(8, 10) + [faces(8, 1)] + [dma(12)],
        out_specs=[VMEM, ANY],
    )
    sends, own = lax.optimization_barrier((sends, own))
    other = lax.ppermute(own, "gx", near(gx))
    blocks = sends.reshape(devices // 2, BLOCK, 128)
    own_blocks = lax.all_to_all(blocks, ("gx", "gy"), 0, 0, axis_index_groups=cores)
    other_blocks = lax.ppermute(own_blocks, "gx", near(gx))
    whole = call(
        functools.partial(global_kernel, gx, gy),
        "global_coeffs",
        [(5 * NZ * (rows3 + rows4), 128)],
        [own, other],
        level(rows3, 6) + [faces(rows3, 1)] + level(rows3, 1) + level(rows4, 6) + [faces(rows4, 1)] + level(rows4, 1)
        + [vm(gx // 2, 2, gy * SHARE, 128), dma(2)],
        in_specs=[ANY] * 2,
    )[0]
    field, residual = call(
        functools.partial(up_kernel, gx, gy),
        "up",
        [(NZ * TX, TY)] * 2,
        [own_blocks, other_blocks, whole, k2, stack, saved],
        [vm(total0, 128), vm(total1, 128)] + level(TX, 3) + [vm(NZ * 2 * TX, 128), vm(*size), vm(*big), vm(*big)]
        + level(rows3, 3) + level(rows4, 2) + [vm(7 * HALF * rows4, 128), dma(2)],
        in_specs=[VMEM] * 5 + [ANY],
    )
    return field.reshape(right_side.shape), residual.reshape(right_side.shape)


def solution(mesh):
    spec = P(None, "gx", "gy")
    fits = (mesh.shape["gx"], mesh.shape["gy"]) == (8, 4)
    plan = body if fits else spread_body
    return jax.shard_map(plan, mesh=mesh, in_specs=(spec,) * 5, out_specs=(spec, spec), check_vma=False)
```

```python
import functools

import jax
import jax.numpy as jnp
from jax import lax
from jax.experimental import pallas as pl
from jax.experimental.pallas import tpu as pltpu
from jax.sharding import PartitionSpec as P

LEVELS = 4
COARSE_SWEEPS = 16


OMEGA = 0.8


def with_halo(cells, sides, width):
    for axis, dim in sides:
        count = lax.axis_size(axis)
        ends = count - 1
        head = lax.slice_in_dim(cells, 0, width, axis=dim)
        tail = lax.slice_in_dim(cells, cells.shape[dim] - width, cells.shape[dim], axis=dim)
        cells = jnp.concatenate(
            [
                lax.ppermute(tail, axis, [(i, (i + 1) % count) for i in range(ends)]),
                cells,
                lax.ppermute(head, axis, [((i + 1) % count, i) for i in range(ends)]),
            ],
            axis=dim,
        )
    return cells


def apply_op(field, padded, coeffs):
    kappa, x_up, x_low, y_up, y_low, z_up, z_low = coeffs
    zpad = jnp.pad(field, ((1, 1), (0, 0), (0, 0)))
    out = (
        kappa * field
        + x_up * (field - padded[:, 2:, 1:-1])
        + x_low * (field - padded[:, :-2, 1:-1])
    )
    out = out + y_up * (field - padded[:, 1:-1, 2:]) + y_low * (field - padded[:, 1:-1, :-2])
    return out + z_up * (field - zpad[2:]) + z_low * (field - zpad[:-2])


def face_pad(field):
    return with_halo(field, (("gx", 1), ("gy", 2)), 1)


def line_factors(coeffs):
    kappa, x_up, x_low, y_up, y_low, z_up, z_low = coeffs
    diag = kappa + x_up + x_low + y_up + y_low + z_up + z_low
    upper_src = z_up.at[-1].set(jnp.zeros_like(z_up[-1]))

    def factor_step(upper_prev, planes):
        diag_k, low_k, up_k = planes
        inv = 1.0 / (diag_k + low_k * upper_prev)
        upper = -up_k * inv
        return (upper, (inv, upper))

    start = jnp.zeros_like(diag[0])
    unused, stacked = lax.scan(factor_step, start, (diag, z_low, upper_src), unroll=True)
    return stacked


def line_solve(rhs, factors, z_low):
    inverses, uppers = factors

    def forward_step(prev, planes):
        rhs_k, low_k, inv_k = planes
        value = (rhs_k + low_k * prev) * inv_k
        return (value, value)

    start = jnp.zeros_like(rhs[0])
    unused, forward = lax.scan(forward_step, start, (rhs, z_low, inverses), unroll=True)

    def back_step(after, planes):
        fwd_k, up_k = planes
        value = fwd_k - up_k * after
        return (value, value)

    unused, result = lax.scan(back_step, start, (forward, uppers), reverse=True, unroll=True)
    return result


def mean_four(field):
    depth, rows, cols = field.shape
    return field.reshape(depth, rows // 2, 2, cols // 2, 2).mean(axis=(2, 4))


def coarsen(coeffs):
    kappa, x_up, x_low, y_up, y_low, z_up, z_low = coeffs
    depth, rows, cols = kappa.shape
    shape = (depth, rows // 2, 2, cols // 2, 2)
    xu_c = x_up.reshape(shape)[:, :, 1].mean(axis=-1) * 0.25
    xl_c = x_low.reshape(shape)[:, :, 0].mean(axis=-1) * 0.25
    yu_c = y_up.reshape(shape)[:, :, :, :, 1].mean(axis=2) * 0.25
    yl_c = y_low.reshape(shape)[:, :, :, :, 0].mean(axis=2) * 0.25
    return (mean_four(kappa), xu_c, xl_c, yu_c, yl_c, mean_four(z_up), mean_four(z_low))


def prolong(padded):
    depth = padded.shape[0]
    rows = padded.shape[1] - 2
    cols = padded.shape[2] - 2
    centre = padded[:, 1:-1, :]
    even = 0.75 * centre + 0.25 * padded[:, :-2, :]
    odd = 0.75 * centre + 0.25 * padded[:, 2:, :]
    spread = jnp.stack([even, odd], axis=2).reshape(depth, 2 * rows, cols + 2)
    centre = spread[:, :, 1:-1]
    even = 0.75 * centre + 0.25 * spread[:, :, :-2]
    odd = 0.75 * centre + 0.25 * spread[:, :, 2:]
    return jnp.stack([even, odd], axis=3).reshape(depth, 2 * rows, 2 * cols)


def coarse_solve(rhs, coeffs):
    factors = line_factors(coeffs)
    field = OMEGA * line_solve(rhs, factors, coeffs[6])

    def spread_sweep(sweep, current):
        padded = with_halo(current, (("gx", 1), ("gy", 2)), 1)
        defect = rhs - apply_op(current, padded, coeffs)
        return current + OMEGA * line_solve(defect, factors, coeffs[6])

    field = lax.fori_loop(0, COARSE_SWEEPS - 1, spread_sweep, field)
    return field


def cycle(rhs, coeffs, level):
    if level == LEVELS:
        return coarse_solve(rhs, coeffs)
    factors = line_factors(coeffs)
    field = OMEGA * line_solve(rhs, factors, coeffs[6])
    padded = face_pad(field)
    defect = rhs - apply_op(field, padded, coeffs)
    correction = cycle(mean_four(defect), coarsen(coeffs), level + 1)
    rimmed = with_halo(correction, (("gx", 1), ("gy", 2)), 1)
    field = field + prolong(rimmed)
    padded = face_pad(field)
    defect = rhs - apply_op(field, padded, coeffs)
    return field + OMEGA * line_solve(defect, factors, coeffs[6])


def spread_body(right_side, kappa_sq, cond_x, cond_y, cond_z):
    padded_x = with_halo(cond_x, (("gx", 1),), 1)
    padded_y = with_halo(cond_y, (("gy", 2),), 1)
    padded_z = jnp.pad(cond_z, ((1, 1), (0, 0), (0, 0)))
    x_up = 0.5 * (cond_x + padded_x[:, 2:, :])
    x_low = 0.5 * (cond_x + padded_x[:, :-2, :])
    y_up = 0.5 * (cond_y + padded_y[:, :, 2:])
    y_low = 0.5 * (cond_y + padded_y[:, :, :-2])
    z_up = 0.5 * (cond_z + padded_z[2:])
    z_low = 0.5 * (cond_z + padded_z[:-2])
    coeffs = (kappa_sq, x_up, x_low, y_up, y_low, z_up, z_low)
    solution_field = cycle(right_side, coeffs, 0)
    residual = right_side - apply_op(solution_field, face_pad(solution_field), coeffs)
    return (solution_field, residual)


F32 = jnp.float32
BF16 = jnp.bfloat16
NZ = 32
HALF = NZ // 2
TX, TY = 16, 128
HALO = 8
SLAB = 5 * NZ * HALO
STRIP = 160
CORNER = 104
SHARE = 40
BLOCK = NZ + 8
VMEM = pl.BlockSpec(memory_space=pltpu.VMEM)
ANY = pl.BlockSpec(memory_space=pl.ANY)
HBM = pl.BlockSpec(memory_space=pltpu.HBM)


def iota(shape, dim):
    return lax.broadcasted_iota(jnp.int32, shape, dim)


def shift(x, by, axis):
    by = by % x.shape[axis]
    return pltpu.roll(x, by, axis) if by else x


def mix(x, weights, parts=2):
    pieces = []
    for n in range(parts):
        piece = x.astype(BF16)
        pieces.append(piece)
        if n < parts - 1:
            x = x - piece.astype(F32)
    out = jnp.dot(jnp.concatenate(pieces, axis=0), weights, preferred_element_type=F32)
    rows = x.shape[0]
    return sum(out[n * rows : (n + 1) * rows] for n in reversed(range(parts)))


def matrix(mask, weight=1.0):
    return jnp.where(mask, weight, 0.0).astype(BF16)


def span(start, size):
    if not isinstance(start, int):
        start = pl.multiple_of(start, 8)
    return pl.ds(start, size)


class Field:
    def __init__(self, ref, rows, tiles=1, planes=NZ, start=0):
        self.ref, self.rows, self.tiles, self.planes, self.start = ref, rows, tiles, planes, start

    def base(self, tile, k):
        return self.start + tile * self.planes * self.rows + k * self.rows

    def part(self, tile, k):
        return self.ref[span(self.base(tile, k), self.rows), :]

    def __getitem__(self, k):
        parts = [self.part(t, k) for t in range(self.tiles)]
        return parts[0] if self.tiles == 1 else jnp.concatenate(parts, axis=1)

    def __setitem__(self, k, value):
        for t in range(self.tiles):
            self.put(t, k, value[:, 128 * t : 128 * (t + 1)])

    def put(self, tile, k, value):
        self.ref[span(self.base(tile, k), self.rows), :] = value

    def every_second(self, at, count, odd):
        parts = []
        for t in range(self.tiles):
            first = self.base(t, 0) + 2 * at + odd
            parts.append(self.ref[pl.ds(first, count, stride=2), :])
        return parts[0] if self.tiles == 1 else jnp.concatenate(parts, axis=1)

    def row(self, row):
        return self.ref[pl.ds(self.start + row, self.planes, stride=self.rows), :]


def stack_fields(ref, rows, count, tiles=1, z_face=True, start=0):
    size = tiles * NZ * rows
    out = [Field(ref, rows, tiles, NZ, start + n * size) for n in range(count)]
    return out + [Field(ref, rows, tiles, NZ + 1, start + count * size)] if z_face else out


def loop(count, step, carry, unroll=None):
    if unroll is None or unroll >= count:
        for i in range(count):
            carry = step(i, carry)
        return carry
    return lax.fori_loop(0, count, step, carry, unroll=unroll)


def neighbours(field, x_face, y_face):
    out = x_face * shift(field, 1, 0) + shift(x_face * field, -1, 0)
    return out + (y_face * shift(field, 1, 1) + shift(y_face * field, -1, 1))


class Line:
    def __init__(self, inv, z_face):
        self.inv, self.z_face = inv, z_face

    def inward(self, k, upper):
        return self.z_face[k + 1 if upper else k] * self.inv[k]

    def outward(self, k, upper):
        return self.z_face[k if upper else k + 1] * self.inv[k]


class StoredLine:
    def __init__(self, inv, g, c):
        self.inv, self.g, self.c = inv, g, c

    def inward(self, k, upper):
        return self.g[k]

    def outward(self, k, upper):
        return self.c[k]


def sweep_in(rhs, line, keep, start, unroll):
    def step(i, carry):
        low, high = carry
        k, m = i, NZ - 1 - i
        low = rhs(k) * line.inv[k] + line.inward(k, False) * low
        high = rhs(m) * line.inv[m] + line.inward(m, True) * high
        keep[k] = low
        keep[m] = high
        return low, high

    return loop(HALF, step, (start, start), unroll)


def sweep_out(ends, kept, line, emit, unroll):
    low, high = ends
    a, b = line.outward(HALF - 1, False), line.outward(HALF, True)
    low = (low + a * high) * (1.0 / (1.0 - a * b))
    high = high + b * low

    def step(i, carry):
        low, high = carry
        k, m = HALF - 1 - i, HALF + i
        emit(k, low)
        emit(m, high)
        low = kept[k - 1] + line.outward(k - 1, False) * low
        high = kept[m + 1] + line.outward(m + 1, True) * high
        return low, high

    low, high = loop(HALF - 1, step, (low, high), unroll)
    emit(0, low)
    emit(NZ - 1, high)


def factor(diag, z_face, tiles, inv_out, unroll, rhs=None, keep=None, g_out=None, c_out=None):
    ends = []
    for t in range(tiles):
        zero = diag.part(t, 0) * 0.0

        def one(k, upper, before, last, prev):
            below, above = z_face.part(t, k), z_face.part(t, k + 1)
            inner, outer = (above, below) if upper else (below, above)
            minor = (diag.part(t, k) + below + above) * last - (inner * inner) * before
            inv = last * (1.0 / minor)
            inv_out.put(t, k, inv)
            if g_out is not None:
                g_out.put(t, k, inner * inv)
                c_out.put(t, k, outer * inv)
            if rhs is not None:
                prev = rhs.part(t, k) * inv + (inner * inv) * prev
                keep.put(t, k, prev)
            return last, minor, prev

        def step(i, carry):
            low, high = carry
            return one(i, False, *low), one(NZ - 1 - i, True, *high)

        start = (zero, zero + 1.0, zero)
        low, high = loop(HALF, step, (start, start), unroll)
        ends.append((low[2], high[2]))
    join = lambda n: ends[0][n] if tiles == 1 else jnp.concatenate([e[n] for e in ends], axis=1)
    return join(0), join(1)


def z_faces(cz, out, tiles=1):
    for t in range(tiles):
        before = None
        for k in range(NZ + 1):
            here = cz.part(t, k) if k < NZ else None
            both = here if before is None else before if here is None else here + before
            out.put(t, k, 0.5 * both)
            before = here


def base_diag(kappa, x_face, y_face):
    return kappa + (x_face + shift(x_face, -1, 0)) + (y_face + shift(y_face, -1, 1))


def window_mask(rows, lanes, tile_x, tile_y, halo, ix, iy, nx, ny):
    x, y = iota((rows, lanes), 0), iota((rows, lanes), 1)
    x = jnp.where(x < (rows + tile_x) // 2, x, x - rows)
    y = jnp.where(y < (lanes + tile_y) // 2, y, y - lanes)
    valid = (y >= -halo) & (y < tile_y + halo) & (x >= -halo) & (x < tile_x + halo)
    x, y = x + ix * tile_x, y + iy * tile_y
    return (valid & (x >= 0) & (x < nx) & (y >= 0) & (y < ny)).astype(F32)


def smooth_down(f, x_face, y_face, line, ends, kept, u, r, unroll):
    def emit(k, value):
        field = OMEGA * value
        u[k] = field
        r[k] = (1.0 - OMEGA) * f[k] + neighbours(field, x_face[k], y_face[k])

    sweep_out(ends, kept, line, emit, unroll)


def smooth_up(f, x_face, y_face, line, u, e, kept, mask, unroll):
    masked = (lambda v: v) if mask is None else (lambda v: v * mask)

    def rhs(k):
        field = masked(u[k] + e[k])
        u[k] = field
        return masked(f[k] + neighbours(field, x_face[k], y_face[k]))

    def emit(k, value):
        u[k] = (1.0 - OMEGA) * u[k] + OMEGA * value

    zero = jnp.zeros((u.rows, 128 * u.tiles), F32)
    ends = sweep_in(rhs, line, kept, zero, unroll)
    sweep_out(ends, kept, line, emit, unroll)


def spread_rows(cells, before, after, dest, size):
    dest[pl.ds(0, size, stride=2), :] = (0.75 * cells + 0.25 * before).reshape(size, 128)
    dest[pl.ds(1, size, stride=2), :] = (0.75 * cells + 0.25 * after).reshape(size, 128)


def spread_matrix(fine, base, coarse_count, circular=False):
    j = iota((128, fine.shape[1]), 0) + base
    parent = (fine + 2048) // 2 - 1024
    partner = parent + 2 * ((fine + 2048) % 2) - 1
    if circular:
        j, parent, partner = j % 128, parent % 128, partner % 128
    weights = jnp.where(j == parent, 0.75, jnp.where(j == partner, 0.25, 0.0))
    if not circular:
        inside = (j >= 0) & (j < coarse_count) & (fine >= 0) & (fine < 2 * coarse_count)
        weights = jnp.where(inside, weights, 0.0)
    return weights.astype(BF16)


def lane_group(rows, width):
    return iota((rows, 128), 1) // width


def fold_planes(cells, turn):
    group = lane_group(8, 32)
    out = cells[:8]
    for n in range(1, 4):
        out = jnp.where(group == n, cells[8 * n : 8 * n + 8], out)
    return pltpu.roll(out, turn, 1)


def share_blocks(kinds):
    iy = lax.axis_index("gy")
    y, lane = iota((128, 128), 0), iota((128, 128), 1)
    x_in, y_in = y // 32, y % 32
    x_out, y_out = lane % 32 // 16, lane % 16
    pair_y, pair_x = y_in // 2 == y_out, x_in // 2 == x_out
    a, b, c, d, kappa, cz = kinds
    eighth = lambda mask: matrix(mask, 0.125)
    blocks = [
        mix(a, eighth(pair_y & (x_in == 2 * x_out))) + mix(b, eighth(pair_y & (x_in == 1) & (x_out == 1))),
        mix(b, eighth(pair_y & (x_in == 3) & (x_out == 0)))
        + mix(d, eighth((x_out == 1) & (y_in == 31) & (x_in // 2 == y_out))),
        mix(c, eighth(pair_x & (y_in == 2 * y_out))) + mix(d, eighth(pair_x & (y_in == 2 * y_out - 1))),
        mix(kappa, matrix(pair_x & pair_y, 0.25)),
        mix(cz, matrix(pair_x & pair_y, 0.25)),
    ]
    return [fold_planes(cells, 16 * iy) for cells in blocks]


def fetch_all(sources, dests, sems, first=0):
    copies = [pltpu.make_async_copy(a, b, sems.at[first + n]) for n, (a, b) in enumerate(zip(sources, dests))]
    for copy in copies:
        copy.start()
    return copies


def pack_kernel(devices, f_in, kappa_in, cx_in, cy_in, cz_in, x_near, x_far, y_near, y_far, share2, stack, copies, sems):
    even_x, even_y = lax.axis_index("gx") % 2 == 0, lax.axis_index("gy") % 2 == 0
    tiles = [stack.at[pl.ds(a * NZ * TX, NZ * TX), :] for a in range(5)]
    for copy in fetch_all((f_in, kappa_in, cx_in, cy_in, cz_in), tiles, sems):
        copy.wait()
    f, kappa, cx, cy, cz = tiles
    for a, ref in enumerate(tiles):
        cells = ref[...].reshape(NZ, TX, TY)
        at = pl.ds(a * NZ * HALO, NZ * HALO)
        head = cells[:, :HALO].reshape(NZ * HALO, TY)
        tail = cells[:, TX - HALO :].reshape(NZ * HALO, TY)
        x_near[at, :] = jnp.where(even_x, tail, head)
        x_far[at, :] = jnp.where(even_x, head, tail)
    y, lane = iota((128, 128), 0), iota((128, 128), 1)
    fourth = y // 4 == lane % 32
    rows = lambda ref: [Field(ref, TX).row(r) for r in range(TX)]
    cx_rows, cy_rows, kappa_rows, cz_rows = rows(cx), rows(cy), rows(kappa), rows(cz)
    totals = lambda v: [(v[4 * i] + v[4 * i + 1]) + (v[4 * i + 2] + v[4 * i + 3]) for i in range(4)]
    stack = [cx_rows[4 * i] for i in range(4)] + [cx_rows[4 * i + 3] for i in range(4)]
    stack = mix(jnp.concatenate(stack + totals(kappa_rows) + totals(cz_rows), axis=0), matrix(fourth))
    ends = [matrix(fourth & (y % 4 == 0)), matrix(fourth & (y % 4 == 3))]
    sides = mix(jnp.concatenate(totals(cy_rows), axis=0), jnp.concatenate(ends, axis=1))
    group = lane_group(NZ, 32)

    def merge(cells, scale):
        out = cells[:NZ]
        for xi in range(1, 4):
            out = jnp.where(group == xi, cells[NZ * xi : NZ * (xi + 1)], out)
        return out * scale

    kinds = [merge(stack[:128], 1 / 128), merge(stack[128:256], 1 / 128)]
    kinds += [merge(sides[:, :128], 1 / 128), merge(sides[:, 128:], 1 / 128)]
    kinds += [merge(stack[256:384], 1 / 16), merge(stack[384:], 1 / 16)]
    for t, cells in enumerate(share_blocks(kinds)):
        for n in range(devices):
            copies[pl.ds(n * SHARE + 8 * t, 8), :] = cells
    head = [jnp.zeros((8, 128), F32)] * 3
    tail = [jnp.zeros((8, 128), F32)] * 3
    slot = iota((8, 128), 1) % 32 // 4
    for t, cells in enumerate(kinds):
        for dest, first in ((share2, 0), (x_near, SLAB), (x_far, SLAB)):
            dest[pl.ds(first + t * NZ, NZ), :] = cells
        for zv in range(4):
            n = 4 * t + zv
            piece = cells[8 * zv : 8 * zv + 8]
            head[n // 8] = jnp.where(slot == n % 8, shift(piece, 4 * (n % 8), 1), head[n // 8])
            tail[n // 8] = jnp.where(slot == n % 8, shift(piece, 4 * (n % 8) + 4, 1), tail[n // 8])
    for n in range(3):
        y_near[pl.ds(STRIP + 8 * n, 8), :] = jnp.where(even_y, tail[n], head[n])
        y_far[pl.ds(STRIP + 8 * n, 8), :] = jnp.where(even_y, head[n], tail[n])

    group = lane_group(8, 8)
    for a, ref in enumerate((f, kappa, cx, cy, cz)):
        for half in range(2):
            for zo in range(2):
                head = jnp.zeros((8, 128), F32)
                tail = jnp.zeros((8, 128), F32)
                for zi in range(16):
                    cells = ref[pl.ds((zo * 16 + zi) * TX + 8 * half, 8), :]
                    cells = shift(cells, 8 * zi, 1)
                    head = jnp.where(group == zi, cells, head)
                    tail = jnp.where(group == (zi - 1) % 16, cells, tail)
                at = pl.ds(((half * 5 + a) * 2 + zo) * 8, 8)
                y_near[at, :] = jnp.where(even_y, tail, head)
                y_far[at, :] = jnp.where(even_y, head, tail)


def window2(tile, after, before, dest, first, iy, gy):
    lane = iota((NZ, 128), 1)
    first_after, first_before = jnp.where(iy < gy - 1, 36, 0), jnp.where(iy > 0, 124, 128)
    for xi in range(4):
        turned = (lane - 32 * xi + 128) % 128
        cells = jnp.where(turned < 32, tile, jnp.where(turned < first_after, after, jnp.where(turned >= first_before, before, 0.0)))
        dest[pl.ds(first + xi, NZ, stride=TX), :] = shift(cells, -32 * xi, 1)


def window_kernel(share2, x_near, x_far, yr, yl, cr, cl, out, a, b, c, d, kappa, cz, diag):
    ix, iy = lax.axis_index("gx"), lax.axis_index("gy")
    gy = lax.axis_size("gy")
    nx, ny = lax.axis_size("gx") * 4, gy * 32
    refs = (a, b, c, d, kappa, cz)

    def unpack(ref, first, t, turn):
        pieces = []
        for zv in range(4):
            n = 4 * t + zv
            pieces.append(shift(ref[span(first + 8 * (n // 8), 8), :], turn - 4 * (n % 8), 1))
        return jnp.concatenate(pieces, axis=0)

    near, far = STRIP // 2, CORNER + STRIP // 2
    even_x = ix % 2 == 0
    for t, dest in enumerate(refs):
        beside = x_near[pl.ds(SLAB + t * NZ, NZ), :], x_far[pl.ds(SLAB + t * NZ, NZ), :]
        for first, cells, right, left, r_at, l_at in (
            (0, share2[pl.ds(t * NZ, NZ), :], yr, yl, STRIP, STRIP),
            (4, jnp.where(even_x, *beside), cr, cr, far, near),
            (12, jnp.where(even_x, *beside[::-1]), cl, cl, far, near),
        ):
            window2(cells, unpack(right, r_at, t, 32), unpack(left, l_at, t, 92), dest, first, iy, gy)
        for x in range(8, 12):
            dest[pl.ds(x, NZ, stride=TX), :] = jnp.zeros((NZ, 128), F32)
    mask = window_mask(TX, 128, 4, 32, 4, ix, iy, nx, ny)
    a, b, c, d, kappa, cz, diag = (Field(ref, TX) for ref in (*refs, diag))
    x_face, y_face, inv, z_face = stack_fields(out, TX, 3)
    for k in range(NZ):
        x_k = a[k] + shift(b[k], 1, 0)
        y_k = c[k] + shift(d[k], 1, 1)
        x_face[k] = x_k
        y_face[k] = y_k
        diag[k] = base_diag(jnp.where(mask > 0, kappa[k], 1.0), x_k, y_k)
    z_faces(cz, z_face)
    factor(diag, z_face, 1, inv, None)


def assemble3(block, dest, gx, gy, rows):
    group = lane_group(8, 16)
    for ix in range(gx):
        blocks = [block(ix, iy) for iy in range(gy)]
        for zo in range(4):
            for xi in range(2):
                q = 2 * zo + xi
                cells = blocks[0]
                for iy in range(1, gy):
                    cells = jnp.where(group == (iy + q) % 8, blocks[iy], cells)
                dest[pl.ds(8 * zo * rows + 2 * ix + xi, 8, stride=rows), :] = shift(cells, -16 * q, 1)


def global_kernel(gx, gy, own, other, *refs):
    out, raw3, raw4, shares, sems = refs[0], refs[1:9], refs[9:17], refs[17], refs[18]
    outs3 = stack_fields(out, 2 * gx, 5, z_face=False)
    outs4 = stack_fields(out, gx, 5, z_face=False, start=5 * NZ * 2 * gx)
    core = lax.axis_index("gx") % 2
    copies = [
        pltpu.make_async_copy(own, shares.at[:, core], sems.at[0]),
        pltpu.make_async_copy(other, shares.at[:, 1 - core], sems.at[1]),
    ]
    for copy in copies:
        copy.start()
    for copy in copies:
        copy.wait()
    rows, cols = 2 * gx, 16 * gy
    for t, n in enumerate((0, 1, 2, 4, 5)):
        block = lambda jx, jy: shares[jx // 2, jx % 2, pl.ds(jy * SHARE + 8 * t, 8), :]
        assemble3(block, raw3[n], gx, gy, rows)
    xl, xu, yl, yu = (Field(ref, rows) for ref in raw3[:4])
    x, y = iota((rows, 128), 0), iota((rows, 128), 1)
    odd_row, inside = x % 2 == 1, y < cols
    for k in range(NZ):
        half = jnp.where(inside, xu[k], 0.0)
        below = jnp.where(odd_row | (x < 2), 0.0, shift(half, 2, 0))
        x_k = jnp.where(inside, xl[k] + below, 0.0)
        xl[k] = x_k
        xu[k] = jnp.where(x == rows - 1, shift(half, 1, 0), shift(x_k, -1, 0))
        next_row = shift(half, -1, 0)
        below = jnp.where(odd_row, shift(half, 15, 1), shift(next_row, 16, 1))
        y_k = jnp.where(inside, yl[k] + jnp.where((y % 16 == 0) & (y > 0), below, 0.0), 0.0)
        yl[k] = y_k
        above = jnp.where(odd_row, shift(half, 14, 1), shift(next_row, 15, 1))
        yu[k] = jnp.where(y == cols - 1, above, jnp.where(inside, shift(y_k, -1, 1), 0.0))
    yy, jj = iota((128, 128), 0), iota((128, 128), 1)
    keep = yy // 2 == jj
    pair, even, odd = matrix(keep), matrix(keep & (yy % 2 == 0)), matrix(keep & (yy % 2 == 1))
    size = NZ * rows // 2
    lows = [Field(ref, rows) for ref in raw3]
    first = lambda n: lows[n].every_second(0, size, 0)
    second = lambda n: lows[n].every_second(0, size, 1)
    raw4[0][...] = 0.125 * mix(first(0), pair)
    raw4[1][...] = 0.125 * mix(second(1), pair)
    raw4[2][...] = 0.125 * mix(first(2) + second(2), even)
    raw4[3][...] = 0.125 * mix(first(3) + second(3), odd)
    raw4[4][...] = 0.25 * mix(first(4) + second(4), pair)
    raw4[5][...] = 0.25 * mix(first(5) + second(5), pair)
    for raw, outs in ((raw3, outs3), (raw4, outs4)):
        x, y = iota((rows, 128), 0), iota((rows, 128), 1)
        xl, xu, yl, yu, kappa, cz = (Field(ref, rows) for ref in raw[:6])
        z_face, diag = Field(raw[6], rows, 1, NZ + 1), Field(raw[7], rows)
        x_face, y_face, inv, g, c = outs
        inside_x, inside_y = (x > 0).astype(F32), ((y > 0) & (y < cols)).astype(F32)
        for k in range(NZ):
            xl_k, yl_k = xl[k], yl[k]
            diag[k] = jnp.where(y < cols, kappa[k], 1.0) + (xl_k + xu[k]) + (yl_k + yu[k])
            x_face[k] = xl_k * inside_x
            y_face[k] = yl_k * inside_y
        z_faces(cz, z_face)
        factor(diag, z_face, 1, inv, None, g_out=g, c_out=c)
        rows, cols = rows // 2, cols // 2


def down_kernel(nx, ny, *refs):
    stack, yr, yl, corner_r, corner_l, x_near, x_far = refs[:7]
    sends, saved = refs[7:9]
    scratch = list(refs[9:-1])
    sems = refs[-1]
    take = lambda n: [scratch.pop(0) for _ in range(n)]
    ix, iy = lax.axis_index("gx"), lax.axis_index("gy")
    gx, gy = lax.axis_size("gx"), lax.axis_size("gy")
    f, kappa, cx, cy, cz = (stack.at[pl.ds(a * NZ * TX, NZ * TX), :] for a in range(5))
    even_x = ix % 2 == 0
    rows, tiles = 2 * TX, 2
    whole = take(11)
    names = [Field(ref, rows, tiles) for ref in whole[:10]]
    x_face, y_face, inv, u, f0, kappa0, cz0, diag, kept, r = names
    z_face = Field(whole[10], rows, tiles, NZ + 1)
    group = lane_group(8, 8)

    def window(a, tile, z, after, before, turn):
        zo = z // 16
        slab = span(a * NZ * HALO + z * HALO, HALO)
        near, far = x_near[slab, :], x_far[slab, :]
        sides = [jnp.where(even_x, near, far), jnp.where(even_x, far, near)]
        main = jnp.concatenate([tile[span(z * TX, TX), :], *sides], axis=0)
        at = lambda first: span(first + (a * 2 + zo) * 8, 8)
        half = STRIP // 2
        sides = []
        for right, left in (
            (yr[at(0), :], yl[at(0), :]),
            (yr[at(half), :], yl[at(half), :]),
            (corner_r[at(CORNER), :], corner_r[at(0), :]),
            (corner_l[at(CORNER), :], corner_l[at(0), :]),
        ):
            cells = jnp.where(after, right, jnp.where(before, left, 0.0))
            sides.append(pltpu.roll(cells, turn, 1))
        return jnp.concatenate([main, jnp.concatenate(sides, axis=0)], axis=1)

    mask0 = window_mask(rows, 256, TX, TY, HALO, ix, iy, nx, ny)

    def prepare(z, cz_prev):
        zi = z % 16
        after, before = group == zi, group == (zi + 15) % 16
        turn = (128 - 8 * zi) % 128
        f_k, kappa_k, cx_k, cy_k, cz_k = (
            window(a, tile, z, after, before, turn) for a, tile in enumerate((f, kappa, cx, cy, cz))
        )
        f0[z] = f_k
        kappa0[z] = kappa_k
        cz0[z] = cz_k
        z_face[z] = 0.5 * (cz_k + cz_prev)
        x_k, y_k = 0.5 * (cx_k + shift(cx_k, 1, 0)), 0.5 * (cy_k + shift(cy_k, 1, 1))
        x_face[z] = x_k
        y_face[z] = y_k
        diag[z] = base_diag(jnp.where(mask0 > 0, kappa_k, 1.0), x_k, y_k)
        return cz_k

    last = loop(NZ, prepare, jnp.zeros((rows, 256), F32), 4)
    z_face[NZ] = 0.5 * last
    ends = factor(diag, z_face, tiles, inv, 8, f0, kept)
    copies = []

    def save(field):
        at = sum(copy[1] for copy in copies)
        count = field.ref.shape[0]
        copy = pltpu.make_async_copy(field.ref, saved.at[pl.ds(at, count), :], sems.at[len(copies)])
        copy.start()
        copies.append((copy, count))

    for field in (x_face, y_face, inv, f0):
        save(field)
    smooth_down(f0, x_face, y_face, Line(inv, z_face), ends, kept, u, r, 5)
    save(u)
    save(z_face)

    fine = (r, kappa0, cz0, x_face, y_face)
    lanes, tile_x, tile_y, halo = 256, TX, TY, HALO
    for level in (1, 2):
        rows, tile_x, tile_y, halo = rows // 2, tile_x // 2, tile_y // 2, halo // 2
        nx, ny = nx // 2, ny // 2
        whole = take(11)
        names = [Field(ref, rows) for ref in whole[:10]]
        x_face, y_face, inv, u, f1, kappa1, cz1, diag, kept, r = names
        z_face = Field(whole[10], rows, 1, NZ + 1)
        mask = window_mask(rows, 128, tile_x, tile_y, halo, ix, iy, nx, ny)
        y, j = iota((lanes, 128), 0), iota((lanes, 128), 1)
        if lanes == 128:
            j = jnp.where(j < 48, j, jnp.where(j >= 80, j - 64, -1))
        pair = matrix(y // 2 == j)
        even = (iota((1, lanes), 1) % 2 == 0).astype(F32)
        part = 128
        for at in range(0, NZ * rows, part):
            here = pl.ds(at, part)
            both = lambda n: fine[n].every_second(at, part, 0) + fine[n].every_second(at, part, 1)
            below = fine[3].every_second(at, part, 0)
            out = mix(jnp.concatenate([both(0), both(1), both(2), below, both(4) * even], axis=0), pair)
            for n, (dest, weight) in enumerate(((f1, 0.25), (kappa1, 0.25), (cz1, 0.25), (x_face, 0.125), (y_face, 0.125))):
                dest.ref[here, :] = weight * out[n * part : (n + 1) * part]
        for k in range(NZ):
            f1[k] = f1[k] * mask
            diag[k] = base_diag(jnp.where(mask > 0, kappa1[k], 1.0), x_face[k], y_face[k])
        z_faces(cz1, z_face)
        ends = factor(diag, z_face, 1, inv, None, f1, kept)
        smooth_down(f1, x_face, y_face, Line(inv, z_face), ends, kept, u, r, None)
        if level == 1:
            for field in (x_face, y_face, inv, f1, u, z_face):
                save(field)
        fine, lanes = (r, kappa1, cz1, x_face, y_face), 128

    group = lane_group(NZ, 32)
    out = f1.row(0)
    for xi in range(1, 4):
        out = jnp.where(group == xi, shift(f1.row(xi), 32 * xi, 1), out)
    for n in range(gx * gy // 2):
        sends[pl.ds(n * BLOCK, NZ), :] = out
    y, lane = iota((128, 128), 0), iota((128, 128), 1)
    total = jnp.zeros((NZ, 128), F32)
    for xi in range(2):
        place = (lane % 32 // 16 == xi) & (y // 2 == lane % 16) & (y < 32)
        total = total + mix(r.row(2 * xi) + r.row(2 * xi + 1), matrix(place, 0.25))
    total = fold_planes(total, 16 * iy)
    for n in range(gx * gy // 2):
        sends[pl.ds(n * BLOCK + NZ, 8), :] = total
    for copy, _ in copies:
        copy.wait()


def up_kernel(gx, gy, *refs):
    own, other, whole, k2, stack, saved, solution_out, residual_out = refs[:8]
    scratch = list(refs[8:-1])
    sems = refs[-1]
    take = lambda n: [scratch.pop(0) for _ in range(n)]
    ix, iy = lax.axis_index("gx"), lax.axis_index("gy")
    held0, held1 = take(2)
    split = held0.shape[0]
    parts = [saved.at[pl.ds(split, held1.shape[0]), :], saved.at[pl.ds(0, split), :]]
    fetched = fetch_all(parts, (held1, held0), sems)
    core = ix % 2

    def gathered(jx, jy, at):
        if isinstance(jx, int):
            same = core == jx % 2
            return jnp.where(same, own[jx // 2 * gy + jy, at, :], other[jx // 2 * gy + jy, at, :])
        return jx[1][jx[0] // 2 * gy + jy, at, :]
    f2, u2, kept2, wide, e_ref, e0_ref, kept0, u3, f3, r3, f4, u4 = take(12)

    rows, cols = 2 * gx, 16 * gy
    assemble3(lambda jx, jy: gathered(jx, jy, pl.ds(NZ, 8)), f3, gx, gy, rows)
    f3, u3, r3 = (Field(ref, rows) for ref in (f3, u3, r3))
    y = iota((rows, 128), 1)
    x_face3, y_face3, inv3, g3, c3 = stack_fields(whole, rows, 5, z_face=False)
    line3 = StoredLine(inv3, g3, c3)
    clean = (y < cols).astype(F32)
    for k in range(NZ):
        f3[k] = f3[k] * clean
    zero = jnp.zeros((rows, 128), F32)
    ends = sweep_in(lambda k: f3[k], line3, r3, zero, None)
    smooth_down(f3, x_face3, y_face3, line3, ends, r3, u3, Field(e_ref, rows), None)
    fine = Field(e_ref, rows)
    rows, cols = rows // 2, cols // 2
    size = NZ * rows
    yy, jj = iota((128, 128), 0), iota((128, 128), 1)
    f4[...] = 0.25 * mix(fine.every_second(0, size, 0) + fine.every_second(0, size, 1), matrix(yy // 2 == jj))
    f4, u4 = Field(f4, rows), Field(u4, rows)
    x_face4, y_face4, inv4, g4, c4 = stack_fields(whole, rows, 5, z_face=False, start=5 * NZ * 2 * rows)
    line4 = StoredLine(inv4, g4, c4)
    zero = jnp.zeros((rows, 128), F32)

    def solve4(rhs, old):
        kept, out = {}, {}
        ends = sweep_in(rhs, line4, kept, zero, None)

        def emit(k, value):
            out[k] = OMEGA * value if old is None else (1.0 - OMEGA) * old[k] + OMEGA * value

        sweep_out(ends, kept, line4, emit, None)
        for k in range(NZ):
            u4[k] = out[k]

    solve4(lambda k: f4[k], None)

    def relax(sweep, carry):
        old = [u4[k] for k in range(NZ)]
        solve4(lambda k: f4[k] + neighbours(old[k], x_face4[k], y_face4[k]), old)
        return carry

    lax.fori_loop(0, COARSE_SWEEPS - 1, relax, 0)

    cells = u4.ref[...].reshape(NZ, rows, 128)
    x = iota((1, rows, 128), 1)
    before = jnp.where(x > 0, shift(cells, 1, 1), 0.0)
    after = jnp.where(x < rows - 1, shift(cells, -1, 1), 0.0)
    spread_rows(cells, before, after, wide, size)
    e_ref[...] = mix(wide[pl.ds(0, 2 * size), :], spread_matrix(iota((128, 128), 1), 0, cols))
    rows, cols = 2 * rows, 2 * cols
    smooth_up(f3, x_face3, y_face3, line3, u3, Field(e_ref, rows), r3, None, None)

    def block(dx, dy):
        inside = ((ix + dx >= 0) & (ix + dx < gx)).astype(F32)
        jx, jy = jnp.clip(ix + dx, 0, gx - 1), jnp.clip(iy + dy, 0, gy - 1)
        return gathered((jx, other if dx else own), jy, pl.ds(0, NZ)) * inside

    for first, dx in ((0, 0), (4, 1), (12, -1)):
        window2(block(dx, 0), shift(block(dx, 1), 32, 1), shift(block(dx, -1), 96, 1), f2, first, iy, gy)
    for x in range(8, 12):
        f2[pl.ds(x, NZ, stride=TX), :] = jnp.zeros((NZ, 128), F32)
    f2, u2, kept2 = (Field(ref, TX) for ref in (f2, u2, kept2))
    x_face2, y_face2, inv2, z_face2 = stack_fields(k2, TX, 3)
    line2 = Line(inv2, z_face2)
    zero = jnp.zeros((TX, 128), F32)
    ends = sweep_in(lambda k: f2[k], line2, kept2, zero, None)

    def emit2(k, value):
        u2[k] = OMEGA * value

    sweep_out(ends, kept2, line2, emit2, None)

    cells = pltpu.roll(u3.ref[...].reshape(NZ, rows, 128), (rows - 2 * ix) % rows, 1)
    x = iota((1, rows, 128), 1)
    place = 2 * ix + jnp.where(x < rows // 2, x, x - rows)
    cells = jnp.where((place >= 0) & (place < rows), cells, 0.0)
    ring = lambda v, first: jnp.where(iota((1, 8, 128), 1) < first, v[:, :8], v[:, rows - 8 :])
    spread_rows(ring(cells, 4), ring(shift(cells, 1, 1), 4), ring(shift(cells, -1, 1), 4), wide, NZ * 8)
    lane = iota((128, 128), 1)
    fine_y = jnp.where(lane < 80, lane, lane - 128) + 32 * iy
    e_ref[...] = mix(wide[pl.ds(0, NZ * TX), :], spread_matrix(fine_y, 0, cols))
    mask2 = window_mask(TX, 128, 4, 32, 4, ix, iy, 4 * gx, 32 * gy)
    smooth_up(f2, x_face2, y_face2, line2, u2, Field(e_ref, TX), kept2, mask2, None)

    cells = u2.ref[...].reshape(NZ, TX, 128)
    ring = lambda v: jnp.where(iota((1, 8, 128), 1) < 6, v[:, :8], v[:, 8:])
    spread_rows(ring(cells), ring(shift(cells, 1, 1)), ring(shift(cells, -1, 1)), wide, NZ * 8)
    fine_y = jnp.where(lane < 96, lane, lane - 128)
    e_ref[...] = mix(wide[pl.ds(0, NZ * TX), :], spread_matrix(fine_y, 0, 0, circular=True))
    fetched[0].wait()
    x_face1, y_face1, inv1, f1, u1, z_face1 = stack_fields(held1, TX, 5)
    line1 = Line(inv1, z_face1)
    mask1 = window_mask(TX, 128, 8, 64, 4, ix, iy, 8 * gx, 64 * gy)
    smooth_up(f1, x_face1, y_face1, line1, u1, Field(e_ref, TX), kept2, mask1, None)

    cells = held1[pl.ds(u1.start, NZ * TX), :].reshape(NZ, TX, 128)
    spread_rows(cells, shift(cells, 1, 1), shift(cells, -1, 1), wide, NZ * TX)
    rows = 2 * TX
    weights = spread_matrix(iota((128, 256), 1), 0, 0, circular=True)
    e0 = Field(e0_ref, rows, 2)
    for k in range(0, NZ, 8):
        cells = mix(wide[pl.ds(k * rows, 8 * rows), :], weights)
        for t in range(2):
            e0_ref[pl.ds(e0.base(t, k), 8 * rows), :] = cells[:, 128 * t : 128 * (t + 1)]
    fetched[1].wait()
    x_face0, y_face0, inv0, f0, u0, z_face0 = stack_fields(held0, rows, 5, 2)
    mask0 = window_mask(rows, 256, TX, TY, HALO, ix, iy, TX * gx, TY * gy)
    smooth_up(f0, x_face0, y_face0, Line(inv0, z_face0), u0, e0, Field(kept0, rows, 2), mask0, 4)

    kappa = Field(stack, TX, start=NZ * TX)

    def residual(k, carry):
        below, flux_z = carry
        column = u0.part(0, k)
        here = column[:TX]
        flux_x = (x_face0.part(0, k) * (column - shift(column, 1, 0)))[: TX + 8]
        row = u0[k][:TX]
        flux_y = y_face0[k][:TX] * (row - shift(row, 1, 1))
        side = (flux_x - shift(flux_x, -1, 0))[:TX] + (flux_y - shift(flux_y, -1, 1))[:, :TY]
        above = u0.part(0, k + 1)[:TX] if k is not NZ - 1 else jnp.zeros((TX, TY), F32)
        flux_up = z_face0.part(0, k + 1)[:TX] * (above - here)
        solution_out[span(k * TX, TX), :] = here
        out = f0.part(0, k)[:TX] - kappa[k] * here - side - flux_z + flux_up
        residual_out[span(k * TX, TX), :] = out
        return here, flux_up

    start = z_face0.part(0, 0)[:TX] * u0.part(0, 0)[:TX]
    carry = loop(NZ - 1, residual, (start, start), 4)
    residual(NZ - 1, carry)


SAVED_ROWS = 72 * 1024
MEBIBYTES = {"pack": 56}
COSTS = {
    "pack": 3 * 10**9, "down": 10**10,
    "window_coeffs": 4 * 10**9, "global_coeffs": 4 * 10**9, "up": 12 * 10**9,
}


def call(kernel, name, outs, ins, scratch=(), in_specs=None, out_specs=None, aliases=None):
    shapes = [jax.ShapeDtypeStruct(s, F32) for s in outs]
    return pl.pallas_call(
        kernel,
        name=name,
        out_shape=shapes,
        in_specs=in_specs or [VMEM] * len(ins),
        out_specs=out_specs or [VMEM] * len(outs),
        scratch_shapes=list(scratch),
        input_output_aliases=aliases or {},
        compiler_params=pltpu.CompilerParams(vmem_limit_bytes=MEBIBYTES.get(name, 32) * 1024 * 1024),
        cost_estimate=pl.CostEstimate(flops=COSTS[name], bytes_accessed=4 * sum(x.size for x in ins), transcendentals=0),
    )(*ins)


def body(right_side, kappa_sq, cond_x, cond_y, cond_z):
    gx, gy = lax.axis_size("gx"), lax.axis_size("gy")
    tiles = [v.reshape(NZ * TX, TY) for v in (right_side, kappa_sq, cond_x, cond_y, cond_z)]
    slab, strip = (SLAB + 6 * NZ, 128), (STRIP + 24, 128)
    vm = lambda *shape: pltpu.VMEM(shape, F32)
    dma = lambda n: pltpu.SemaphoreType.DMA((n,))
    devices = gx * gy
    near = lambda n: [(i, i ^ 1) for i in range(n)]
    far = lambda n: [(i, (i + 1 ^ 1) - 1) for i in range(1, n - 1)]
    even_x, even_y = lax.axis_index("gx") % 2 == 0, lax.axis_index("gy") % 2 == 0
    x_near, x_far, y_near, y_far, share2, stack, copies = call(
        functools.partial(pack_kernel, devices // 2),
        "pack",
        [slab, slab, strip, strip, (6 * NZ, 128), (5 * NZ * TX, TY), (devices // 2 * SHARE, 128)],
        tiles,
        [dma(5)],
        [HBM] * 5,
    )
    y_near = lax.ppermute(y_near, "gy", near(gy))
    y_far = lax.ppermute(y_far, "gy", far(gy))
    x_near = lax.ppermute(x_near, "gx", near(gx))
    x_far = lax.ppermute(x_far, "gx", far(gx))
    yr, yl = jnp.where(even_y, y_near, y_far), jnp.where(even_y, y_far, y_near)
    half = STRIP // 2
    head = jnp.concatenate([yl[:half], yl[STRIP:], yr[:half], yr[STRIP:]])
    tail = jnp.concatenate([yl[half:], yr[half:]])
    c_near = lax.ppermute(jnp.where(even_x, tail, head), "gx", near(gx))
    c_far = lax.ppermute(jnp.where(even_x, head, tail), "gx", far(gx))
    copies, c_near = lax.optimization_barrier((copies, c_near))
    corner_r, corner_l = jnp.where(even_x, c_near, c_far), jnp.where(even_x, c_far, c_near)
    cores = [[x * gy + y for x in range(core, gx, 2) for y in range(gy)] for core in range(2)]
    blocks = copies.reshape(devices // 2, SHARE, 128)
    own = lax.all_to_all(blocks, ("gx", "gy"), 0, 0, axis_index_groups=cores).reshape(gx // 2, gy * SHARE, 128)
    level = lambda rows, n: [vm(NZ * rows, 128)] * n
    faces = lambda rows, tiles: vm(tiles * (NZ + 1) * rows, 128)
    rows3, rows4 = 2 * gx, gx
    size, tall = (NZ * TX, 128), ((NZ + 1) * TX, 128)
    k2 = call(
        window_kernel, "window_coeffs", [(NZ * TX * 4 + TX, 128)], [share2, x_near, x_far, yr, yl, corner_r, corner_l], level(TX, 7)
    )[0]
    big, big_z = (2 * NZ * 2 * TX, 128), (2 * (NZ + 1) * 2 * TX, 128)
    total0, total1 = 2 * (NZ * 6 + 1) * 2 * TX, (NZ * 6 + 1) * TX
    sends, saved = call(
        functools.partial(down_kernel, gx * TX, gy * TY),
        "down",
        [(devices // 2 * BLOCK, 128), (max(total0 + total1, SAVED_ROWS), 128)],
        [stack, yr, yl, corner_r, corner_l, x_near, x_far],
        [vm(*big)] * 10 + [vm(*big_z)] + level(TX, 10) + [faces(TX, 1)] + level(8, 10) + [faces(8, 1)] + [dma(12)],
        out_specs=[VMEM, ANY],
    )
    sends, own = lax.optimization_barrier((sends, own))
    other = lax.ppermute(own, "gx", near(gx))
    blocks = sends.reshape(devices // 2, BLOCK, 128)
    own_blocks = lax.all_to_all(blocks, ("gx", "gy"), 0, 0, axis_index_groups=cores)
    other_blocks = lax.ppermute(own_blocks, "gx", near(gx))
    whole = call(
        functools.partial(global_kernel, gx, gy),
        "global_coeffs",
        [(5 * NZ * (rows3 + rows4), 128)],
        [own, other],
        level(rows3, 6) + [faces(rows3, 1)] + level(rows3, 1) + level(rows4, 6) + [faces(rows4, 1)] + level(rows4, 1)
        + [vm(gx // 2, 2, gy * SHARE, 128), dma(2)],
        in_specs=[ANY] * 2,
    )[0]
    field, residual = call(
        functools.partial(up_kernel, gx, gy),
        "up",
        [(NZ * TX, TY)] * 2,
        [own_blocks, other_blocks, whole, k2, stack, saved],
        [vm(total0, 128), vm(total1, 128)] + level(TX, 3) + [vm(NZ * 2 * TX, 128), vm(*size), vm(*big), vm(*big)]
        + level(rows3, 3) + level(rows4, 2) + [dma(2)],
        in_specs=[VMEM] * 5 + [ANY],
    )
    return field.reshape(right_side.shape), residual.reshape(right_side.shape)


def solution(mesh):
    spec = P(None, "gx", "gy")
    fits = (mesh.shape["gx"], mesh.shape["gy"]) == (8, 4)
    plan = body if fits else spread_body
    return jax.shard_map(plan, mesh=mesh, in_specs=(spec,) * 5, out_specs=(spec, spec), check_vma=False)
```

```python
import functools

import jax
import jax.numpy as jnp
from jax import lax
from jax.experimental import pallas as pl
from jax.experimental.pallas import tpu as pltpu
from jax.sharding import PartitionSpec as P

LEVELS = 4
COARSE_SWEEPS = 16


OMEGA = 0.8


def with_halo(cells, sides, width):
    for axis, dim in sides:
        count = lax.axis_size(axis)
        ends = count - 1
        head = lax.slice_in_dim(cells, 0, width, axis=dim)
        tail = lax.slice_in_dim(cells, cells.shape[dim] - width, cells.shape[dim], axis=dim)
        cells = jnp.concatenate(
            [
                lax.ppermute(tail, axis, [(i, (i + 1) % count) for i in range(ends)]),
                cells,
                lax.ppermute(head, axis, [((i + 1) % count, i) for i in range(ends)]),
            ],
            axis=dim,
        )
    return cells


def apply_op(field, padded, coeffs):
    kappa, x_up, x_low, y_up, y_low, z_up, z_low = coeffs
    zpad = jnp.pad(field, ((1, 1), (0, 0), (0, 0)))
    out = (
        kappa * field
        + x_up * (field - padded[:, 2:, 1:-1])
        + x_low * (field - padded[:, :-2, 1:-1])
    )
    out = out + y_up * (field - padded[:, 1:-1, 2:]) + y_low * (field - padded[:, 1:-1, :-2])
    return out + z_up * (field - zpad[2:]) + z_low * (field - zpad[:-2])


def face_pad(field):
    return with_halo(field, (("gx", 1), ("gy", 2)), 1)


def line_factors(coeffs):
    kappa, x_up, x_low, y_up, y_low, z_up, z_low = coeffs
    diag = kappa + x_up + x_low + y_up + y_low + z_up + z_low
    upper_src = z_up.at[-1].set(jnp.zeros_like(z_up[-1]))

    def factor_step(upper_prev, planes):
        diag_k, low_k, up_k = planes
        inv = 1.0 / (diag_k + low_k * upper_prev)
        upper = -up_k * inv
        return (upper, (inv, upper))

    start = jnp.zeros_like(diag[0])
    unused, stacked = lax.scan(factor_step, start, (diag, z_low, upper_src), unroll=True)
    return stacked


def line_solve(rhs, factors, z_low):
    inverses, uppers = factors

    def forward_step(prev, planes):
        rhs_k, low_k, inv_k = planes
        value = (rhs_k + low_k * prev) * inv_k
        return (value, value)

    start = jnp.zeros_like(rhs[0])
    unused, forward = lax.scan(forward_step, start, (rhs, z_low, inverses), unroll=True)

    def back_step(after, planes):
        fwd_k, up_k = planes
        value = fwd_k - up_k * after
        return (value, value)

    unused, result = lax.scan(back_step, start, (forward, uppers), reverse=True, unroll=True)
    return result


def mean_four(field):
    depth, rows, cols = field.shape
    return field.reshape(depth, rows // 2, 2, cols // 2, 2).mean(axis=(2, 4))


def coarsen(coeffs):
    kappa, x_up, x_low, y_up, y_low, z_up, z_low = coeffs
    depth, rows, cols = kappa.shape
    shape = (depth, rows // 2, 2, cols // 2, 2)
    xu_c = x_up.reshape(shape)[:, :, 1].mean(axis=-1) * 0.25
    xl_c = x_low.reshape(shape)[:, :, 0].mean(axis=-1) * 0.25
    yu_c = y_up.reshape(shape)[:, :, :, :, 1].mean(axis=2) * 0.25
    yl_c = y_low.reshape(shape)[:, :, :, :, 0].mean(axis=2) * 0.25
    return (mean_four(kappa), xu_c, xl_c, yu_c, yl_c, mean_four(z_up), mean_four(z_low))


def prolong(padded):
    depth = padded.shape[0]
    rows = padded.shape[1] - 2
    cols = padded.shape[2] - 2
    centre = padded[:, 1:-1, :]
    even = 0.75 * centre + 0.25 * padded[:, :-2, :]
    odd = 0.75 * centre + 0.25 * padded[:, 2:, :]
    spread = jnp.stack([even, odd], axis=2).reshape(depth, 2 * rows, cols + 2)
    centre = spread[:, :, 1:-1]
    even = 0.75 * centre + 0.25 * spread[:, :, :-2]
    odd = 0.75 * centre + 0.25 * spread[:, :, 2:]
    return jnp.stack([even, odd], axis=3).reshape(depth, 2 * rows, 2 * cols)


def coarse_solve(rhs, coeffs):
    factors = line_factors(coeffs)
    field = OMEGA * line_solve(rhs, factors, coeffs[6])

    def spread_sweep(sweep, current):
        padded = with_halo(current, (("gx", 1), ("gy", 2)), 1)
        defect = rhs - apply_op(current, padded, coeffs)
        return current + OMEGA * line_solve(defect, factors, coeffs[6])

    field = lax.fori_loop(0, COARSE_SWEEPS - 1, spread_sweep, field)
    return field


def cycle(rhs, coeffs, level):
    if level == LEVELS:
        return coarse_solve(rhs, coeffs)
    factors = line_factors(coeffs)
    field = OMEGA * line_solve(rhs, factors, coeffs[6])
    padded = face_pad(field)
    defect = rhs - apply_op(field, padded, coeffs)
    correction = cycle(mean_four(defect), coarsen(coeffs), level + 1)
    rimmed = with_halo(correction, (("gx", 1), ("gy", 2)), 1)
    field = field + prolong(rimmed)
    padded = face_pad(field)
    defect = rhs - apply_op(field, padded, coeffs)
    return field + OMEGA * line_solve(defect, factors, coeffs[6])


def spread_body(right_side, kappa_sq, cond_x, cond_y, cond_z):
    padded_x = with_halo(cond_x, (("gx", 1),), 1)
    padded_y = with_halo(cond_y, (("gy", 2),), 1)
    padded_z = jnp.pad(cond_z, ((1, 1), (0, 0), (0, 0)))
    x_up = 0.5 * (cond_x + padded_x[:, 2:, :])
    x_low = 0.5 * (cond_x + padded_x[:, :-2, :])
    y_up = 0.5 * (cond_y + padded_y[:, :, 2:])
    y_low = 0.5 * (cond_y + padded_y[:, :, :-2])
    z_up = 0.5 * (cond_z + padded_z[2:])
    z_low = 0.5 * (cond_z + padded_z[:-2])
    coeffs = (kappa_sq, x_up, x_low, y_up, y_low, z_up, z_low)
    solution_field = cycle(right_side, coeffs, 0)
    residual = right_side - apply_op(solution_field, face_pad(solution_field), coeffs)
    return (solution_field, residual)


F32 = jnp.float32
BF16 = jnp.bfloat16
NZ = 32
HALF = NZ // 2
TX, TY = 16, 128
HALO = 8
SLAB = 5 * NZ * HALO
STRIP = 160
CORNER = 104
SHARE = 40
BLOCK = NZ + 8
VMEM = pl.BlockSpec(memory_space=pltpu.VMEM)
ANY = pl.BlockSpec(memory_space=pl.ANY)
HBM = pl.BlockSpec(memory_space=pltpu.HBM)


def iota(shape, dim):
    return lax.broadcasted_iota(jnp.int32, shape, dim)


def shift(x, by, axis):
    by = by % x.shape[axis]
    return pltpu.roll(x, by, axis) if by else x


def mix(x, weights, parts=2):
    pieces = []
    for n in range(parts):
        piece = x.astype(BF16)
        pieces.append(piece)
        if n < parts - 1:
            x = x - piece.astype(F32)
    out = jnp.dot(jnp.concatenate(pieces, axis=0), weights, preferred_element_type=F32)
    rows = x.shape[0]
    return sum(out[n * rows : (n + 1) * rows] for n in reversed(range(parts)))


def matrix(mask, weight=1.0):
    return jnp.where(mask, weight, 0.0).astype(BF16)


def span(start, size):
    if not isinstance(start, int):
        start = pl.multiple_of(start, 8)
    return pl.ds(start, size)


class Field:
    def __init__(self, ref, rows, tiles=1, planes=NZ, start=0):
        self.ref, self.rows, self.tiles, self.planes, self.start = ref, rows, tiles, planes, start

    def base(self, tile, k):
        return self.start + tile * self.planes * self.rows + k * self.rows

    def part(self, tile, k):
        return self.ref[span(self.base(tile, k), self.rows), :]

    def __getitem__(self, k):
        parts = [self.part(t, k) for t in range(self.tiles)]
        return parts[0] if self.tiles == 1 else jnp.concatenate(parts, axis=1)

    def __setitem__(self, k, value):
        for t in range(self.tiles):
            self.put(t, k, value[:, 128 * t : 128 * (t + 1)])

    def put(self, tile, k, value):
        self.ref[span(self.base(tile, k), self.rows), :] = value

    def every_second(self, at, count, odd):
        parts = []
        for t in range(self.tiles):
            first = self.base(t, 0) + 2 * at + odd
            parts.append(self.ref[pl.ds(first, count, stride=2), :])
        return parts[0] if self.tiles == 1 else jnp.concatenate(parts, axis=1)

    def row(self, row):
        return self.ref[pl.ds(self.start + row, self.planes, stride=self.rows), :]


def stack_fields(ref, rows, count, tiles=1, z_face=True, start=0):
    size = tiles * NZ * rows
    out = [Field(ref, rows, tiles, NZ, start + n * size) for n in range(count)]
    return out + [Field(ref, rows, tiles, NZ + 1, start + count * size)] if z_face else out


def loop(count, step, carry, unroll=None):
    if unroll is None or unroll >= count:
        for i in range(count):
            carry = step(i, carry)
        return carry
    return lax.fori_loop(0, count, step, carry, unroll=unroll)


def neighbours(field, x_face, y_face):
    out = x_face * shift(field, 1, 0) + shift(x_face * field, -1, 0)
    return out + (y_face * shift(field, 1, 1) + shift(y_face * field, -1, 1))


class Line:
    def __init__(self, inv, z_face):
        self.inv, self.z_face = inv, z_face

    def inward(self, k, upper):
        return self.z_face[k + 1 if upper else k] * self.inv[k]

    def outward(self, k, upper):
        return self.z_face[k if upper else k + 1] * self.inv[k]


class StoredLine:
    def __init__(self, inv, g, c):
        self.inv, self.g, self.c = inv, g, c

    def inward(self, k, upper):
        return self.g[k]

    def outward(self, k, upper):
        return self.c[k]


def sweep_in(rhs, line, keep, start, unroll):
    def step(i, carry):
        low, high = carry
        k, m = i, NZ - 1 - i
        low = rhs(k) * line.inv[k] + line.inward(k, False) * low
        high = rhs(m) * line.inv[m] + line.inward(m, True) * high
        keep[k] = low
        keep[m] = high
        return low, high

    return loop(HALF, step, (start, start), unroll)


def sweep_out(ends, kept, line, emit, unroll):
    low, high = ends
    a, b = line.outward(HALF - 1, False), line.outward(HALF, True)
    low = (low + a * high) * (1.0 / (1.0 - a * b))
    high = high + b * low

    def step(i, carry):
        low, high = carry
        k, m = HALF - 1 - i, HALF + i
        emit(k, low)
        emit(m, high)
        low = kept[k - 1] + line.outward(k - 1, False) * low
        high = kept[m + 1] + line.outward(m + 1, True) * high
        return low, high

    low, high = loop(HALF - 1, step, (low, high), unroll)
    emit(0, low)
    emit(NZ - 1, high)


def factor(diag, z_face, tiles, inv_out, unroll, rhs=None, keep=None, g_out=None, c_out=None):
    ends = []
    for t in range(tiles):
        zero = diag.part(t, 0) * 0.0

        def one(k, upper, before, last, prev):
            below, above = z_face.part(t, k), z_face.part(t, k + 1)
            inner, outer = (above, below) if upper else (below, above)
            minor = (diag.part(t, k) + below + above) * last - (inner * inner) * before
            inv = last * (1.0 / minor)
            inv_out.put(t, k, inv)
            if g_out is not None:
                g_out.put(t, k, inner * inv)
                c_out.put(t, k, outer * inv)
            if rhs is not None:
                prev = rhs.part(t, k) * inv + (inner * inv) * prev
                keep.put(t, k, prev)
            return last, minor, prev

        def step(i, carry):
            low, high = carry
            return one(i, False, *low), one(NZ - 1 - i, True, *high)

        start = (zero, zero + 1.0, zero)
        low, high = loop(HALF, step, (start, start), unroll)
        ends.append((low[2], high[2]))
    join = lambda n: ends[0][n] if tiles == 1 else jnp.concatenate([e[n] for e in ends], axis=1)
    return join(0), join(1)


def z_faces(cz, out, tiles=1):
    for t in range(tiles):
        before = None
        for k in range(NZ + 1):
            here = cz.part(t, k) if k < NZ else None
            both = here if before is None else before if here is None else here + before
            out.put(t, k, 0.5 * both)
            before = here


def base_diag(kappa, x_face, y_face):
    return kappa + (x_face + shift(x_face, -1, 0)) + (y_face + shift(y_face, -1, 1))


def window_mask(rows, lanes, tile_x, tile_y, halo, ix, iy, nx, ny):
    x, y = iota((rows, lanes), 0), iota((rows, lanes), 1)
    x = jnp.where(x < (rows + tile_x) // 2, x, x - rows)
    y = jnp.where(y < (lanes + tile_y) // 2, y, y - lanes)
    valid = (y >= -halo) & (y < tile_y + halo) & (x >= -halo) & (x < tile_x + halo)
    x, y = x + ix * tile_x, y + iy * tile_y
    return (valid & (x >= 0) & (x < nx) & (y >= 0) & (y < ny)).astype(F32)


def smooth_down(f, x_face, y_face, line, ends, kept, u, r, unroll):
    def emit(k, value):
        field = OMEGA * value
        u[k] = field
        r[k] = (1.0 - OMEGA) * f[k] + neighbours(field, x_face[k], y_face[k])

    sweep_out(ends, kept, line, emit, unroll)


def smooth_up(f, x_face, y_face, line, u, e, kept, mask, unroll):
    masked = (lambda v: v) if mask is None else (lambda v: v * mask)

    def rhs(k):
        field = masked(u[k] + e[k])
        u[k] = field
        return masked(f[k] + neighbours(field, x_face[k], y_face[k]))

    def emit(k, value):
        u[k] = (1.0 - OMEGA) * u[k] + OMEGA * value

    zero = jnp.zeros((u.rows, 128 * u.tiles), F32)
    ends = sweep_in(rhs, line, kept, zero, unroll)
    sweep_out(ends, kept, line, emit, unroll)


def spread_rows(cells, before, after, dest, size):
    dest[pl.ds(0, size, stride=2), :] = (0.75 * cells + 0.25 * before).reshape(size, 128)
    dest[pl.ds(1, size, stride=2), :] = (0.75 * cells + 0.25 * after).reshape(size, 128)


def spread_matrix(fine, base, coarse_count, circular=False):
    j = iota((128, fine.shape[1]), 0) + base
    parent = (fine + 2048) // 2 - 1024
    partner = parent + 2 * ((fine + 2048) % 2) - 1
    if circular:
        j, parent, partner = j % 128, parent % 128, partner % 128
    weights = jnp.where(j == parent, 0.75, jnp.where(j == partner, 0.25, 0.0))
    if not circular:
        inside = (j >= 0) & (j < coarse_count) & (fine >= 0) & (fine < 2 * coarse_count)
        weights = jnp.where(inside, weights, 0.0)
    return weights.astype(BF16)


def lane_group(rows, width):
    return iota((rows, 128), 1) // width


def fold_planes(cells, turn):
    group = lane_group(8, 32)
    out = cells[:8]
    for n in range(1, 4):
        out = jnp.where(group == n, cells[8 * n : 8 * n + 8], out)
    return pltpu.roll(out, turn, 1)


def share_blocks(kinds):
    iy = lax.axis_index("gy")
    y, lane = iota((128, 128), 0), iota((128, 128), 1)
    x_in, y_in = y // 32, y % 32
    x_out, y_out = lane % 32 // 16, lane % 16
    pair_y, pair_x = y_in // 2 == y_out, x_in // 2 == x_out
    a, b, c, d, kappa, cz = kinds
    eighth = lambda mask: matrix(mask, 0.125)
    blocks = [
        mix(a, eighth(pair_y & (x_in == 2 * x_out))) + mix(b, eighth(pair_y & (x_in == 1) & (x_out == 1))),
        mix(b, eighth(pair_y & (x_in == 3) & (x_out == 0)))
        + mix(d, eighth((x_out == 1) & (y_in == 31) & (x_in // 2 == y_out))),
        mix(c, eighth(pair_x & (y_in == 2 * y_out))) + mix(d, eighth(pair_x & (y_in == 2 * y_out - 1))),
        mix(kappa, matrix(pair_x & pair_y, 0.25)),
        mix(cz, matrix(pair_x & pair_y, 0.25)),
    ]
    return [fold_planes(cells, 16 * iy) for cells in blocks]


def fetch_all(sources, dests, sems, first=0):
    copies = [pltpu.make_async_copy(a, b, sems.at[first + n]) for n, (a, b) in enumerate(zip(sources, dests))]
    for copy in copies:
        copy.start()
    return copies


def pack_kernel(devices, f_in, kappa_in, cx_in, cy_in, cz_in, x_near, x_far, y_near, y_far, share2, stack, copies, sems):
    even_x, even_y = lax.axis_index("gx") % 2 == 0, lax.axis_index("gy") % 2 == 0
    tiles = [stack.at[pl.ds(a * NZ * TX, NZ * TX), :] for a in range(5)]
    for copy in fetch_all((f_in, kappa_in, cx_in, cy_in, cz_in), tiles, sems):
        copy.wait()
    f, kappa, cx, cy, cz = tiles
    for a, ref in enumerate(tiles):
        cells = ref[...].reshape(NZ, TX, TY)
        at = pl.ds(a * NZ * HALO, NZ * HALO)
        head = cells[:, :HALO].reshape(NZ * HALO, TY)
        tail = cells[:, TX - HALO :].reshape(NZ * HALO, TY)
        x_near[at, :] = jnp.where(even_x, tail, head)
        x_far[at, :] = jnp.where(even_x, head, tail)
    y, lane = iota((128, 128), 0), iota((128, 128), 1)
    fourth = y // 4 == lane % 32
    rows = lambda ref: [Field(ref, TX).row(r) for r in range(TX)]
    cx_rows, cy_rows, kappa_rows, cz_rows = rows(cx), rows(cy), rows(kappa), rows(cz)
    totals = lambda v: [(v[4 * i] + v[4 * i + 1]) + (v[4 * i + 2] + v[4 * i + 3]) for i in range(4)]
    stack = [cx_rows[4 * i] for i in range(4)] + [cx_rows[4 * i + 3] for i in range(4)]
    stack = mix(jnp.concatenate(stack + totals(kappa_rows) + totals(cz_rows), axis=0), matrix(fourth))
    ends = [matrix(fourth & (y % 4 == 0)), matrix(fourth & (y % 4 == 3))]
    sides = mix(jnp.concatenate(totals(cy_rows), axis=0), jnp.concatenate(ends, axis=1))
    group = lane_group(NZ, 32)

    def merge(cells, scale):
        out = cells[:NZ]
        for xi in range(1, 4):
            out = jnp.where(group == xi, cells[NZ * xi : NZ * (xi + 1)], out)
        return out * scale

    kinds = [merge(stack[:128], 1 / 128), merge(stack[128:256], 1 / 128)]
    kinds += [merge(sides[:, :128], 1 / 128), merge(sides[:, 128:], 1 / 128)]
    kinds += [merge(stack[256:384], 1 / 16), merge(stack[384:], 1 / 16)]
    for t, cells in enumerate(share_blocks(kinds)):
        for n in range(devices):
            copies[pl.ds(n * SHARE + 8 * t, 8), :] = cells
    head = [jnp.zeros((8, 128), F32)] * 3
    tail = [jnp.zeros((8, 128), F32)] * 3
    slot = iota((8, 128), 1) % 32 // 4
    for t, cells in enumerate(kinds):
        for dest, first in ((share2, 0), (x_near, SLAB), (x_far, SLAB)):
            dest[pl.ds(first + t * NZ, NZ), :] = cells
        for zv in range(4):
            n = 4 * t + zv
            piece = cells[8 * zv : 8 * zv + 8]
            head[n // 8] = jnp.where(slot == n % 8, shift(piece, 4 * (n % 8), 1), head[n // 8])
            tail[n // 8] = jnp.where(slot == n % 8, shift(piece, 4 * (n % 8) + 4, 1), tail[n // 8])
    for n in range(3):
        y_near[pl.ds(STRIP + 8 * n, 8), :] = jnp.where(even_y, tail[n], head[n])
        y_far[pl.ds(STRIP + 8 * n, 8), :] = jnp.where(even_y, head[n], tail[n])

    group = lane_group(8, 8)
    for a, ref in enumerate((f, kappa, cx, cy, cz)):
        for half in range(2):
            for zo in range(2):
                head = jnp.zeros((8, 128), F32)
                tail = jnp.zeros((8, 128), F32)
                for zi in range(16):
                    cells = ref[pl.ds((zo * 16 + zi) * TX + 8 * half, 8), :]
                    cells = shift(cells, 8 * zi, 1)
                    head = jnp.where(group == zi, cells, head)
                    tail = jnp.where(group == (zi - 1) % 16, cells, tail)
                at = pl.ds(((half * 5 + a) * 2 + zo) * 8, 8)
                y_near[at, :] = jnp.where(even_y, tail, head)
                y_far[at, :] = jnp.where(even_y, head, tail)


def window2(tile, after, before, dest, first, iy, gy):
    lane = iota((NZ, 128), 1)
    first_after, first_before = jnp.where(iy < gy - 1, 36, 0), jnp.where(iy > 0, 124, 128)
    for xi in range(4):
        turned = (lane - 32 * xi + 128) % 128
        cells = jnp.where(turned < 32, tile, jnp.where(turned < first_after, after, jnp.where(turned >= first_before, before, 0.0)))
        dest[pl.ds(first + xi, NZ, stride=TX), :] = shift(cells, -32 * xi, 1)


def window_kernel(share2, x_near, x_far, yr, yl, cr, cl, out, a, b, c, d, kappa, cz, diag):
    ix, iy = lax.axis_index("gx"), lax.axis_index("gy")
    gy = lax.axis_size("gy")
    nx, ny = lax.axis_size("gx") * 4, gy * 32
    refs = (a, b, c, d, kappa, cz)

    def unpack(ref, first, t, turn):
        pieces = []
        for zv in range(4):
            n = 4 * t + zv
            pieces.append(shift(ref[span(first + 8 * (n // 8), 8), :], turn - 4 * (n % 8), 1))
        return jnp.concatenate(pieces, axis=0)

    near, far = STRIP // 2, CORNER + STRIP // 2
    even_x = ix % 2 == 0
    for t, dest in enumerate(refs):
        beside = x_near[pl.ds(SLAB + t * NZ, NZ), :], x_far[pl.ds(SLAB + t * NZ, NZ), :]
        for first, cells, right, left, r_at, l_at in (
            (0, share2[pl.ds(t * NZ, NZ), :], yr, yl, STRIP, STRIP),
            (4, jnp.where(even_x, *beside), cr, cr, far, near),
            (12, jnp.where(even_x, *beside[::-1]), cl, cl, far, near),
        ):
            window2(cells, unpack(right, r_at, t, 32), unpack(left, l_at, t, 92), dest, first, iy, gy)
        for x in range(8, 12):
            dest[pl.ds(x, NZ, stride=TX), :] = jnp.zeros((NZ, 128), F32)
    mask = window_mask(TX, 128, 4, 32, 4, ix, iy, nx, ny)
    a, b, c, d, kappa, cz, diag = (Field(ref, TX) for ref in (*refs, diag))
    x_face, y_face, inv, z_face = stack_fields(out, TX, 3)
    for k in range(NZ):
        x_k = a[k] + shift(b[k], 1, 0)
        y_k = c[k] + shift(d[k], 1, 1)
        x_face[k] = x_k
        y_face[k] = y_k
        diag[k] = base_diag(jnp.where(mask > 0, kappa[k], 1.0), x_k, y_k)
    z_faces(cz, z_face)
    factor(diag, z_face, 1, inv, None)


def assemble3(block, dest, gx, gy, rows):
    group = lane_group(8, 16)
    for ix in range(gx):
        blocks = [block(ix, iy) for iy in range(gy)]
        for zo in range(4):
            for xi in range(2):
                q = 2 * zo + xi
                cells = blocks[0]
                for iy in range(1, gy):
                    cells = jnp.where(group == (iy + q) % 8, blocks[iy], cells)
                dest[pl.ds(8 * zo * rows + 2 * ix + xi, 8, stride=rows), :] = shift(cells, -16 * q, 1)


def global_kernel(gx, gy, own, other, *refs):
    out, raw3, raw4, shares, sems = refs[0], refs[1:9], refs[9:17], refs[17], refs[18]
    outs3 = stack_fields(out, 2 * gx, 5, z_face=False)
    outs4 = stack_fields(out, gx, 5, z_face=False, start=5 * NZ * 2 * gx)
    core = lax.axis_index("gx") % 2
    copies = [
        pltpu.make_async_copy(own, shares.at[:, core], sems.at[0]),
        pltpu.make_async_copy(other, shares.at[:, 1 - core], sems.at[1]),
    ]
    for copy in copies:
        copy.start()
    for copy in copies:
        copy.wait()
    rows, cols = 2 * gx, 16 * gy
    for t, n in enumerate((0, 1, 2, 4, 5)):
        block = lambda jx, jy: shares[jx // 2, jx % 2, pl.ds(jy * SHARE + 8 * t, 8), :]
        assemble3(block, raw3[n], gx, gy, rows)
    xl, xu, yl, yu = (Field(ref, rows) for ref in raw3[:4])
    x, y = iota((rows, 128), 0), iota((rows, 128), 1)
    odd_row, inside = x % 2 == 1, y < cols
    for k in range(NZ):
        half = jnp.where(inside, xu[k], 0.0)
        below = jnp.where(odd_row | (x < 2), 0.0, shift(half, 2, 0))
        x_k = jnp.where(inside, xl[k] + below, 0.0)
        xl[k] = x_k
        xu[k] = jnp.where(x == rows - 1, shift(half, 1, 0), shift(x_k, -1, 0))
        next_row = shift(half, -1, 0)
        below = jnp.where(odd_row, shift(half, 15, 1), shift(next_row, 16, 1))
        y_k = jnp.where(inside, yl[k] + jnp.where((y % 16 == 0) & (y > 0), below, 0.0), 0.0)
        yl[k] = y_k
        above = jnp.where(odd_row, shift(half, 14, 1), shift(next_row, 15, 1))
        yu[k] = jnp.where(y == cols - 1, above, jnp.where(inside, shift(y_k, -1, 1), 0.0))
    yy, jj = iota((128, 128), 0), iota((128, 128), 1)
    keep = yy // 2 == jj
    pair, even, odd = matrix(keep), matrix(keep & (yy % 2 == 0)), matrix(keep & (yy % 2 == 1))
    size = NZ * rows // 2
    lows = [Field(ref, rows) for ref in raw3]
    first = lambda n: lows[n].every_second(0, size, 0)
    second = lambda n: lows[n].every_second(0, size, 1)
    raw4[0][...] = 0.125 * mix(first(0), pair)
    raw4[1][...] = 0.125 * mix(second(1), pair)
    raw4[2][...] = 0.125 * mix(first(2) + second(2), even)
    raw4[3][...] = 0.125 * mix(first(3) + second(3), odd)
    raw4[4][...] = 0.25 * mix(first(4) + second(4), pair)
    raw4[5][...] = 0.25 * mix(first(5) + second(5), pair)
    for raw, outs in ((raw3, outs3), (raw4, outs4)):
        x, y = iota((rows, 128), 0), iota((rows, 128), 1)
        xl, xu, yl, yu, kappa, cz = (Field(ref, rows) for ref in raw[:6])
        z_face, diag = Field(raw[6], rows, 1, NZ + 1), Field(raw[7], rows)
        x_face, y_face, inv, g, c = outs
        inside_x, inside_y = (x > 0).astype(F32), ((y > 0) & (y < cols)).astype(F32)
        for k in range(NZ):
            xl_k, yl_k = xl[k], yl[k]
            diag[k] = jnp.where(y < cols, kappa[k], 1.0) + (xl_k + xu[k]) + (yl_k + yu[k])
            x_face[k] = xl_k * inside_x
            y_face[k] = yl_k * inside_y
        z_faces(cz, z_face)
        factor(diag, z_face, 1, inv, None, g_out=g, c_out=c)
        rows, cols = rows // 2, cols // 2


def down_kernel(nx, ny, *refs):
    stack, yr, yl, corner_r, corner_l, x_near, x_far = refs[:7]
    sends, saved = refs[7:9]
    scratch = list(refs[9:-1])
    sems = refs[-1]
    take = lambda n: [scratch.pop(0) for _ in range(n)]
    ix, iy = lax.axis_index("gx"), lax.axis_index("gy")
    gx, gy = lax.axis_size("gx"), lax.axis_size("gy")
    f, kappa, cx, cy, cz = (stack.at[pl.ds(a * NZ * TX, NZ * TX), :] for a in range(5))
    even_x = ix % 2 == 0
    rows, tiles = 2 * TX, 2
    whole = take(11)
    names = [Field(ref, rows, tiles) for ref in whole[:10]]
    x_face, y_face, inv, u, f0, kappa0, cz0, diag, kept, r = names
    z_face = Field(whole[10], rows, tiles, NZ + 1)
    group = lane_group(8, 8)

    def window(a, tile, z, after, before, turn):
        zo = z // 16
        slab = span(a * NZ * HALO + z * HALO, HALO)
        near, far = x_near[slab, :], x_far[slab, :]
        sides = [jnp.where(even_x, near, far), jnp.where(even_x, far, near)]
        main = jnp.concatenate([tile[span(z * TX, TX), :], *sides], axis=0)
        at = lambda first: span(first + (a * 2 + zo) * 8, 8)
        half = STRIP // 2
        sides = []
        for right, left in (
            (yr[at(0), :], yl[at(0), :]),
            (yr[at(half), :], yl[at(half), :]),
            (corner_r[at(CORNER), :], corner_r[at(0), :]),
            (corner_l[at(CORNER), :], corner_l[at(0), :]),
        ):
            cells = jnp.where(after, right, jnp.where(before, left, 0.0))
            sides.append(pltpu.roll(cells, turn, 1))
        return jnp.concatenate([main, jnp.concatenate(sides, axis=0)], axis=1)

    mask0 = window_mask(rows, 256, TX, TY, HALO, ix, iy, nx, ny)

    def prepare(z, cz_prev):
        zi = z % 16
        after, before = group == zi, group == (zi + 15) % 16
        turn = (128 - 8 * zi) % 128
        f_k, kappa_k, cx_k, cy_k, cz_k = (
            window(a, tile, z, after, before, turn) for a, tile in enumerate((f, kappa, cx, cy, cz))
        )
        f0[z] = f_k
        kappa0[z] = kappa_k
        cz0[z] = cz_k
        z_face[z] = 0.5 * (cz_k + cz_prev)
        x_k, y_k = 0.5 * (cx_k + shift(cx_k, 1, 0)), 0.5 * (cy_k + shift(cy_k, 1, 1))
        x_face[z] = x_k
        y_face[z] = y_k
        diag[z] = base_diag(jnp.where(mask0 > 0, kappa_k, 1.0), x_k, y_k)
        return cz_k

    last = loop(NZ, prepare, jnp.zeros((rows, 256), F32), 8)
    z_face[NZ] = 0.5 * last
    ends = factor(diag, z_face, tiles, inv, None, f0, kept)
    copies = []

    def save(field):
        at = sum(copy[1] for copy in copies)
        count = field.ref.shape[0]
        copy = pltpu.make_async_copy(field.ref, saved.at[pl.ds(at, count), :], sems.at[len(copies)])
        copy.start()
        copies.append((copy, count))

    for field in (x_face, y_face, inv, f0):
        save(field)
    smooth_down(f0, x_face, y_face, Line(inv, z_face), ends, kept, u, r, None)
    save(u)
    save(z_face)

    fine = (r, kappa0, cz0, x_face, y_face)
    lanes, tile_x, tile_y, halo = 256, TX, TY, HALO
    for level in (1, 2):
        rows, tile_x, tile_y, halo = rows // 2, tile_x // 2, tile_y // 2, halo // 2
        nx, ny = nx // 2, ny // 2
        whole = take(11)
        names = [Field(ref, rows) for ref in whole[:10]]
        x_face, y_face, inv, u, f1, kappa1, cz1, diag, kept, r = names
        z_face = Field(whole[10], rows, 1, NZ + 1)
        mask = window_mask(rows, 128, tile_x, tile_y, halo, ix, iy, nx, ny)
        y, j = iota((lanes, 128), 0), iota((lanes, 128), 1)
        if lanes == 128:
            j = jnp.where(j < 48, j, jnp.where(j >= 80, j - 64, -1))
        pair = matrix(y // 2 == j)
        even = (iota((1, lanes), 1) % 2 == 0).astype(F32)
        part = 128
        for at in range(0, NZ * rows, part):
            here = pl.ds(at, part)
            both = lambda n: fine[n].every_second(at, part, 0) + fine[n].every_second(at, part, 1)
            below = fine[3].every_second(at, part, 0)
            out = mix(jnp.concatenate([both(0), both(1), both(2), below, both(4) * even], axis=0), pair)
            for n, (dest, weight) in enumerate(((f1, 0.25), (kappa1, 0.25), (cz1, 0.25), (x_face, 0.125), (y_face, 0.125))):
                dest.ref[here, :] = weight * out[n * part : (n + 1) * part]
        for k in range(NZ):
            f1[k] = f1[k] * mask
            diag[k] = base_diag(jnp.where(mask > 0, kappa1[k], 1.0), x_face[k], y_face[k])
        z_faces(cz1, z_face)
        ends = factor(diag, z_face, 1, inv, None, f1, kept)
        smooth_down(f1, x_face, y_face, Line(inv, z_face), ends, kept, u, r, None)
        if level == 1:
            for field in (x_face, y_face, inv, f1, u, z_face):
                save(field)
        fine, lanes = (r, kappa1, cz1, x_face, y_face), 128

    group = lane_group(NZ, 32)
    out = f1.row(0)
    for xi in range(1, 4):
        out = jnp.where(group == xi, shift(f1.row(xi), 32 * xi, 1), out)
    for n in range(gx * gy // 2):
        sends[pl.ds(n * BLOCK, NZ), :] = out
    y, lane = iota((128, 128), 0), iota((128, 128), 1)
    total = jnp.zeros((NZ, 128), F32)
    for xi in range(2):
        place = (lane % 32 // 16 == xi) & (y // 2 == lane % 16) & (y < 32)
        total = total + mix(r.row(2 * xi) + r.row(2 * xi + 1), matrix(place, 0.25))
    total = fold_planes(total, 16 * iy)
    for n in range(gx * gy // 2):
        sends[pl.ds(n * BLOCK + NZ, 8), :] = total
    for copy, _ in copies:
        copy.wait()


def up_kernel(gx, gy, *refs):
    own, other, whole, k2, stack, saved, solution_out, residual_out = refs[:8]
    scratch = list(refs[8:-1])
    sems = refs[-1]
    take = lambda n: [scratch.pop(0) for _ in range(n)]
    ix, iy = lax.axis_index("gx"), lax.axis_index("gy")
    held0, held1 = take(2)
    split = held0.shape[0]
    parts = [saved.at[pl.ds(split, held1.shape[0]), :], saved.at[pl.ds(0, split), :]]
    fetched = fetch_all(parts, (held1, held0), sems)
    core = ix % 2

    def gathered(jx, jy, at):
        if isinstance(jx, int):
            same = core == jx % 2
            return jnp.where(same, own[jx // 2 * gy + jy, at, :], other[jx // 2 * gy + jy, at, :])
        return jx[1][jx[0] // 2 * gy + jy, at, :]
    f2, u2, kept2, wide, e_ref, e0_ref, kept0, u3, f3, r3, f4, u4 = take(12)

    rows, cols = 2 * gx, 16 * gy
    assemble3(lambda jx, jy: gathered(jx, jy, pl.ds(NZ, 8)), f3, gx, gy, rows)
    f3, u3, r3 = (Field(ref, rows) for ref in (f3, u3, r3))
    y = iota((rows, 128), 1)
    x_face3, y_face3, inv3, g3, c3 = stack_fields(whole, rows, 5, z_face=False)
    line3 = StoredLine(inv3, g3, c3)
    clean = (y < cols).astype(F32)
    for k in range(NZ):
        f3[k] = f3[k] * clean
    zero = jnp.zeros((rows, 128), F32)
    ends = sweep_in(lambda k: f3[k], line3, r3, zero, None)
    smooth_down(f3, x_face3, y_face3, line3, ends, r3, u3, Field(e_ref, rows), None)
    fine = Field(e_ref, rows)
    rows, cols = rows // 2, cols // 2
    size = NZ * rows
    yy, jj = iota((128, 128), 0), iota((128, 128), 1)
    f4[...] = 0.25 * mix(fine.every_second(0, size, 0) + fine.every_second(0, size, 1), matrix(yy // 2 == jj))
    f4, u4 = Field(f4, rows), Field(u4, rows)
    x_face4, y_face4, inv4, g4, c4 = stack_fields(whole, rows, 5, z_face=False, start=5 * NZ * 2 * rows)
    line4 = StoredLine(inv4, g4, c4)
    zero = jnp.zeros((rows, 128), F32)

    def solve4(rhs, old):
        kept, out = {}, {}
        ends = sweep_in(rhs, line4, kept, zero, None)

        def emit(k, value):
            out[k] = OMEGA * value if old is None else (1.0 - OMEGA) * old[k] + OMEGA * value

        sweep_out(ends, kept, line4, emit, None)
        for k in range(NZ):
            u4[k] = out[k]

    solve4(lambda k: f4[k], None)

    def relax(sweep, carry):
        old = [u4[k] for k in range(NZ)]
        solve4(lambda k: f4[k] + neighbours(old[k], x_face4[k], y_face4[k]), old)
        return carry

    lax.fori_loop(0, COARSE_SWEEPS - 1, relax, 0, unroll=5)

    cells = u4.ref[...].reshape(NZ, rows, 128)
    x = iota((1, rows, 128), 1)
    before = jnp.where(x > 0, shift(cells, 1, 1), 0.0)
    after = jnp.where(x < rows - 1, shift(cells, -1, 1), 0.0)
    spread_rows(cells, before, after, wide, size)
    e_ref[...] = mix(wide[pl.ds(0, 2 * size), :], spread_matrix(iota((128, 128), 1), 0, cols))
    rows, cols = 2 * rows, 2 * cols
    smooth_up(f3, x_face3, y_face3, line3, u3, Field(e_ref, rows), r3, None, None)

    def block(dx, dy):
        inside = ((ix + dx >= 0) & (ix + dx < gx)).astype(F32)
        jx, jy = jnp.clip(ix + dx, 0, gx - 1), jnp.clip(iy + dy, 0, gy - 1)
        return gathered((jx, other if dx else own), jy, pl.ds(0, NZ)) * inside

    for first, dx in ((0, 0), (4, 1), (12, -1)):
        window2(block(dx, 0), shift(block(dx, 1), 32, 1), shift(block(dx, -1), 96, 1), f2, first, iy, gy)
    for x in range(8, 12):
        f2[pl.ds(x, NZ, stride=TX), :] = jnp.zeros((NZ, 128), F32)
    f2, u2, kept2 = (Field(ref, TX) for ref in (f2, u2, kept2))
    x_face2, y_face2, inv2, z_face2 = stack_fields(k2, TX, 3)
    line2 = Line(inv2, z_face2)
    zero = jnp.zeros((TX, 128), F32)
    ends = sweep_in(lambda k: f2[k], line2, kept2, zero, None)

    def emit2(k, value):
        u2[k] = OMEGA * value

    sweep_out(ends, kept2, line2, emit2, None)

    cells = pltpu.roll(u3.ref[...].reshape(NZ, rows, 128), (rows - 2 * ix) % rows, 1)
    x = iota((1, rows, 128), 1)
    place = 2 * ix + jnp.where(x < rows // 2, x, x - rows)
    cells = jnp.where((place >= 0) & (place < rows), cells, 0.0)
    ring = lambda v, first: jnp.where(iota((1, 8, 128), 1) < first, v[:, :8], v[:, rows - 8 :])
    spread_rows(ring(cells, 4), ring(shift(cells, 1, 1), 4), ring(shift(cells, -1, 1), 4), wide, NZ * 8)
    lane = iota((128, 128), 1)
    fine_y = jnp.where(lane < 80, lane, lane - 128) + 32 * iy
    e_ref[...] = mix(wide[pl.ds(0, NZ * TX), :], spread_matrix(fine_y, 0, cols))
    mask2 = window_mask(TX, 128, 4, 32, 4, ix, iy, 4 * gx, 32 * gy)
    smooth_up(f2, x_face2, y_face2, line2, u2, Field(e_ref, TX), kept2, mask2, None)

    cells = u2.ref[...].reshape(NZ, TX, 128)
    ring = lambda v: jnp.where(iota((1, 8, 128), 1) < 6, v[:, :8], v[:, 8:])
    spread_rows(ring(cells), ring(shift(cells, 1, 1)), ring(shift(cells, -1, 1)), wide, NZ * 8)
    fine_y = jnp.where(lane < 96, lane, lane - 128)
    e_ref[...] = mix(wide[pl.ds(0, NZ * TX), :], spread_matrix(fine_y, 0, 0, circular=True))
    fetched[0].wait()
    x_face1, y_face1, inv1, f1, u1, z_face1 = stack_fields(held1, TX, 5)
    line1 = Line(inv1, z_face1)
    mask1 = window_mask(TX, 128, 8, 64, 4, ix, iy, 8 * gx, 64 * gy)
    smooth_up(f1, x_face1, y_face1, line1, u1, Field(e_ref, TX), kept2, mask1, None)

    cells = held1[pl.ds(u1.start, NZ * TX), :].reshape(NZ, TX, 128)
    spread_rows(cells, shift(cells, 1, 1), shift(cells, -1, 1), wide, NZ * TX)
    rows = 2 * TX
    weights = spread_matrix(iota((128, 256), 1), 0, 0, circular=True)
    e0 = Field(e0_ref, rows, 2)
    for k in range(0, NZ, 8):
        cells = mix(wide[pl.ds(k * rows, 8 * rows), :], weights)
        for t in range(2):
            e0_ref[pl.ds(e0.base(t, k), 8 * rows), :] = cells[:, 128 * t : 128 * (t + 1)]
    fetched[1].wait()
    x_face0, y_face0, inv0, f0, u0, z_face0 = stack_fields(held0, rows, 5, 2)
    mask0 = window_mask(rows, 256, TX, TY, HALO, ix, iy, TX * gx, TY * gy)
    smooth_up(f0, x_face0, y_face0, Line(inv0, z_face0), u0, e0, Field(kept0, rows, 2), mask0, None)

    kappa = Field(stack, TX, start=NZ * TX)

    def residual(k, carry):
        below, flux_z = carry
        column = u0.part(0, k)
        here = column[:TX]
        flux_x = (x_face0.part(0, k) * (column - shift(column, 1, 0)))[: TX + 8]
        row = u0[k][:TX]
        flux_y = y_face0[k][:TX] * (row - shift(row, 1, 1))
        side = (flux_x - shift(flux_x, -1, 0))[:TX] + (flux_y - shift(flux_y, -1, 1))[:, :TY]
        above = u0.part(0, k + 1)[:TX] if k is not NZ - 1 else jnp.zeros((TX, TY), F32)
        flux_up = z_face0.part(0, k + 1)[:TX] * (above - here)
        solution_out[span(k * TX, TX), :] = here
        out = f0.part(0, k)[:TX] - kappa[k] * here - side - flux_z + flux_up
        residual_out[span(k * TX, TX), :] = out
        return here, flux_up

    start = z_face0.part(0, 0)[:TX] * u0.part(0, 0)[:TX]
    carry = loop(NZ - 1, residual, (start, start), 4)
    residual(NZ - 1, carry)


SAVED_ROWS = 72 * 1024
MEBIBYTES = {"pack": 56}
COSTS = {
    "pack": 3 * 10**9, "down": 10**10,
    "window_coeffs": 4 * 10**9, "global_coeffs": 4 * 10**9, "up": 12 * 10**9,
}


def call(kernel, name, outs, ins, scratch=(), in_specs=None, out_specs=None, aliases=None):
    shapes = [jax.ShapeDtypeStruct(s, F32) for s in outs]
    return pl.pallas_call(
        kernel,
        name=name,
        out_shape=shapes,
        in_specs=in_specs or [VMEM] * len(ins),
        out_specs=out_specs or [VMEM] * len(outs),
        scratch_shapes=list(scratch),
        input_output_aliases=aliases or {},
        compiler_params=pltpu.CompilerParams(vmem_limit_bytes=MEBIBYTES.get(name, 32) * 1024 * 1024),
        cost_estimate=pl.CostEstimate(flops=COSTS[name], bytes_accessed=4 * sum(x.size for x in ins), transcendentals=0),
    )(*ins)


def body(right_side, kappa_sq, cond_x, cond_y, cond_z):
    gx, gy = lax.axis_size("gx"), lax.axis_size("gy")
    tiles = [v.reshape(NZ * TX, TY) for v in (right_side, kappa_sq, cond_x, cond_y, cond_z)]
    slab, strip = (SLAB + 6 * NZ, 128), (STRIP + 24, 128)
    vm = lambda *shape: pltpu.VMEM(shape, F32)
    dma = lambda n: pltpu.SemaphoreType.DMA((n,))
    devices = gx * gy
    near = lambda n: [(i, i ^ 1) for i in range(n)]
    far = lambda n: [(i, (i + 1 ^ 1) - 1) for i in range(1, n - 1)]
    even_x, even_y = lax.axis_index("gx") % 2 == 0, lax.axis_index("gy") % 2 == 0
    x_near, x_far, y_near, y_far, share2, stack, copies = call(
        functools.partial(pack_kernel, devices // 2),
        "pack",
        [slab, slab, strip, strip, (6 * NZ, 128), (5 * NZ * TX, TY), (devices // 2 * SHARE, 128)],
        tiles,
        [dma(5)],
        [HBM] * 5,
    )
    y_near = lax.ppermute(y_near, "gy", near(gy))
    y_far = lax.ppermute(y_far, "gy", far(gy))
    x_near = lax.ppermute(x_near, "gx", near(gx))
    x_far = lax.ppermute(x_far, "gx", far(gx))
    yr, yl = jnp.where(even_y, y_near, y_far), jnp.where(even_y, y_far, y_near)
    half = STRIP // 2
    head = jnp.concatenate([yl[:half], yl[STRIP:], yr[:half], yr[STRIP:]])
    tail = jnp.concatenate([yl[half:], yr[half:]])
    c_near = lax.ppermute(jnp.where(even_x, tail, head), "gx", near(gx))
    c_far = lax.ppermute(jnp.where(even_x, head, tail), "gx", far(gx))
    copies, c_near = lax.optimization_barrier((copies, c_near))
    corner_r, corner_l = jnp.where(even_x, c_near, c_far), jnp.where(even_x, c_far, c_near)
    cores = [[x * gy + y for x in range(core, gx, 2) for y in range(gy)] for core in range(2)]
    blocks = copies.reshape(devices // 2, SHARE, 128)
    own = lax.all_to_all(blocks, ("gx", "gy"), 0, 0, axis_index_groups=cores).reshape(gx // 2, gy * SHARE, 128)
    level = lambda rows, n: [vm(NZ * rows, 128)] * n
    faces = lambda rows, tiles: vm(tiles * (NZ + 1) * rows, 128)
    rows3, rows4 = 2 * gx, gx
    size, tall = (NZ * TX, 128), ((NZ + 1) * TX, 128)
    k2 = call(
        window_kernel, "window_coeffs", [(NZ * TX * 4 + TX, 128)], [share2, x_near, x_far, yr, yl, corner_r, corner_l], level(TX, 7)
    )[0]
    big, big_z = (2 * NZ * 2 * TX, 128), (2 * (NZ + 1) * 2 * TX, 128)
    total0, total1 = 2 * (NZ * 6 + 1) * 2 * TX, (NZ * 6 + 1) * TX
    sends, saved = call(
        functools.partial(down_kernel, gx * TX, gy * TY),
        "down",
        [(devices // 2 * BLOCK, 128), (max(total0 + total1, SAVED_ROWS), 128)],
        [stack, yr, yl, corner_r, corner_l, x_near, x_far],
        [vm(*big)] * 10 + [vm(*big_z)] + level(TX, 10) + [faces(TX, 1)] + level(8, 10) + [faces(8, 1)] + [dma(12)],
        out_specs=[VMEM, ANY],
    )
    sends, own = lax.optimization_barrier((sends, own))
    other = lax.ppermute(own, "gx", near(gx))
    blocks = sends.reshape(devices // 2, BLOCK, 128)
    own_blocks = lax.all_to_all(blocks, ("gx", "gy"), 0, 0, axis_index_groups=cores)
    other_blocks = lax.ppermute(own_blocks, "gx", near(gx))
    whole = call(
        functools.partial(global_kernel, gx, gy),
        "global_coeffs",
        [(5 * NZ * (rows3 + rows4), 128)],
        [own, other],
        level(rows3, 6) + [faces(rows3, 1)] + level(rows3, 1) + level(rows4, 6) + [faces(rows4, 1)] + level(rows4, 1)
        + [vm(gx // 2, 2, gy * SHARE, 128), dma(2)],
        in_specs=[ANY] * 2,
    )[0]
    field, residual = call(
        functools.partial(up_kernel, gx, gy),
        "up",
        [(NZ * TX, TY)] * 2,
        [own_blocks, other_blocks, whole, k2, stack, saved],
        [vm(total0, 128), vm(total1, 128)] + level(TX, 3) + [vm(NZ * 2 * TX, 128), vm(*size), vm(*big), vm(*big)]
        + level(rows3, 3) + level(rows4, 2) + [dma(2)],
        in_specs=[VMEM] * 5 + [ANY],
    )
    return field.reshape(right_side.shape), residual.reshape(right_side.shape)


def solution(mesh):
    spec = P(None, "gx", "gy")
    fits = (mesh.shape["gx"], mesh.shape["gy"]) == (8, 4)
    plan = body if fits else spread_body
    return jax.shard_map(plan, mesh=mesh, in_specs=(spec,) * 5, out_specs=(spec, spec), check_vma=False)
```

```python
import functools

import jax
import jax.numpy as jnp
from jax import lax
from jax.experimental import pallas as pl
from jax.experimental.pallas import tpu as pltpu
from jax.sharding import PartitionSpec as P

LEVELS = 4
COARSE_SWEEPS = 16


OMEGA = 0.8


def with_halo(cells, sides, width):
    for axis, dim in sides:
        count = lax.axis_size(axis)
        ends = count - 1
        head = lax.slice_in_dim(cells, 0, width, axis=dim)
        tail = lax.slice_in_dim(cells, cells.shape[dim] - width, cells.shape[dim], axis=dim)
        cells = jnp.concatenate(
            [
                lax.ppermute(tail, axis, [(i, (i + 1) % count) for i in range(ends)]),
                cells,
                lax.ppermute(head, axis, [((i + 1) % count, i) for i in range(ends)]),
            ],
            axis=dim,
        )
    return cells


def apply_op(field, padded, coeffs):
    kappa, x_up, x_low, y_up, y_low, z_up, z_low = coeffs
    zpad = jnp.pad(field, ((1, 1), (0, 0), (0, 0)))
    out = (
        kappa * field
        + x_up * (field - padded[:, 2:, 1:-1])
        + x_low * (field - padded[:, :-2, 1:-1])
    )
    out = out + y_up * (field - padded[:, 1:-1, 2:]) + y_low * (field - padded[:, 1:-1, :-2])
    return out + z_up * (field - zpad[2:]) + z_low * (field - zpad[:-2])


def face_pad(field):
    return with_halo(field, (("gx", 1), ("gy", 2)), 1)


def line_factors(coeffs):
    kappa, x_up, x_low, y_up, y_low, z_up, z_low = coeffs
    diag = kappa + x_up + x_low + y_up + y_low + z_up + z_low
    upper_src = z_up.at[-1].set(jnp.zeros_like(z_up[-1]))

    def factor_step(upper_prev, planes):
        diag_k, low_k, up_k = planes
        inv = 1.0 / (diag_k + low_k * upper_prev)
        upper = -up_k * inv
        return (upper, (inv, upper))

    start = jnp.zeros_like(diag[0])
    unused, stacked = lax.scan(factor_step, start, (diag, z_low, upper_src), unroll=True)
    return stacked


def line_solve(rhs, factors, z_low):
    inverses, uppers = factors

    def forward_step(prev, planes):
        rhs_k, low_k, inv_k = planes
        value = (rhs_k + low_k * prev) * inv_k
        return (value, value)

    start = jnp.zeros_like(rhs[0])
    unused, forward = lax.scan(forward_step, start, (rhs, z_low, inverses), unroll=True)

    def back_step(after, planes):
        fwd_k, up_k = planes
        value = fwd_k - up_k * after
        return (value, value)

    unused, result = lax.scan(back_step, start, (forward, uppers), reverse=True, unroll=True)
    return result


def mean_four(field):
    depth, rows, cols = field.shape
    return field.reshape(depth, rows // 2, 2, cols // 2, 2).mean(axis=(2, 4))


def coarsen(coeffs):
    kappa, x_up, x_low, y_up, y_low, z_up, z_low = coeffs
    depth, rows, cols = kappa.shape
    shape = (depth, rows // 2, 2, cols // 2, 2)
    xu_c = x_up.reshape(shape)[:, :, 1].mean(axis=-1) * 0.25
    xl_c = x_low.reshape(shape)[:, :, 0].mean(axis=-1) * 0.25
    yu_c = y_up.reshape(shape)[:, :, :, :, 1].mean(axis=2) * 0.25
    yl_c = y_low.reshape(shape)[:, :, :, :, 0].mean(axis=2) * 0.25
    return (mean_four(kappa), xu_c, xl_c, yu_c, yl_c, mean_four(z_up), mean_four(z_low))


def prolong(padded):
    depth = padded.shape[0]
    rows = padded.shape[1] - 2
    cols = padded.shape[2] - 2
    centre = padded[:, 1:-1, :]
    even = 0.75 * centre + 0.25 * padded[:, :-2, :]
    odd = 0.75 * centre + 0.25 * padded[:, 2:, :]
    spread = jnp.stack([even, odd], axis=2).reshape(depth, 2 * rows, cols + 2)
    centre = spread[:, :, 1:-1]
    even = 0.75 * centre + 0.25 * spread[:, :, :-2]
    odd = 0.75 * centre + 0.25 * spread[:, :, 2:]
    return jnp.stack([even, odd], axis=3).reshape(depth, 2 * rows, 2 * cols)


def coarse_solve(rhs, coeffs):
    factors = line_factors(coeffs)
    field = OMEGA * line_solve(rhs, factors, coeffs[6])

    def spread_sweep(sweep, current):
        padded = with_halo(current, (("gx", 1), ("gy", 2)), 1)
        defect = rhs - apply_op(current, padded, coeffs)
        return current + OMEGA * line_solve(defect, factors, coeffs[6])

    field = lax.fori_loop(0, COARSE_SWEEPS - 1, spread_sweep, field)
    return field


def cycle(rhs, coeffs, level):
    if level == LEVELS:
        return coarse_solve(rhs, coeffs)
    factors = line_factors(coeffs)
    field = OMEGA * line_solve(rhs, factors, coeffs[6])
    padded = face_pad(field)
    defect = rhs - apply_op(field, padded, coeffs)
    correction = cycle(mean_four(defect), coarsen(coeffs), level + 1)
    rimmed = with_halo(correction, (("gx", 1), ("gy", 2)), 1)
    field = field + prolong(rimmed)
    padded = face_pad(field)
    defect = rhs - apply_op(field, padded, coeffs)
    return field + OMEGA * line_solve(defect, factors, coeffs[6])


def spread_body(right_side, kappa_sq, cond_x, cond_y, cond_z):
    padded_x = with_halo(cond_x, (("gx", 1),), 1)
    padded_y = with_halo(cond_y, (("gy", 2),), 1)
    padded_z = jnp.pad(cond_z, ((1, 1), (0, 0), (0, 0)))
    x_up = 0.5 * (cond_x + padded_x[:, 2:, :])
    x_low = 0.5 * (cond_x + padded_x[:, :-2, :])
    y_up = 0.5 * (cond_y + padded_y[:, :, 2:])
    y_low = 0.5 * (cond_y + padded_y[:, :, :-2])
    z_up = 0.5 * (cond_z + padded_z[2:])
    z_low = 0.5 * (cond_z + padded_z[:-2])
    coeffs = (kappa_sq, x_up, x_low, y_up, y_low, z_up, z_low)
    solution_field = cycle(right_side, coeffs, 0)
    residual = right_side - apply_op(solution_field, face_pad(solution_field), coeffs)
    return (solution_field, residual)


F32 = jnp.float32
BF16 = jnp.bfloat16
NZ = 32
HALF = NZ // 2
TX, TY = 16, 128
HALO = 8
SLAB = 5 * NZ * HALO
STRIP = 160
CORNER = 104
SHARE = 40
BLOCK = NZ + 8
VMEM = pl.BlockSpec(memory_space=pltpu.VMEM)
ANY = pl.BlockSpec(memory_space=pl.ANY)
HBM = pl.BlockSpec(memory_space=pltpu.HBM)


def iota(shape, dim):
    return lax.broadcasted_iota(jnp.int32, shape, dim)


def shift(x, by, axis):
    by = by % x.shape[axis]
    return pltpu.roll(x, by, axis) if by else x


def mix(x, weights, parts=2):
    pieces = []
    for n in range(parts):
        piece = x.astype(BF16)
        pieces.append(piece)
        if n < parts - 1:
            x = x - piece.astype(F32)
    out = jnp.dot(jnp.concatenate(pieces, axis=0), weights, preferred_element_type=F32)
    rows = x.shape[0]
    return sum(out[n * rows : (n + 1) * rows] for n in reversed(range(parts)))


def matrix(mask, weight=1.0):
    return jnp.where(mask, weight, 0.0).astype(BF16)


def span(start, size):
    if not isinstance(start, int):
        start = pl.multiple_of(start, 8)
    return pl.ds(start, size)


class Field:
    def __init__(self, ref, rows, tiles=1, planes=NZ, start=0):
        self.ref, self.rows, self.tiles, self.planes, self.start = ref, rows, tiles, planes, start

    def base(self, tile, k):
        return self.start + tile * self.planes * self.rows + k * self.rows

    def part(self, tile, k):
        return self.ref[span(self.base(tile, k), self.rows), :]

    def __getitem__(self, k):
        parts = [self.part(t, k) for t in range(self.tiles)]
        return parts[0] if self.tiles == 1 else jnp.concatenate(parts, axis=1)

    def __setitem__(self, k, value):
        for t in range(self.tiles):
            self.put(t, k, value[:, 128 * t : 128 * (t + 1)])

    def put(self, tile, k, value):
        self.ref[span(self.base(tile, k), self.rows), :] = value

    def every_second(self, at, count, odd):
        parts = []
        for t in range(self.tiles):
            first = self.base(t, 0) + 2 * at + odd
            parts.append(self.ref[pl.ds(first, count, stride=2), :])
        return parts[0] if self.tiles == 1 else jnp.concatenate(parts, axis=1)

    def row(self, row):
        return self.ref[pl.ds(self.start + row, self.planes, stride=self.rows), :]


def stack_fields(ref, rows, count, tiles=1, z_face=True, start=0):
    size = tiles * NZ * rows
    out = [Field(ref, rows, tiles, NZ, start + n * size) for n in range(count)]
    return out + [Field(ref, rows, tiles, NZ + 1, start + count * size)] if z_face else out


def loop(count, step, carry, unroll=None):
    if unroll is None or unroll >= count:
        for i in range(count):
            carry = step(i, carry)
        return carry
    return lax.fori_loop(0, count, step, carry, unroll=unroll)


def neighbours(field, x_face, y_face):
    out = x_face * shift(field, 1, 0) + shift(x_face * field, -1, 0)
    return out + (y_face * shift(field, 1, 1) + shift(y_face * field, -1, 1))


class Line:
    def __init__(self, inv, z_face):
        self.inv, self.z_face = inv, z_face

    def inward(self, k, upper):
        return self.z_face[k + 1 if upper else k] * self.inv[k]

    def outward(self, k, upper):
        return self.z_face[k if upper else k + 1] * self.inv[k]


class StoredLine:
    def __init__(self, inv, g, c):
        self.inv, self.g, self.c = inv, g, c

    def inward(self, k, upper):
        return self.g[k]

    def outward(self, k, upper):
        return self.c[k]


def sweep_in(rhs, line, keep, start, unroll):
    def step(i, carry):
        low, high = carry
        k, m = i, NZ - 1 - i
        low = rhs(k) * line.inv[k] + line.inward(k, False) * low
        high = rhs(m) * line.inv[m] + line.inward(m, True) * high
        keep[k] = low
        keep[m] = high
        return low, high

    return loop(HALF, step, (start, start), unroll)


def sweep_out(ends, kept, line, emit, unroll):
    low, high = ends
    a, b = line.outward(HALF - 1, False), line.outward(HALF, True)
    low = (low + a * high) * (1.0 / (1.0 - a * b))
    high = high + b * low

    def step(i, carry):
        low, high = carry
        k, m = HALF - 1 - i, HALF + i
        emit(k, low)
        emit(m, high)
        low = kept[k - 1] + line.outward(k - 1, False) * low
        high = kept[m + 1] + line.outward(m + 1, True) * high
        return low, high

    low, high = loop(HALF - 1, step, (low, high), unroll)
    emit(0, low)
    emit(NZ - 1, high)


def factor(diag, z_face, tiles, inv_out, unroll, rhs=None, keep=None, g_out=None, c_out=None):
    ends = []
    for t in range(tiles):
        zero = diag.part(t, 0) * 0.0

        def one(k, upper, before, last, prev):
            below, above = z_face.part(t, k), z_face.part(t, k + 1)
            inner, outer = (above, below) if upper else (below, above)
            minor = (diag.part(t, k) + below + above) * last - (inner * inner) * before
            inv = last * (1.0 / minor)
            inv_out.put(t, k, inv)
            if g_out is not None:
                g_out.put(t, k, inner * inv)
                c_out.put(t, k, outer * inv)
            if rhs is not None:
                prev = rhs.part(t, k) * inv + (inner * inv) * prev
                keep.put(t, k, prev)
            return last, minor, prev

        def step(i, carry):
            low, high = carry
            return one(i, False, *low), one(NZ - 1 - i, True, *high)

        start = (zero, zero + 1.0, zero)
        low, high = loop(HALF, step, (start, start), unroll)
        ends.append((low[2], high[2]))
    join = lambda n: ends[0][n] if tiles == 1 else jnp.concatenate([e[n] for e in ends], axis=1)
    return join(0), join(1)


def z_faces(cz, out, tiles=1):
    for t in range(tiles):
        before = None
        for k in range(NZ + 1):
            here = cz.part(t, k) if k < NZ else None
            both = here if before is None else before if here is None else here + before
            out.put(t, k, 0.5 * both)
            before = here


def base_diag(kappa, x_face, y_face):
    return kappa + (x_face + shift(x_face, -1, 0)) + (y_face + shift(y_face, -1, 1))


def window_mask(rows, lanes, tile_x, tile_y, halo, ix, iy, nx, ny):
    x, y = iota((rows, lanes), 0), iota((rows, lanes), 1)
    x = jnp.where(x < (rows + tile_x) // 2, x, x - rows)
    y = jnp.where(y < (lanes + tile_y) // 2, y, y - lanes)
    valid = (y >= -halo) & (y < tile_y + halo) & (x >= -halo) & (x < tile_x + halo)
    x, y = x + ix * tile_x, y + iy * tile_y
    return (valid & (x >= 0) & (x < nx) & (y >= 0) & (y < ny)).astype(F32)


def smooth_down(f, x_face, y_face, line, ends, kept, u, r, unroll):
    def emit(k, value):
        field = OMEGA * value
        u[k] = field
        r[k] = (1.0 - OMEGA) * f[k] + neighbours(field, x_face[k], y_face[k])

    sweep_out(ends, kept, line, emit, unroll)


def smooth_up(f, x_face, y_face, line, u, e, kept, mask, unroll):
    masked = (lambda v: v) if mask is None else (lambda v: v * mask)

    def rhs(k):
        field = masked(u[k] + e[k])
        u[k] = field
        return masked(f[k] + neighbours(field, x_face[k], y_face[k]))

    def emit(k, value):
        u[k] = (1.0 - OMEGA) * u[k] + OMEGA * value

    zero = jnp.zeros((u.rows, 128 * u.tiles), F32)
    ends = sweep_in(rhs, line, kept, zero, unroll)
    sweep_out(ends, kept, line, emit, unroll)


def spread_rows(cells, before, after, dest, size):
    dest[pl.ds(0, size, stride=2), :] = (0.75 * cells + 0.25 * before).reshape(size, 128)
    dest[pl.ds(1, size, stride=2), :] = (0.75 * cells + 0.25 * after).reshape(size, 128)


def spread_matrix(fine, base, coarse_count, circular=False):
    j = iota((128, fine.shape[1]), 0) + base
    parent = (fine + 2048) // 2 - 1024
    partner = parent + 2 * ((fine + 2048) % 2) - 1
    if circular:
        j, parent, partner = j % 128, parent % 128, partner % 128
    weights = jnp.where(j == parent, 0.75, jnp.where(j == partner, 0.25, 0.0))
    if not circular:
        inside = (j >= 0) & (j < coarse_count) & (fine >= 0) & (fine < 2 * coarse_count)
        weights = jnp.where(inside, weights, 0.0)
    return weights.astype(BF16)


def lane_group(rows, width):
    return iota((rows, 128), 1) // width


def fold_planes(cells, turn):
    group = lane_group(8, 32)
    out = cells[:8]
    for n in range(1, 4):
        out = jnp.where(group == n, cells[8 * n : 8 * n + 8], out)
    return pltpu.roll(out, turn, 1)


def share_blocks(kinds):
    iy = lax.axis_index("gy")
    y, lane = iota((128, 128), 0), iota((128, 128), 1)
    x_in, y_in = y // 32, y % 32
    x_out, y_out = lane % 32 // 16, lane % 16
    pair_y, pair_x = y_in // 2 == y_out, x_in // 2 == x_out
    a, b, c, d, kappa, cz = kinds
    eighth = lambda mask: matrix(mask, 0.125)
    blocks = [
        mix(a, eighth(pair_y & (x_in == 2 * x_out))) + mix(b, eighth(pair_y & (x_in == 1) & (x_out == 1))),
        mix(b, eighth(pair_y & (x_in == 3) & (x_out == 0)))
        + mix(d, eighth((x_out == 1) & (y_in == 31) & (x_in // 2 == y_out))),
        mix(c, eighth(pair_x & (y_in == 2 * y_out))) + mix(d, eighth(pair_x & (y_in == 2 * y_out - 1))),
        mix(kappa, matrix(pair_x & pair_y, 0.25)),
        mix(cz, matrix(pair_x & pair_y, 0.25)),
    ]
    return [fold_planes(cells, 16 * iy) for cells in blocks]


def fetch_all(sources, dests, sems, first=0):
    copies = [pltpu.make_async_copy(a, b, sems.at[first + n]) for n, (a, b) in enumerate(zip(sources, dests))]
    for copy in copies:
        copy.start()
    return copies


def pack_kernel(devices, f_in, kappa_in, cx_in, cy_in, cz_in, x_near, x_far, y_near, y_far, share2, stack, copies, sems):
    even_x, even_y = lax.axis_index("gx") % 2 == 0, lax.axis_index("gy") % 2 == 0
    tiles = [stack.at[pl.ds(a * NZ * TX, NZ * TX), :] for a in range(5)]
    for copy in fetch_all((f_in, kappa_in, cx_in, cy_in, cz_in), tiles, sems):
        copy.wait()
    f, kappa, cx, cy, cz = tiles
    for a, ref in enumerate(tiles):
        cells = ref[...].reshape(NZ, TX, TY)
        at = pl.ds(a * NZ * HALO, NZ * HALO)
        head = cells[:, :HALO].reshape(NZ * HALO, TY)
        tail = cells[:, TX - HALO :].reshape(NZ * HALO, TY)
        x_near[at, :] = jnp.where(even_x, tail, head)
        x_far[at, :] = jnp.where(even_x, head, tail)
    y, lane = iota((128, 128), 0), iota((128, 128), 1)
    fourth = y // 4 == lane % 32
    rows = lambda ref: [Field(ref, TX).row(r) for r in range(TX)]
    cx_rows, cy_rows, kappa_rows, cz_rows = rows(cx), rows(cy), rows(kappa), rows(cz)
    totals = lambda v: [(v[4 * i] + v[4 * i + 1]) + (v[4 * i + 2] + v[4 * i + 3]) for i in range(4)]
    stack = [cx_rows[4 * i] for i in range(4)] + [cx_rows[4 * i + 3] for i in range(4)]
    stack = mix(jnp.concatenate(stack + totals(kappa_rows) + totals(cz_rows), axis=0), matrix(fourth))
    ends = [matrix(fourth & (y % 4 == 0)), matrix(fourth & (y % 4 == 3))]
    sides = mix(jnp.concatenate(totals(cy_rows), axis=0), jnp.concatenate(ends, axis=1))
    group = lane_group(NZ, 32)

    def merge(cells, scale):
        out = cells[:NZ]
        for xi in range(1, 4):
            out = jnp.where(group == xi, cells[NZ * xi : NZ * (xi + 1)], out)
        return out * scale

    kinds = [merge(stack[:128], 1 / 128), merge(stack[128:256], 1 / 128)]
    kinds += [merge(sides[:, :128], 1 / 128), merge(sides[:, 128:], 1 / 128)]
    kinds += [merge(stack[256:384], 1 / 16), merge(stack[384:], 1 / 16)]
    for t, cells in enumerate(share_blocks(kinds)):
        for n in range(devices):
            copies[pl.ds(n * SHARE + 8 * t, 8), :] = cells
    head = [jnp.zeros((8, 128), F32)] * 3
    tail = [jnp.zeros((8, 128), F32)] * 3
    slot = iota((8, 128), 1) % 32 // 4
    for t, cells in enumerate(kinds):
        for dest, first in ((share2, 0), (x_near, SLAB), (x_far, SLAB)):
            dest[pl.ds(first + t * NZ, NZ), :] = cells
        for zv in range(4):
            n = 4 * t + zv
            piece = cells[8 * zv : 8 * zv + 8]
            head[n // 8] = jnp.where(slot == n % 8, shift(piece, 4 * (n % 8), 1), head[n // 8])
            tail[n // 8] = jnp.where(slot == n % 8, shift(piece, 4 * (n % 8) + 4, 1), tail[n // 8])
    for n in range(3):
        y_near[pl.ds(STRIP + 8 * n, 8), :] = jnp.where(even_y, tail[n], head[n])
        y_far[pl.ds(STRIP + 8 * n, 8), :] = jnp.where(even_y, head[n], tail[n])

    group = lane_group(8, 8)
    for a, ref in enumerate((f, kappa, cx, cy, cz)):
        for half in range(2):
            for zo in range(2):
                head = jnp.zeros((8, 128), F32)
                tail = jnp.zeros((8, 128), F32)
                for zi in range(16):
                    cells = ref[pl.ds((zo * 16 + zi) * TX + 8 * half, 8), :]
                    cells = shift(cells, 8 * zi, 1)
                    head = jnp.where(group == zi, cells, head)
                    tail = jnp.where(group == (zi - 1) % 16, cells, tail)
                at = pl.ds(((half * 5 + a) * 2 + zo) * 8, 8)
                y_near[at, :] = jnp.where(even_y, tail, head)
                y_far[at, :] = jnp.where(even_y, head, tail)


def window2(tile, after, before, dest, first, iy, gy):
    lane = iota((NZ, 128), 1)
    first_after, first_before = jnp.where(iy < gy - 1, 36, 0), jnp.where(iy > 0, 124, 128)
    for xi in range(4):
        turned = (lane - 32 * xi + 128) % 128
        cells = jnp.where(turned < 32, tile, jnp.where(turned < first_after, after, jnp.where(turned >= first_before, before, 0.0)))
        dest[pl.ds(first + xi, NZ, stride=TX), :] = shift(cells, -32 * xi, 1)


def window_kernel(share2, x_near, x_far, yr, yl, cr, cl, out, a, b, c, d, kappa, cz, diag):
    ix, iy = lax.axis_index("gx"), lax.axis_index("gy")
    gy = lax.axis_size("gy")
    nx, ny = lax.axis_size("gx") * 4, gy * 32
    refs = (a, b, c, d, kappa, cz)

    def unpack(ref, first, t, turn):
        pieces = []
        for zv in range(4):
            n = 4 * t + zv
            pieces.append(shift(ref[span(first + 8 * (n // 8), 8), :], turn - 4 * (n % 8), 1))
        return jnp.concatenate(pieces, axis=0)

    near, far = STRIP // 2, CORNER + STRIP // 2
    even_x = ix % 2 == 0
    for t, dest in enumerate(refs):
        beside = x_near[pl.ds(SLAB + t * NZ, NZ), :], x_far[pl.ds(SLAB + t * NZ, NZ), :]
        for first, cells, right, left, r_at, l_at in (
            (0, share2[pl.ds(t * NZ, NZ), :], yr, yl, STRIP, STRIP),
            (4, jnp.where(even_x, *beside), cr, cr, far, near),
            (12, jnp.where(even_x, *beside[::-1]), cl, cl, far, near),
        ):
            window2(cells, unpack(right, r_at, t, 32), unpack(left, l_at, t, 92), dest, first, iy, gy)
        for x in range(8, 12):
            dest[pl.ds(x, NZ, stride=TX), :] = jnp.zeros((NZ, 128), F32)
    mask = window_mask(TX, 128, 4, 32, 4, ix, iy, nx, ny)
    a, b, c, d, kappa, cz, diag = (Field(ref, TX) for ref in (*refs, diag))
    x_face, y_face, inv, z_face = stack_fields(out, TX, 3)
    for k in range(NZ):
        x_k = a[k] + shift(b[k], 1, 0)
        y_k = c[k] + shift(d[k], 1, 1)
        x_face[k] = x_k
        y_face[k] = y_k
        diag[k] = base_diag(jnp.where(mask > 0, kappa[k], 1.0), x_k, y_k)
    z_faces(cz, z_face)
    factor(diag, z_face, 1, inv, None)


def assemble3(block, dest, gx, gy, rows):
    group = lane_group(8, 16)
    for ix in range(gx):
        blocks = [block(ix, iy) for iy in range(gy)]
        for zo in range(4):
            for xi in range(2):
                q = 2 * zo + xi
                cells = blocks[0]
                for iy in range(1, gy):
                    cells = jnp.where(group == (iy + q) % 8, blocks[iy], cells)
                dest[pl.ds(8 * zo * rows + 2 * ix + xi, 8, stride=rows), :] = shift(cells, -16 * q, 1)


def global_kernel(gx, gy, own, other, *refs):
    out, raw3, raw4, shares, sems = refs[0], refs[1:9], refs[9:17], refs[17], refs[18]
    outs3 = stack_fields(out, 2 * gx, 5, z_face=False)
    outs4 = stack_fields(out, gx, 5, z_face=False, start=5 * NZ * 2 * gx)
    core = lax.axis_index("gx") % 2
    copies = [
        pltpu.make_async_copy(own, shares.at[:, core], sems.at[0]),
        pltpu.make_async_copy(other, shares.at[:, 1 - core], sems.at[1]),
    ]
    for copy in copies:
        copy.start()
    for copy in copies:
        copy.wait()
    rows, cols = 2 * gx, 16 * gy
    for t, n in enumerate((0, 1, 2, 4, 5)):
        block = lambda jx, jy: shares[jx // 2, jx % 2, pl.ds(jy * SHARE + 8 * t, 8), :]
        assemble3(block, raw3[n], gx, gy, rows)
    xl, xu, yl, yu = (Field(ref, rows) for ref in raw3[:4])
    x, y = iota((rows, 128), 0), iota((rows, 128), 1)
    odd_row, inside = x % 2 == 1, y < cols
    for k in range(NZ):
        half = jnp.where(inside, xu[k], 0.0)
        below = jnp.where(odd_row | (x < 2), 0.0, shift(half, 2, 0))
        x_k = jnp.where(inside, xl[k] + below, 0.0)
        xl[k] = x_k
        xu[k] = jnp.where(x == rows - 1, shift(half, 1, 0), shift(x_k, -1, 0))
        next_row = shift(half, -1, 0)
        below = jnp.where(odd_row, shift(half, 15, 1), shift(next_row, 16, 1))
        y_k = jnp.where(inside, yl[k] + jnp.where((y % 16 == 0) & (y > 0), below, 0.0), 0.0)
        yl[k] = y_k
        above = jnp.where(odd_row, shift(half, 14, 1), shift(next_row, 15, 1))
        yu[k] = jnp.where(y == cols - 1, above, jnp.where(inside, shift(y_k, -1, 1), 0.0))
    yy, jj = iota((128, 128), 0), iota((128, 128), 1)
    keep = yy // 2 == jj
    pair, even, odd = matrix(keep), matrix(keep & (yy % 2 == 0)), matrix(keep & (yy % 2 == 1))
    size = NZ * rows // 2
    lows = [Field(ref, rows) for ref in raw3]
    first = lambda n: lows[n].every_second(0, size, 0)
    second = lambda n: lows[n].every_second(0, size, 1)
    raw4[0][...] = 0.125 * mix(first(0), pair)
    raw4[1][...] = 0.125 * mix(second(1), pair)
    raw4[2][...] = 0.125 * mix(first(2) + second(2), even)
    raw4[3][...] = 0.125 * mix(first(3) + second(3), odd)
    raw4[4][...] = 0.25 * mix(first(4) + second(4), pair)
    raw4[5][...] = 0.25 * mix(first(5) + second(5), pair)
    for raw, outs in ((raw3, outs3), (raw4, outs4)):
        x, y = iota((rows, 128), 0), iota((rows, 128), 1)
        xl, xu, yl, yu, kappa, cz = (Field(ref, rows) for ref in raw[:6])
        z_face, diag = Field(raw[6], rows, 1, NZ + 1), Field(raw[7], rows)
        x_face, y_face, inv, g, c = outs
        inside_x, inside_y = (x > 0).astype(F32), ((y > 0) & (y < cols)).astype(F32)
        for k in range(NZ):
            xl_k, yl_k = xl[k], yl[k]
            diag[k] = jnp.where(y < cols, kappa[k], 1.0) + (xl_k + xu[k]) + (yl_k + yu[k])
            x_face[k] = xl_k * inside_x
            y_face[k] = yl_k * inside_y
        z_faces(cz, z_face)
        factor(diag, z_face, 1, inv, None, g_out=g, c_out=c)
        rows, cols = rows // 2, cols // 2


def down_kernel(nx, ny, *refs):
    stack, yr, yl, corner_r, corner_l, x_near, x_far = refs[:7]
    sends, saved = refs[7:9]
    scratch = list(refs[9:-1])
    sems = refs[-1]
    take = lambda n: [scratch.pop(0) for _ in range(n)]
    ix, iy = lax.axis_index("gx"), lax.axis_index("gy")
    gx, gy = lax.axis_size("gx"), lax.axis_size("gy")
    f, kappa, cx, cy, cz = (stack.at[pl.ds(a * NZ * TX, NZ * TX), :] for a in range(5))
    even_x = ix % 2 == 0
    rows, tiles = 2 * TX, 2
    whole = take(11)
    names = [Field(ref, rows, tiles) for ref in whole[:10]]
    x_face, y_face, inv, u, f0, kappa0, cz0, diag, kept, r = names
    z_face = Field(whole[10], rows, tiles, NZ + 1)
    group = lane_group(8, 8)

    def window(a, tile, z, after, before, turn):
        zo = z // 16
        slab = span(a * NZ * HALO + z * HALO, HALO)
        near, far = x_near[slab, :], x_far[slab, :]
        sides = [jnp.where(even_x, near, far), jnp.where(even_x, far, near)]
        main = jnp.concatenate([tile[span(z * TX, TX), :], *sides], axis=0)
        at = lambda first: span(first + (a * 2 + zo) * 8, 8)
        half = STRIP // 2
        sides = []
        for right, left in (
            (yr[at(0), :], yl[at(0), :]),
            (yr[at(half), :], yl[at(half), :]),
            (corner_r[at(CORNER), :], corner_r[at(0), :]),
            (corner_l[at(CORNER), :], corner_l[at(0), :]),
        ):
            cells = jnp.where(after, right, jnp.where(before, left, 0.0))
            sides.append(pltpu.roll(cells, turn, 1))
        return jnp.concatenate([main, jnp.concatenate(sides, axis=0)], axis=1)

    mask0 = window_mask(rows, 256, TX, TY, HALO, ix, iy, nx, ny)

    def prepare(z, cz_prev):
        zi = z % 16
        after, before = group == zi, group == (zi + 15) % 16
        turn = (128 - 8 * zi) % 128
        f_k, kappa_k, cx_k, cy_k, cz_k = (
            window(a, tile, z, after, before, turn) for a, tile in enumerate((f, kappa, cx, cy, cz))
        )
        f0[z] = f_k
        kappa0[z] = kappa_k
        cz0[z] = cz_k
        z_face[z] = 0.5 * (cz_k + cz_prev)
        x_k, y_k = 0.5 * (cx_k + shift(cx_k, 1, 0)), 0.5 * (cy_k + shift(cy_k, 1, 1))
        x_face[z] = x_k
        y_face[z] = y_k
        diag[z] = base_diag(jnp.where(mask0 > 0, kappa_k, 1.0), x_k, y_k)
        return cz_k

    last = loop(NZ, prepare, jnp.zeros((rows, 256), F32), 4)
    z_face[NZ] = 0.5 * last
    ends = factor(diag, z_face, tiles, inv, 8, f0, kept)
    copies = []

    def save(field):
        at = sum(copy[1] for copy in copies)
        count = field.ref.shape[0]
        copy = pltpu.make_async_copy(field.ref, saved.at[pl.ds(at, count), :], sems.at[len(copies)])
        copy.start()
        copies.append((copy, count))

    for field in (x_face, y_face, inv, f0):
        save(field)
    smooth_down(f0, x_face, y_face, Line(inv, z_face), ends, kept, u, r, 5)
    save(u)
    save(z_face)

    fine = (r, kappa0, cz0, x_face, y_face)
    lanes, tile_x, tile_y, halo = 256, TX, TY, HALO
    for level in (1, 2):
        rows, tile_x, tile_y, halo = rows // 2, tile_x // 2, tile_y // 2, halo // 2
        nx, ny = nx // 2, ny // 2
        whole = take(11)
        names = [Field(ref, rows) for ref in whole[:10]]
        x_face, y_face, inv, u, f1, kappa1, cz1, diag, kept, r = names
        z_face = Field(whole[10], rows, 1, NZ + 1)
        mask = window_mask(rows, 128, tile_x, tile_y, halo, ix, iy, nx, ny)
        y, j = iota((lanes, 128), 0), iota((lanes, 128), 1)
        if lanes == 128:
            j = jnp.where(j < 48, j, jnp.where(j >= 80, j - 64, -1))
        pair = matrix(y // 2 == j)
        even = (iota((1, lanes), 1) % 2 == 0).astype(F32)
        part = 128
        for at in range(0, NZ * rows, part):
            here = pl.ds(at, part)
            both = lambda n: fine[n].every_second(at, part, 0) + fine[n].every_second(at, part, 1)
            below = fine[3].every_second(at, part, 0)
            out = mix(jnp.concatenate([both(0), both(1), both(2), below, both(4) * even], axis=0), pair)
            for n, (dest, weight) in enumerate(((f1, 0.25), (kappa1, 0.25), (cz1, 0.25), (x_face, 0.125), (y_face, 0.125))):
                dest.ref[here, :] = weight * out[n * part : (n + 1) * part]
        for k in range(NZ):
            f1[k] = f1[k] * mask
            diag[k] = base_diag(jnp.where(mask > 0, kappa1[k], 1.0), x_face[k], y_face[k])
        z_faces(cz1, z_face)
        ends = factor(diag, z_face, 1, inv, None, f1, kept)
        smooth_down(f1, x_face, y_face, Line(inv, z_face), ends, kept, u, r, None)
        if level == 1:
            for field in (x_face, y_face, inv, f1, u, z_face):
                save(field)
        fine, lanes = (r, kappa1, cz1, x_face, y_face), 128

    group = lane_group(NZ, 32)
    out = f1.row(0)
    for xi in range(1, 4):
        out = jnp.where(group == xi, shift(f1.row(xi), 32 * xi, 1), out)
    for n in range(gx * gy // 2):
        sends[pl.ds(n * BLOCK, NZ), :] = out
    y, lane = iota((128, 128), 0), iota((128, 128), 1)
    total = jnp.zeros((NZ, 128), F32)
    for xi in range(2):
        place = (lane % 32 // 16 == xi) & (y // 2 == lane % 16) & (y < 32)
        total = total + mix(r.row(2 * xi) + r.row(2 * xi + 1), matrix(place, 0.25))
    total = fold_planes(total, 16 * iy)
    for n in range(gx * gy // 2):
        sends[pl.ds(n * BLOCK + NZ, 8), :] = total
    for copy, _ in copies:
        copy.wait()


def up_kernel(gx, gy, *refs):
    own, other, whole, k2, stack, saved, solution_out, residual_out = refs[:8]
    scratch = list(refs[8:-1])
    sems = refs[-1]
    take = lambda n: [scratch.pop(0) for _ in range(n)]
    ix, iy = lax.axis_index("gx"), lax.axis_index("gy")
    held0, held1 = take(2)
    split = held0.shape[0]
    parts = [saved.at[pl.ds(split, held1.shape[0]), :], saved.at[pl.ds(0, split), :]]
    fetched = fetch_all(parts, (held1, held0), sems)
    core = ix % 2

    def gathered(jx, jy, at):
        if isinstance(jx, int):
            same = core == jx % 2
            return jnp.where(same, own[jx // 2 * gy + jy, at, :], other[jx // 2 * gy + jy, at, :])
        return jx[1][jx[0] // 2 * gy + jy, at, :]
    f2, u2, kept2, wide, e_ref, e0_ref, kept0, u3, f3, r3, f4, u4 = take(12)

    rows, cols = 2 * gx, 16 * gy
    assemble3(lambda jx, jy: gathered(jx, jy, pl.ds(NZ, 8)), f3, gx, gy, rows)
    f3, u3, r3 = (Field(ref, rows) for ref in (f3, u3, r3))
    y = iota((rows, 128), 1)
    x_face3, y_face3, inv3, g3, c3 = stack_fields(whole, rows, 5, z_face=False)
    line3 = StoredLine(inv3, g3, c3)
    clean = (y < cols).astype(F32)
    for k in range(NZ):
        f3[k] = f3[k] * clean
    zero = jnp.zeros((rows, 128), F32)
    ends = sweep_in(lambda k: f3[k], line3, r3, zero, None)
    smooth_down(f3, x_face3, y_face3, line3, ends, r3, u3, Field(e_ref, rows), None)
    fine = Field(e_ref, rows)
    rows, cols = rows // 2, cols // 2
    size = NZ * rows
    yy, jj = iota((128, 128), 0), iota((128, 128), 1)
    f4[...] = 0.25 * mix(fine.every_second(0, size, 0) + fine.every_second(0, size, 1), matrix(yy // 2 == jj))
    f4, u4 = Field(f4, rows), Field(u4, rows)
    x_face4, y_face4, inv4, g4, c4 = stack_fields(whole, rows, 5, z_face=False, start=5 * NZ * 2 * rows)
    line4 = StoredLine(inv4, g4, c4)
    zero = jnp.zeros((rows, 128), F32)

    def solve4(rhs, old):
        kept, out = {}, {}
        ends = sweep_in(rhs, line4, kept, zero, None)

        def emit(k, value):
            out[k] = OMEGA * value if old is None else (1.0 - OMEGA) * old[k] + OMEGA * value

        sweep_out(ends, kept, line4, emit, None)
        for k in range(NZ):
            u4[k] = out[k]

    solve4(lambda k: f4[k], None)

    def relax(sweep, carry):
        old = [u4[k] for k in range(NZ)]
        solve4(lambda k: f4[k] + neighbours(old[k], x_face4[k], y_face4[k]), old)
        return carry

    lax.fori_loop(0, COARSE_SWEEPS - 1, relax, 0, unroll=5)

    cells = u4.ref[...].reshape(NZ, rows, 128)
    x = iota((1, rows, 128), 1)
    before = jnp.where(x > 0, shift(cells, 1, 1), 0.0)
    after = jnp.where(x < rows - 1, shift(cells, -1, 1), 0.0)
    spread_rows(cells, before, after, wide, size)
    e_ref[...] = mix(wide[pl.ds(0, 2 * size), :], spread_matrix(iota((128, 128), 1), 0, cols))
    rows, cols = 2 * rows, 2 * cols
    smooth_up(f3, x_face3, y_face3, line3, u3, Field(e_ref, rows), r3, None, None)

    def block(dx, dy):
        inside = ((ix + dx >= 0) & (ix + dx < gx)).astype(F32)
        jx, jy = jnp.clip(ix + dx, 0, gx - 1), jnp.clip(iy + dy, 0, gy - 1)
        return gathered((jx, other if dx else own), jy, pl.ds(0, NZ)) * inside

    for first, dx in ((0, 0), (4, 1), (12, -1)):
        window2(block(dx, 0), shift(block(dx, 1), 32, 1), shift(block(dx, -1), 96, 1), f2, first, iy, gy)
    for x in range(8, 12):
        f2[pl.ds(x, NZ, stride=TX), :] = jnp.zeros((NZ, 128), F32)
    f2, u2, kept2 = (Field(ref, TX) for ref in (f2, u2, kept2))
    x_face2, y_face2, inv2, z_face2 = stack_fields(k2, TX, 3)
    line2 = Line(inv2, z_face2)
    zero = jnp.zeros((TX, 128), F32)
    ends = sweep_in(lambda k: f2[k], line2, kept2, zero, None)

    def emit2(k, value):
        u2[k] = OMEGA * value

    sweep_out(ends, kept2, line2, emit2, None)

    cells = pltpu.roll(u3.ref[...].reshape(NZ, rows, 128), (rows - 2 * ix) % rows, 1)
    x = iota((1, rows, 128), 1)
    place = 2 * ix + jnp.where(x < rows // 2, x, x - rows)
    cells = jnp.where((place >= 0) & (place < rows), cells, 0.0)
    ring = lambda v, first: jnp.where(iota((1, 8, 128), 1) < first, v[:, :8], v[:, rows - 8 :])
    spread_rows(ring(cells, 4), ring(shift(cells, 1, 1), 4), ring(shift(cells, -1, 1), 4), wide, NZ * 8)
    lane = iota((128, 128), 1)
    fine_y = jnp.where(lane < 80, lane, lane - 128) + 32 * iy
    e_ref[...] = mix(wide[pl.ds(0, NZ * TX), :], spread_matrix(fine_y, 0, cols))
    mask2 = window_mask(TX, 128, 4, 32, 4, ix, iy, 4 * gx, 32 * gy)
    smooth_up(f2, x_face2, y_face2, line2, u2, Field(e_ref, TX), kept2, mask2, None)

    cells = u2.ref[...].reshape(NZ, TX, 128)
    ring = lambda v: jnp.where(iota((1, 8, 128), 1) < 6, v[:, :8], v[:, 8:])
    spread_rows(ring(cells), ring(shift(cells, 1, 1)), ring(shift(cells, -1, 1)), wide, NZ * 8)
    fine_y = jnp.where(lane < 96, lane, lane - 128)
    e_ref[...] = mix(wide[pl.ds(0, NZ * TX), :], spread_matrix(fine_y, 0, 0, circular=True))
    fetched[0].wait()
    x_face1, y_face1, inv1, f1, u1, z_face1 = stack_fields(held1, TX, 5)
    line1 = Line(inv1, z_face1)
    mask1 = window_mask(TX, 128, 8, 64, 4, ix, iy, 8 * gx, 64 * gy)
    smooth_up(f1, x_face1, y_face1, line1, u1, Field(e_ref, TX), kept2, mask1, None)

    cells = held1[pl.ds(u1.start, NZ * TX), :].reshape(NZ, TX, 128)
    spread_rows(cells, shift(cells, 1, 1), shift(cells, -1, 1), wide, NZ * TX)
    rows = 2 * TX
    weights = spread_matrix(iota((128, 256), 1), 0, 0, circular=True)
    e0 = Field(e0_ref, rows, 2)
    for k in range(0, NZ, 8):
        cells = mix(wide[pl.ds(k * rows, 8 * rows), :], weights)
        for t in range(2):
            e0_ref[pl.ds(e0.base(t, k), 8 * rows), :] = cells[:, 128 * t : 128 * (t + 1)]
    fetched[1].wait()
    x_face0, y_face0, inv0, f0, u0, z_face0 = stack_fields(held0, rows, 5, 2)
    mask0 = window_mask(rows, 256, TX, TY, HALO, ix, iy, TX * gx, TY * gy)
    smooth_up(f0, x_face0, y_face0, Line(inv0, z_face0), u0, e0, Field(kept0, rows, 2), mask0, None)

    kappa = Field(stack, TX, start=NZ * TX)

    def residual(k, carry):
        below, flux_z = carry
        column = u0.part(0, k)
        here = column[:TX]
        flux_x = (x_face0.part(0, k) * (column - shift(column, 1, 0)))[: TX + 8]
        row = u0[k][:TX]
        flux_y = y_face0[k][:TX] * (row - shift(row, 1, 1))
        side = (flux_x - shift(flux_x, -1, 0))[:TX] + (flux_y - shift(flux_y, -1, 1))[:, :TY]
        above = u0.part(0, k + 1)[:TX] if k is not NZ - 1 else jnp.zeros((TX, TY), F32)
        flux_up = z_face0.part(0, k + 1)[:TX] * (above - here)
        solution_out[span(k * TX, TX), :] = here
        out = f0.part(0, k)[:TX] - kappa[k] * here - side - flux_z + flux_up
        residual_out[span(k * TX, TX), :] = out
        return here, flux_up

    start = z_face0.part(0, 0)[:TX] * u0.part(0, 0)[:TX]
    carry = loop(NZ - 1, residual, (start, start), 4)
    residual(NZ - 1, carry)


SAVED_ROWS = 72 * 1024
MEBIBYTES = {"pack": 56}
COSTS = {
    "pack": 3 * 10**9, "down": 10**10,
    "window_coeffs": 4 * 10**9, "global_coeffs": 4 * 10**9, "up": 12 * 10**9,
}


def call(kernel, name, outs, ins, scratch=(), in_specs=None, out_specs=None, aliases=None):
    shapes = [jax.ShapeDtypeStruct(s, F32) for s in outs]
    return pl.pallas_call(
        kernel,
        name=name,
        out_shape=shapes,
        in_specs=in_specs or [VMEM] * len(ins),
        out_specs=out_specs or [VMEM] * len(outs),
        scratch_shapes=list(scratch),
        input_output_aliases=aliases or {},
        compiler_params=pltpu.CompilerParams(vmem_limit_bytes=MEBIBYTES.get(name, 32) * 1024 * 1024),
        cost_estimate=pl.CostEstimate(flops=COSTS[name], bytes_accessed=4 * sum(x.size for x in ins), transcendentals=0),
    )(*ins)


def body(right_side, kappa_sq, cond_x, cond_y, cond_z):
    gx, gy = lax.axis_size("gx"), lax.axis_size("gy")
    tiles = [v.reshape(NZ * TX, TY) for v in (right_side, kappa_sq, cond_x, cond_y, cond_z)]
    slab, strip = (SLAB + 6 * NZ, 128), (STRIP + 24, 128)
    vm = lambda *shape: pltpu.VMEM(shape, F32)
    dma = lambda n: pltpu.SemaphoreType.DMA((n,))
    devices = gx * gy
    near = lambda n: [(i, i ^ 1) for i in range(n)]
    far = lambda n: [(i, (i + 1 ^ 1) - 1) for i in range(1, n - 1)]
    even_x, even_y = lax.axis_index("gx") % 2 == 0, lax.axis_index("gy") % 2 == 0
    x_near, x_far, y_near, y_far, share2, stack, copies = call(
        functools.partial(pack_kernel, devices // 2),
        "pack",
        [slab, slab, strip, strip, (6 * NZ, 128), (5 * NZ * TX, TY), (devices // 2 * SHARE, 128)],
        tiles,
        [dma(5)],
        [HBM] * 5,
    )
    y_near = lax.ppermute(y_near, "gy", near(gy))
    y_far = lax.ppermute(y_far, "gy", far(gy))
    x_near = lax.ppermute(x_near, "gx", near(gx))
    x_far = lax.ppermute(x_far, "gx", far(gx))
    yr, yl = jnp.where(even_y, y_near, y_far), jnp.where(even_y, y_far, y_near)
    half = STRIP // 2
    head = jnp.concatenate([yl[:half], yl[STRIP:], yr[:half], yr[STRIP:]])
    tail = jnp.concatenate([yl[half:], yr[half:]])
    c_near = lax.ppermute(jnp.where(even_x, tail, head), "gx", near(gx))
    c_far = lax.ppermute(jnp.where(even_x, head, tail), "gx", far(gx))
    copies, c_near = lax.optimization_barrier((copies, c_near))
    corner_r, corner_l = jnp.where(even_x, c_near, c_far), jnp.where(even_x, c_far, c_near)
    cores = [[x * gy + y for x in range(core, gx, 2) for y in range(gy)] for core in range(2)]
    blocks = copies.reshape(devices // 2, SHARE, 128)
    own = lax.all_to_all(blocks, ("gx", "gy"), 0, 0, axis_index_groups=cores).reshape(gx // 2, gy * SHARE, 128)
    level = lambda rows, n: [vm(NZ * rows, 128)] * n
    faces = lambda rows, tiles: vm(tiles * (NZ + 1) * rows, 128)
    rows3, rows4 = 2 * gx, gx
    size, tall = (NZ * TX, 128), ((NZ + 1) * TX, 128)
    k2 = call(
        window_kernel, "window_coeffs", [(NZ * TX * 4 + TX, 128)], [share2, x_near, x_far, yr, yl, corner_r, corner_l], level(TX, 7)
    )[0]
    big, big_z = (2 * NZ * 2 * TX, 128), (2 * (NZ + 1) * 2 * TX, 128)
    total0, total1 = 2 * (NZ * 6 + 1) * 2 * TX, (NZ * 6 + 1) * TX
    sends, saved = call(
        functools.partial(down_kernel, gx * TX, gy * TY),
        "down",
        [(devices // 2 * BLOCK, 128), (max(total0 + total1, SAVED_ROWS), 128)],
        [stack, yr, yl, corner_r, corner_l, x_near, x_far],
        [vm(*big)] * 10 + [vm(*big_z)] + level(TX, 10) + [faces(TX, 1)] + level(8, 10) + [faces(8, 1)] + [dma(12)],
        out_specs=[VMEM, ANY],
    )
    sends, own = lax.optimization_barrier((sends, own))
    other = lax.ppermute(own, "gx", near(gx))
    blocks = sends.reshape(devices // 2, BLOCK, 128)
    own_blocks = lax.all_to_all(blocks, ("gx", "gy"), 0, 0, axis_index_groups=cores)
    other_blocks = lax.ppermute(own_blocks, "gx", near(gx))
    whole = call(
        functools.partial(global_kernel, gx, gy),
        "global_coeffs",
        [(5 * NZ * (rows3 + rows4), 128)],
        [own, other],
        level(rows3, 6) + [faces(rows3, 1)] + level(rows3, 1) + level(rows4, 6) + [faces(rows4, 1)] + level(rows4, 1)
        + [vm(gx // 2, 2, gy * SHARE, 128), dma(2)],
        in_specs=[ANY] * 2,
    )[0]
    field, residual = call(
        functools.partial(up_kernel, gx, gy),
        "up",
        [(NZ * TX, TY)] * 2,
        [own_blocks, other_blocks, whole, k2, stack, saved],
        [vm(total0, 128), vm(total1, 128)] + level(TX, 3) + [vm(NZ * 2 * TX, 128), vm(*size), vm(*big), vm(*big)]
        + level(rows3, 3) + level(rows4, 2) + [dma(2)],
        in_specs=[VMEM] * 5 + [ANY],
    )
    return field.reshape(right_side.shape), residual.reshape(right_side.shape)


def solution(mesh):
    spec = P(None, "gx", "gy")
    fits = (mesh.shape["gx"], mesh.shape["gy"]) == (8, 4)
    plan = body if fits else spread_body
    return jax.shard_map(plan, mesh=mesh, in_specs=(spec,) * 5, out_specs=(spec, spec), check_vma=False)
```
